32 devices in a mesh: head: 2 (over core), seq: 16 (over z, y, x).
Axes of the slice: x: 2, y: 2, z: 4, core: 2. Of those that a mesh axis runs over, the one named last changes fastest.
Arguments:
- inputs: bfloat16 [2, 4096, 1152], P('head', 'seq'), may hold values from -6 to 6
- cotangent: bfloat16 [2, 4096, 1152], P('head', 'seq'), may hold values from -6 to 6
- teacher: bfloat16 [2, 4096, 1152], P('head', 'seq'), may hold values from -6 to 6
- segments: int32 [2, 4096], replicated, may hold values from 0 to 3, as said below
- valid_mask: int32 [2, 4096], P('head', 'seq'), may hold values from 0 to 1, as said below
- w_qkv: float32 [2, 1152, 1536], P(None, 'seq', 'head'), may hold values from -0.1875 to 0.1875
- w_out: float32 [2, 1024, 1152], P(None, 'seq', 'head'), may hold values from -0.1875 to 0.1875
- w_gu: float32 [2, 1152, 13824], P(None, 'seq', 'head'), may hold values from -0.1875 to 0.1875
- w_down: float32 [2, 6912, 1152], P(None, 'seq', 'head'), may hold values from -0.078125 to 0.078125
- norm_gains: float32 [2, 2, 2560], P(None, 'head', 'seq'), may hold values from 0.5 to 1.5
- mom_qkv: float32 [2, 1152, 1536], P(None, 'seq', 'head')
- mom_out: float32 [2, 1024, 1152], P(None, 'seq', 'head')
- mom_gu: float32 [2, 1152, 13824], P(None, 'seq', 'head')
- mom_down: float32 [2, 6912, 1152], P(None, 'seq', 'head')
- gain_first: float32 [2, 2, 2560], P(None, 'head', 'seq'), may hold values from -2275.5556 to 2275.5556
- gain_second: float32 [2, 2, 2560], P(None, 'head', 'seq'), may hold values from 431.1579 to 3532045.5
Outputs:
- mse_loss: float32 [], replicated
- layer_output: float32 [2, 4096, 1152], P('head', 'seq')
- input_grad: float32 [2, 4096, 1152], P('head', 'seq')
- qkv_new: float32 [2, 1152, 1536], P(None, 'seq', 'head')
- out_new: float32 [2, 1024, 1152], P(None, 'seq', 'head')
- gate_up_new: float32 [2, 1152, 13824], P(None, 'seq', 'head')
- down_new: float32 [2, 6912, 1152], P(None, 'seq', 'head')
- qkv_moment: float32 [2, 1152, 1536], P(None, 'seq', 'head')
- out_moment: float32 [2, 1024, 1152], P(None, 'seq', 'head')
- gate_up_moment: float32 [2, 1152, 13824], P(None, 'seq', 'head')
- down_moment: float32 [2, 6912, 1152], P(None, 'seq', 'head')
- gains_new: float32 [2, 2, 2560], P(None, 'head', 'seq')
- gain_first_new: float32 [2, 2, 2560], P(None, 'head', 'seq')
- gain_second_new: float32 [2, 2, 2560], P(None, 'head', 'seq')
The draws below stay inside these ranges and needn't reach their ends.
Inputs may be any that keep to these rules, and one draw needn't show every extreme that they name: `segments`: along each sequence the ids start at 0 and never fall; a document is a run of equal ids. In every draw one sequence is one document from end to end, and every other sequence holds exactly four documents, ids 0 to 3. `valid_mask`: the last position of every sequence is valid.
All inputs are finite; a program needn't handle non-finite values.
Results may differ from the reference program's by a relative error of at most 0.02.
The reference program's roundings to bfloat16 on the way count: a program that leaves them out, or rounds other values in their place, can miss the bound.
Values may be sent and summed in bfloat16 or wider, within the bound.
A program may use at most 512 MiB of HBM per device.

```python
import math
import jax
import jax.numpy as jnp
from jax import lax

D = 1152
HEADS = 4
HD = 256
FF = 6912
WINDOW = 512
LAYERS = 2
NS_ITERS = 5
STEP = 10
SEQ_LEN = 4096
Q_WIDTH = 1024
QKV_WIDTH = 1536
GAIN_LEN = 2560
SEQS = 2
TOKENS = 8192
LOSS_WEIGHT = 2359296
N_SEQ = 16


def draw_segments(key, part):
    key = jax.random.fold_in(key, 11)
    start_key, pick_key = jax.random.split(key)
    places = jnp.arange(SEQ_LEN, dtype=jnp.int32)[None, :]
    logit_scores = jax.random.randint(start_key, (SEQS, SEQ_LEN), 0, 2 ** 18) * SEQ_LEN + places
    logit_scores = jnp.where(places > 0, logit_scores, -1)
    third = lax.top_k(logit_scores, 3)[0][:, 2:3]
    whole = jax.random.randint(pick_key, (), 0, SEQS)
    seq_rank = jnp.arange(SEQS, dtype=jnp.int32)[:, None]
    starts = (logit_scores >= third) & (seq_rank != whole) & (places > 0)
    return jnp.cumsum(starts.astype(jnp.int32), axis=1).astype(jnp.int32)


def draw_valid_mask(key, part):
    key = jax.random.fold_in(key, 12)
    seq_rank = jnp.arange(SEQS, dtype=jnp.int32)[:, None]
    places = jnp.arange(SEQ_LEN, dtype=jnp.int32)[None, :]
    along = 20 + places * 44 // SEQ_LEN
    across = 24 + seq_rank * 40 // max(SEQS - 1, 1)
    drawn = jax.random.randint(key, (SEQS, SEQ_LEN), 0, 4096)
    chosen = (drawn < along * across) | (places == SEQ_LEN - 1)
    return chosen.astype(jnp.int32)


def shaped(base, rise):
    columns = base.shape[-1]
    ramp = 1.0 + rise * jnp.arange(columns, dtype=jnp.float32) / columns
    return base * ramp * TOKENS ** 0.5 / (1.0 + 0.5 * rise)


def draw_mom_qkv(key, part):
    key = jax.random.fold_in(key, 21)
    shape = (LAYERS, D, HEADS * HD + 2 * HD)
    return shaped(jnp.clip(jax.random.normal(key, shape, jnp.float32), -5.0, 5.0), 2.0)


def draw_mom_out(key, part):
    key = jax.random.fold_in(key, 22)
    shape = (LAYERS, HEADS * HD, D)
    return shaped(jnp.clip(jax.random.normal(key, shape, jnp.float32), -5.0, 5.0), 2.0)


def draw_mom_gu(key, part):
    key = jax.random.fold_in(key, 23)
    shape = (LAYERS, D, 2 * FF)
    return shaped(jnp.clip(jax.random.normal(key, shape, jnp.float32), -5.0, 5.0), 2.0)


def draw_mom_down(key, part):
    key = jax.random.fold_in(key, 24)
    shape = (LAYERS, FF, D)
    return shaped(jnp.clip(jax.random.normal(key, shape, jnp.float32), -5.0, 5.0), 2.0)


def gain_kind_scale():
    columns = jnp.arange(2 * D + HD, dtype=jnp.int32)
    outer = (columns >= D) & (columns < 2 * D)
    return jnp.where(outer, 0.5 * TOKENS, TOKENS ** 0.5).astype(jnp.float32)


def draw_gain_first(key, part):
    key = jax.random.fold_in(key, 31)
    shape = (LAYERS, 2, 2 * D + HD)
    base = jnp.clip(jax.random.normal(key, shape, jnp.float32), -5.0, 5.0)
    return base * gain_kind_scale() / 9.0


def draw_gain_second(key, part):
    key = jax.random.fold_in(key, 32)
    shape = (LAYERS, 2, 2 * D + HD)
    factor = jnp.exp(jax.random.uniform(key, shape, jnp.float32, 0.0, math.log(4.0)))
    scale = gain_kind_scale()
    return factor * scale * scale / 19.0


def block_scale(stream_key, extent, cuts, smallest, high):
    def one(dim, shards_of):
        steps = jax.random.uniform(jax.random.fold_in(jax.random.fold_in(stream_key, 6), dim), (shards_of,), jnp.float32, smallest / len(cuts), high / len(cuts))
        return jnp.repeat(jnp.exp(steps), extent[dim] // shards_of).reshape((-1,) + (1,) * (len(extent) - dim - 1))

    level = one(*cuts[0])
    for cut in cuts[1:]:
        level = level * one(*cut)
    return level


def bell_draw(key, extent, deviation, most, cuts=(), kind=jnp.bfloat16):
    result = deviation * jax.random.normal(key, extent, jnp.float32)
    if cuts:
        result = result * block_scale(key, extent, cuts, -0.22, 0.18)
    return jnp.clip(result, -most, most).astype(kind)


def setup_inputs(seed: int = 0) -> dict:
    key_of = jax.random.split(jax.random.key(seed), 17)
    return {
        "inputs": bell_draw(key_of[0], (SEQS, SEQ_LEN, D), 1.0, 6.0, ((0, 2), (1, 16))),
        "cotangent": bell_draw(key_of[1], (SEQS, SEQ_LEN, D), 1.0, 6.0, ((0, 2), (1, 16))),
        "teacher": bell_draw(key_of[2], (SEQS, SEQ_LEN, D), 1.0, 6.0, ((0, 2), (1, 16))),
        "segments": draw_segments(jax.random.fold_in(key_of[16], 71), 0),
        "valid_mask": draw_valid_mask(jax.random.fold_in(key_of[16], 71), 0),
        "w_qkv": bell_draw(key_of[5], (LAYERS, D, QKV_WIDTH), D ** -0.5, 0.1875, ((1, 16), (2, 2)), jnp.float32),
        "w_out": bell_draw(key_of[6], (LAYERS, Q_WIDTH, D), Q_WIDTH ** -0.5, 0.1875, ((1, 16), (2, 2)), jnp.float32),
        "w_gu": bell_draw(key_of[7], (LAYERS, D, 2 * FF), D ** -0.5, 0.1875, ((1, 16), (2, 2)), jnp.float32),
        "w_down": bell_draw(key_of[8], (LAYERS, FF, D), FF ** -0.5, 0.078125, ((1, 16), (2, 2)), jnp.float32),
        "norm_gains": jnp.clip(1.0 + 0.1 * jax.random.normal(key_of[9], (LAYERS, 2, GAIN_LEN), jnp.float32), 0.5, 1.5),
        "mom_qkv": draw_mom_qkv(jax.random.fold_in(key_of[16], 71), 0),
        "mom_out": draw_mom_out(jax.random.fold_in(key_of[16], 71), 0),
        "mom_gu": draw_mom_gu(jax.random.fold_in(key_of[16], 71), 0),
        "mom_down": draw_mom_down(jax.random.fold_in(key_of[16], 71), 0),
        "gain_first": draw_gain_first(jax.random.fold_in(key_of[16], 71), 0),
        "gain_second": draw_gain_second(jax.random.fold_in(key_of[16], 71), 0),
    }


@jax.custom_vjp
def reduced_precision(v):
    return lax.optimization_barrier(v.astype(jnp.bfloat16)).astype(jnp.float32)

@jax.custom_vjp
def reduced_backward(v):
    return v

def low_keep(v):
    return (reduced_precision(v), None)

def low_pass(kept, grad):
    return (grad,)

def back_keep(v):
    return (v, None)

def back_low(kept, grad):
    return (reduced_precision(grad),)
reduced_precision.defvjp(low_keep, low_pass)
reduced_backward.defvjp(back_keep, back_low)
norm_eps = 1e-06
rope_base = 10000.0
newton_one = 3.4445
newton_two = -4.775
newton_three = 2.0315
muon_decay = 0.95
muon_rate = 0.15
muon_shrink = 0.01
muon_scale = 0.2
beta_one = 0.9
beta_two = 0.95
adam_rate = 0.7
adam_epsilon = 1e-08
finest_precision = lax.Precision.HIGHEST

def rms_norm(values, norm_gain):
    return values * lax.rsqrt(lax.optimization_barrier(jnp.mean(values * values, axis=-1, keepdims=True)) + norm_eps) * norm_gain

def rope_tables(positions, head_dim):
    half_dim = head_dim // 2
    frequency = jnp.exp(jnp.arange(half_dim, dtype=jnp.float32) * (-2.0 * math.log(rope_base) / head_dim))
    angles = positions.astype(jnp.float32)[:, None] * frequency[None, :]
    return (jnp.cos(angles), jnp.sin(angles))

def rotate(values, cosine_table, sine_table):
    half_dim = values.shape[-1] // 2
    lower_half = values[..., :half_dim]
    upper_half = values[..., half_dim:]
    return jnp.concatenate([lower_half * cosine_table - upper_half * sine_table, upper_half * cosine_table + lower_half * sine_table], axis=-1)

def attention(queries, key_heads, values, segments):
    seq_count = segments.shape[0]
    seq_length = segments.shape[1]
    block_rows = min(512, seq_length)
    padded_keys = jnp.pad(key_heads, ((0, 0), (WINDOW, 0), (0, 0)))
    padded_values = jnp.pad(values, ((0, 0), (WINDOW, 0), (0, 0)))
    padded_segments = jnp.pad(segments, ((0, 0), (WINDOW, 0)), constant_values=-1)
    logit_scale = 1.0 / math.sqrt(HD)

    def one_block(block_start):
        tiled_query_rows = lax.dynamic_slice_in_dim(queries, block_start, block_rows, 1)
        tiled_key_rows = lax.dynamic_slice_in_dim(padded_keys, block_start, block_rows + WINDOW, 1)
        tiled_value_rows = lax.dynamic_slice_in_dim(padded_values, block_start, block_rows + WINDOW, 1)
        query_segments = lax.dynamic_slice_in_dim(segments, block_start, block_rows, 1)
        key_segments = lax.dynamic_slice_in_dim(padded_segments, block_start, block_rows + WINDOW, 1)
        query_places = block_start + jnp.arange(block_rows, dtype=jnp.int32)
        key_places = block_start - WINDOW + jnp.arange(block_rows + WINDOW, dtype=jnp.int32)
        spacing = query_places[:, None] - key_places[None, :]
        allowed = (spacing >= 0) & (spacing < WINDOW) & (key_places[None, :] >= 0)
        allowed = allowed[None] & (query_segments[:, :, None] == key_segments[:, None, :])
        logit_scores = reduced_backward(jnp.einsum('njgp,ncp->ngjc', tiled_query_rows, tiled_key_rows, precision=finest_precision) * logit_scale)
        logit_scores = jnp.where(allowed[:, None], logit_scores, -jnp.inf)
        attention_weights_soft = jax.nn.softmax(logit_scores, axis=-1)
        return jnp.einsum('asiz,azc->aisc', reduced_precision(attention_weights_soft), tiled_value_rows, precision=finest_precision)
    starts = (jnp.arange(seq_length // block_rows) * block_rows).astype(jnp.int32)
    blocks = lax.map(jax.checkpoint(one_block), starts)
    return jnp.moveaxis(blocks, 0, 1).reshape(seq_count, seq_length, queries.shape[2], queries.shape[3])

def one_layer(hidden, params, cosine_table, sine_table, segments):
    w_mixed, w_project, w_gate_up, w_down_proj, gain_pack = params
    norm_attn = gain_pack[0, :D]
    post_attn = gain_pack[0, D:2 * D]
    query_gain = gain_pack[0, 2 * D:]
    norm_ffn = gain_pack[1, :D]
    post_ffn = gain_pack[1, D:2 * D]
    key_gain = gain_pack[1, 2 * D:]
    seq_count = hidden.shape[0]
    seq_length = hidden.shape[1]
    normed = reduced_precision(rms_norm(hidden, norm_attn))
    mixed_proj = reduced_backward(jnp.einsum('bld,de->ble', normed, w_mixed, precision=finest_precision))
    queries = mixed_proj[..., :HEADS * HD].reshape(seq_count, seq_length, HEADS, HD)
    key_heads = mixed_proj[..., HEADS * HD:HEADS * HD + HD]
    values = reduced_precision(mixed_proj[..., HEADS * HD + HD:])
    queries = reduced_precision(rotate(rms_norm(queries, query_gain), cosine_table[:, None, :], sine_table[:, None, :]))
    key_heads = reduced_precision(rotate(rms_norm(key_heads, key_gain), cosine_table, sine_table))
    attended = attention(queries, key_heads, values, segments)
    attended = reduced_precision(reduced_backward(attended)).reshape(seq_count, seq_length, HEADS * HD)
    projected = reduced_backward(jnp.einsum('blq,qd->bld', attended, w_project, precision=finest_precision))
    hidden = hidden + rms_norm(projected, post_attn)
    normed = reduced_precision(rms_norm(hidden, norm_ffn))
    gate_up = reduced_backward(jnp.einsum('bld,de->ble', normed, w_gate_up, precision=finest_precision))
    inner_act = reduced_precision(jax.nn.gelu(gate_up[..., :FF], approximate=True) * gate_up[..., FF:])
    down_out = reduced_backward(jnp.einsum('blf,fd->bld', inner_act, w_down_proj, precision=finest_precision))
    return hidden + rms_norm(down_out, post_ffn)

def orthogonal(block_rows):
    present_iterate = block_rows / (jnp.sqrt(jnp.sum(block_rows * block_rows)) + 1e-07)
    for iteration in range(NS_ITERS):
        gram_matrix = jnp.dot(present_iterate, present_iterate.T, precision=finest_precision)
        polynomial = newton_two * gram_matrix + newton_three * jnp.dot(gram_matrix, gram_matrix, precision=finest_precision)
        present_iterate = newton_one * present_iterate + jnp.dot(polynomial, present_iterate, precision=finest_precision)
    return present_iterate

def muon_step(weight, moment, gradient):
    new_moment = muon_decay * moment + gradient
    layer_count = weight.shape[0]
    row_count = weight.shape[1]
    columns = weight.shape[2]
    blocks = new_moment.reshape(layer_count * N_SEQ, row_count // N_SEQ, columns)
    orthogonalized = jax.vmap(orthogonal)(blocks).reshape(layer_count, row_count, columns)
    new_weight = weight * (1.0 - muon_rate * muon_shrink) - muon_rate * muon_scale * math.sqrt(columns) * orthogonalized
    return (new_weight, new_moment)

def reference(inputs, cotangent, teacher, segments, valid_mask, w_qkv, w_out, w_gu, w_down, norm_gains, mom_qkv, mom_out, mom_gu, mom_down, gain_first, gain_second):
    cosine_table, sine_table = rope_tables(jnp.arange(SEQ_LEN, dtype=jnp.int32), HD)
    valid_weight = valid_mask.astype(jnp.float32)
    valid_count = jnp.sum(valid_weight)
    target = teacher.astype(jnp.float32)

    def forward(inputs_f, matrices):
        hidden = inputs_f
        for layer_index in range(LAYERS):
            params = tuple((reduced_precision(matrix[layer_index]) for matrix in matrices))
            hidden = one_layer(hidden, params, cosine_table, sine_table, segments)
        difference = hidden - target
        loss_value = jnp.sum(valid_weight[:, :, None] * difference * difference) / (valid_count * D)
        return (hidden, loss_value)
    matrices = (w_qkv, w_out, w_gu, w_down, norm_gains)
    (layer_output, mse_loss), pullback = jax.vjp(forward, inputs.astype(jnp.float32), matrices)
    input_grad, grads = pullback((cotangent.astype(jnp.float32), jnp.asarray(float(LOSS_WEIGHT), dtype=jnp.float32)))
    qkv_new, qkv_moment = muon_step(w_qkv, mom_qkv, grads[0])
    out_new, out_moment = muon_step(w_out, mom_out, grads[1])
    gate_up_new, gate_up_moment = muon_step(w_gu, mom_gu, grads[2])
    down_new, down_moment = muon_step(w_down, mom_down, grads[3])
    gain_grad = grads[4]
    gain_first_new = beta_one * gain_first + (1.0 - beta_one) * gain_grad
    gain_second_new = beta_two * gain_second + (1.0 - beta_two) * gain_grad * gain_grad
    gains_new = norm_gains - adam_rate * (gain_first_new / (1.0 - beta_one ** STEP)) / (jnp.sqrt(gain_second_new / (1.0 - beta_two ** STEP)) + adam_epsilon)
    return (mse_loss, layer_output, input_grad, qkv_new, out_new, gate_up_new, down_new, qkv_moment, out_moment, gate_up_moment, down_moment, gains_new, gain_first_new, gain_second_new)
```

```python
from functools import partial
import itertools
import math

import jax
import jax.numpy as jnp
from jax import lax
from jax.experimental import pallas as pl
from jax.experimental.pallas import tpu as pltpu
from jax.sharding import Mesh, PartitionSpec as P

D = 1152
HEADS = 4
HD = 256
FF = 6912
WINDOW = 512
LAYERS = 2
NS_ITERS = 5
STEP = 10
PLANE = 4

norm_eps = 1e-06
rope_base = 10000.0
newton_one = 3.4445
newton_two = -4.775
newton_three = 2.0315
muon_decay = 0.95
muon_rate = 0.15
muon_shrink = 0.01
muon_scale = 0.2
beta_one = 0.9
beta_two = 0.95
adam_rate = 0.7
adam_epsilon = 1e-08
finest_precision = lax.Precision.HIGHEST
MESH = pl.DeviceIdType.MESH
SEQ = ("zd", "tp")
GROUP = ("head", "tp")
EVERY = ("head", "zd", "tp")
bf16 = jnp.bfloat16
f32 = jnp.float32


def linear(places, sizes):
    index = 0
    for place, size in zip(places, sizes):
        index = index * size + place
    return index


def enter(partners):
    barrier = pltpu.get_barrier_semaphore()
    for partner in partners:
        pl.semaphore_signal(barrier, inc=1, device_id=partner, device_id_type=MESH)
    pl.semaphore_wait(barrier, len(partners))


def exchange_kernel(axes, sizes, count, gather, *refs):
    sources, results = refs[:count], refs[count : 2 * count]
    send_sem, recv_sem, own_sem = refs[2 * count :]
    mine = [lax.axis_index(axis) for axis in axes]
    me = linear(mine, sizes)
    offsets = list(itertools.product(*[range(size) for size in sizes]))[1:]
    partners = []
    for offset in offsets:
        places = [lax.rem(m + o, s) for m, o, s in zip(mine, offset, sizes)]
        partners.append((dict(zip(axes, places)), linear(places, sizes)))
    enter([device for device, _ in partners])
    copies = []
    for step, (device, index) in enumerate(partners):
        for k in range(count):
            copy = pltpu.make_async_remote_copy(
                src_ref=sources[k] if gather else sources[k].at[index],
                dst_ref=results[k].at[me],
                send_sem=send_sem.at[k, step],
                recv_sem=recv_sem.at[k, step],
                device_id=device,
                device_id_type=MESH,
            )
            copy.start()
            copies.append(copy)
    for k in range(count):
        own = pltpu.make_async_copy(
            sources[k] if gather else sources[k].at[me], results[k].at[me], own_sem.at[k]
        )
        own.start()
        copies.append(own)
    for copy in copies:
        copy.wait()


def exchange(arrays, axes, ident, gather=False):
    sizes = tuple(lax.axis_size(axis) for axis in axes)
    members = math.prod(sizes)
    count = len(arrays)
    shapes = [((members,) + a.shape) if gather else a.shape for a in arrays]
    return pl.pallas_call(
        partial(exchange_kernel, axes, sizes, count, gather),
        out_shape=[jax.ShapeDtypeStruct(s, a.dtype) for s, a in zip(shapes, arrays)],
        in_specs=[pl.BlockSpec(memory_space=pl.ANY)] * count,
        out_specs=[pl.BlockSpec(memory_space=pl.ANY)] * count,
        scratch_shapes=[
            pltpu.SemaphoreType.DMA((count, members - 1)),
            pltpu.SemaphoreType.DMA((count, members - 1)),
            pltpu.SemaphoreType.DMA((count,)),
        ],
        compiler_params=pltpu.CompilerParams(collective_id=ident, has_side_effects=True),
    )(*arrays)


def shift_kernel(planes, reach, back, source, result, send_sem, recv_sem):
    place = linear([lax.axis_index("zd"), lax.axis_index("tp")], (planes, PLANE))
    total = planes * PLANE
    sign = -1 if back else 1
    to, sources = [], []
    for distance in range(1, reach + 1):
        there = lax.rem(place + sign * distance + total, total)
        to.append({"zd": there // PLANE, "tp": lax.rem(there, PLANE)})
        here = lax.rem(place - sign * distance + total, total)
        sources.append({"zd": here // PLANE, "tp": lax.rem(here, PLANE)})
    barrier = pltpu.get_barrier_semaphore()
    for device in to + sources:
        pl.semaphore_signal(barrier, inc=1, device_id=device, device_id_type=MESH)
    pl.semaphore_wait(barrier, 2 * reach)
    copies = []
    for k, device in enumerate(to):
        copy = pltpu.make_async_remote_copy(
            src_ref=source.at[k] if back else source,
            dst_ref=result.at[k],
            send_sem=send_sem.at[k],
            recv_sem=recv_sem.at[k],
            device_id=device,
            device_id_type=MESH,
        )
        copy.start()
        copies.append(copy)
    for copy in copies:
        copy.wait()


def shift(array, planes, reach, back, ident):
    shape = array.shape if back else (reach,) + array.shape
    return pl.pallas_call(
        partial(shift_kernel, planes, reach, back),
        out_shape=jax.ShapeDtypeStruct(shape, array.dtype),
        in_specs=[pl.BlockSpec(memory_space=pl.ANY)],
        out_specs=pl.BlockSpec(memory_space=pl.ANY),
        scratch_shapes=[pltpu.SemaphoreType.DMA((reach,)), pltpu.SemaphoreType.DMA((reach,))],
        compiler_params=pltpu.CompilerParams(collective_id=ident, has_side_effects=True),
    )(array)


def padded(array, multiple=16):
    extra = -array.shape[-2] % multiple
    if extra == 0:
        return array
    return jnp.pad(array, [(0, 0)] * (array.ndim - 2) + [(0, extra), (0, 0)])


def rms_norm(values, norm_gain):
    return (
        values * lax.rsqrt(jnp.mean(values * values, axis=-1, keepdims=True) + norm_eps) * norm_gain
    )


def rope_tables(positions, head_dim):
    half_dim = head_dim // 2
    frequency = jnp.exp(
        jnp.arange(half_dim, dtype=jnp.float32) * (-2.0 * math.log(rope_base) / head_dim)
    )
    angles = positions.astype(jnp.float32)[:, None] * frequency[None, :]
    return (jnp.cos(angles), jnp.sin(angles))


def rotate(values, cosine_table, sine_table):
    half_dim = values.shape[-1] // 2
    lower_half = values[..., :half_dim]
    upper_half = values[..., half_dim:]
    return jnp.concatenate(
        [
            lower_half * cosine_table - upper_half * sine_table,
            upper_half * cosine_table + lower_half * sine_table,
        ],
        axis=-1,
    )


def head_prep(mixed_proj, query_gain, key_gain, cosine_table, sine_table):
    seq_rows = mixed_proj.shape[0]
    place_rows = mixed_proj.shape[1]
    queries = mixed_proj[..., : HEADS * HD].reshape(seq_rows, place_rows, HEADS, HD)
    key_heads = mixed_proj[..., HEADS * HD : HEADS * HD + HD]
    values = mixed_proj[..., HEADS * HD + HD :]
    queries = rotate(
        rms_norm(queries, query_gain), cosine_table[:, None, :], sine_table[:, None, :]
    )
    key_heads = rotate(rms_norm(key_heads, key_gain), cosine_table, sine_table)
    return (queries, jnp.concatenate([key_heads, values], axis=-1))


def geglu(gate, up):
    return jax.nn.gelu(gate, approximate=True) * up


def attend_scores(query_rows, key_tile_rows, allowed):
    logit_scores = jnp.einsum(
        "tals,tes->tlae", query_rows, key_tile_rows, preferred_element_type=jnp.float32
    ) * (1.0 / math.sqrt(HD))
    return jnp.where(allowed[:, None], logit_scores, -jnp.inf)


def matmul(left, right):
    return jnp.dot(left, right, preferred_element_type=f32)


def exact(spec, left, right):
    return jnp.einsum(spec, left, right, precision=finest_precision)


def newton_factor(gram):
    scale = 1.0 / (jnp.sqrt(jnp.trace(gram, axis1=-2, axis2=-1)) + 1e-07)
    scale = scale[..., None, None]
    present = gram * (scale * scale)
    unit = jnp.eye(gram.shape[-1], dtype=f32)
    product = None
    for iteration in range(NS_ITERS):
        square = exact("...rs,...st->...rt", present, present)
        factor = newton_one * unit + newton_two * present + newton_three * square
        product = factor if product is None else exact("...rs,...st->...rt", factor, product)
        if iteration < NS_ITERS - 1:
            present = exact(
                "...rs,...st->...rt", exact("...rs,...st->...rt", factor, present), factor
            )
    return product * scale


def body(
    inputs,
    cotangent,
    teacher,
    segments,
    valid_mask,
    w_qkv,
    w_out,
    w_gu,
    w_down,
    norm_gains,
    mom_qkv,
    mom_out,
    mom_gu,
    mom_down,
    gain_first,
    gain_second,
):
    cores = lax.axis_size("head")
    planes = lax.axis_size("zd")
    seq_devices = planes * PLANE
    core = lax.axis_index("head")
    seq_place = lax.axis_index("zd") * PLANE + lax.axis_index("tp")
    half_seqs, stretch_len = inputs.shape[:2]
    tokens = half_seqs * stretch_len
    all_seqs = half_seqs * cores
    seq_length = stretch_len * seq_devices
    reach = -(-WINDOW // stretch_len)
    key_len = (reach + 1) * stretch_len
    qkv_rows, qkv_cols = w_qkv.shape[1:]
    out_rows, out_cols = w_out.shape[1:]
    gu_rows = w_gu.shape[1]
    ff_block = w_down.shape[1]
    share = FF // (cores * PLANE)
    half_planes = planes // cores
    gain_cols = norm_gains.shape[-1]
    gain_len = gain_cols * seq_devices
    lanes = -(-gain_cols // 128) * 128

    packet = jnp.zeros((8, lanes), f32)
    packet = packet.at[:LAYERS, :gain_cols].set(norm_gains[:, 0].astype(bf16).astype(f32))
    packet = packet.at[LAYERS, 0].set(jnp.sum(valid_mask.astype(f32)))
    (packets,) = exchange([packet], EVERY, 0, gather=True)
    packets = packets.reshape(cores, seq_devices, 8, lanes)
    valid_count = jnp.sum(packets[:, :, LAYERS, 0])
    gain_rows = [
        packets[:, :, layer, :gain_cols].reshape(cores, gain_len) for layer in range(LAYERS)
    ]

    full = []
    for layer in range(LAYERS):
        w_mixed = lax.all_gather(w_qkv[layer].astype(bf16), SEQ, axis=0, tiled=True)
        w_project = lax.all_gather(w_out[layer].astype(bf16), SEQ, axis=0, tiled=True)
        pieces = w_gu[layer].astype(bf16).reshape(gu_rows, cores, half_planes, PLANE, ff_block)
        pieces = pieces.transpose(1, 3, 0, 2, 4).reshape(cores * PLANE, gu_rows, share)
        (pieces,) = exchange([padded(pieces)], GROUP, 1 + layer)
        pieces = lax.all_gather(pieces, "zd", axis=0)
        pieces = pieces.reshape(planes, cores, PLANE, -1, share)[:, :, :, :gu_rows]
        w_gate_up = pieces.transpose(1, 0, 2, 3, 4).reshape(2, D, share)
        rows = lax.all_gather(w_down[layer].astype(bf16), "zd", axis=0)
        rows = rows.reshape(cores, half_planes * ff_block, out_cols)
        rows = lax.all_to_all(rows, "head", split_axis=0, concat_axis=0, tiled=True)
        w_down_share = rows.transpose(1, 0, 2).reshape(share, D)
        w_mixed = lax.all_gather(w_mixed, "head", axis=1, tiled=True)
        w_project = lax.all_gather(w_project, "head", axis=1, tiled=True)
        full.append((w_mixed, w_project, w_gate_up, w_down_share))

    own_places = seq_place * stretch_len + jnp.arange(stretch_len, dtype=jnp.int32)
    key_places = (seq_place - reach) * stretch_len + jnp.arange(key_len, dtype=jnp.int32)
    cosine_table, sine_table = rope_tables(own_places, HD)
    own_rows = lax.dynamic_slice_in_dim(segments, core * half_seqs, half_seqs, 0)
    own_segments = lax.dynamic_slice_in_dim(own_rows, seq_place * stretch_len, stretch_len, 1)
    padded_segments = jnp.pad(own_rows, ((0, 0), (reach * stretch_len, 0)), constant_values=-1)
    key_segments = lax.dynamic_slice_in_dim(padded_segments, seq_place * stretch_len, key_len, 1)
    spacing = own_places[:, None] - key_places[None, :]
    allowed = (spacing >= 0) & (spacing < WINDOW) & (key_places[None, :] >= 0)
    allowed = allowed[None] & (own_segments[:, :, None] == key_segments[:, None, :])

    hidden = inputs.astype(f32)
    saved = []
    for layer in range(LAYERS):
        w_mixed, w_project, w_gate_up, w_down_share = full[layer]
        gain_pack = gain_rows[layer]
        norm_attn = gain_pack[0, :D]
        post_attn = gain_pack[0, D : 2 * D]
        query_gain = gain_pack[0, 2 * D :]
        norm_ffn = gain_pack[1, :D]
        post_ffn = gain_pack[1, D : 2 * D]
        key_gain = gain_pack[1, 2 * D :]
        normed_f, pre_attn_back = jax.vjp(rms_norm, hidden, norm_attn)
        normed = normed_f.astype(bf16)
        mixed_proj = jnp.einsum("bpd,de->bpe", normed, w_mixed, preferred_element_type=f32)
        prepared, prep_back = jax.vjp(
            partial(head_prep, cosine_table=cosine_table, sine_table=sine_table),
            mixed_proj,
            query_gain,
            key_gain,
        )
        query_rows = prepared[0].astype(bf16)
        own_keyvals = prepared[1].astype(bf16)
        earlier = shift(
            own_keyvals.reshape(tokens, 2 * HD), planes, reach, False, 3 + layer
        ).reshape(reach, half_seqs, stretch_len, 2 * HD)
        keyvals = jnp.concatenate(
            [earlier[reach - 1 - k] for k in range(reach)] + [own_keyvals], axis=1
        )
        key_tile_rows = keyvals[..., :HD]
        value_tile_rows = keyvals[..., HD:]
        logit_scores = attend_scores(query_rows, key_tile_rows, allowed)
        log_total = jax.nn.logsumexp(logit_scores, axis=-1)
        soft = jnp.exp(logit_scores - log_total[..., None])
        attended = jnp.einsum(
            "zusi,zix->zsux", soft.astype(bf16), value_tile_rows, preferred_element_type=f32
        ).astype(bf16)
        attended_rows = attended.reshape(half_seqs, stretch_len, HEADS * HD)
        projected = jnp.einsum("bpq,qd->bpd", attended_rows, w_project, preferred_element_type=f32)
        branch_out, post_attn_back = jax.vjp(rms_norm, projected, post_attn)
        hidden_half = hidden + branch_out
        normed_f, pre_ffn_back = jax.vjp(rms_norm, hidden_half, norm_ffn)
        (group_normed,) = exchange(
            [normed_f.astype(bf16).reshape(tokens, D)], GROUP, 5 + layer, gather=True
        )
        group_normed = group_normed.reshape(-1, D)
        gate = matmul(group_normed, w_gate_up[0])
        up = matmul(group_normed, w_gate_up[1])
        inner_f, geglu_back = jax.vjp(geglu, gate, up)
        inner_act = inner_f.astype(bf16)
        partial_down = matmul(inner_act, w_down_share).astype(bf16)
        (partials,) = exchange(
            [partial_down.reshape(cores * PLANE, tokens, D)], GROUP, 7 + layer
        )
        down_out = jnp.sum(partials.astype(f32), axis=0).reshape(half_seqs, stretch_len, D)
        branch_out, post_ffn_back = jax.vjp(rms_norm, down_out, post_ffn)
        hidden = hidden_half + branch_out
        saved.append(
            (
                normed,
                pre_attn_back,
                prep_back,
                query_rows,
                keyvals,
                log_total,
                attended_rows,
                post_attn_back,
                pre_ffn_back,
                group_normed,
                geglu_back,
                inner_act,
                post_ffn_back,
            )
        )

    target_gap = hidden - teacher.astype(f32)
    valid_weight = valid_mask.astype(f32)[:, :, None]
    square_sum = jnp.sum(valid_weight * target_gap * target_gap)
    loss_weight = float(all_seqs * seq_length * D // 4)
    grad_hidden = (
        cotangent.astype(f32)
        + 2.0 * loss_weight / (valid_count * D) * valid_weight * target_gap
    )

    grads = [None] * LAYERS
    gain_grads = [None] * LAYERS
    logit_scale = 1.0 / math.sqrt(HD)
    for layer in reversed(range(LAYERS)):
        (
            normed,
            pre_attn_back,
            prep_back,
            query_rows,
            keyvals,
            log_total,
            attended_rows,
            post_attn_back,
            pre_ffn_back,
            group_normed,
            geglu_back,
            inner_act,
            post_ffn_back,
        ) = saved[layer]
        w_mixed, w_project, w_gate_up, w_down_share = full[layer]
        key_tile_rows = keyvals[..., :HD]
        value_tile_rows = keyvals[..., HD:]
        d_down, d_post_ffn = post_ffn_back(grad_hidden)
        (group_d_down,) = exchange(
            [d_down.astype(bf16).reshape(tokens, D)], GROUP, 9 + layer, gather=True
        )
        group_d_down = group_d_down.reshape(-1, D)
        d_inner = lax.dot_general(
            group_d_down, w_down_share, (((1,), (1,)), ((), ())), preferred_element_type=f32
        )
        d_gate, d_up = geglu_back(d_inner)
        d_gate, d_up = d_gate.astype(bf16), d_up.astype(bf16)
        across = (((1,), (1,)), ((), ()))
        along = (((0,), (0,)), ((), ()))
        d_partial = lax.dot_general(
            d_gate, w_gate_up[0], across, preferred_element_type=f32
        ) + lax.dot_general(d_up, w_gate_up[1], across, preferred_element_type=f32)
        (partials,) = exchange(
            [d_partial.astype(bf16).reshape(cores * PLANE, tokens, D)], GROUP, 11 + layer
        )
        d_normed_ffn = jnp.sum(partials.astype(f32), axis=0).reshape(half_seqs, stretch_len, D)

        grad_down = lax.dot_general(inner_act, group_d_down, along, preferred_element_type=f32)
        grad_gate = lax.dot_general(group_normed, d_gate, along, preferred_element_type=f32)
        grad_up = lax.dot_general(group_normed, d_up, along, preferred_element_type=f32)
        down_pieces = grad_down.astype(bf16).reshape(share, cores, out_cols).transpose(1, 0, 2)
        down_pieces = lax.all_to_all(
            down_pieces, "head", split_axis=0, concat_axis=0, tiled=True
        ).reshape(planes, ff_block, out_cols)
        gu_pieces = jnp.stack([grad_gate.astype(bf16), grad_up.astype(bf16)])
        gu_pieces = gu_pieces.reshape(2, planes, PLANE * gu_rows, share).transpose(1, 0, 2, 3)
        gu_pieces = gu_pieces.reshape(planes, 2 * PLANE * gu_rows, share)
        gu_parts, down_parts = exchange(
            [padded(gu_pieces), padded(down_pieces)], ("zd",), 13 + layer
        )
        grad_down = jnp.sum(down_parts[:, :ff_block].astype(f32), axis=0)
        gu_sum = jnp.sum(gu_parts[:, : 2 * PLANE * gu_rows].astype(f32), axis=0)
        (gu_own,) = exchange(
            [padded(gu_sum.reshape(2 * PLANE, gu_rows, share), 8)], GROUP, 15 + layer
        )
        grad_gu = gu_own[:, :gu_rows].reshape(cores, PLANE, gu_rows, half_planes, ff_block)
        grad_gu = grad_gu.transpose(2, 0, 3, 1, 4).reshape(gu_rows, FF)

        d_half, d_norm_ffn = pre_ffn_back(d_normed_ffn)
        d_half = d_half + grad_hidden
        d_projected, d_post_attn = post_attn_back(d_half)
        d_proj_low = d_projected.astype(bf16)
        grad_project = jnp.einsum(
            "bpq,bpd->qd", attended_rows, d_proj_low, preferred_element_type=f32
        )
        d_attended = (
            jnp.einsum("bpd,qd->bpq", d_proj_low, w_project, preferred_element_type=f32)
            .astype(bf16)
            .reshape(half_seqs, stretch_len, HEADS, HD)
        )
        logit_scores = attend_scores(query_rows, key_tile_rows, allowed)
        soft = jnp.exp(logit_scores - log_total[..., None])
        d_probs = jnp.einsum(
            "tals,tes->tlae", d_attended, value_tile_rows, preferred_element_type=f32
        )
        row_total = jnp.sum(soft * d_probs, axis=-1, keepdims=True)
        score_gradient = (soft * (d_probs - row_total)).astype(bf16)
        d_queries = (
            jnp.einsum("zusi,zix->zsux", score_gradient, key_tile_rows, preferred_element_type=f32)
            * logit_scale
        )
        d_keys = (
            jnp.einsum("lqkp,lkqf->lpf", score_gradient, query_rows, preferred_element_type=f32)
            * logit_scale
        )
        d_values = jnp.einsum(
            "lqkp,lkqf->lpf", soft.astype(bf16), d_attended, preferred_element_type=f32
        )
        d_keyvals = jnp.concatenate([d_keys, d_values], axis=-1)
        pieces = [
            d_keyvals[:, (reach - k) * stretch_len : (reach - k + 1) * stretch_len]
            for k in range(reach + 1)
        ]
        outgoing = jnp.stack(pieces[1:]).reshape(reach, tokens, 2 * HD)
        incoming = shift(outgoing, planes, reach, True, 17 + layer)
        d_own = pieces[0] + jnp.sum(incoming, axis=0).reshape(half_seqs, stretch_len, 2 * HD)
        d_mixed, d_query_gain, d_key_gain = prep_back((d_queries, d_own))
        d_mixed_low = d_mixed.astype(bf16)
        grad_mixed = jnp.einsum("bpd,bpe->de", normed, d_mixed_low, preferred_element_type=f32)
        d_normed = jnp.einsum("bpe,de->bpd", d_mixed_low, w_mixed, preferred_element_type=f32)
        d_hidden, d_norm_attn = pre_attn_back(d_normed)
        grad_hidden = d_hidden + d_half
        gain_grads[layer] = jnp.stack(
            [
                jnp.concatenate([d_norm_attn, d_post_attn, d_query_gain]),
                jnp.concatenate([d_norm_ffn, d_post_ffn, d_key_gain]),
            ]
        )

        sums = []
        for gradient, columns in ((grad_mixed, qkv_cols), (grad_project, out_cols)):
            halves = gradient.astype(bf16).reshape(-1, cores, columns).transpose(1, 0, 2)
            halves = lax.all_to_all(halves, "head", split_axis=0, concat_axis=0, tiled=True)
            total = jnp.sum(halves.astype(f32), axis=0).astype(bf16)
            total = total.reshape(planes, PLANE, -1, columns).transpose(1, 0, 2, 3)
            sums.append(padded(total.reshape(PLANE, -1, columns)))
        parts = exchange(sums, ("tp",), 19 + layer)
        sums = []
        for part, rows, columns in zip(parts, (qkv_rows, out_rows), (qkv_cols, out_cols)):
            total = jnp.sum(part[:, : planes * rows].astype(f32), axis=0).astype(bf16)
            sums.append(padded(total.reshape(planes, rows, columns)))
        parts = exchange(sums, ("zd",), 21 + layer)
        grad_qkv = jnp.sum(parts[0][:, :qkv_rows].astype(f32), axis=0)
        grad_out = jnp.sum(parts[1][:, :out_rows].astype(f32), axis=0)
        grads[layer] = (grad_qkv, grad_out, grad_gu, grad_down)

    packet = jnp.stack(gain_grads, axis=1).reshape(cores, LAYERS, seq_devices, gain_cols)
    packet = packet.transpose(0, 2, 1, 3)
    packet = jnp.pad(packet, ((0, 0), (0, 0), (0, 8 - LAYERS), (0, lanes - gain_cols)))
    packet = packet.at[:, :, LAYERS, 0].set(square_sum)
    (packets,) = exchange([packet.reshape(cores * seq_devices, 8, lanes)], EVERY, 23)
    packets = jnp.sum(packets, axis=0)
    mse_loss = packets[LAYERS, 0] / (valid_count * D)
    gain_grad = packets[:LAYERS, None, :gain_cols]

    old_weights = (w_qkv, w_out, w_gu, w_down)
    old_moments = (mom_qkv, mom_out, mom_gu, mom_down)
    moments = tuple(
        muon_decay * old_moments[k] + jnp.stack([grads[layer][k] for layer in range(LAYERS)])
        for k in range(4)
    )
    grams = [exact("lrc,lsc->lrs", m, m) for m in moments]
    grams = [
        jnp.sum(
            lax.all_to_all(g[:, None], "head", split_axis=0, concat_axis=1, tiled=True), axis=1
        )
        for g in grams
    ]
    factors = [newton_factor(g) for g in grams]
    factors = [lax.all_gather(f, "head", axis=0, tiled=True) for f in factors]
    new_weights = tuple(
        old_weights[k] * (1.0 - muon_rate * muon_shrink)
        - muon_rate
        * muon_scale
        * math.sqrt(moments[k].shape[-1] * cores)
        * exact("lrs,lsc->lrc", factors[k], moments[k])
        for k in range(4)
    )
    gain_first_new = beta_one * gain_first + (1.0 - beta_one) * gain_grad
    gain_second_new = beta_two * gain_second + (1.0 - beta_two) * gain_grad * gain_grad
    gains_new = norm_gains - adam_rate * (gain_first_new / (1.0 - beta_one**STEP)) / (
        jnp.sqrt(gain_second_new / (1.0 - beta_two**STEP)) + adam_epsilon
    )
    return (
        mse_loss,
        hidden,
        grad_hidden,
        *new_weights,
        *moments,
        gains_new,
        gain_first_new,
        gain_second_new,
    )


def solution(mesh):
    cores, length = mesh.devices.shape
    split = Mesh(mesh.devices.reshape(cores, length // PLANE, PLANE), EVERY)
    stream = P("head", SEQ, None)
    matrix = P(None, SEQ, "head")
    gains = P(None, "head", SEQ)
    return jax.shard_map(
        body,
        mesh=split,
        in_specs=(stream, stream, stream, P(), P("head", SEQ))
        + (matrix,) * 4
        + (gains,)
        + (matrix,) * 4
        + (gains,) * 2,
        out_specs=(P(), stream, stream) + (matrix,) * 8 + (gains,) * 3,
        check_vma=False,
    )
```

```python
from functools import partial
import itertools
import math

import jax
import jax.numpy as jnp
from jax import lax
from jax.experimental import pallas as pl
from jax.experimental.pallas import tpu as pltpu
from jax.sharding import Mesh, PartitionSpec as P

D = 1152
HEADS = 4
HD = 256
FF = 6912
WINDOW = 512
LAYERS = 2
NS_ITERS = 5
STEP = 10
PLANE = 4

norm_eps = 1e-06
rope_base = 10000.0
newton_one = 3.4445
newton_two = -4.775
newton_three = 2.0315
muon_decay = 0.95
muon_rate = 0.15
muon_shrink = 0.01
muon_scale = 0.2
beta_one = 0.9
beta_two = 0.95
adam_rate = 0.7
adam_epsilon = 1e-08
finest_precision = lax.Precision.HIGHEST
MESH = pl.DeviceIdType.MESH
SEQ = ("zd", "tp")
GROUP = ("head", "tp")
EVERY = ("head", "zd", "tp")
bf16 = jnp.bfloat16
f32 = jnp.float32


def linear(places, sizes):
    index = 0
    for place, size in zip(places, sizes):
        index = index * size + place
    return index


def enter(partners):
    barrier = pltpu.get_barrier_semaphore()
    for partner in partners:
        pl.semaphore_signal(barrier, inc=1, device_id=partner, device_id_type=MESH)
    pl.semaphore_wait(barrier, len(partners))


def exchange_kernel(axes, sizes, count, gather, *refs):
    sources, results = refs[:count], refs[count : 2 * count]
    send_sem, recv_sem, own_sem = refs[2 * count :]
    mine = [lax.axis_index(axis) for axis in axes]
    me = linear(mine, sizes)
    offsets = list(itertools.product(*[range(size) for size in sizes]))[1:]
    partners = []
    for offset in offsets:
        places = [lax.rem(m + o, s) for m, o, s in zip(mine, offset, sizes)]
        partners.append((dict(zip(axes, places)), linear(places, sizes)))
    enter([device for device, _ in partners])
    copies = []
    for step, (device, index) in enumerate(partners):
        for k in range(count):
            copy = pltpu.make_async_remote_copy(
                src_ref=sources[k] if gather else sources[k].at[index],
                dst_ref=results[k].at[me],
                send_sem=send_sem.at[k, step],
                recv_sem=recv_sem.at[k, step],
                device_id=device,
                device_id_type=MESH,
            )
            copy.start()
            copies.append(copy)
    for k in range(count):
        own = pltpu.make_async_copy(
            sources[k] if gather else sources[k].at[me], results[k].at[me], own_sem.at[k]
        )
        own.start()
        copies.append(own)
    for copy in copies:
        copy.wait()


def exchange(arrays, axes, ident, gather=False):
    sizes = tuple(lax.axis_size(axis) for axis in axes)
    members = math.prod(sizes)
    count = len(arrays)
    shapes = [((members,) + a.shape) if gather else a.shape for a in arrays]
    return pl.pallas_call(
        partial(exchange_kernel, axes, sizes, count, gather),
        out_shape=[jax.ShapeDtypeStruct(s, a.dtype) for s, a in zip(shapes, arrays)],
        in_specs=[pl.BlockSpec(memory_space=pl.ANY)] * count,
        out_specs=[pl.BlockSpec(memory_space=pl.ANY)] * count,
        scratch_shapes=[
            pltpu.SemaphoreType.DMA((count, members - 1)),
            pltpu.SemaphoreType.DMA((count, members - 1)),
            pltpu.SemaphoreType.DMA((count,)),
        ],
        compiler_params=pltpu.CompilerParams(collective_id=ident, has_side_effects=True),
    )(*arrays)


def spread_kernel(axes, sizes, order, count, *refs):
    sources, results = refs[:count], refs[count : 2 * count]
    send_sem, recv_sem, own_sem = refs[2 * count :]
    place = {axis: lax.axis_index(axis) for axis in axes}
    size = dict(zip(axes, sizes))
    partners = [
        {axis: lax.rem(place[axis] + step, size[axis])}
        for axis in order
        for step in range(1, size[axis])
    ]
    enter(partners)

    def slot(k, where):
        ref = results[k]
        return ref.at[tuple(where[axis] for axis in axes)]

    copies, held, number = [], [(place, None)], 0
    for k in range(count):
        own = pltpu.make_async_copy(sources[k], slot(k, place), own_sem.at[k])
        own.start()
        copies.append(own)
    sends = []
    for axis in order:
        arriving = []
        for where, arrivals in held:
            if arrivals is not None:
                while arrivals:
                    arrivals.pop().wait_recv()
            for step in range(1, size[axis]):
                to = lax.rem(place[axis] + step, size[axis])
                back = lax.rem(place[axis] - step + size[axis], size[axis])
                landing = []
                for k in range(count):
                    copy = pltpu.make_async_remote_copy(
                        src_ref=sources[k] if arrivals is None else slot(k, where),
                        dst_ref=slot(k, where),
                        send_sem=send_sem.at[k, number],
                        recv_sem=recv_sem.at[k, number],
                        device_id={axis: to},
                        device_id_type=MESH,
                    )
                    copy.start()
                    sends.append(copy)
                    landing.append(copy)
                number += 1
                arriving.append((dict(where, **{axis: back}), landing))
        held = held + arriving
    last = len(held) // size[order[-1]]
    for where, arrivals in held[last:]:
        for copy in arrivals:
            copy.wait_recv()
    for copy in sends:
        copy.wait_send()
    for copy in copies:
        copy.wait()


def spread(arrays, axes, order, ident):
    sizes = tuple(lax.axis_size(axis) for axis in axes)
    moves = math.prod(sizes) - 1
    count = len(arrays)
    return pl.pallas_call(
        partial(spread_kernel, axes, sizes, order, count),
        out_shape=[jax.ShapeDtypeStruct(sizes + a.shape, a.dtype) for a in arrays],
        in_specs=[pl.BlockSpec(memory_space=pl.ANY)] * count,
        out_specs=[pl.BlockSpec(memory_space=pl.ANY)] * count,
        scratch_shapes=[
            pltpu.SemaphoreType.DMA((count, moves)),
            pltpu.SemaphoreType.DMA((count, moves)),
            pltpu.SemaphoreType.DMA((count,)),
        ],
        compiler_params=pltpu.CompilerParams(collective_id=ident, has_side_effects=True),
    )(*arrays)


def by_rows(rows, work, step=16):
    @pl.loop(0, rows // step)
    def _(index):
        work(pl.ds(pl.multiple_of(index * step, step), step))


def collect_kernel(cores, members, planes, count, *refs):
    sources, results = refs[:count], refs[count : 2 * count]
    scratch, sems = refs[2 * count : -6], refs[-6:]
    lands, sums = scratch[:count], scratch[count : 2 * count]
    plane_lands = scratch[2 * count : 3 * count]
    totals, z_sums, z_lands = (scratch[i * count : (i + 1) * count] for i in (3, 4, 5))
    core_send, core_recv, tp_send, tp_recv, z_send, z_recv = sems
    core, zd, tp = (lax.axis_index(axis) for axis in EVERY)
    sibling = {"head": 1 - core}
    enter(
        [sibling]
        + [{"tp": lax.rem(tp + step, members)} for step in range(1, members)]
        + [{"zd": lax.rem(zd + step, planes)} for step in range(1, planes)]
    )
    order = list(range(1, members)) + [0]
    sends = []
    core_moves = {}
    for step in order:
        there = lax.rem(tp + step, members)
        for k in range(count):
            copy = pltpu.make_async_remote_copy(
                src_ref=sources[k].at[1 - core, there],
                dst_ref=lands[k].at[step],
                send_sem=core_send.at[k, step],
                recv_sem=core_recv.at[k, step],
                device_id=sibling,
                device_id_type=MESH,
            )
            copy.start()
            core_moves[k, step] = copy
            sends.append(copy)
    plane_moves = {}
    for step in order:
        there = lax.rem(tp + step, members)
        for k in range(count):
            core_moves[k, step].wait_recv()
            source, land, total, summed = sources[k], lands[k], totals[k], sums[k]

            def add(rows):
                value = source[core, there, rows].astype(f32) + land[step, rows].astype(f32)
                if step == 0:
                    total[rows] = value
                else:
                    summed[step, rows] = value.astype(bf16)

            by_rows(total.shape[0], add)
            if step > 0:
                copy = pltpu.make_async_remote_copy(
                    src_ref=summed.at[step],
                    dst_ref=plane_lands[k].at[step],
                    send_sem=tp_send.at[k, step],
                    recv_sem=tp_recv.at[k, step],
                    device_id={"tp": there},
                    device_id_type=MESH,
                )
                copy.start()
                plane_moves[k, step] = copy
                sends.append(copy)
    z_moves = {}
    for k in range(count):
        for step in range(1, members):
            plane_moves[k, step].wait_recv()
        total, land, result = totals[k], plane_lands[k], results[k]

        def gather_plane(rows):
            value = total[rows]
            for step in range(1, members):
                value = value + land[step, rows].astype(f32)
            if planes == 1:
                result[rows] = value
            else:
                total[rows] = value

        by_rows(total.shape[0], gather_plane)
        if planes == 1:
            continue
        height = result.shape[0]
        for step in range(1, planes):
            there = lax.rem(zd + step, planes)
            z_sum = z_sums[k]

            def round_off(rows):
                at = pl.multiple_of(there * height + rows.start, 16)
                z_sum[step, rows] = total[pl.ds(at, rows.size)].astype(bf16)

            by_rows(height, round_off)
            copy = pltpu.make_async_remote_copy(
                src_ref=z_sum.at[step],
                dst_ref=z_lands[k].at[step],
                send_sem=z_send.at[k, step],
                recv_sem=z_recv.at[k, step],
                device_id={"zd": there},
                device_id_type=MESH,
            )
            copy.start()
            z_moves[k, step] = copy
            sends.append(copy)
    if planes > 1:
        for k in range(count):
            for step in range(1, planes):
                z_moves[k, step].wait_recv()
            total, land, result = totals[k], z_lands[k], results[k]
            height = result.shape[0]

            def gather_z(rows):
                at = pl.multiple_of(zd * height + rows.start, 16)
                value = total[pl.ds(at, rows.size)]
                for step in range(1, planes):
                    value = value + land[step, rows].astype(f32)
                result[rows] = value

            by_rows(height, gather_z)
    for copy in sends:
        copy.wait_send()


def collect(arrays, planes, ident):
    cores, members = arrays[0].shape[:2]
    count = len(arrays)
    tall = [a.shape[2:] for a in arrays]
    short = [(rows // planes, columns) for rows, columns in tall]
    z_slots = [(planes,) + s if planes > 1 else (1, 16, 128) for s in short]
    vmem = pltpu.VMEM
    scratch = (
        [vmem((members,) + s, bf16) for s in tall] * 1
        + [vmem((members,) + s, bf16) for s in tall]
        + [vmem((members,) + s, bf16) for s in tall]
        + [vmem(s, f32) for s in tall]
        + [vmem(s, bf16) for s in z_slots]
        + [vmem(s, bf16) for s in z_slots]
    )
    dma = pltpu.SemaphoreType.DMA
    return pl.pallas_call(
        partial(collect_kernel, cores, members, planes, count),
        out_shape=[jax.ShapeDtypeStruct(s, f32) for s in short],
        in_specs=[pl.BlockSpec(memory_space=pltpu.VMEM)] * count,
        out_specs=[pl.BlockSpec(memory_space=pltpu.VMEM)] * count,
        scratch_shapes=scratch
        + [dma((count, members))] * 4
        + [dma((count, planes))] * 2,
        compiler_params=pltpu.CompilerParams(
            collective_id=ident, has_side_effects=True, vmem_limit_bytes=48 * 2**20
        ),
    )(*arrays)


def shift_kernel(planes, reach, back, source, result, send_sem, recv_sem):
    place = linear([lax.axis_index("zd"), lax.axis_index("tp")], (planes, PLANE))
    total = planes * PLANE
    sign = -1 if back else 1
    to, sources = [], []
    for distance in range(1, reach + 1):
        there = lax.rem(place + sign * distance + total, total)
        to.append({"zd": there // PLANE, "tp": lax.rem(there, PLANE)})
        here = lax.rem(place - sign * distance + total, total)
        sources.append({"zd": here // PLANE, "tp": lax.rem(here, PLANE)})
    barrier = pltpu.get_barrier_semaphore()
    for device in to + sources:
        pl.semaphore_signal(barrier, inc=1, device_id=device, device_id_type=MESH)
    pl.semaphore_wait(barrier, 2 * reach)
    copies = []
    for k, device in enumerate(to):
        copy = pltpu.make_async_remote_copy(
            src_ref=source.at[k] if back else source,
            dst_ref=result.at[k],
            send_sem=send_sem.at[k],
            recv_sem=recv_sem.at[k],
            device_id=device,
            device_id_type=MESH,
        )
        copy.start()
        copies.append(copy)
    for copy in copies:
        copy.wait()


def shift(array, planes, reach, back, ident):
    shape = array.shape if back else (reach,) + array.shape
    return pl.pallas_call(
        partial(shift_kernel, planes, reach, back),
        out_shape=jax.ShapeDtypeStruct(shape, array.dtype),
        in_specs=[pl.BlockSpec(memory_space=pl.ANY)],
        out_specs=pl.BlockSpec(memory_space=pl.ANY),
        scratch_shapes=[pltpu.SemaphoreType.DMA((reach,)), pltpu.SemaphoreType.DMA((reach,))],
        compiler_params=pltpu.CompilerParams(collective_id=ident, has_side_effects=True),
    )(array)


def padded(array, multiple=16):
    extra = -array.shape[-2] % multiple
    if extra == 0:
        return array
    return jnp.pad(array, [(0, 0)] * (array.ndim - 2) + [(0, extra), (0, 0)])


def rms_norm(values, norm_gain):
    return (
        values * lax.rsqrt(jnp.mean(values * values, axis=-1, keepdims=True) + norm_eps) * norm_gain
    )


def rope_tables(positions, head_dim):
    half_dim = head_dim // 2
    frequency = jnp.exp(
        jnp.arange(half_dim, dtype=jnp.float32) * (-2.0 * math.log(rope_base) / head_dim)
    )
    angles = positions.astype(jnp.float32)[:, None] * frequency[None, :]
    return (jnp.cos(angles), jnp.sin(angles))


def rotate(values, cosine_table, sine_table):
    half_dim = values.shape[-1] // 2
    lower_half = values[..., :half_dim]
    upper_half = values[..., half_dim:]
    return jnp.concatenate(
        [
            lower_half * cosine_table - upper_half * sine_table,
            upper_half * cosine_table + lower_half * sine_table,
        ],
        axis=-1,
    )


def head_prep(mixed_proj, query_gain, key_gain, cosine_table, sine_table):
    seq_rows = mixed_proj.shape[0]
    place_rows = mixed_proj.shape[1]
    queries = mixed_proj[..., : HEADS * HD].reshape(seq_rows, place_rows, HEADS, HD)
    key_heads = mixed_proj[..., HEADS * HD : HEADS * HD + HD]
    values = mixed_proj[..., HEADS * HD + HD :]
    queries = rotate(
        rms_norm(queries, query_gain), cosine_table[:, None, :], sine_table[:, None, :]
    )
    key_heads = rotate(rms_norm(key_heads, key_gain), cosine_table, sine_table)
    return (queries, jnp.concatenate([key_heads, values], axis=-1))


def geglu(gate, up):
    return jax.nn.gelu(gate, approximate=True) * up


def attend_scores(query_rows, key_tile_rows, allowed):
    logit_scores = jnp.einsum(
        "tals,tes->tlae", query_rows, key_tile_rows, preferred_element_type=jnp.float32
    ) * (1.0 / math.sqrt(HD))
    return jnp.where(allowed[:, None], logit_scores, -jnp.inf)


def matmul(left, right):
    return jnp.dot(left, right, preferred_element_type=f32)


def exact(spec, left, right):
    return jnp.einsum(spec, left, right, precision=finest_precision)


def newton_factor(gram):
    scale = 1.0 / (jnp.sqrt(jnp.trace(gram, axis1=-2, axis2=-1)) + 1e-07)
    scale = scale[..., None, None]
    present = gram * (scale * scale)
    unit = jnp.eye(gram.shape[-1], dtype=f32)
    product = None
    for iteration in range(NS_ITERS):
        square = exact("...rs,...st->...rt", present, present)
        factor = newton_one * unit + newton_two * present + newton_three * square
        product = factor if product is None else exact("...rs,...st->...rt", factor, product)
        if iteration < NS_ITERS - 1:
            present = exact(
                "...rs,...st->...rt", exact("...rs,...st->...rt", factor, present), factor
            )
    return product * scale


def body(
    inputs,
    cotangent,
    teacher,
    segments,
    valid_mask,
    w_qkv,
    w_out,
    w_gu,
    w_down,
    norm_gains,
    mom_qkv,
    mom_out,
    mom_gu,
    mom_down,
    gain_first,
    gain_second,
):
    cores = lax.axis_size("head")
    planes = lax.axis_size("zd")
    seq_devices = planes * PLANE
    core = lax.axis_index("head")
    seq_place = lax.axis_index("zd") * PLANE + lax.axis_index("tp")
    half_seqs, stretch_len = inputs.shape[:2]
    tokens = half_seqs * stretch_len
    all_seqs = half_seqs * cores
    seq_length = stretch_len * seq_devices
    reach = -(-WINDOW // stretch_len)
    key_len = (reach + 1) * stretch_len
    qkv_rows, qkv_cols = w_qkv.shape[1:]
    out_rows, out_cols = w_out.shape[1:]
    gu_rows = w_gu.shape[1]
    ff_block = w_down.shape[1]
    share = FF // (cores * PLANE)
    half_planes = planes // cores
    gain_cols = norm_gains.shape[-1]
    gain_len = gain_cols * seq_devices
    lanes = -(-gain_cols // 128) * 128

    packet = jnp.zeros((8, lanes), f32)
    packet = packet.at[:LAYERS, :gain_cols].set(norm_gains[:, 0].astype(bf16).astype(f32))
    packet = packet.at[LAYERS, 0].set(jnp.sum(valid_mask.astype(f32)))
    pieces = w_gu.astype(bf16).reshape(LAYERS, gu_rows, cores, half_planes, PLANE, ff_block)
    pieces = pieces.transpose(2, 4, 0, 1, 3, 5).reshape(cores * PLANE, LAYERS * gu_rows, share)
    (gu_pieces,) = exchange([padded(pieces)], GROUP, 0)
    gu_pieces = gu_pieces[:, : LAYERS * gu_rows].reshape(cores * PLANE, LAYERS, gu_rows, share)
    packets, mixed_parts, project_parts = spread(
        [
            packet,
            padded(w_qkv.astype(bf16).reshape(LAYERS * qkv_rows, qkv_cols)),
            padded(w_out.astype(bf16).reshape(LAYERS * out_rows, out_cols)),
        ],
        EVERY,
        ("zd", "tp", "head"),
        1,
    )
    packets = packets.reshape(cores, seq_devices, 8, lanes)
    valid_count = jnp.sum(packets[:, :, LAYERS, 0])
    gain_rows = [
        packets[:, :, layer, :gain_cols].reshape(cores, gain_len) for layer in range(LAYERS)
    ]

    def whole(parts, rows, columns, layer):
        parts = parts[..., layer * rows : (layer + 1) * rows, :]
        return parts.reshape(cores, -1, columns).transpose(1, 0, 2).reshape(-1, cores * columns)

    def ffn_weights(layer, after):
        pieces, rows = gu_pieces[:, layer], w_down[layer].astype(bf16)
        if after is not None:
            pieces, rows, after = lax.optimization_barrier((pieces, rows, after))
        pieces = lax.all_gather(pieces, "zd", axis=0)
        pieces = pieces.reshape(planes, cores, PLANE, gu_rows, share)
        w_gate_up = pieces.transpose(1, 0, 2, 3, 4).reshape(2, D, share)
        rows = lax.all_gather(rows, "zd", axis=0)
        rows = rows.reshape(cores, half_planes * ff_block, out_cols)
        rows = lax.all_to_all(rows, "head", split_axis=0, concat_axis=0, tiled=True)
        return w_gate_up, rows.transpose(1, 0, 2).reshape(share, D)

    full = [ffn_weights(0, None)] + [None] * (LAYERS - 1)

    own_places = seq_place * stretch_len + jnp.arange(stretch_len, dtype=jnp.int32)
    key_places = (seq_place - reach) * stretch_len + jnp.arange(key_len, dtype=jnp.int32)
    cosine_table, sine_table = rope_tables(own_places, HD)
    own_rows = lax.dynamic_slice_in_dim(segments, core * half_seqs, half_seqs, 0)
    own_segments = lax.dynamic_slice_in_dim(own_rows, seq_place * stretch_len, stretch_len, 1)
    padded_segments = jnp.pad(own_rows, ((0, 0), (reach * stretch_len, 0)), constant_values=-1)
    key_segments = lax.dynamic_slice_in_dim(padded_segments, seq_place * stretch_len, key_len, 1)
    spacing = own_places[:, None] - key_places[None, :]
    allowed = (spacing >= 0) & (spacing < WINDOW) & (key_places[None, :] >= 0)
    allowed = allowed[None] & (own_segments[:, :, None] == key_segments[:, None, :])

    hidden = inputs.astype(f32)
    saved = []
    for layer in range(LAYERS):
        w_mixed = whole(mixed_parts, qkv_rows, qkv_cols, layer)
        w_project = whole(project_parts, out_rows, out_cols, layer)
        gain_pack = gain_rows[layer]
        norm_attn = gain_pack[0, :D]
        post_attn = gain_pack[0, D : 2 * D]
        query_gain = gain_pack[0, 2 * D :]
        norm_ffn = gain_pack[1, :D]
        post_ffn = gain_pack[1, D : 2 * D]
        key_gain = gain_pack[1, 2 * D :]
        normed_f, pre_attn_back = jax.vjp(rms_norm, hidden, norm_attn)
        normed = normed_f.astype(bf16)
        mixed_proj = jnp.einsum("bpd,de->bpe", normed, w_mixed, preferred_element_type=f32)
        prepared, prep_back = jax.vjp(
            partial(head_prep, cosine_table=cosine_table, sine_table=sine_table),
            mixed_proj,
            query_gain,
            key_gain,
        )
        query_rows = prepared[0].astype(bf16)
        own_keyvals = prepared[1].astype(bf16)
        earlier = shift(
            own_keyvals.reshape(tokens, 2 * HD), planes, reach, False, 3 + layer
        ).reshape(reach, half_seqs, stretch_len, 2 * HD)
        if layer + 1 < LAYERS:
            full[layer + 1] = ffn_weights(layer + 1, earlier)
        w_gate_up, w_down_share = full[layer]
        full[layer] = (w_mixed, w_project, w_gate_up, w_down_share)
        keyvals = jnp.concatenate(
            [earlier[reach - 1 - k] for k in range(reach)] + [own_keyvals], axis=1
        )
        key_tile_rows = keyvals[..., :HD]
        value_tile_rows = keyvals[..., HD:]
        logit_scores = attend_scores(query_rows, key_tile_rows, allowed)
        log_total = jax.nn.logsumexp(logit_scores, axis=-1)
        soft = jnp.exp(logit_scores - log_total[..., None])
        attended = jnp.einsum(
            "zusi,zix->zsux", soft.astype(bf16), value_tile_rows, preferred_element_type=f32
        ).astype(bf16)
        attended_rows = attended.reshape(half_seqs, stretch_len, HEADS * HD)
        projected = jnp.einsum("bpq,qd->bpd", attended_rows, w_project, preferred_element_type=f32)
        branch_out, post_attn_back = jax.vjp(rms_norm, projected, post_attn)
        hidden_half = hidden + branch_out
        normed_f, pre_ffn_back = jax.vjp(rms_norm, hidden_half, norm_ffn)
        (group_normed,) = spread(
            [normed_f.astype(bf16).reshape(tokens, D)], GROUP, ("tp", "head"), 5 + layer
        )
        group_normed = group_normed.reshape(-1, D)
        gate = matmul(group_normed, w_gate_up[0])
        up = matmul(group_normed, w_gate_up[1])
        inner_f, geglu_back = jax.vjp(geglu, gate, up)
        inner_act = inner_f.astype(bf16)
        partial_down = matmul(inner_act, w_down_share).astype(bf16)
        (down_out,) = collect([partial_down.reshape(cores, PLANE, tokens, D)], 1, 7 + layer)
        down_out = down_out.reshape(half_seqs, stretch_len, D)
        branch_out, post_ffn_back = jax.vjp(rms_norm, down_out, post_ffn)
        hidden = hidden_half + branch_out
        saved.append(
            (
                normed,
                pre_attn_back,
                prep_back,
                query_rows,
                keyvals,
                log_total,
                attended_rows,
                post_attn_back,
                pre_ffn_back,
                group_normed,
                geglu_back,
                inner_act,
                post_ffn_back,
            )
        )

    target_gap = hidden - teacher.astype(f32)
    valid_weight = valid_mask.astype(f32)[:, :, None]
    square_sum = jnp.sum(valid_weight * target_gap * target_gap)
    loss_weight = float(all_seqs * seq_length * D // 4)
    grad_hidden = (
        cotangent.astype(f32)
        + 2.0 * loss_weight / (valid_count * D) * valid_weight * target_gap
    )

    grads = [None] * LAYERS
    gain_grads = [None] * LAYERS
    gu_sums = [None] * LAYERS
    logit_scale = 1.0 / math.sqrt(HD)
    for layer in reversed(range(LAYERS)):
        (
            normed,
            pre_attn_back,
            prep_back,
            query_rows,
            keyvals,
            log_total,
            attended_rows,
            post_attn_back,
            pre_ffn_back,
            group_normed,
            geglu_back,
            inner_act,
            post_ffn_back,
        ) = saved[layer]
        w_mixed, w_project, w_gate_up, w_down_share = full[layer]
        key_tile_rows = keyvals[..., :HD]
        value_tile_rows = keyvals[..., HD:]
        d_down, d_post_ffn = post_ffn_back(grad_hidden)
        (group_d_down,) = spread(
            [d_down.astype(bf16).reshape(tokens, D)], GROUP, ("tp", "head"), 9 + layer
        )
        group_d_down = group_d_down.reshape(-1, D)
        d_inner = lax.dot_general(
            group_d_down, w_down_share, (((1,), (1,)), ((), ())), preferred_element_type=f32
        )
        d_gate, d_up = geglu_back(d_inner)
        d_gate, d_up = d_gate.astype(bf16), d_up.astype(bf16)
        across = (((1,), (1,)), ((), ()))
        along = (((0,), (0,)), ((), ()))
        d_partial = lax.dot_general(
            d_gate, w_gate_up[0], across, preferred_element_type=f32
        ) + lax.dot_general(d_up, w_gate_up[1], across, preferred_element_type=f32)
        (d_normed_ffn,) = collect(
            [d_partial.astype(bf16).reshape(cores, PLANE, tokens, D)], 1, 11 + layer
        )
        d_normed_ffn = d_normed_ffn.reshape(half_seqs, stretch_len, D)

        grad_down = lax.dot_general(inner_act, group_d_down, along, preferred_element_type=f32)
        grad_gate = lax.dot_general(group_normed, d_gate, along, preferred_element_type=f32)
        grad_up = lax.dot_general(group_normed, d_up, along, preferred_element_type=f32)
        down_pieces = grad_down.astype(bf16).reshape(share, cores, out_cols).transpose(1, 0, 2)
        down_pieces = lax.all_to_all(
            down_pieces, "head", split_axis=0, concat_axis=0, tiled=True
        ).reshape(planes * ff_block, out_cols)
        grad_down = lax.psum_scatter(
            down_pieces, "zd", scatter_dimension=0, tiled=True
        ).astype(f32)
        gu_sums[layer] = [
            lax.psum_scatter(g.astype(bf16), "zd", scatter_dimension=0, tiled=True)
            for g in (grad_gate, grad_up)
        ]

        d_half, d_norm_ffn = pre_ffn_back(d_normed_ffn)
        d_half = d_half + grad_hidden
        d_projected, d_post_attn = post_attn_back(d_half)
        d_proj_low = d_projected.astype(bf16)
        grad_project = jnp.einsum(
            "bpq,bpd->qd", attended_rows, d_proj_low, preferred_element_type=f32
        )
        d_attended = (
            jnp.einsum("bpd,qd->bpq", d_proj_low, w_project, preferred_element_type=f32)
            .astype(bf16)
            .reshape(half_seqs, stretch_len, HEADS, HD)
        )
        logit_scores = attend_scores(query_rows, key_tile_rows, allowed)
        soft = jnp.exp(logit_scores - log_total[..., None])
        d_probs = jnp.einsum(
            "tals,tes->tlae", d_attended, value_tile_rows, preferred_element_type=f32
        )
        row_total = jnp.sum(soft * d_probs, axis=-1, keepdims=True)
        score_gradient = (soft * (d_probs - row_total)).astype(bf16)
        d_queries = (
            jnp.einsum("zusi,zix->zsux", score_gradient, key_tile_rows, preferred_element_type=f32)
            * logit_scale
        )
        d_keys = (
            jnp.einsum("lqkp,lkqf->lpf", score_gradient, query_rows, preferred_element_type=f32)
            * logit_scale
        )
        d_values = jnp.einsum(
            "lqkp,lkqf->lpf", soft.astype(bf16), d_attended, preferred_element_type=f32
        )
        d_keyvals = jnp.concatenate([d_keys, d_values], axis=-1)
        pieces = [
            d_keyvals[:, (reach - k) * stretch_len : (reach - k + 1) * stretch_len]
            for k in range(reach + 1)
        ]
        outgoing = jnp.stack(pieces[1:]).reshape(reach, tokens, 2 * HD)
        incoming = shift(outgoing, planes, reach, True, 17 + layer)
        d_own = pieces[0] + jnp.sum(incoming, axis=0).reshape(half_seqs, stretch_len, 2 * HD)
        d_mixed, d_query_gain, d_key_gain = prep_back((d_queries, d_own))
        d_mixed_low = d_mixed.astype(bf16)
        grad_mixed = jnp.einsum("bpd,bpe->de", normed, d_mixed_low, preferred_element_type=f32)
        d_normed = jnp.einsum("bpe,de->bpd", d_mixed_low, w_mixed, preferred_element_type=f32)
        d_hidden, d_norm_attn = pre_attn_back(d_normed)
        grad_hidden = d_hidden + d_half
        gain_grads[layer] = jnp.stack(
            [
                jnp.concatenate([d_norm_attn, d_post_attn, d_query_gain]),
                jnp.concatenate([d_norm_ffn, d_post_ffn, d_key_gain]),
            ]
        )

        if layer > 0:
            grad_qkv, grad_out = (
                lax.psum_scatter(
                    lax.psum_scatter(g, "head", scatter_dimension=1, tiled=True),
                    SEQ,
                    scatter_dimension=0,
                    tiled=True,
                )
                for g in (grad_mixed, grad_project)
            )
        else:
            blocks = []
            for gradient, columns in ((grad_mixed, qkv_cols), (grad_project, out_cols)):
                block = gradient.astype(bf16).reshape(planes, PLANE, -1, cores, columns)
                block = padded(block.transpose(3, 1, 0, 2, 4))
                blocks.append(block.reshape(cores, PLANE, -1, columns))
            grad_qkv, grad_out = collect(blocks, planes, 19)
            grad_qkv, grad_out = grad_qkv[:qkv_rows], grad_out[:out_rows]
        grads[layer] = [grad_qkv, grad_out, None, grad_down]

    pieces = jnp.stack([jnp.stack(pair) for pair in zip(*gu_sums)])
    pieces = pieces.reshape(2, LAYERS, PLANE, gu_rows, share).transpose(0, 2, 1, 3, 4)
    pieces = padded(pieces.reshape(2 * PLANE, LAYERS * gu_rows, share))
    (pieces,) = exchange([pieces], GROUP, 15)
    pieces = pieces[:, : LAYERS * gu_rows].astype(f32)
    pieces = pieces.reshape(cores, PLANE, LAYERS, gu_rows, half_planes, ff_block)
    grad_gu = pieces.transpose(2, 3, 0, 4, 1, 5).reshape(LAYERS, gu_rows, FF)
    for layer in range(LAYERS):
        grads[layer][2] = grad_gu[layer]

    packet = jnp.stack(gain_grads, axis=1).reshape(cores, LAYERS, seq_devices, gain_cols)
    packet = packet.transpose(0, 2, 1, 3)
    packet = jnp.pad(packet, ((0, 0), (0, 0), (0, 8 - LAYERS), (0, lanes - gain_cols)))
    packet = packet.at[:, :, LAYERS, 0].set(square_sum)
    (packets,) = exchange([packet.reshape(cores * seq_devices, 8, lanes)], EVERY, 23)
    packets = jnp.sum(packets, axis=0)
    mse_loss = packets[LAYERS, 0] / (valid_count * D)
    gain_grad = packets[:LAYERS, None, :gain_cols]

    old_weights = (w_qkv, w_out, w_gu, w_down)
    old_moments = (mom_qkv, mom_out, mom_gu, mom_down)
    moments = tuple(
        muon_decay * old_moments[k] + jnp.stack([grads[layer][k] for layer in range(LAYERS)])
        for k in range(4)
    )
    grams = [exact("lrc,lsc->lrs", m, m) for m in moments]
    grams = [
        jnp.sum(
            lax.all_to_all(g[:, None], "head", split_axis=0, concat_axis=1, tiled=True), axis=1
        )
        for g in grams
    ]
    factors = [newton_factor(g) for g in grams]
    factors = [lax.all_gather(f, "head", axis=0, tiled=True) for f in factors]
    new_weights = tuple(
        old_weights[k] * (1.0 - muon_rate * muon_shrink)
        - muon_rate
        * muon_scale
        * math.sqrt(moments[k].shape[-1] * cores)
        * exact("lrs,lsc->lrc", factors[k], moments[k])
        for k in range(4)
    )
    gain_first_new = beta_one * gain_first + (1.0 - beta_one) * gain_grad
    gain_second_new = beta_two * gain_second + (1.0 - beta_two) * gain_grad * gain_grad
    gains_new = norm_gains - adam_rate * (gain_first_new / (1.0 - beta_one**STEP)) / (
        jnp.sqrt(gain_second_new / (1.0 - beta_two**STEP)) + adam_epsilon
    )
    return (
        mse_loss,
        hidden,
        grad_hidden,
        *new_weights,
        *moments,
        gains_new,
        gain_first_new,
        gain_second_new,
    )


def solution(mesh):
    cores, length = mesh.devices.shape
    split = Mesh(mesh.devices.reshape(cores, length // PLANE, PLANE), EVERY)
    stream = P("head", SEQ, None)
    matrix = P(None, SEQ, "head")
    gains = P(None, "head", SEQ)
    return jax.shard_map(
        body,
        mesh=split,
        in_specs=(stream, stream, stream, P(), P("head", SEQ))
        + (matrix,) * 4
        + (gains,)
        + (matrix,) * 4
        + (gains,) * 2,
        out_specs=(P(), stream, stream) + (matrix,) * 8 + (gains,) * 3,
        check_vma=False,
    )
```

```python
from functools import partial
import itertools
import math

import jax
import jax.numpy as jnp
from jax import lax
from jax.experimental import pallas as pl
from jax.experimental.pallas import tpu as pltpu
from jax.sharding import Mesh, PartitionSpec as P

D = 1152
HEADS = 4
HD = 256
FF = 6912
WINDOW = 512
LAYERS = 2
NS_ITERS = 5
STEP = 10
PLANE = 4

norm_eps = 1e-06
rope_base = 10000.0
newton_one = 3.4445
newton_two = -4.775
newton_three = 2.0315
muon_decay = 0.95
muon_rate = 0.15
muon_shrink = 0.01
muon_scale = 0.2
beta_one = 0.9
beta_two = 0.95
adam_rate = 0.7
adam_epsilon = 1e-08
finest_precision = lax.Precision.HIGHEST
MESH = pl.DeviceIdType.MESH
SEQ = ("zd", "tp")
GROUP = ("head", "tp")
EVERY = ("head", "zd", "tp")
bf16 = jnp.bfloat16
f32 = jnp.float32


def linear(places, sizes):
    index = 0
    for place, size in zip(places, sizes):
        index = index * size + place
    return index


def enter(partners):
    barrier = pltpu.get_barrier_semaphore()
    for partner in partners:
        pl.semaphore_signal(barrier, inc=1, device_id=partner, device_id_type=MESH)
    pl.semaphore_wait(barrier, len(partners))


def exchange_kernel(axes, sizes, count, gather, *refs):
    sources, results = refs[:count], refs[count : 2 * count]
    send_sem, recv_sem, own_sem = refs[2 * count :]
    mine = [lax.axis_index(axis) for axis in axes]
    me = linear(mine, sizes)
    offsets = list(itertools.product(*[range(size) for size in sizes]))[1:]
    partners = []
    for offset in offsets:
        places = [lax.rem(m + o, s) for m, o, s in zip(mine, offset, sizes)]
        partners.append((dict(zip(axes, places)), linear(places, sizes)))
    enter([device for device, _ in partners])
    copies = []
    for step, (device, index) in enumerate(partners):
        for k in range(count):
            copy = pltpu.make_async_remote_copy(
                src_ref=sources[k] if gather else sources[k].at[index],
                dst_ref=results[k].at[me],
                send_sem=send_sem.at[k, step],
                recv_sem=recv_sem.at[k, step],
                device_id=device,
                device_id_type=MESH,
            )
            copy.start()
            copies.append(copy)
    for k in range(count):
        own = pltpu.make_async_copy(
            sources[k] if gather else sources[k].at[me], results[k].at[me], own_sem.at[k]
        )
        own.start()
        copies.append(own)
    for copy in copies:
        copy.wait()


def exchange(arrays, axes, ident, gather=False):
    sizes = tuple(lax.axis_size(axis) for axis in axes)
    members = math.prod(sizes)
    count = len(arrays)
    shapes = [((members,) + a.shape) if gather else a.shape for a in arrays]
    return pl.pallas_call(
        partial(exchange_kernel, axes, sizes, count, gather),
        out_shape=[jax.ShapeDtypeStruct(s, a.dtype) for s, a in zip(shapes, arrays)],
        in_specs=[pl.BlockSpec(memory_space=pl.ANY)] * count,
        out_specs=[pl.BlockSpec(memory_space=pl.ANY)] * count,
        scratch_shapes=[
            pltpu.SemaphoreType.DMA((count, members - 1)),
            pltpu.SemaphoreType.DMA((count, members - 1)),
            pltpu.SemaphoreType.DMA((count,)),
        ],
        compiler_params=pltpu.CompilerParams(collective_id=ident, has_side_effects=True),
    )(*arrays)


def spread_kernel(axes, sizes, order, count, *refs):
    sources, results = refs[:count], refs[count : 2 * count]
    send_sem, recv_sem, own_sem = refs[2 * count :]
    place = {axis: lax.axis_index(axis) for axis in axes}
    size = dict(zip(axes, sizes))
    partners = [
        {axis: lax.rem(place[axis] + step, size[axis])}
        for axis in order
        for step in range(1, size[axis])
    ]
    enter(partners)

    def slot(k, where):
        ref = results[k]
        return ref.at[tuple(where[axis] for axis in axes)]

    copies, held, number = [], [(place, None)], 0
    for k in range(count):
        own = pltpu.make_async_copy(sources[k], slot(k, place), own_sem.at[k])
        own.start()
        copies.append(own)
    sends = []
    for axis in order:
        arriving = []
        for where, arrivals in held:
            if arrivals is not None:
                while arrivals:
                    arrivals.pop().wait_recv()
            for step in range(1, size[axis]):
                to = lax.rem(place[axis] + step, size[axis])
                back = lax.rem(place[axis] - step + size[axis], size[axis])
                landing = []
                for k in range(count):
                    copy = pltpu.make_async_remote_copy(
                        src_ref=sources[k] if arrivals is None else slot(k, where),
                        dst_ref=slot(k, where),
                        send_sem=send_sem.at[k, number],
                        recv_sem=recv_sem.at[k, number],
                        device_id={axis: to},
                        device_id_type=MESH,
                    )
                    copy.start()
                    sends.append(copy)
                    landing.append(copy)
                number += 1
                arriving.append((dict(where, **{axis: back}), landing))
        held = held + arriving
    last = len(held) // size[order[-1]]
    for where, arrivals in held[last:]:
        for copy in arrivals:
            copy.wait_recv()
    for copy in sends:
        copy.wait_send()
    for copy in copies:
        copy.wait()


def spread(arrays, axes, order, ident):
    sizes = tuple(lax.axis_size(axis) for axis in axes)
    moves = math.prod(sizes) - 1
    count = len(arrays)
    return pl.pallas_call(
        partial(spread_kernel, axes, sizes, order, count),
        out_shape=[jax.ShapeDtypeStruct(sizes + a.shape, a.dtype) for a in arrays],
        in_specs=[pl.BlockSpec(memory_space=pl.ANY)] * count,
        out_specs=[pl.BlockSpec(memory_space=pl.ANY)] * count,
        scratch_shapes=[
            pltpu.SemaphoreType.DMA((count, moves)),
            pltpu.SemaphoreType.DMA((count, moves)),
            pltpu.SemaphoreType.DMA((count,)),
        ],
        compiler_params=pltpu.CompilerParams(collective_id=ident, has_side_effects=True),
    )(*arrays)


def by_rows(rows, work, step=16):
    @pl.loop(0, rows // step)
    def _(index):
        work(pl.ds(pl.multiple_of(index * step, step), step))


def collect_kernel(cores, members, planes, count, *refs):
    sources, results = refs[:count], refs[count : 2 * count]
    scratch, sems = refs[2 * count : -6], refs[-6:]
    lands, sums = scratch[:count], scratch[count : 2 * count]
    plane_lands = scratch[2 * count : 3 * count]
    totals, z_sums, z_lands = (scratch[i * count : (i + 1) * count] for i in (3, 4, 5))
    core_send, core_recv, tp_send, tp_recv, z_send, z_recv = sems
    core, zd, tp = (lax.axis_index(axis) for axis in EVERY)
    sibling = {"head": 1 - core}
    enter(
        [sibling]
        + [{"tp": lax.rem(tp + step, members)} for step in range(1, members)]
        + [{"zd": lax.rem(zd + step, planes)} for step in range(1, planes)]
    )
    order = list(range(1, members)) + [0]
    sends = []
    core_moves = {}
    for step in order:
        there = lax.rem(tp + step, members)
        for k in range(count):
            copy = pltpu.make_async_remote_copy(
                src_ref=sources[k].at[1 - core, there],
                dst_ref=lands[k].at[step],
                send_sem=core_send.at[k, step],
                recv_sem=core_recv.at[k, step],
                device_id=sibling,
                device_id_type=MESH,
            )
            copy.start()
            core_moves[k, step] = copy
            sends.append(copy)
    plane_moves = {}
    for step in order:
        there = lax.rem(tp + step, members)
        for k in range(count):
            core_moves[k, step].wait_recv()
            source, land, total, summed = sources[k], lands[k], totals[k], sums[k]

            def add(rows):
                value = source[core, there, rows].astype(f32) + land[step, rows].astype(f32)
                if step == 0:
                    total[rows] = value
                else:
                    summed[step, rows] = value.astype(summed.dtype)

            by_rows(total.shape[0], add, 8 if summed.dtype == f32 else 16)
            if step > 0:
                copy = pltpu.make_async_remote_copy(
                    src_ref=summed.at[step],
                    dst_ref=plane_lands[k].at[step],
                    send_sem=tp_send.at[k, step],
                    recv_sem=tp_recv.at[k, step],
                    device_id={"tp": there},
                    device_id_type=MESH,
                )
                copy.start()
                plane_moves[k, step] = copy
                sends.append(copy)
    z_moves = {}
    for k in range(count):
        for step in range(1, members):
            plane_moves[k, step].wait_recv()
        total, land, result = totals[k], plane_lands[k], results[k]

        def gather_plane(rows):
            value = total[rows]
            for step in range(1, members):
                value = value + land[step, rows].astype(f32)
            if planes == 1:
                result[rows] = value
            else:
                total[rows] = value

        stride = 8 if land.dtype == f32 else 16
        by_rows(total.shape[0], gather_plane, stride)
        if planes == 1:
            continue
        height = result.shape[0]
        for step in range(1, planes):
            there = lax.rem(zd + step, planes)
            z_sum = z_sums[k]

            def round_off(rows):
                at = pl.multiple_of(there * height + rows.start, stride)
                z_sum[step, rows] = total[pl.ds(at, rows.size)].astype(z_sum.dtype)

            by_rows(height, round_off, stride)
            copy = pltpu.make_async_remote_copy(
                src_ref=z_sum.at[step],
                dst_ref=z_lands[k].at[step],
                send_sem=z_send.at[k, step],
                recv_sem=z_recv.at[k, step],
                device_id={"zd": there},
                device_id_type=MESH,
            )
            copy.start()
            z_moves[k, step] = copy
            sends.append(copy)
    if planes > 1:
        for k in range(count):
            for step in range(1, planes):
                z_moves[k, step].wait_recv()
            total, land, result = totals[k], z_lands[k], results[k]
            height = result.shape[0]
            stride = 8 if land.dtype == f32 else 16

            def gather_z(rows):
                at = pl.multiple_of(zd * height + rows.start, stride)
                value = total[pl.ds(at, rows.size)]
                for step in range(1, planes):
                    value = value + land[step, rows].astype(f32)
                result[rows] = value

            by_rows(height, gather_z, stride)
    for copy in sends:
        copy.wait_send()


def collect(arrays, planes, ident):
    cores, members = arrays[0].shape[:2]
    count = len(arrays)
    kinds = [a.dtype for a in arrays]
    tall = [a.shape[2:] for a in arrays]
    short = [(rows // planes, columns) for rows, columns in tall]
    z_slots = [(planes,) + s if planes > 1 else (1, 16, 128) for s in short]
    vmem = pltpu.VMEM
    scratch = (
        [vmem((members,) + s, kind) for s, kind in zip(tall, kinds)] * 3
        + [vmem(s, f32) for s in tall]
        + [vmem(s, kind) for s, kind in zip(z_slots, kinds)] * 2
    )
    dma = pltpu.SemaphoreType.DMA
    return pl.pallas_call(
        partial(collect_kernel, cores, members, planes, count),
        out_shape=[jax.ShapeDtypeStruct(s, f32) for s in short],
        in_specs=[pl.BlockSpec(memory_space=pltpu.VMEM)] * count,
        out_specs=[pl.BlockSpec(memory_space=pltpu.VMEM)] * count,
        scratch_shapes=scratch
        + [dma((count, members))] * 4
        + [dma((count, planes))] * 2,
        compiler_params=pltpu.CompilerParams(
            collective_id=ident, has_side_effects=True, vmem_limit_bytes=48 * 2**20
        ),
    )(*arrays)


def shift_kernel(planes, reach, back, source, result, send_sem, recv_sem):
    place = linear([lax.axis_index("zd"), lax.axis_index("tp")], (planes, PLANE))
    total = planes * PLANE
    sign = -1 if back else 1
    to, sources = [], []
    for distance in range(1, reach + 1):
        there = lax.rem(place + sign * distance + total, total)
        to.append({"zd": there // PLANE, "tp": lax.rem(there, PLANE)})
        here = lax.rem(place - sign * distance + total, total)
        sources.append({"zd": here // PLANE, "tp": lax.rem(here, PLANE)})
    barrier = pltpu.get_barrier_semaphore()
    for device in to + sources:
        pl.semaphore_signal(barrier, inc=1, device_id=device, device_id_type=MESH)
    pl.semaphore_wait(barrier, 2 * reach)
    copies = []
    for k, device in enumerate(to):
        copy = pltpu.make_async_remote_copy(
            src_ref=source.at[k] if back else source,
            dst_ref=result.at[k],
            send_sem=send_sem.at[k],
            recv_sem=recv_sem.at[k],
            device_id=device,
            device_id_type=MESH,
        )
        copy.start()
        copies.append(copy)
    for copy in copies:
        copy.wait()


def shift(array, planes, reach, back, ident):
    shape = array.shape if back else (reach,) + array.shape
    return pl.pallas_call(
        partial(shift_kernel, planes, reach, back),
        out_shape=jax.ShapeDtypeStruct(shape, array.dtype),
        in_specs=[pl.BlockSpec(memory_space=pl.ANY)],
        out_specs=pl.BlockSpec(memory_space=pl.ANY),
        scratch_shapes=[pltpu.SemaphoreType.DMA((reach,)), pltpu.SemaphoreType.DMA((reach,))],
        compiler_params=pltpu.CompilerParams(collective_id=ident, has_side_effects=True),
    )(array)


def padded(array, multiple=16):
    extra = -array.shape[-2] % multiple
    if extra == 0:
        return array
    return jnp.pad(array, [(0, 0)] * (array.ndim - 2) + [(0, extra), (0, 0)])


def rms_norm(values, norm_gain):
    return (
        values * lax.rsqrt(jnp.mean(values * values, axis=-1, keepdims=True) + norm_eps) * norm_gain
    )


def rope_tables(positions, head_dim):
    half_dim = head_dim // 2
    frequency = jnp.exp(
        jnp.arange(half_dim, dtype=jnp.float32) * (-2.0 * math.log(rope_base) / head_dim)
    )
    angles = positions.astype(jnp.float32)[:, None] * frequency[None, :]
    return (jnp.cos(angles), jnp.sin(angles))


def rotate(values, cosine_table, sine_table):
    half_dim = values.shape[-1] // 2
    lower_half = values[..., :half_dim]
    upper_half = values[..., half_dim:]
    return jnp.concatenate(
        [
            lower_half * cosine_table - upper_half * sine_table,
            upper_half * cosine_table + lower_half * sine_table,
        ],
        axis=-1,
    )


def head_prep(mixed_proj, query_gain, key_gain, cosine_table, sine_table):
    seq_rows = mixed_proj.shape[0]
    place_rows = mixed_proj.shape[1]
    queries = mixed_proj[..., : HEADS * HD].reshape(seq_rows, place_rows, HEADS, HD)
    key_heads = mixed_proj[..., HEADS * HD : HEADS * HD + HD]
    values = mixed_proj[..., HEADS * HD + HD :]
    queries = rotate(
        rms_norm(queries, query_gain), cosine_table[:, None, :], sine_table[:, None, :]
    )
    key_heads = rotate(rms_norm(key_heads, key_gain), cosine_table, sine_table)
    return (queries, jnp.concatenate([key_heads, values], axis=-1))


def geglu(gate, up):
    return jax.nn.gelu(gate, approximate=True) * up


def attend_scores(query_rows, key_tile_rows, allowed):
    logit_scores = jnp.einsum(
        "tals,tes->tlae", query_rows, key_tile_rows, preferred_element_type=jnp.float32
    ) * (1.0 / math.sqrt(HD))
    return jnp.where(allowed[:, None], logit_scores, -jnp.inf)


def matmul(left, right):
    return jnp.dot(left, right, preferred_element_type=f32)


def exact(spec, left, right):
    return jnp.einsum(spec, left, right, precision=finest_precision)


def newton_factor(gram):
    scale = 1.0 / (jnp.sqrt(jnp.trace(gram, axis1=-2, axis2=-1)) + 1e-07)
    scale = scale[..., None, None]
    present = gram * (scale * scale)
    unit = jnp.eye(gram.shape[-1], dtype=f32)
    product = None
    for iteration in range(NS_ITERS):
        square = exact("...rs,...st->...rt", present, present)
        factor = newton_one * unit + newton_two * present + newton_three * square
        product = factor if product is None else exact("...rs,...st->...rt", factor, product)
        if iteration < NS_ITERS - 1:
            present = exact(
                "...rs,...st->...rt", exact("...rs,...st->...rt", factor, present), factor
            )
    return product * scale


def body(
    inputs,
    cotangent,
    teacher,
    segments,
    valid_mask,
    w_qkv,
    w_out,
    w_gu,
    w_down,
    norm_gains,
    mom_qkv,
    mom_out,
    mom_gu,
    mom_down,
    gain_first,
    gain_second,
):
    cores = lax.axis_size("head")
    planes = lax.axis_size("zd")
    seq_devices = planes * PLANE
    core = lax.axis_index("head")
    seq_place = lax.axis_index("zd") * PLANE + lax.axis_index("tp")
    half_seqs, stretch_len = inputs.shape[:2]
    tokens = half_seqs * stretch_len
    all_seqs = half_seqs * cores
    seq_length = stretch_len * seq_devices
    reach = -(-WINDOW // stretch_len)
    key_len = (reach + 1) * stretch_len
    qkv_rows, qkv_cols = w_qkv.shape[1:]
    out_rows, out_cols = w_out.shape[1:]
    gu_rows = w_gu.shape[1]
    ff_block = w_down.shape[1]
    share = FF // (cores * PLANE)
    half_planes = planes // cores
    gain_cols = norm_gains.shape[-1]
    gain_len = gain_cols * seq_devices
    lanes = -(-gain_cols // 128) * 128

    packet = jnp.zeros((8, lanes), f32)
    packet = packet.at[:LAYERS, :gain_cols].set(norm_gains[:, 0].astype(bf16).astype(f32))
    packet = packet.at[LAYERS, 0].set(jnp.sum(valid_mask.astype(f32)))
    pieces = w_gu.astype(bf16).reshape(LAYERS, gu_rows, cores, half_planes, PLANE, ff_block)
    pieces = pieces.transpose(2, 4, 0, 1, 3, 5).reshape(cores * PLANE, LAYERS * gu_rows, share)
    (gu_pieces,) = exchange([padded(pieces)], GROUP, 0)
    gu_pieces = gu_pieces[:, : LAYERS * gu_rows].reshape(cores * PLANE, LAYERS, gu_rows, share)
    packets, mixed_parts, project_parts = spread(
        [
            packet,
            padded(w_qkv.astype(bf16).reshape(LAYERS * qkv_rows, qkv_cols)),
            padded(w_out.astype(bf16).reshape(LAYERS * out_rows, out_cols)),
        ],
        EVERY,
        ("zd", "tp", "head"),
        1,
    )
    packets = packets.reshape(cores, seq_devices, 8, lanes)
    valid_count = jnp.sum(packets[:, :, LAYERS, 0])
    gain_rows = [
        packets[:, :, layer, :gain_cols].reshape(cores, gain_len) for layer in range(LAYERS)
    ]

    def whole(parts, rows, columns, layer):
        parts = parts[..., layer * rows : (layer + 1) * rows, :]
        return parts.reshape(cores, -1, columns).transpose(1, 0, 2).reshape(-1, cores * columns)

    def ffn_weights(layer, after):
        pieces, rows = gu_pieces[:, layer], w_down[layer].astype(bf16)
        if after is not None:
            pieces, rows, after = lax.optimization_barrier((pieces, rows, after))
        pieces = lax.all_gather(pieces, "zd", axis=0)
        pieces = pieces.reshape(planes, cores, PLANE, gu_rows, share)
        w_gate_up = pieces.transpose(1, 0, 2, 3, 4).reshape(2, D, share)
        rows = lax.all_gather(rows, "zd", axis=0)
        rows = rows.reshape(cores, half_planes * ff_block, out_cols)
        rows = lax.all_to_all(rows, "head", split_axis=0, concat_axis=0, tiled=True)
        return w_gate_up, rows.transpose(1, 0, 2).reshape(share, D)

    full = [ffn_weights(0, None)] + [None] * (LAYERS - 1)

    own_places = seq_place * stretch_len + jnp.arange(stretch_len, dtype=jnp.int32)
    key_places = (seq_place - reach) * stretch_len + jnp.arange(key_len, dtype=jnp.int32)
    cosine_table, sine_table = rope_tables(own_places, HD)
    own_rows = lax.dynamic_slice_in_dim(segments, core * half_seqs, half_seqs, 0)
    own_segments = lax.dynamic_slice_in_dim(own_rows, seq_place * stretch_len, stretch_len, 1)
    padded_segments = jnp.pad(own_rows, ((0, 0), (reach * stretch_len, 0)), constant_values=-1)
    key_segments = lax.dynamic_slice_in_dim(padded_segments, seq_place * stretch_len, key_len, 1)
    spacing = own_places[:, None] - key_places[None, :]
    allowed = (spacing >= 0) & (spacing < WINDOW) & (key_places[None, :] >= 0)
    allowed = allowed[None] & (own_segments[:, :, None] == key_segments[:, None, :])

    hidden = inputs.astype(f32)
    saved = []
    for layer in range(LAYERS):
        w_mixed = whole(mixed_parts, qkv_rows, qkv_cols, layer)
        w_project = whole(project_parts, out_rows, out_cols, layer)
        gain_pack = gain_rows[layer]
        norm_attn = gain_pack[0, :D]
        post_attn = gain_pack[0, D : 2 * D]
        query_gain = gain_pack[0, 2 * D :]
        norm_ffn = gain_pack[1, :D]
        post_ffn = gain_pack[1, D : 2 * D]
        key_gain = gain_pack[1, 2 * D :]
        normed_f, pre_attn_back = jax.vjp(rms_norm, hidden, norm_attn)
        normed = normed_f.astype(bf16)
        mixed_proj = jnp.einsum("bpd,de->bpe", normed, w_mixed, preferred_element_type=f32)
        prepared, prep_back = jax.vjp(
            partial(head_prep, cosine_table=cosine_table, sine_table=sine_table),
            mixed_proj,
            query_gain,
            key_gain,
        )
        query_rows = prepared[0].astype(bf16)
        own_keyvals = prepared[1].astype(bf16)
        earlier = shift(
            own_keyvals.reshape(tokens, 2 * HD), planes, reach, False, 3 + layer
        ).reshape(reach, half_seqs, stretch_len, 2 * HD)
        if layer + 1 < LAYERS:
            full[layer + 1] = ffn_weights(layer + 1, earlier)
        w_gate_up, w_down_share = full[layer]
        full[layer] = (w_mixed, w_project, w_gate_up, w_down_share)
        keyvals = jnp.concatenate(
            [earlier[reach - 1 - k] for k in range(reach)] + [own_keyvals], axis=1
        )
        key_tile_rows = keyvals[..., :HD]
        value_tile_rows = keyvals[..., HD:]
        logit_scores = attend_scores(query_rows, key_tile_rows, allowed)
        log_total = jax.nn.logsumexp(logit_scores, axis=-1)
        soft = jnp.exp(logit_scores - log_total[..., None])
        attended = jnp.einsum(
            "zusi,zix->zsux", soft.astype(bf16), value_tile_rows, preferred_element_type=f32
        ).astype(bf16)
        attended_rows = attended.reshape(half_seqs, stretch_len, HEADS * HD)
        projected = jnp.einsum("bpq,qd->bpd", attended_rows, w_project, preferred_element_type=f32)
        branch_out, post_attn_back = jax.vjp(rms_norm, projected, post_attn)
        hidden_half = hidden + branch_out
        normed_f, pre_ffn_back = jax.vjp(rms_norm, hidden_half, norm_ffn)
        (group_normed,) = spread(
            [normed_f.astype(bf16).reshape(tokens, D)], GROUP, ("tp", "head"), 5 + layer
        )
        group_normed = group_normed.reshape(-1, D)
        gate = matmul(group_normed, w_gate_up[0])
        up = matmul(group_normed, w_gate_up[1])
        inner_f, geglu_back = jax.vjp(geglu, gate, up)
        inner_act = inner_f.astype(bf16)
        partial_down = matmul(inner_act, w_down_share).astype(bf16)
        (down_out,) = collect([partial_down.reshape(cores, PLANE, tokens, D)], 1, 7 + layer)
        down_out = down_out.reshape(half_seqs, stretch_len, D)
        branch_out, post_ffn_back = jax.vjp(rms_norm, down_out, post_ffn)
        hidden = hidden_half + branch_out
        saved.append(
            (
                normed,
                pre_attn_back,
                prep_back,
                query_rows,
                keyvals,
                log_total,
                attended_rows,
                post_attn_back,
                pre_ffn_back,
                group_normed,
                geglu_back,
                inner_act,
                post_ffn_back,
            )
        )

    target_gap = hidden - teacher.astype(f32)
    valid_weight = valid_mask.astype(f32)[:, :, None]
    square_sum = jnp.sum(valid_weight * target_gap * target_gap)
    loss_weight = float(all_seqs * seq_length * D // 4)
    grad_hidden = (
        cotangent.astype(f32)
        + 2.0 * loss_weight / (valid_count * D) * valid_weight * target_gap
    )

    attn_grads = [None] * LAYERS
    down_grads = [None] * LAYERS
    gain_grads = [None] * LAYERS
    gu_sums = [None] * LAYERS
    logit_scale = 1.0 / math.sqrt(HD)
    for layer in reversed(range(LAYERS)):
        (
            normed,
            pre_attn_back,
            prep_back,
            query_rows,
            keyvals,
            log_total,
            attended_rows,
            post_attn_back,
            pre_ffn_back,
            group_normed,
            geglu_back,
            inner_act,
            post_ffn_back,
        ) = saved[layer]
        w_mixed, w_project, w_gate_up, w_down_share = full[layer]
        key_tile_rows = keyvals[..., :HD]
        value_tile_rows = keyvals[..., HD:]
        d_down, d_post_ffn = post_ffn_back(grad_hidden)
        (group_d_down,) = spread(
            [d_down.astype(bf16).reshape(tokens, D)], GROUP, ("tp", "head"), 9 + layer
        )
        group_d_down = group_d_down.reshape(-1, D)
        d_inner = lax.dot_general(
            group_d_down, w_down_share, (((1,), (1,)), ((), ())), preferred_element_type=f32
        )
        d_gate, d_up = geglu_back(d_inner)
        d_gate, d_up = d_gate.astype(bf16), d_up.astype(bf16)
        across = (((1,), (1,)), ((), ()))
        along = (((0,), (0,)), ((), ()))
        d_partial = lax.dot_general(
            d_gate, w_gate_up[0], across, preferred_element_type=f32
        ) + lax.dot_general(d_up, w_gate_up[1], across, preferred_element_type=f32)
        (d_normed_ffn,) = collect(
            [d_partial.astype(bf16).reshape(cores, PLANE, tokens, D)], 1, 11 + layer
        )
        d_normed_ffn = d_normed_ffn.reshape(half_seqs, stretch_len, D)

        grad_down = lax.dot_general(inner_act, group_d_down, along, preferred_element_type=f32)
        grad_gate = lax.dot_general(group_normed, d_gate, along, preferred_element_type=f32)
        grad_up = lax.dot_general(group_normed, d_up, along, preferred_element_type=f32)
        down_pieces = grad_down.astype(bf16).reshape(share, cores, out_cols).transpose(1, 0, 2)
        down_pieces = lax.all_to_all(
            down_pieces, "head", split_axis=0, concat_axis=0, tiled=True
        ).reshape(planes * ff_block, out_cols)
        grad_down = lax.psum_scatter(
            down_pieces, "zd", scatter_dimension=0, tiled=True
        ).astype(f32)
        gu_sums[layer] = [
            lax.psum_scatter(g.astype(bf16), "zd", scatter_dimension=0, tiled=True)
            for g in (grad_gate, grad_up)
        ]

        d_half, d_norm_ffn = pre_ffn_back(d_normed_ffn)
        d_half = d_half + grad_hidden
        d_projected, d_post_attn = post_attn_back(d_half)
        d_proj_low = d_projected.astype(bf16)
        grad_project = jnp.einsum(
            "bpq,bpd->qd", attended_rows, d_proj_low, preferred_element_type=f32
        )
        d_attended = (
            jnp.einsum("bpd,qd->bpq", d_proj_low, w_project, preferred_element_type=f32)
            .astype(bf16)
            .reshape(half_seqs, stretch_len, HEADS, HD)
        )
        logit_scores = attend_scores(query_rows, key_tile_rows, allowed)
        soft = jnp.exp(logit_scores - log_total[..., None])
        d_probs = jnp.einsum(
            "tals,tes->tlae", d_attended, value_tile_rows, preferred_element_type=f32
        )
        row_total = jnp.sum(soft * d_probs, axis=-1, keepdims=True)
        score_gradient = (soft * (d_probs - row_total)).astype(bf16)
        d_queries = (
            jnp.einsum("zusi,zix->zsux", score_gradient, key_tile_rows, preferred_element_type=f32)
            * logit_scale
        )
        d_keys = (
            jnp.einsum("lqkp,lkqf->lpf", score_gradient, query_rows, preferred_element_type=f32)
            * logit_scale
        )
        d_values = jnp.einsum(
            "lqkp,lkqf->lpf", soft.astype(bf16), d_attended, preferred_element_type=f32
        )
        d_keyvals = jnp.concatenate([d_keys, d_values], axis=-1)
        pieces = [
            d_keyvals[:, (reach - k) * stretch_len : (reach - k + 1) * stretch_len]
            for k in range(reach + 1)
        ]
        outgoing = jnp.stack(pieces[1:]).astype(bf16).reshape(reach, tokens, 2 * HD)
        incoming = shift(outgoing, planes, reach, True, 17 + layer)
        d_own = pieces[0] + jnp.sum(incoming.astype(f32), axis=0).reshape(
            half_seqs, stretch_len, 2 * HD
        )
        d_mixed, d_query_gain, d_key_gain = prep_back((d_queries, d_own))
        d_mixed_low = d_mixed.astype(bf16)
        grad_mixed = jnp.einsum("bpd,bpe->de", normed, d_mixed_low, preferred_element_type=f32)
        d_normed = jnp.einsum("bpe,de->bpd", d_mixed_low, w_mixed, preferred_element_type=f32)
        d_hidden, d_norm_attn = pre_attn_back(d_normed)
        grad_hidden = d_hidden + d_half
        gain_grads[layer] = jnp.stack(
            [
                jnp.concatenate([d_norm_attn, d_post_attn, d_query_gain]),
                jnp.concatenate([d_norm_ffn, d_post_ffn, d_key_gain]),
            ]
        )

        attn_grads[layer] = (grad_mixed.astype(bf16), grad_project.astype(bf16))
        down_grads[layer] = grad_down

    pieces = jnp.stack([jnp.stack(pair) for pair in zip(*gu_sums)])
    pieces = pieces.reshape(2, LAYERS, PLANE, gu_rows, share).transpose(0, 2, 1, 3, 4)
    pieces = padded(pieces.reshape(2 * PLANE, LAYERS * gu_rows, share))
    (pieces,) = exchange([pieces], GROUP, 15)
    pieces = pieces[:, : LAYERS * gu_rows].astype(f32)
    pieces = pieces.reshape(cores, PLANE, LAYERS, gu_rows, half_planes, ff_block)
    grad_gu = pieces.transpose(2, 3, 0, 4, 1, 5).reshape(LAYERS, gu_rows, FF)
    blocks = []
    for parts, columns in zip(zip(*attn_grads), (qkv_cols, out_cols)):
        block = jnp.stack(parts).reshape(LAYERS, planes, PLANE, -1, cores, columns)
        block = block.transpose(4, 2, 1, 0, 3, 5).reshape(cores, PLANE, planes, -1, columns)
        blocks.append(padded(block).reshape(cores, PLANE, -1, columns))
    packet = jnp.stack(gain_grads, axis=1).reshape(cores, LAYERS, planes, PLANE, gain_cols)
    packet = packet.transpose(0, 3, 2, 1, 4)
    packet = jnp.pad(packet, [(0, 0)] * 3 + [(0, 8 - LAYERS), (0, lanes - gain_cols)])
    packet = packet.at[:, :, :, LAYERS, 0].set(square_sum)
    blocks.append(packet.reshape(cores, PLANE, planes * 8, lanes))
    grad_qkv, grad_out, packet = collect(blocks, planes, 19)
    grad_qkv = grad_qkv[: LAYERS * qkv_rows].reshape(LAYERS, qkv_rows, qkv_cols)
    grad_out = grad_out[: LAYERS * out_rows].reshape(LAYERS, out_rows, out_cols)
    mse_loss = packet[LAYERS, 0] / (valid_count * D)
    gain_grad = packet[:LAYERS, None, :gain_cols]

    old_weights = (w_qkv, w_out, w_gu, w_down)
    old_moments = (mom_qkv, mom_out, mom_gu, mom_down)
    gradients = (grad_qkv, grad_out, grad_gu, jnp.stack(down_grads))
    moments = tuple(muon_decay * old_moments[k] + gradients[k] for k in range(4))
    grams = [exact("lrc,lsc->lrs", m, m) for m in moments]
    grams = [
        jnp.sum(
            lax.all_to_all(g[:, None], "head", split_axis=0, concat_axis=1, tiled=True), axis=1
        )
        for g in grams
    ]
    factors = [newton_factor(g) for g in grams]
    factors = [lax.all_gather(f, "head", axis=0, tiled=True) for f in factors]
    new_weights = tuple(
        old_weights[k] * (1.0 - muon_rate * muon_shrink)
        - muon_rate
        * muon_scale
        * math.sqrt(moments[k].shape[-1] * cores)
        * exact("lrs,lsc->lrc", factors[k], moments[k])
        for k in range(4)
    )
    gain_first_new = beta_one * gain_first + (1.0 - beta_one) * gain_grad
    gain_second_new = beta_two * gain_second + (1.0 - beta_two) * gain_grad * gain_grad
    gains_new = norm_gains - adam_rate * (gain_first_new / (1.0 - beta_one**STEP)) / (
        jnp.sqrt(gain_second_new / (1.0 - beta_two**STEP)) + adam_epsilon
    )
    return (
        mse_loss,
        hidden,
        grad_hidden,
        *new_weights,
        *moments,
        gains_new,
        gain_first_new,
        gain_second_new,
    )


def solution(mesh):
    cores, length = mesh.devices.shape
    split = Mesh(mesh.devices.reshape(cores, length // PLANE, PLANE), EVERY)
    stream = P("head", SEQ, None)
    matrix = P(None, SEQ, "head")
    gains = P(None, "head", SEQ)
    return jax.shard_map(
        body,
        mesh=split,
        in_specs=(stream, stream, stream, P(), P("head", SEQ))
        + (matrix,) * 4
        + (gains,)
        + (matrix,) * 4
        + (gains,) * 2,
        out_specs=(P(), stream, stream) + (matrix,) * 8 + (gains,) * 3,
        check_vma=False,
    )
```

```python
from functools import partial
import itertools
import math

import jax
import jax.numpy as jnp
from jax import lax
from jax.experimental import pallas as pl
from jax.experimental.pallas import tpu as pltpu
from jax.sharding import Mesh, PartitionSpec as P

D = 1152
HEADS = 4
HD = 256
FF = 6912
WINDOW = 512
LAYERS = 2
NS_ITERS = 5
STEP = 10
PLANE = 4

norm_eps = 1e-06
rope_base = 10000.0
newton_one = 3.4445
newton_two = -4.775
newton_three = 2.0315
muon_decay = 0.95
muon_rate = 0.15
muon_shrink = 0.01
muon_scale = 0.2
beta_one = 0.9
beta_two = 0.95
adam_rate = 0.7
adam_epsilon = 1e-08
finest_precision = lax.Precision.HIGHEST
MESH = pl.DeviceIdType.MESH
SEQ = ("zd", "tp")
GROUP = ("head", "tp")
EVERY = ("head", "zd", "tp")
bf16 = jnp.bfloat16
f32 = jnp.float32


def linear(places, sizes):
    index = 0
    for place, size in zip(places, sizes):
        index = index * size + place
    return index


def enter(partners):
    barrier = pltpu.get_barrier_semaphore()
    for partner in partners:
        pl.semaphore_signal(barrier, inc=1, device_id=partner, device_id_type=MESH)
    pl.semaphore_wait(barrier, len(partners))


def exchange_kernel(axes, sizes, count, gather, *refs):
    sources, results = refs[:count], refs[count : 2 * count]
    send_sem, recv_sem, own_sem = refs[2 * count :]
    mine = [lax.axis_index(axis) for axis in axes]
    me = linear(mine, sizes)
    offsets = list(itertools.product(*[range(size) for size in sizes]))[1:]
    partners = []
    for offset in offsets:
        places = [lax.rem(m + o, s) for m, o, s in zip(mine, offset, sizes)]
        partners.append((dict(zip(axes, places)), linear(places, sizes)))
    enter([device for device, _ in partners])
    copies = []
    for step, (device, index) in enumerate(partners):
        for k in range(count):
            copy = pltpu.make_async_remote_copy(
                src_ref=sources[k] if gather else sources[k].at[index],
                dst_ref=results[k].at[me],
                send_sem=send_sem.at[k, step],
                recv_sem=recv_sem.at[k, step],
                device_id=device,
                device_id_type=MESH,
            )
            copy.start()
            copies.append(copy)
    for k in range(count):
        own = pltpu.make_async_copy(
            sources[k] if gather else sources[k].at[me], results[k].at[me], own_sem.at[k]
        )
        own.start()
        copies.append(own)
    for copy in copies:
        copy.wait()


def exchange(arrays, axes, ident, gather=False):
    sizes = tuple(lax.axis_size(axis) for axis in axes)
    members = math.prod(sizes)
    count = len(arrays)
    shapes = [((members,) + a.shape) if gather else a.shape for a in arrays]
    return pl.pallas_call(
        partial(exchange_kernel, axes, sizes, count, gather),
        out_shape=[jax.ShapeDtypeStruct(s, a.dtype) for s, a in zip(shapes, arrays)],
        in_specs=[pl.BlockSpec(memory_space=pl.ANY)] * count,
        out_specs=[pl.BlockSpec(memory_space=pl.ANY)] * count,
        scratch_shapes=[
            pltpu.SemaphoreType.DMA((count, members - 1)),
            pltpu.SemaphoreType.DMA((count, members - 1)),
            pltpu.SemaphoreType.DMA((count,)),
        ],
        compiler_params=pltpu.CompilerParams(collective_id=ident, has_side_effects=True),
    )(*arrays)


def spread_kernel(axes, sizes, order, count, *refs):
    sources, results = refs[:count], refs[count : 2 * count]
    send_sem, recv_sem, own_sem = refs[2 * count :]
    place = {axis: lax.axis_index(axis) for axis in axes}
    size = dict(zip(axes, sizes))
    partners = [
        {axis: lax.rem(place[axis] + step, size[axis])}
        for axis in order
        for step in range(1, size[axis])
    ]
    enter(partners)

    def slot(k, where):
        ref = results[k]
        return ref.at[tuple(where[axis] for axis in axes)]

    copies, held, number = [], [(place, None)], 0
    for k in range(count):
        own = pltpu.make_async_copy(sources[k], slot(k, place), own_sem.at[k])
        own.start()
        copies.append(own)
    sends = []
    for axis in order:
        arriving = []
        for where, arrivals in held:
            if arrivals is not None:
                while arrivals:
                    arrivals.pop().wait_recv()
            for step in range(1, size[axis]):
                to = lax.rem(place[axis] + step, size[axis])
                back = lax.rem(place[axis] - step + size[axis], size[axis])
                landing = []
                for k in range(count):
                    copy = pltpu.make_async_remote_copy(
                        src_ref=sources[k] if arrivals is None else slot(k, where),
                        dst_ref=slot(k, where),
                        send_sem=send_sem.at[k, number],
                        recv_sem=recv_sem.at[k, number],
                        device_id={axis: to},
                        device_id_type=MESH,
                    )
                    copy.start()
                    sends.append(copy)
                    landing.append(copy)
                number += 1
                arriving.append((dict(where, **{axis: back}), landing))
        held = held + arriving
    last = len(held) // size[order[-1]]
    for where, arrivals in held[last:]:
        for copy in arrivals:
            copy.wait_recv()
    for copy in sends:
        copy.wait_send()
    for copy in copies:
        copy.wait()


def spread(arrays, axes, order, ident):
    sizes = tuple(lax.axis_size(axis) for axis in axes)
    moves = math.prod(sizes) - 1
    count = len(arrays)
    return pl.pallas_call(
        partial(spread_kernel, axes, sizes, order, count),
        out_shape=[jax.ShapeDtypeStruct(sizes + a.shape, a.dtype) for a in arrays],
        in_specs=[pl.BlockSpec(memory_space=pl.ANY)] * count,
        out_specs=[pl.BlockSpec(memory_space=pl.ANY)] * count,
        scratch_shapes=[
            pltpu.SemaphoreType.DMA((count, moves)),
            pltpu.SemaphoreType.DMA((count, moves)),
            pltpu.SemaphoreType.DMA((count,)),
        ],
        compiler_params=pltpu.CompilerParams(collective_id=ident, has_side_effects=True),
    )(*arrays)


def by_rows(rows, work, step=16):
    @pl.loop(0, rows // step)
    def _(index):
        work(pl.ds(pl.multiple_of(index * step, step), step))


def collect_kernel(cores, members, planes, count, *refs):
    sources, results = refs[:count], refs[count : 2 * count]
    scratch, sems = refs[2 * count : -6], refs[-6:]
    lands, sums = scratch[:count], scratch[count : 2 * count]
    plane_lands = scratch[2 * count : 3 * count]
    totals, z_sums, z_lands = (scratch[i * count : (i + 1) * count] for i in (3, 4, 5))
    core_send, core_recv, tp_send, tp_recv, z_send, z_recv = sems
    core, zd, tp = (lax.axis_index(axis) for axis in EVERY)
    sibling = {"head": 1 - core}
    enter(
        [sibling]
        + [{"tp": lax.rem(tp + step, members)} for step in range(1, members)]
        + [{"zd": lax.rem(zd + step, planes)} for step in range(1, planes)]
    )
    order = list(range(1, members)) + [0]
    sends = []
    core_moves = {}
    for step in order:
        there = lax.rem(tp + step, members)
        for k in range(count):
            copy = pltpu.make_async_remote_copy(
                src_ref=sources[k].at[1 - core, there],
                dst_ref=lands[k].at[step],
                send_sem=core_send.at[k, step],
                recv_sem=core_recv.at[k, step],
                device_id=sibling,
                device_id_type=MESH,
            )
            copy.start()
            core_moves[k, step] = copy
            sends.append(copy)
    plane_moves = {}
    for step in order:
        there = lax.rem(tp + step, members)
        for k in range(count):
            core_moves[k, step].wait_recv()
            source, land, total, summed = sources[k], lands[k], totals[k], sums[k]

            def add(rows):
                value = source[core, there, rows].astype(f32) + land[step, rows].astype(f32)
                if step == 0:
                    total[rows] = value
                else:
                    summed[step, rows] = value.astype(summed.dtype)

            by_rows(total.shape[0], add, 8 if summed.dtype == f32 else 16)
            if step > 0:
                copy = pltpu.make_async_remote_copy(
                    src_ref=summed.at[step],
                    dst_ref=plane_lands[k].at[step],
                    send_sem=tp_send.at[k, step],
                    recv_sem=tp_recv.at[k, step],
                    device_id={"tp": there},
                    device_id_type=MESH,
                )
                copy.start()
                plane_moves[k, step] = copy
                sends.append(copy)
    z_moves = {}
    for k in range(count):
        for step in range(1, members):
            plane_moves[k, step].wait_recv()
        total, land, result = totals[k], plane_lands[k], results[k]

        def gather_plane(rows):
            value = total[rows]
            for step in range(1, members):
                value = value + land[step, rows].astype(f32)
            if planes == 1:
                result[rows] = value
            else:
                total[rows] = value

        stride = 8 if land.dtype == f32 else 16
        by_rows(total.shape[0], gather_plane, stride)
        if planes == 1:
            continue
        height = result.shape[0]
        for step in range(1, planes):
            there = lax.rem(zd + step, planes)
            z_sum = z_sums[k]

            def round_off(rows):
                at = pl.multiple_of(there * height + rows.start, stride)
                z_sum[step, rows] = total[pl.ds(at, rows.size)].astype(z_sum.dtype)

            by_rows(height, round_off, stride)
            copy = pltpu.make_async_remote_copy(
                src_ref=z_sum.at[step],
                dst_ref=z_lands[k].at[step],
                send_sem=z_send.at[k, step],
                recv_sem=z_recv.at[k, step],
                device_id={"zd": there},
                device_id_type=MESH,
            )
            copy.start()
            z_moves[k, step] = copy
            sends.append(copy)
    if planes > 1:
        for k in range(count):
            for step in range(1, planes):
                z_moves[k, step].wait_recv()
            total, land, result = totals[k], z_lands[k], results[k]
            height = result.shape[0]
            stride = 8 if land.dtype == f32 else 16

            def gather_z(rows):
                at = pl.multiple_of(zd * height + rows.start, stride)
                value = total[pl.ds(at, rows.size)]
                for step in range(1, planes):
                    value = value + land[step, rows].astype(f32)
                result[rows] = value

            by_rows(height, gather_z, stride)
    for copy in sends:
        copy.wait_send()


def collect(arrays, planes, ident):
    cores, members = arrays[0].shape[:2]
    count = len(arrays)
    kinds = [a.dtype for a in arrays]
    tall = [a.shape[2:] for a in arrays]
    short = [(rows // planes, columns) for rows, columns in tall]
    z_slots = [(planes,) + s if planes > 1 else (1, 16, 128) for s in short]
    vmem = pltpu.VMEM
    scratch = (
        [vmem((members,) + s, kind) for s, kind in zip(tall, kinds)] * 3
        + [vmem(s, f32) for s in tall]
        + [vmem(s, kind) for s, kind in zip(z_slots, kinds)] * 2
    )
    dma = pltpu.SemaphoreType.DMA
    return pl.pallas_call(
        partial(collect_kernel, cores, members, planes, count),
        out_shape=[jax.ShapeDtypeStruct(s, f32) for s in short],
        in_specs=[pl.BlockSpec(memory_space=pltpu.VMEM)] * count,
        out_specs=[pl.BlockSpec(memory_space=pltpu.VMEM)] * count,
        scratch_shapes=scratch
        + [dma((count, members))] * 4
        + [dma((count, planes))] * 2,
        compiler_params=pltpu.CompilerParams(
            collective_id=ident, has_side_effects=True, vmem_limit_bytes=48 * 2**20
        ),
    )(*arrays)


def shift_kernel(planes, reach, back, source, result, send_sem, recv_sem):
    place = linear([lax.axis_index("zd"), lax.axis_index("tp")], (planes, PLANE))
    total = planes * PLANE
    sign = -1 if back else 1
    to, sources = [], []
    for distance in range(1, reach + 1):
        there = lax.rem(place + sign * distance + total, total)
        to.append({"zd": there // PLANE, "tp": lax.rem(there, PLANE)})
        here = lax.rem(place - sign * distance + total, total)
        sources.append({"zd": here // PLANE, "tp": lax.rem(here, PLANE)})
    barrier = pltpu.get_barrier_semaphore()
    for device in to + sources:
        pl.semaphore_signal(barrier, inc=1, device_id=device, device_id_type=MESH)
    pl.semaphore_wait(barrier, 2 * reach)
    copies = []
    for k, device in enumerate(to):
        copy = pltpu.make_async_remote_copy(
            src_ref=source.at[k] if back else source,
            dst_ref=result.at[k],
            send_sem=send_sem.at[k],
            recv_sem=recv_sem.at[k],
            device_id=device,
            device_id_type=MESH,
        )
        copy.start()
        copies.append(copy)
    for copy in copies:
        copy.wait()


def shift(array, planes, reach, back, ident):
    shape = array.shape if back else (reach,) + array.shape
    return pl.pallas_call(
        partial(shift_kernel, planes, reach, back),
        out_shape=jax.ShapeDtypeStruct(shape, array.dtype),
        in_specs=[pl.BlockSpec(memory_space=pl.ANY)],
        out_specs=pl.BlockSpec(memory_space=pl.ANY),
        scratch_shapes=[pltpu.SemaphoreType.DMA((reach,)), pltpu.SemaphoreType.DMA((reach,))],
        compiler_params=pltpu.CompilerParams(collective_id=ident, has_side_effects=True),
    )(array)


GELU_SLOPE = math.sqrt(2.0 / math.pi)
GELU_CUBE = 0.044715
ACROSS = (((1,), (1,)), ((), ()))
ALONG = (((0,), (0,)), ((), ()))


class Plane:
    def __init__(self, own, bufs, sems):
        self.own = own
        self.rows, self.partial, self.other, self.lands, self.sums, self.arrived = bufs
        self.x_send, self.x_recv, self.f_send, self.f_recv = sems[:4]
        self.c_send, self.c_recv, self.p_send, self.p_recv, self.first = sems[4:]
        self.tp = lax.axis_index("tp")
        self.sibling = {"head": 1 - lax.axis_index("head")}

    def member(self, m):
        tp = self.tp
        upper = lax.rem(lax.div(tp, 2) + lax.div(m, 2), 2)
        lower = lax.rem(lax.rem(tp, 2) + lax.rem(m, 2), 2)
        return {"tp": upper * 2 + lower}

    def remote(self, src, dst, send, recv, device):
        return pltpu.make_async_remote_copy(
            src_ref=src,
            dst_ref=dst,
            send_sem=send,
            recv_sem=recv,
            device_id=device,
            device_id_type=MESH,
        )

    def push(self, m):
        return self.remote(
            self.own, self.rows.at[0, m], self.x_send.at[m], self.x_recv.at[m], self.member(m)
        )

    def keep(self):
        return pltpu.make_async_copy(self.own, self.rows.at[0, 0], self.first)

    def forward(self, m):
        return self.remote(
            self.rows.at[0, m],
            self.rows.at[1, m],
            self.f_send.at[m],
            self.f_recv.at[m],
            self.sibling,
        )

    def cross(self, m):
        return self.remote(
            self.other.at[m], self.lands.at[m], self.c_send.at[m], self.c_recv.at[m], self.sibling
        )

    def home(self, m):
        return self.remote(
            self.sums.at[m],
            self.arrived.at[m],
            self.p_send.at[m],
            self.p_recv.at[m],
            self.member(m),
        )

    def begin(self):
        self.keep().start()
        enter([self.sibling] + [self.member(jnp.int32(m)) for m in range(1, PLANE)])
        for m in range(1, PLANE):
            self.push(jnp.int32(m)).start()

    def work(self, compute):
        def settle(m):
            self.cross(m).wait_recv()

            def add(rows):
                value = self.partial[m, rows] + self.lands[m, rows].astype(f32)
                self.sums[m, rows] = value.astype(bf16)

            by_rows(self.partial.shape[1], add)
            self.home(m).start()

        def step(m, carry):
            @pl.when(m == 0)
            def _():
                self.keep().wait()

            @pl.when(m > 0)
            def _():
                self.push(m).wait_recv()

            self.forward(m).start()
            self.partial[m] = compute(0, m)
            self.forward(m).wait_recv()
            self.other[m] = compute(1, m).astype(bf16)
            self.cross(m).start()

            @pl.when(m >= 2)
            def _():
                settle(m - 1)

            return carry

        lax.fori_loop(0, PLANE, step, 0)
        settle(jnp.int32(PLANE - 1))

    def finish(self, result):
        self.cross(jnp.int32(0)).wait_recv()
        for m in range(1, PLANE):
            self.home(jnp.int32(m)).wait_recv()

        def add(rows):
            value = self.partial[0, rows] + self.lands[0, rows].astype(f32)
            for m in range(1, PLANE):
                value = value + self.arrived[m, rows].astype(f32)
            result[rows] = value

        by_rows(result.shape[0], add)
        for m in range(PLANE):
            m = jnp.int32(m)
            self.forward(m).wait_send()
            self.cross(m).wait_send()
        for m in range(1, PLANE):
            m = jnp.int32(m)
            self.push(m).wait_send()
            self.home(m).wait_send()


def weight_copies(gu_ref, down_ref, gate_up, down, sem):
    blocks = gu_ref.shape[0]
    rows = gate_up.shape[1] // blocks
    copies = [pltpu.make_async_copy(down_ref, down, sem.at[2 * blocks])]
    for block in range(blocks):
        for part in range(2):
            copies.append(
                pltpu.make_async_copy(
                    gu_ref.at[block, part],
                    gate_up.at[part, pl.ds(block * rows, rows)],
                    sem.at[2 * block + part],
                )
            )
    return copies


def ffn_forward_kernel(own, gu_ref, down_ref, group, result, *scratch):
    rows, gate_up, down = scratch[:3]
    plane = Plane(own, (rows,) + scratch[3:8], scratch[8:17])
    weight_sem, group_sem = scratch[17:]
    copies = weight_copies(gu_ref, down_ref, gate_up, down, weight_sem)
    for copy in copies:
        copy.start()
    plane.begin()
    for copy in copies:
        copy.wait()

    def compute(side, m):
        tokens = rows[side, m]
        gate = matmul(tokens, gate_up[0])
        up = matmul(tokens, gate_up[1])
        bend = jnp.tanh(GELU_SLOPE * (gate + GELU_CUBE * (gate * gate * gate)))
        inner = (0.5 * gate * (1.0 + bend) * up).astype(bf16)
        return matmul(inner, down[...])

    plane.work(compute)
    save = pltpu.make_async_copy(rows, group, group_sem)
    save.start()
    plane.finish(result)
    save.wait()


def ffn_backward_kernel(
    own, group, gu_ref, down_ref, result, grad_gu, grad_down, *scratch
):
    rows, gate_up, down = scratch[:3]
    plane = Plane(own, (rows,) + scratch[3:8], scratch[8:17])
    weight_sem, group_sem, saved, d_gate, d_up, inner = scratch[17:23]
    copies = weight_copies(gu_ref, down_ref, gate_up, down, weight_sem)
    for copy in copies:
        copy.start()
    load = pltpu.make_async_copy(group, saved, group_sem)
    load.start()
    plane.begin()
    for copy in copies:
        copy.wait()
    load.wait()

    def recompute(index, carry):
        side, m = lax.div(index, PLANE), lax.rem(index, PLANE)
        tokens = saved[side, m]
        gate = matmul(tokens, gate_up[0])
        up = matmul(tokens, gate_up[1])
        square = gate * gate
        bend = jnp.tanh(GELU_SLOPE * (gate + GELU_CUBE * (square * gate)))
        half = 0.5 * (1.0 + bend)
        value = gate * half
        slope = half + (0.5 * GELU_SLOPE) * gate * (1.0 - bend * bend) * (
            1.0 + (3.0 * GELU_CUBE) * square
        )
        inner[side, m] = (value * up).astype(bf16)
        d_gate[side, m] = (slope * up).astype(bf16)
        d_up[side, m] = value.astype(bf16)
        return carry

    lax.fori_loop(0, 2 * PLANE, recompute, 0)

    def compute(side, m):
        d_inner = lax.dot_general(rows[side, m], down[...], ACROSS, preferred_element_type=f32)
        gate = (d_inner * d_gate[side, m].astype(f32)).astype(bf16)
        up = (d_inner * d_up[side, m].astype(f32)).astype(bf16)
        d_gate[side, m] = gate
        d_up[side, m] = up
        return lax.dot_general(
            gate, gate_up[0], ACROSS, preferred_element_type=f32
        ) + lax.dot_general(up, gate_up[1], ACROSS, preferred_element_type=f32)

    plane.work(compute)
    width = rows.shape[-1]
    step = width // 3

    def tall(ref, columns=slice(None)):
        value = ref[:, :, :, columns]
        return value.reshape(-1, value.shape[-1])

    @pl.loop(0, 3)
    def _(index):
        at = pl.ds(pl.multiple_of(index * step, step), step)
        tokens = tall(saved, at)
        for part, other in enumerate((d_gate, d_up)):
            grad_gu[part, at] = lax.dot_general(
                tokens, tall(other), ALONG, preferred_element_type=f32
            ).astype(bf16)
        product = lax.dot_general(
            tall(rows, at), tall(inner), ALONG, preferred_element_type=f32
        )
        grad_down[:, at] = product.T.astype(bf16)

    plane.finish(result)


def ffn(own, weights, ident, group=None):
    gate_up, down = weights
    tokens, width = own.shape
    share = down.shape[0]
    blocks = gate_up.shape[0]
    vmem, dma = pltpu.VMEM, pltpu.SemaphoreType.DMA
    scratch = [
        vmem((2, PLANE, tokens, width), bf16),
        vmem((2, width, share), bf16),
        vmem((share, width), bf16),
        vmem((PLANE, tokens, width), f32),
    ]
    scratch += [vmem((PLANE, tokens, width), bf16)] * 4
    scratch += [dma((PLANE,))] * 8 + [dma, dma((2 * blocks + 1,)), dma]
    here, there = pl.BlockSpec(memory_space=pltpu.VMEM), pl.BlockSpec(memory_space=pl.ANY)
    gathered = jax.ShapeDtypeStruct((2, PLANE, tokens, width), bf16)
    summed = jax.ShapeDtypeStruct((tokens, width), f32)
    work = 2 * 2 * PLANE * tokens * width * share
    if group is None:
        kernel, operands = ffn_forward_kernel, (own, gate_up, down)
        in_specs, out_specs = [here, there, there], [there, here]
        out_shape, flops = [gathered, summed], 3 * work
    else:
        kernel, operands = ffn_backward_kernel, (own, group, gate_up, down)
        in_specs, out_specs = [here, there, there, there], [here] * 3
        out_shape, flops = [
            summed,
            jax.ShapeDtypeStruct((2, width, share), bf16),
            jax.ShapeDtypeStruct((share, width), bf16),
        ], 8 * work
        scratch += [vmem((2, PLANE, tokens, width), bf16)]
        scratch += [vmem((2, PLANE, tokens, share), bf16)] * 3
    return pl.pallas_call(
        kernel,
        out_shape=out_shape,
        in_specs=in_specs,
        out_specs=out_specs,
        scratch_shapes=scratch,
        compiler_params=pltpu.CompilerParams(
            collective_id=ident, has_side_effects=True, vmem_limit_bytes=60 * 2**20
        ),
        cost_estimate=pl.CostEstimate(
            flops=flops, bytes_accessed=24 * 2**20, transcendentals=2 * PLANE * tokens * share
        ),
    )(*operands)


def padded(array, multiple=16):
    extra = -array.shape[-2] % multiple
    if extra == 0:
        return array
    return jnp.pad(array, [(0, 0)] * (array.ndim - 2) + [(0, extra), (0, 0)])


def rms_norm(values, norm_gain):
    return (
        values * lax.rsqrt(jnp.mean(values * values, axis=-1, keepdims=True) + norm_eps) * norm_gain
    )


def rope_tables(positions, head_dim):
    half_dim = head_dim // 2
    frequency = jnp.exp(
        jnp.arange(half_dim, dtype=jnp.float32) * (-2.0 * math.log(rope_base) / head_dim)
    )
    angles = positions.astype(jnp.float32)[:, None] * frequency[None, :]
    return (jnp.cos(angles), jnp.sin(angles))


def rotate(values, cosine_table, sine_table):
    half_dim = values.shape[-1] // 2
    lower_half = values[..., :half_dim]
    upper_half = values[..., half_dim:]
    return jnp.concatenate(
        [
            lower_half * cosine_table - upper_half * sine_table,
            upper_half * cosine_table + lower_half * sine_table,
        ],
        axis=-1,
    )


def head_prep(mixed_proj, query_gain, key_gain, cosine_table, sine_table):
    seq_rows = mixed_proj.shape[0]
    place_rows = mixed_proj.shape[1]
    queries = mixed_proj[..., : HEADS * HD].reshape(seq_rows, place_rows, HEADS, HD)
    key_heads = mixed_proj[..., HEADS * HD : HEADS * HD + HD]
    values = mixed_proj[..., HEADS * HD + HD :]
    queries = rotate(
        rms_norm(queries, query_gain), cosine_table[:, None, :], sine_table[:, None, :]
    )
    key_heads = rotate(rms_norm(key_heads, key_gain), cosine_table, sine_table)
    return (queries, jnp.concatenate([key_heads, values], axis=-1))


def attend_scores(query_rows, key_tile_rows, allowed):
    logit_scores = jnp.einsum(
        "tals,tes->tlae", query_rows, key_tile_rows, preferred_element_type=jnp.float32
    ) * (1.0 / math.sqrt(HD))
    return jnp.where(allowed[:, None], logit_scores, -jnp.inf)


def matmul(left, right):
    return jnp.dot(left, right, preferred_element_type=f32)


def exact(spec, left, right):
    return jnp.einsum(spec, left, right, precision=finest_precision)


def newton_factor(gram):
    scale = 1.0 / (jnp.sqrt(jnp.trace(gram, axis1=-2, axis2=-1)) + 1e-07)
    scale = scale[..., None, None]
    present = gram * (scale * scale)
    unit = jnp.eye(gram.shape[-1], dtype=f32)
    product = None
    for iteration in range(NS_ITERS):
        square = exact("...rs,...st->...rt", present, present)
        factor = newton_one * unit + newton_two * present + newton_three * square
        product = factor if product is None else exact("...rs,...st->...rt", factor, product)
        if iteration < NS_ITERS - 1:
            present = exact(
                "...rs,...st->...rt", exact("...rs,...st->...rt", factor, present), factor
            )
    return product * scale


def body(
    inputs,
    cotangent,
    teacher,
    segments,
    valid_mask,
    w_qkv,
    w_out,
    w_gu,
    w_down,
    norm_gains,
    mom_qkv,
    mom_out,
    mom_gu,
    mom_down,
    gain_first,
    gain_second,
):
    cores = lax.axis_size("head")
    planes = lax.axis_size("zd")
    seq_devices = planes * PLANE
    core = lax.axis_index("head")
    seq_place = lax.axis_index("zd") * PLANE + lax.axis_index("tp")
    half_seqs, stretch_len = inputs.shape[:2]
    tokens = half_seqs * stretch_len
    all_seqs = half_seqs * cores
    seq_length = stretch_len * seq_devices
    reach = -(-WINDOW // stretch_len)
    key_len = (reach + 1) * stretch_len
    qkv_rows, qkv_cols = w_qkv.shape[1:]
    out_rows, out_cols = w_out.shape[1:]
    gu_rows = w_gu.shape[1]
    ff_block = w_down.shape[1]
    share = FF // (cores * PLANE)
    half_planes = planes // cores
    gain_cols = norm_gains.shape[-1]
    gain_len = gain_cols * seq_devices
    lanes = -(-gain_cols // 128) * 128

    packet = jnp.zeros((8, lanes), f32)
    packet = packet.at[:LAYERS, :gain_cols].set(norm_gains[:, 0].astype(bf16).astype(f32))
    packet = packet.at[LAYERS, 0].set(jnp.sum(valid_mask.astype(f32)))
    pieces = w_gu.astype(bf16).reshape(LAYERS, gu_rows, cores, half_planes, PLANE, ff_block)
    pieces = pieces.transpose(2, 4, 0, 1, 3, 5).reshape(cores * PLANE, LAYERS * gu_rows, share)
    (gu_pieces,) = exchange([padded(pieces)], GROUP, 0)
    gu_pieces = gu_pieces[:, : LAYERS * gu_rows].reshape(cores * PLANE, LAYERS, gu_rows, share)
    packets, mixed_parts, project_parts = spread(
        [
            packet,
            padded(w_qkv.astype(bf16).reshape(LAYERS * qkv_rows, qkv_cols)),
            padded(w_out.astype(bf16).reshape(LAYERS * out_rows, out_cols)),
        ],
        EVERY,
        ("zd", "tp", "head"),
        1,
    )
    packets = packets.reshape(cores, seq_devices, 8, lanes)
    valid_count = jnp.sum(packets[:, :, LAYERS, 0])
    gain_rows = [
        packets[:, :, layer, :gain_cols].reshape(cores, gain_len) for layer in range(LAYERS)
    ]

    def whole(parts, rows, columns, layer):
        parts = parts[..., layer * rows : (layer + 1) * rows, :]
        return parts.reshape(cores, -1, columns).transpose(1, 0, 2).reshape(-1, cores * columns)

    def ffn_weights(layer, after):
        pieces, rows = gu_pieces[:, layer], w_down[layer].astype(bf16)
        if after is not None:
            pieces, rows, after = lax.optimization_barrier((pieces, rows, after))
        pieces = lax.all_gather(pieces.reshape(2, PLANE * gu_rows, share), "zd", axis=0)
        if PLANE * gu_rows % 16:
            pieces = pieces.transpose(1, 0, 2, 3).reshape(1, 2, D, share)
        rows = lax.all_gather(rows, "zd", axis=0)
        rows = rows.reshape(cores, half_planes * ff_block, out_cols)
        rows = lax.all_to_all(rows, "head", split_axis=0, concat_axis=0, tiled=True)
        return pieces, rows.transpose(1, 0, 2).reshape(share, D)

    full = [ffn_weights(0, None)] + [None] * (LAYERS - 1)

    own_places = seq_place * stretch_len + jnp.arange(stretch_len, dtype=jnp.int32)
    key_places = (seq_place - reach) * stretch_len + jnp.arange(key_len, dtype=jnp.int32)
    cosine_table, sine_table = rope_tables(own_places, HD)
    own_rows = lax.dynamic_slice_in_dim(segments, core * half_seqs, half_seqs, 0)
    own_segments = lax.dynamic_slice_in_dim(own_rows, seq_place * stretch_len, stretch_len, 1)
    padded_segments = jnp.pad(own_rows, ((0, 0), (reach * stretch_len, 0)), constant_values=-1)
    key_segments = lax.dynamic_slice_in_dim(padded_segments, seq_place * stretch_len, key_len, 1)
    spacing = own_places[:, None] - key_places[None, :]
    allowed = (spacing >= 0) & (spacing < WINDOW) & (key_places[None, :] >= 0)
    allowed = allowed[None] & (own_segments[:, :, None] == key_segments[:, None, :])

    hidden = inputs.astype(f32)
    saved = []
    for layer in range(LAYERS):
        w_mixed = whole(mixed_parts, qkv_rows, qkv_cols, layer)
        w_project = whole(project_parts, out_rows, out_cols, layer)
        gain_pack = gain_rows[layer]
        norm_attn = gain_pack[0, :D]
        post_attn = gain_pack[0, D : 2 * D]
        query_gain = gain_pack[0, 2 * D :]
        norm_ffn = gain_pack[1, :D]
        post_ffn = gain_pack[1, D : 2 * D]
        key_gain = gain_pack[1, 2 * D :]
        normed_f, pre_attn_back = jax.vjp(rms_norm, hidden, norm_attn)
        normed = normed_f.astype(bf16)
        mixed_proj = jnp.einsum("bpd,de->bpe", normed, w_mixed, preferred_element_type=f32)
        prepared, prep_back = jax.vjp(
            partial(head_prep, cosine_table=cosine_table, sine_table=sine_table),
            mixed_proj,
            query_gain,
            key_gain,
        )
        query_rows = prepared[0].astype(bf16)
        own_keyvals = prepared[1].astype(bf16)
        earlier = shift(
            own_keyvals.reshape(tokens, 2 * HD), planes, reach, False, 3 + layer
        ).reshape(reach, half_seqs, stretch_len, 2 * HD)
        if layer + 1 < LAYERS:
            full[layer + 1] = ffn_weights(layer + 1, earlier)
        ffn_share = full[layer]
        full[layer] = (w_mixed, w_project, ffn_share)
        keyvals = jnp.concatenate(
            [earlier[reach - 1 - k] for k in range(reach)] + [own_keyvals], axis=1
        )
        key_tile_rows = keyvals[..., :HD]
        value_tile_rows = keyvals[..., HD:]
        logit_scores = attend_scores(query_rows, key_tile_rows, allowed)
        log_total = jax.nn.logsumexp(logit_scores, axis=-1)
        soft = jnp.exp(logit_scores - log_total[..., None])
        attended = jnp.einsum(
            "zusi,zix->zsux", soft.astype(bf16), value_tile_rows, preferred_element_type=f32
        ).astype(bf16)
        attended_rows = attended.reshape(half_seqs, stretch_len, HEADS * HD)
        projected = jnp.einsum("bpq,qd->bpd", attended_rows, w_project, preferred_element_type=f32)
        branch_out, post_attn_back = jax.vjp(rms_norm, projected, post_attn)
        hidden_half = hidden + branch_out
        normed_f, pre_ffn_back = jax.vjp(rms_norm, hidden_half, norm_ffn)
        group_normed, down_out = ffn(
            normed_f.astype(bf16).reshape(tokens, D), ffn_share, 5 + layer
        )
        down_out = down_out.reshape(half_seqs, stretch_len, D)
        branch_out, post_ffn_back = jax.vjp(rms_norm, down_out, post_ffn)
        hidden = hidden_half + branch_out
        saved.append(
            (
                normed,
                pre_attn_back,
                prep_back,
                query_rows,
                keyvals,
                log_total,
                attended_rows,
                post_attn_back,
                pre_ffn_back,
                group_normed,
                post_ffn_back,
            )
        )

    target_gap = hidden - teacher.astype(f32)
    valid_weight = valid_mask.astype(f32)[:, :, None]
    square_sum = jnp.sum(valid_weight * target_gap * target_gap)
    loss_weight = float(all_seqs * seq_length * D // 4)
    grad_hidden = (
        cotangent.astype(f32)
        + 2.0 * loss_weight / (valid_count * D) * valid_weight * target_gap
    )

    attn_grads = [None] * LAYERS
    down_grads = [None] * LAYERS
    gain_grads = [None] * LAYERS
    gu_sums = [None] * LAYERS
    logit_scale = 1.0 / math.sqrt(HD)
    for layer in reversed(range(LAYERS)):
        (
            normed,
            pre_attn_back,
            prep_back,
            query_rows,
            keyvals,
            log_total,
            attended_rows,
            post_attn_back,
            pre_ffn_back,
            group_normed,
            post_ffn_back,
        ) = saved[layer]
        w_mixed, w_project, ffn_share = full[layer]
        key_tile_rows = keyvals[..., :HD]
        value_tile_rows = keyvals[..., HD:]
        d_down, d_post_ffn = post_ffn_back(grad_hidden)
        d_normed_ffn, grad_gu, grad_down = ffn(
            d_down.astype(bf16).reshape(tokens, D), ffn_share, 9 + layer, group_normed
        )
        d_normed_ffn = d_normed_ffn.reshape(half_seqs, stretch_len, D)

        down_pieces = grad_down.reshape(share, cores, out_cols).transpose(1, 0, 2)
        down_pieces = lax.all_to_all(
            down_pieces, "head", split_axis=0, concat_axis=0, tiled=True
        ).reshape(planes * ff_block, out_cols)
        grad_down = lax.psum_scatter(
            down_pieces, "zd", scatter_dimension=0, tiled=True
        ).astype(f32)
        gu_sums[layer] = [
            lax.psum_scatter(g, "zd", scatter_dimension=0, tiled=True) for g in grad_gu
        ]

        d_half, d_norm_ffn = pre_ffn_back(d_normed_ffn)
        d_half = d_half + grad_hidden
        d_projected, d_post_attn = post_attn_back(d_half)
        d_proj_low = d_projected.astype(bf16)
        grad_project = jnp.einsum(
            "bpq,bpd->qd", attended_rows, d_proj_low, preferred_element_type=f32
        )
        d_attended = (
            jnp.einsum("bpd,qd->bpq", d_proj_low, w_project, preferred_element_type=f32)
            .astype(bf16)
            .reshape(half_seqs, stretch_len, HEADS, HD)
        )
        logit_scores = attend_scores(query_rows, key_tile_rows, allowed)
        soft = jnp.exp(logit_scores - log_total[..., None])
        d_probs = jnp.einsum(
            "tals,tes->tlae", d_attended, value_tile_rows, preferred_element_type=f32
        )
        row_total = jnp.sum(soft * d_probs, axis=-1, keepdims=True)
        score_gradient = (soft * (d_probs - row_total)).astype(bf16)
        d_queries = (
            jnp.einsum("zusi,zix->zsux", score_gradient, key_tile_rows, preferred_element_type=f32)
            * logit_scale
        )
        d_keys = (
            jnp.einsum("lqkp,lkqf->lpf", score_gradient, query_rows, preferred_element_type=f32)
            * logit_scale
        )
        d_values = jnp.einsum(
            "lqkp,lkqf->lpf", soft.astype(bf16), d_attended, preferred_element_type=f32
        )
        d_keyvals = jnp.concatenate([d_keys, d_values], axis=-1)
        pieces = [
            d_keyvals[:, (reach - k) * stretch_len : (reach - k + 1) * stretch_len]
            for k in range(reach + 1)
        ]
        outgoing = jnp.stack(pieces[1:]).astype(bf16).reshape(reach, tokens, 2 * HD)
        incoming = shift(outgoing, planes, reach, True, 17 + layer)
        d_own = pieces[0] + jnp.sum(incoming.astype(f32), axis=0).reshape(
            half_seqs, stretch_len, 2 * HD
        )
        d_mixed, d_query_gain, d_key_gain = prep_back((d_queries, d_own))
        d_mixed_low = d_mixed.astype(bf16)
        grad_mixed = jnp.einsum("bpd,bpe->de", normed, d_mixed_low, preferred_element_type=f32)
        d_normed = jnp.einsum("bpe,de->bpd", d_mixed_low, w_mixed, preferred_element_type=f32)
        d_hidden, d_norm_attn = pre_attn_back(d_normed)
        grad_hidden = d_hidden + d_half
        gain_grads[layer] = jnp.stack(
            [
                jnp.concatenate([d_norm_attn, d_post_attn, d_query_gain]),
                jnp.concatenate([d_norm_ffn, d_post_ffn, d_key_gain]),
            ]
        )

        attn_grads[layer] = (grad_mixed.astype(bf16), grad_project.astype(bf16))
        down_grads[layer] = grad_down

    pieces = jnp.stack([jnp.stack(pair) for pair in zip(*gu_sums)])
    pieces = pieces.reshape(2, LAYERS, PLANE, gu_rows, share).transpose(0, 2, 1, 3, 4)
    pieces = padded(pieces.reshape(2 * PLANE, LAYERS * gu_rows, share))
    (pieces,) = exchange([pieces], GROUP, 15)
    pieces = pieces[:, : LAYERS * gu_rows].astype(f32)
    pieces = pieces.reshape(cores, PLANE, LAYERS, gu_rows, half_planes, ff_block)
    grad_gu = pieces.transpose(2, 3, 0, 4, 1, 5).reshape(LAYERS, gu_rows, FF)
    blocks = []
    for parts, columns in zip(zip(*attn_grads), (qkv_cols, out_cols)):
        block = jnp.stack(parts).reshape(LAYERS, planes, PLANE, -1, cores, columns)
        block = block.transpose(4, 2, 1, 0, 3, 5).reshape(cores, PLANE, planes, -1, columns)
        blocks.append(padded(block).reshape(cores, PLANE, -1, columns))
    packet = jnp.stack(gain_grads, axis=1).reshape(cores, LAYERS, planes, PLANE, gain_cols)
    packet = packet.transpose(0, 3, 2, 1, 4)
    packet = jnp.pad(packet, [(0, 0)] * 3 + [(0, 8 - LAYERS), (0, lanes - gain_cols)])
    packet = packet.at[:, :, :, LAYERS, 0].set(square_sum)
    blocks.append(packet.reshape(cores, PLANE, planes * 8, lanes))
    grad_qkv, grad_out, packet = collect(blocks, planes, 19)
    grad_qkv = grad_qkv[: LAYERS * qkv_rows].reshape(LAYERS, qkv_rows, qkv_cols)
    grad_out = grad_out[: LAYERS * out_rows].reshape(LAYERS, out_rows, out_cols)
    mse_loss = packet[LAYERS, 0] / (valid_count * D)
    gain_grad = packet[:LAYERS, None, :gain_cols]

    old_weights = (w_qkv, w_out, w_gu, w_down)
    old_moments = (mom_qkv, mom_out, mom_gu, mom_down)
    gradients = (grad_qkv, grad_out, grad_gu, jnp.stack(down_grads))
    moments = tuple(muon_decay * old_moments[k] + gradients[k] for k in range(4))
    grams = [exact("lrc,lsc->lrs", m, m) for m in moments]
    grams = [
        jnp.sum(
            lax.all_to_all(g[:, None], "head", split_axis=0, concat_axis=1, tiled=True), axis=1
        )
        for g in grams
    ]
    factors = [newton_factor(g) for g in grams]
    factors = [lax.all_gather(f, "head", axis=0, tiled=True) for f in factors]
    new_weights = tuple(
        old_weights[k] * (1.0 - muon_rate * muon_shrink)
        - muon_rate
        * muon_scale
        * math.sqrt(moments[k].shape[-1] * cores)
        * exact("lrs,lsc->lrc", factors[k], moments[k])
        for k in range(4)
    )
    gain_first_new = beta_one * gain_first + (1.0 - beta_one) * gain_grad
    gain_second_new = beta_two * gain_second + (1.0 - beta_two) * gain_grad * gain_grad
    gains_new = norm_gains - adam_rate * (gain_first_new / (1.0 - beta_one**STEP)) / (
        jnp.sqrt(gain_second_new / (1.0 - beta_two**STEP)) + adam_epsilon
    )
    return (
        mse_loss,
        hidden,
        grad_hidden,
        *new_weights,
        *moments,
        gains_new,
        gain_first_new,
        gain_second_new,
    )


def solution(mesh):
    cores, length = mesh.devices.shape
    split = Mesh(mesh.devices.reshape(cores, length // PLANE, PLANE), EVERY)
    stream = P("head", SEQ, None)
    matrix = P(None, SEQ, "head")
    gains = P(None, "head", SEQ)
    return jax.shard_map(
        body,
        mesh=split,
        in_specs=(stream, stream, stream, P(), P("head", SEQ))
        + (matrix,) * 4
        + (gains,)
        + (matrix,) * 4
        + (gains,) * 2,
        out_specs=(P(), stream, stream) + (matrix,) * 8 + (gains,) * 3,
        check_vma=False,
    )
```

```python
from functools import partial
import itertools
import math

import jax
import jax.numpy as jnp
from jax import lax
from jax.experimental import pallas as pl
from jax.experimental.pallas import tpu as pltpu
from jax.sharding import Mesh, PartitionSpec as P

D = 1152
HEADS = 4
HD = 256
FF = 6912
WINDOW = 512
LAYERS = 2
NS_ITERS = 5
STEP = 10
PLANE = 4

norm_eps = 1e-06
rope_base = 10000.0
newton_one = 3.4445
newton_two = -4.775
newton_three = 2.0315
muon_decay = 0.95
muon_rate = 0.15
muon_shrink = 0.01
muon_scale = 0.2
beta_one = 0.9
beta_two = 0.95
adam_rate = 0.7
adam_epsilon = 1e-08
finest_precision = lax.Precision.HIGHEST
MESH = pl.DeviceIdType.MESH
SEQ = ("zd", "tp")
GROUP = ("head", "tp")
EVERY = ("head", "zd", "tp")
bf16 = jnp.bfloat16
f32 = jnp.float32
LIGHT = pl.CostEstimate(flops=1, bytes_accessed=1, transcendentals=0)


def linear(places, sizes):
    index = 0
    for place, size in zip(places, sizes):
        index = index * size + place
    return index


def enter(partners):
    barrier = pltpu.get_barrier_semaphore()
    for partner in partners:
        pl.semaphore_signal(barrier, inc=1, device_id=partner, device_id_type=MESH)
    pl.semaphore_wait(barrier, len(partners))


def exchange_kernel(axes, sizes, count, gather, *refs):
    sources, results = refs[:count], refs[count : 2 * count]
    send_sem, recv_sem, own_sem = refs[2 * count :]
    mine = [lax.axis_index(axis) for axis in axes]
    me = linear(mine, sizes)
    offsets = list(itertools.product(*[range(size) for size in sizes]))[1:]
    partners = []
    for offset in offsets:
        places = [lax.rem(m + o, s) for m, o, s in zip(mine, offset, sizes)]
        partners.append((dict(zip(axes, places)), linear(places, sizes)))
    enter([device for device, _ in partners])
    copies = []
    for step, (device, index) in enumerate(partners):
        for k in range(count):
            copy = pltpu.make_async_remote_copy(
                src_ref=sources[k] if gather else sources[k].at[index],
                dst_ref=results[k].at[me],
                send_sem=send_sem.at[k, step],
                recv_sem=recv_sem.at[k, step],
                device_id=device,
                device_id_type=MESH,
            )
            copy.start()
            copies.append(copy)
    for k in range(count):
        own = pltpu.make_async_copy(
            sources[k] if gather else sources[k].at[me], results[k].at[me], own_sem.at[k]
        )
        own.start()
        copies.append(own)
    for copy in copies:
        copy.wait()


def exchange(arrays, axes, ident, gather=False):
    sizes = tuple(lax.axis_size(axis) for axis in axes)
    members = math.prod(sizes)
    count = len(arrays)
    shapes = [((members,) + a.shape) if gather else a.shape for a in arrays]
    return pl.pallas_call(
        partial(exchange_kernel, axes, sizes, count, gather),
        out_shape=[jax.ShapeDtypeStruct(s, a.dtype) for s, a in zip(shapes, arrays)],
        in_specs=[pl.BlockSpec(memory_space=pl.ANY)] * count,
        out_specs=[pl.BlockSpec(memory_space=pl.ANY)] * count,
        scratch_shapes=[
            pltpu.SemaphoreType.DMA((count, members - 1)),
            pltpu.SemaphoreType.DMA((count, members - 1)),
            pltpu.SemaphoreType.DMA((count,)),
        ],
        cost_estimate=LIGHT,
        compiler_params=pltpu.CompilerParams(collective_id=ident, has_side_effects=True),
    )(*arrays)


class Spread:
    ORDER = ("zd", "tp", "head")

    def __init__(self, sizes, slots, send_sem, recv_sem):
        self.size = dict(zip(EVERY, sizes))
        self.place = {axis: lax.axis_index(axis) for axis in EVERY}
        self.slots, self.send_sem, self.recv_sem = slots, send_sem, recv_sem
        self.held, self.sends, self.number = [(self.place, None)], [], 0

    def partners(self):
        return [
            {axis: lax.rem(self.place[axis] + step, self.size[axis])}
            for axis in self.ORDER
            for step in range(1, self.size[axis])
        ]

    def stage(self, axis):
        arriving = []
        for where, arrivals in self.held:
            while arrivals:
                arrivals.pop().wait_recv()
            for step in range(1, self.size[axis]):
                to = lax.rem(self.place[axis] + step, self.size[axis])
                back = lax.rem(self.place[axis] - step + self.size[axis], self.size[axis])
                landing = []
                for k, slot in enumerate(self.slots):
                    ref = slot.at[tuple(where[name] for name in EVERY)]
                    copy = pltpu.make_async_remote_copy(
                        src_ref=ref,
                        dst_ref=ref,
                        send_sem=self.send_sem.at[k, self.number],
                        recv_sem=self.recv_sem.at[k, self.number],
                        device_id={axis: to},
                        device_id_type=MESH,
                    )
                    copy.start()
                    self.sends.append(copy)
                    landing.append(copy)
                self.number += 1
                arriving.append((dict(where, **{axis: back}), landing))
        self.held = self.held + arriving

    def finish(self):
        for _, arrivals in self.held:
            while arrivals:
                arrivals.pop().wait_recv()
        for copy in self.sends:
            copy.wait_send()


def start_kernel(sizes, layer, first, *refs):
    cores, planes, members = sizes
    if first:
        gu, qkv, out, packet, gu_result, mixed, project, packets = refs[:8]
        qkv_slots, out_slots, packet_slots, send_sem, recv_sem = refs[8:13]
        pieces, gu_send, gu_recv, gu_own = refs[13:]
        slots = [packet_slots, qkv_slots, out_slots]
    else:
        qkv, out, mixed, project, qkv_slots, out_slots, send_sem, recv_sem = refs
        slots = [qkv_slots, out_slots]
    gather = Spread(sizes, slots, send_sem, recv_sem)
    here = tuple(gather.place[name] for name in EVERY)
    core, _, tp = here
    group = []
    for step in range(1, cores * members):
        far = lax.rem(core + step // members, cores), lax.rem(tp + step % members, members)
        group.append((dict(zip(GROUP, far)), linear(far, (cores, members))))
    if first:
        enter(gather.partners() + [device for device, _ in group])
        packet_slots[here] = packet[...]
    else:
        enter(gather.partners())
    for source, slot in ((qkv, qkv_slots), (out, out_slots)):
        rows = source.shape[1]
        slot[here + (slice(0, rows),)] = source[layer].astype(bf16)
        if slot.shape[3] > rows:
            slot[here + (slice(rows, None),)] = jnp.zeros(
                (slot.shape[3] - rows, slot.shape[4]), bf16
            )
    gather.stage("zd")
    moves = []
    if first:
        layers, rows, columns = gu.shape
        block = columns // (planes * members)
        half = planes // cores
        for c in range(cores):
            for j in range(members):
                for i in range(layers):
                    cut = [
                        gu[i, :, pl.ds(((c * half + k) * members + j) * block, block)]
                        for k in range(half)
                    ]
                    value = jnp.concatenate(cut, axis=1) if half > 1 else cut[0]
                    pieces[c * members + j, i * rows : (i + 1) * rows] = value.astype(bf16)
        if pieces.shape[1] > layers * rows:
            for piece in range(cores * members):
                pieces[piece, layers * rows :] = jnp.zeros(
                    (pieces.shape[1] - layers * rows, pieces.shape[2]), bf16
                )
        me = linear((core, tp), (cores, members))
        for step, (device, index) in enumerate(group):
            copy = pltpu.make_async_remote_copy(
                src_ref=pieces.at[index],
                dst_ref=gu_result.at[me],
                send_sem=gu_send.at[step],
                recv_sem=gu_recv.at[step],
                device_id=device,
                device_id_type=MESH,
            )
            copy.start()
            moves.append(copy)
        own = pltpu.make_async_copy(pieces.at[me], gu_result.at[me], gu_own)
        own.start()
        moves.append(own)
    gather.stage("tp")
    gather.stage("head")
    gather.finish()
    for slot, result, rows in ((qkv_slots, mixed, qkv.shape[1]), (out_slots, project, out.shape[1])):
        columns = slot.shape[4]
        for h, z, t in itertools.product(range(cores), range(planes), range(members)):
            row = (z * members + t) * rows
            result[row : row + rows, h * columns : (h + 1) * columns] = slot[h, z, t, :rows]
    if first:
        packets[...] = packet_slots[...]
    for copy in moves:
        copy.wait()


def start(w_qkv, w_out, layer, ident, w_gu=None, packet=None):
    sizes = tuple(lax.axis_size(axis) for axis in EVERY)
    cores, planes, members = sizes
    vmem, dma = pltpu.VMEM, pltpu.SemaphoreType.DMA
    here, there = pl.BlockSpec(memory_space=pltpu.VMEM), pl.BlockSpec(memory_space=pl.ANY)
    shape = jax.ShapeDtypeStruct
    (_, qkv_rows, qkv_cols), (_, out_rows, out_cols) = w_qkv.shape, w_out.shape
    outs = [
        shape((qkv_rows * planes * members, qkv_cols * cores), bf16),
        shape((out_rows * planes * members, out_cols * cores), bf16),
    ]
    slots = [vmem(sizes + (-(-w.shape[1] // 16) * 16, w.shape[2]), bf16) for w in (w_qkv, w_out)]
    count, moves = 2, math.prod(sizes) - 1
    operands, out_specs, extra = [w_qkv, w_out], [here] * 2, []
    if w_gu is not None:
        layers, rows, columns = w_gu.shape
        tall = -(-layers * rows // 16) * 16
        piece = (cores * members, tall, columns // (cores * members))
        operands = [w_gu] + operands + [packet]
        outs = [shape(piece, bf16)] + outs + [shape(sizes + packet.shape, f32)]
        out_specs = [there] + out_specs + [here]
        slots, count = slots + [vmem(sizes + packet.shape, f32)], 3
        extra = [vmem(piece, bf16), dma((cores * members - 1,)), dma((cores * members - 1,)), dma]
    return pl.pallas_call(
        partial(start_kernel, sizes, layer, w_gu is not None),
        out_shape=outs,
        in_specs=[here] * len(operands),
        out_specs=out_specs,
        scratch_shapes=slots + [dma((count, moves))] * 2 + extra,
        cost_estimate=LIGHT,
        compiler_params=pltpu.CompilerParams(
            collective_id=ident, has_side_effects=True, vmem_limit_bytes=48 * 2**20
        ),
    )(*operands)


def by_rows(rows, work, step=16):
    @pl.loop(0, rows // step)
    def _(index):
        work(pl.ds(pl.multiple_of(index * step, step), step))


def collect_kernel(sizes, layers, *refs):
    cores, planes, members = sizes
    acts, packet, results = refs[: 4 * layers], refs[4 * layers], refs[4 * layers + 1 :][:3]
    rest = list(refs[4 * layers + 4 :])
    take = lambda number: [rest.pop(0) for _ in range(number)]
    far, halves = take(4 * layers), take(2 * layers)
    packet_land = rest.pop(0)
    pieces, plane_lands, totals, z_sums, z_lands = (take(3) for _ in range(5))
    act_send, act_recv, packet_send, packet_recv = take(4)
    tp_send, tp_recv, z_send, z_recv = take(4)
    core, zd, tp = (lax.axis_index(axis) for axis in EVERY)
    sibling = {"head": 1 - core}
    enter(
        [sibling]
        + [{"tp": lax.rem(tp + step, members)} for step in range(1, members)]
        + [{"zd": lax.rem(zd + step, planes)} for step in range(1, planes)]
    )
    sends = []

    def send(src, dst, send_sem, recv_sem, device):
        copy = pltpu.make_async_remote_copy(
            src_ref=src,
            dst_ref=dst,
            send_sem=send_sem,
            recv_sem=recv_sem,
            device_id=device,
            device_id_type=MESH,
        )
        copy.start()
        sends.append(copy)
        return copy

    for k in range(2 * layers):
        grad, half = acts[2 * k + 1], halves[k]
        width = half.shape[2]
        for h in range(cores):
            half[h] = grad[:, h * width : (h + 1) * width]
    moves = []
    for k in range(2 * layers):
        moves.append(
            send(acts[2 * k], far[2 * k], act_send.at[2 * k], act_recv.at[2 * k], sibling)
        )
        moves.append(
            send(
                halves[k].at[1 - core],
                far[2 * k + 1],
                act_send.at[2 * k + 1],
                act_recv.at[2 * k + 1],
                sibling,
            )
        )
    gains = send(packet.at[1 - core], packet_land, packet_send, packet_recv, sibling)
    plane_moves, z_moves = {}, {}
    for kind in range(3):
        piece = pieces[kind]
        if kind < 2:
            for layer in range(layers):
                k = 2 * layer + kind
                near = lax.dot_general(
                    acts[2 * k][...], halves[k][core], ALONG, preferred_element_type=f32
                )
                moves[2 * k].wait_recv()
                moves[2 * k + 1].wait_recv()
                value = near + lax.dot_general(
                    far[2 * k][...], far[2 * k + 1][...], ALONG, preferred_element_type=f32
                )
                value = value.astype(bf16)
                rows = value.shape[0] // (planes * members)
                slab = piece.shape[1] // planes
                for z, t in itertools.product(range(planes), range(members)):
                    at = (z * members + t) * rows
                    to = z * slab + layer * rows
                    piece[t, to : to + rows] = value[at : at + rows]
            if slab > layers * rows:
                for z, t in itertools.product(range(planes), range(members)):
                    piece[t, z * slab + layers * rows : (z + 1) * slab] = jnp.zeros(
                        (slab - layers * rows, piece.shape[2]), bf16
                    )
        else:
            gains.wait_recv()
            piece[...] = packet[core] + packet_land[...]
        for step in range(1, members):
            there = lax.rem(tp + step, members)
            plane_moves[kind, step] = send(
                piece.at[there],
                plane_lands[kind].at[step],
                tp_send.at[kind, step],
                tp_recv.at[kind, step],
                {"tp": there},
            )
    for kind in range(3):
        for step in range(1, members):
            plane_moves[kind, step].wait_recv()
        piece, total, land, result = pieces[kind], totals[kind], plane_lands[kind], results[kind]
        stride = 8 if land.dtype == f32 else 16

        def gather_plane(rows):
            value = piece[tp, rows].astype(f32)
            for step in range(1, members):
                value = value + land[step, rows].astype(f32)
            total[rows] = value

        by_rows(total.shape[0], gather_plane, stride)
        height = result.shape[0]
        z_sum = z_sums[kind]
        for step in range(1, planes):
            there = lax.rem(zd + step, planes)

            def round_off(rows):
                at = pl.multiple_of(there * height + rows.start, stride)
                z_sum[step, rows] = total[pl.ds(at, rows.size)].astype(z_sum.dtype)

            by_rows(height, round_off, stride)
            z_moves[kind, step] = send(
                z_sum.at[step],
                z_lands[kind].at[step],
                z_send.at[kind, step],
                z_recv.at[kind, step],
                {"zd": there},
            )
    for kind in range(3):
        for step in range(1, planes):
            z_moves[kind, step].wait_recv()
        total, land, result = totals[kind], z_lands[kind], results[kind]
        height = result.shape[0]
        stride = 8 if land.dtype == f32 else 16

        def gather_z(rows):
            at = pl.multiple_of(zd * height + rows.start, stride)
            value = total[pl.ds(at, rows.size)]
            for step in range(1, planes):
                value = value + land[step, rows].astype(f32)
            result[rows] = value

        by_rows(height, gather_z, stride)
    for copy in sends:
        copy.wait_send()


def collect(acts, packet, ident):
    sizes = tuple(lax.axis_size(axis) for axis in EVERY)
    cores, planes, members = sizes
    layers = len(acts) // 4
    vmem, dma = pltpu.VMEM, pltpu.SemaphoreType.DMA
    tokens = acts[0].shape[0]
    halves = [acts[2 * k + 1].shape[1] // cores for k in range(2 * layers)]
    slabs = []
    for kind in range(2):
        rows = layers * acts[2 * kind].shape[1] // (planes * members)
        slabs.append((-(-rows // 16) * 16, halves[kind], bf16))
    slabs.append((packet.shape[2] // planes, packet.shape[3], f32))
    far = []
    for k in range(2 * layers):
        far += [vmem(acts[2 * k].shape, bf16), vmem((tokens, halves[k]), bf16)]
    scratch = far + [vmem((cores, tokens, width), bf16) for width in halves]
    scratch += [vmem(packet.shape[1:], f32)]
    scratch += [vmem((members, planes * r, c), kind) for r, c, kind in slabs] * 2
    scratch += [vmem((planes * r, c), f32) for r, c, _ in slabs]
    scratch += [vmem((planes, r, c), kind) for r, c, kind in slabs] * 2
    scratch += [dma((4 * layers,))] * 2 + [dma] * 2
    scratch += [dma((3, members))] * 2 + [dma((3, planes))] * 2
    here = pl.BlockSpec(memory_space=pltpu.VMEM)
    return pl.pallas_call(
        partial(collect_kernel, sizes, layers),
        out_shape=[jax.ShapeDtypeStruct((r, c), f32) for r, c, _ in slabs],
        in_specs=[here] * (len(acts) + 1),
        out_specs=[here] * 3,
        scratch_shapes=scratch,
        cost_estimate=LIGHT,
        compiler_params=pltpu.CompilerParams(
            collective_id=ident, has_side_effects=True, vmem_limit_bytes=56 * 2**20
        ),
    )(*acts, packet)


def shift_kernel(planes, reach, back, source, result, send_sem, recv_sem):
    place = linear([lax.axis_index("zd"), lax.axis_index("tp")], (planes, PLANE))
    total = planes * PLANE
    sign = -1 if back else 1
    to, sources = [], []
    for distance in range(1, reach + 1):
        there = lax.rem(place + sign * distance + total, total)
        to.append({"zd": there // PLANE, "tp": lax.rem(there, PLANE)})
        here = lax.rem(place - sign * distance + total, total)
        sources.append({"zd": here // PLANE, "tp": lax.rem(here, PLANE)})
    barrier = pltpu.get_barrier_semaphore()
    for device in to + sources:
        pl.semaphore_signal(barrier, inc=1, device_id=device, device_id_type=MESH)
    pl.semaphore_wait(barrier, 2 * reach)
    copies = []
    for k, device in enumerate(to):
        copy = pltpu.make_async_remote_copy(
            src_ref=source.at[k] if back else source,
            dst_ref=result.at[k],
            send_sem=send_sem.at[k],
            recv_sem=recv_sem.at[k],
            device_id=device,
            device_id_type=MESH,
        )
        copy.start()
        copies.append(copy)
    for copy in copies:
        copy.wait()


def shift(array, planes, reach, back, ident):
    shape = array.shape if back else (reach,) + array.shape
    return pl.pallas_call(
        partial(shift_kernel, planes, reach, back),
        out_shape=jax.ShapeDtypeStruct(shape, array.dtype),
        in_specs=[pl.BlockSpec(memory_space=pl.ANY)],
        out_specs=pl.BlockSpec(memory_space=pl.ANY),
        scratch_shapes=[pltpu.SemaphoreType.DMA((reach,)), pltpu.SemaphoreType.DMA((reach,))],
        cost_estimate=LIGHT,
        compiler_params=pltpu.CompilerParams(collective_id=ident, has_side_effects=True),
    )(array)


GELU_SLOPE = math.sqrt(2.0 / math.pi)
GELU_CUBE = 0.044715
ACROSS = (((1,), (1,)), ((), ()))
ALONG = (((0,), (0,)), ((), ()))


class Plane:
    def __init__(self, own, bufs, sems):
        self.own = own
        self.rows, self.partial, self.other, self.lands, self.sums, self.arrived = bufs
        self.x_send, self.x_recv, self.f_send, self.f_recv = sems[:4]
        self.c_send, self.c_recv, self.p_send, self.p_recv, self.first = sems[4:]
        self.tp = lax.axis_index("tp")
        self.sibling = {"head": 1 - lax.axis_index("head")}

    def member(self, m):
        tp = self.tp
        upper = lax.rem(lax.div(tp, 2) + lax.div(m, 2), 2)
        lower = lax.rem(lax.rem(tp, 2) + lax.rem(m, 2), 2)
        return {"tp": upper * 2 + lower}

    def remote(self, src, dst, send, recv, device):
        return pltpu.make_async_remote_copy(
            src_ref=src,
            dst_ref=dst,
            send_sem=send,
            recv_sem=recv,
            device_id=device,
            device_id_type=MESH,
        )

    def push(self, m):
        return self.remote(
            self.own, self.rows.at[0, m], self.x_send.at[m], self.x_recv.at[m], self.member(m)
        )

    def keep(self):
        return pltpu.make_async_copy(self.own, self.rows.at[0, 0], self.first)

    def forward(self, m):
        return self.remote(
            self.rows.at[0, m],
            self.rows.at[1, m],
            self.f_send.at[m],
            self.f_recv.at[m],
            self.sibling,
        )

    def cross(self, m):
        return self.remote(
            self.other.at[m], self.lands.at[m], self.c_send.at[m], self.c_recv.at[m], self.sibling
        )

    def home(self, m):
        return self.remote(
            self.sums.at[m],
            self.arrived.at[m],
            self.p_send.at[m],
            self.p_recv.at[m],
            self.member(m),
        )

    def begin(self):
        self.keep().start()
        enter([self.sibling] + [self.member(jnp.int32(m)) for m in range(1, PLANE)])
        for m in range(1, PLANE):
            self.push(jnp.int32(m)).start()

    def work(self, compute):
        def settle(m):
            self.cross(m).wait_recv()

            def add(rows):
                value = self.partial[m, rows] + self.lands[m, rows].astype(f32)
                self.sums[m, rows] = value.astype(bf16)

            by_rows(self.partial.shape[1], add)
            self.home(m).start()

        def step(m, carry):
            @pl.when(m == 0)
            def _():
                self.keep().wait()

            @pl.when(m > 0)
            def _():
                self.push(m).wait_recv()

            self.forward(m).start()
            self.partial[m] = compute(0, m)
            self.forward(m).wait_recv()
            self.other[m] = compute(1, m).astype(bf16)
            self.cross(m).start()

            @pl.when(m >= 2)
            def _():
                settle(m - 1)

            return carry

        lax.fori_loop(0, PLANE, step, 0)
        settle(jnp.int32(PLANE - 1))

    def finish(self, result):
        self.cross(jnp.int32(0)).wait_recv()
        for m in range(1, PLANE):
            self.home(jnp.int32(m)).wait_recv()

        def add(rows):
            value = self.partial[0, rows] + self.lands[0, rows].astype(f32)
            for m in range(1, PLANE):
                value = value + self.arrived[m, rows].astype(f32)
            result[rows] = value

        by_rows(result.shape[0], add)
        for m in range(PLANE):
            m = jnp.int32(m)
            self.forward(m).wait_send()
            self.cross(m).wait_send()
        for m in range(1, PLANE):
            m = jnp.int32(m)
            self.push(m).wait_send()
            self.home(m).wait_send()


def gate_up_copies(gu_ref, gate_up, sem):
    blocks = gu_ref.shape[0]
    rows = gate_up.shape[1] // blocks
    return [
        pltpu.make_async_copy(
            gu_ref.at[block, part],
            gate_up.at[part, pl.ds(block * rows, rows)],
            sem.at[2 * block + part],
        )
        for block in range(blocks)
        for part in range(2)
    ]


def ffn_forward_kernel(own, gu_ref, halves_ref, group, saved_down, result, *scratch):
    rows, gate_up, down = scratch[:3]
    plane = Plane(own, (rows,) + scratch[3:8], scratch[8:17])
    weight_sem, group_sem, halves, half_send, half_recv, half_own, save_sem = scratch[17:]
    core = lax.axis_index("head")
    share, width = halves.shape[1:]
    copies = gate_up_copies(gu_ref, gate_up, weight_sem)
    copies.append(
        pltpu.make_async_copy(
            halves_ref.at[0, pl.ds(pl.multiple_of(core * share, 16), share)],
            halves.at[core],
            half_own,
        )
    )
    for copy in copies:
        copy.start()
    plane.begin()
    half = plane.remote(
        halves_ref.at[0, pl.ds(pl.multiple_of((1 - core) * share, 16), share)],
        halves.at[core],
        half_send,
        half_recv,
        plane.sibling,
    )
    half.start()
    for copy in copies:
        copy.wait()
    pltpu.make_async_remote_copy(
        src_ref=halves_ref.at[0, pl.ds(pl.multiple_of((1 - core) * share, 16), share)],
        dst_ref=halves.at[1 - core],
        send_sem=half_send,
        recv_sem=half_recv,
        device_id=plane.sibling,
        device_id_type=MESH,
    ).wait_recv()

    def join(at):
        down[at] = jnp.concatenate([halves[h, at] for h in range(2)], axis=1)

    by_rows(share, join, 32)
    keep_down = pltpu.make_async_copy(down, saved_down, save_sem)
    keep_down.start()

    def compute(side, m):
        tokens = rows[side, m]
        gate = matmul(tokens, gate_up[0])
        up = matmul(tokens, gate_up[1])
        bend = jnp.tanh(GELU_SLOPE * (gate + GELU_CUBE * (gate * gate * gate)))
        inner = (0.5 * gate * (1.0 + bend) * up).astype(bf16)
        return matmul(inner, down[...])

    plane.work(compute)
    save = pltpu.make_async_copy(rows, group, group_sem)
    save.start()
    plane.finish(result)
    save.wait()
    keep_down.wait()
    half.wait_send()


def ffn_backward_kernel(
    own, group, gu_ref, down_ref, result, grad_gate, grad_up, grad_down, *scratch
):
    rows, gate_up, down = scratch[:3]
    plane = Plane(own, (rows,) + scratch[3:8], scratch[8:17])
    weight_sem, group_sem, saved, d_gate, d_up, inner = scratch[17:23]
    down_sem, turned, down_halves, half_send, half_recv, half_own = scratch[23:]
    core = lax.axis_index("head")
    copies = gate_up_copies(gu_ref, gate_up, weight_sem)
    copies.append(pltpu.make_async_copy(down_ref, down, down_sem))
    for copy in copies:
        copy.start()
    load = pltpu.make_async_copy(group, saved, group_sem)
    load.start()
    plane.begin()
    for copy in copies:
        copy.wait()
    load.wait()

    def recompute(index, carry):
        side, m = lax.div(index, PLANE), lax.rem(index, PLANE)
        tokens = saved[side, m]
        gate = matmul(tokens, gate_up[0])
        up = matmul(tokens, gate_up[1])
        square = gate * gate
        bend = jnp.tanh(GELU_SLOPE * (gate + GELU_CUBE * (square * gate)))
        half = 0.5 * (1.0 + bend)
        value = gate * half
        slope = half + (0.5 * GELU_SLOPE) * gate * (1.0 - bend * bend) * (
            1.0 + (3.0 * GELU_CUBE) * square
        )
        inner[side, m] = (value * up).astype(bf16)
        d_gate[side, m] = (slope * up).astype(bf16)
        d_up[side, m] = value.astype(bf16)
        return carry

    lax.fori_loop(0, 2 * PLANE, recompute, 0)

    def compute(side, m):
        d_inner = lax.dot_general(rows[side, m], down[...], ACROSS, preferred_element_type=f32)
        gate = (d_inner * d_gate[side, m].astype(f32)).astype(bf16)
        up = (d_inner * d_up[side, m].astype(f32)).astype(bf16)
        d_gate[side, m] = gate
        d_up[side, m] = up
        return lax.dot_general(
            gate, gate_up[0], ACROSS, preferred_element_type=f32
        ) + lax.dot_general(up, gate_up[1], ACROSS, preferred_element_type=f32)

    plane.work(compute)
    width = rows.shape[-1]
    step = width // 3

    def tall(ref, columns=slice(None)):
        value = ref[:, :, :, columns]
        return value.reshape(-1, value.shape[-1])

    @pl.loop(0, 3)
    def _(index):
        at = pl.ds(pl.multiple_of(index * step, step), step)
        tokens = tall(saved, at)
        for target, other in ((grad_gate, d_gate), (grad_up, d_up)):
            target[at] = lax.dot_general(
                tokens, tall(other), ALONG, preferred_element_type=f32
            ).astype(bf16)
        turned[at] = lax.dot_general(
            tall(rows, at), tall(inner), ALONG, preferred_element_type=f32
        ).astype(bf16)

    half_width = down_halves.shape[2]
    for h in range(2):
        down_halves[h] = turned[h * half_width : (h + 1) * half_width].T
    half = plane.remote(
        down_halves.at[1 - core], grad_down.at[core], half_send, half_recv, plane.sibling
    )
    half.start()
    stay = pltpu.make_async_copy(down_halves.at[core], grad_down.at[core], half_own)
    stay.start()
    plane.finish(result)
    half.wait()
    stay.wait()


def ffn(own, weights, ident, group=None):
    gate_up, down = weights
    tokens, width = own.shape
    blocks, _, _, share = gate_up.shape
    vmem, dma = pltpu.VMEM, pltpu.SemaphoreType.DMA
    scratch = [
        vmem((2, PLANE, tokens, width), bf16),
        vmem((2, width, share), bf16),
        vmem((share, width), bf16),
        vmem((PLANE, tokens, width), f32),
    ]
    scratch += [vmem((PLANE, tokens, width), bf16)] * 4
    scratch += [dma((PLANE,))] * 8 + [dma, dma((2 * blocks,)), dma]
    here, there = pl.BlockSpec(memory_space=pltpu.VMEM), pl.BlockSpec(memory_space=pl.ANY)
    shape = jax.ShapeDtypeStruct
    summed = shape((tokens, width), f32)
    if group is None:
        kernel, operands = ffn_forward_kernel, (own, gate_up, down)
        in_specs, out_specs = [here, there, there], [there, there, here]
        out_shape = [
            shape((2, PLANE, tokens, width), bf16),
            shape((share, width), bf16),
            summed,
        ]
        scratch += [vmem((2, share, width // 2), bf16)] + [dma] * 4
    else:
        kernel, operands = ffn_backward_kernel, (own, group, gate_up, down)
        in_specs, out_specs = [here, there, there, there], [here] * 3 + [there]
        out_shape = [
            summed,
            shape((width, share), bf16),
            shape((width, share), bf16),
            shape((2, share, width // 2), bf16),
        ]
        scratch += [vmem((2, PLANE, tokens, width), bf16)]
        scratch += [vmem((2, PLANE, tokens, share), bf16)] * 3
        scratch += [dma, vmem((width, share), bf16), vmem((2, share, width // 2), bf16)]
        scratch += [dma] * 3
    return pl.pallas_call(
        kernel,
        out_shape=out_shape,
        in_specs=in_specs,
        out_specs=out_specs,
        scratch_shapes=scratch,
        cost_estimate=LIGHT,
        compiler_params=pltpu.CompilerParams(
            collective_id=ident, has_side_effects=True, vmem_limit_bytes=60 * 2**20
        ),
    )(*operands)


def padded(array, multiple=16):
    extra = -array.shape[-2] % multiple
    if extra == 0:
        return array
    return jnp.pad(array, [(0, 0)] * (array.ndim - 2) + [(0, extra), (0, 0)])


def rms_norm(values, norm_gain):
    return (
        values * lax.rsqrt(jnp.mean(values * values, axis=-1, keepdims=True) + norm_eps) * norm_gain
    )


def rope_tables(positions, head_dim):
    half_dim = head_dim // 2
    frequency = jnp.exp(
        jnp.arange(half_dim, dtype=jnp.float32) * (-2.0 * math.log(rope_base) / head_dim)
    )
    angles = positions.astype(jnp.float32)[:, None] * frequency[None, :]
    return (jnp.cos(angles), jnp.sin(angles))


def rotate(values, cosine_table, sine_table):
    half_dim = values.shape[-1] // 2
    lower_half = values[..., :half_dim]
    upper_half = values[..., half_dim:]
    return jnp.concatenate(
        [
            lower_half * cosine_table - upper_half * sine_table,
            upper_half * cosine_table + lower_half * sine_table,
        ],
        axis=-1,
    )


def head_prep(mixed_proj, query_gain, key_gain, cosine_table, sine_table):
    seq_rows = mixed_proj.shape[0]
    place_rows = mixed_proj.shape[1]
    queries = mixed_proj[..., : HEADS * HD].reshape(seq_rows, place_rows, HEADS, HD)
    key_heads = mixed_proj[..., HEADS * HD : HEADS * HD + HD]
    values = mixed_proj[..., HEADS * HD + HD :]
    queries = rotate(
        rms_norm(queries, query_gain), cosine_table[:, None, :], sine_table[:, None, :]
    )
    key_heads = rotate(rms_norm(key_heads, key_gain), cosine_table, sine_table)
    return (queries, jnp.concatenate([key_heads, values], axis=-1))


def attend_scores(query_rows, key_tile_rows, allowed):
    logit_scores = jnp.einsum(
        "tals,tes->tlae", query_rows, key_tile_rows, preferred_element_type=jnp.float32
    ) * (1.0 / math.sqrt(HD))
    return jnp.where(allowed[:, None], logit_scores, -jnp.inf)


def matmul(left, right):
    return jnp.dot(left, right, preferred_element_type=f32)


def exact(spec, left, right):
    return jnp.einsum(spec, left, right, precision=finest_precision)


def newton_factor(gram):
    scale = 1.0 / (jnp.sqrt(jnp.trace(gram, axis1=-2, axis2=-1)) + 1e-07)
    scale = scale[..., None, None]
    present = gram * (scale * scale)
    unit = jnp.eye(gram.shape[-1], dtype=f32)
    product = None
    for iteration in range(NS_ITERS):
        square = exact("...rs,...st->...rt", present, present)
        factor = newton_one * unit + newton_two * present + newton_three * square
        product = factor if product is None else exact("...rs,...st->...rt", factor, product)
        if iteration < NS_ITERS - 1:
            present = exact(
                "...rs,...st->...rt", exact("...rs,...st->...rt", factor, present), factor
            )
    return product * scale


def body(
    inputs,
    cotangent,
    teacher,
    segments,
    valid_mask,
    w_qkv,
    w_out,
    w_gu,
    w_down,
    norm_gains,
    mom_qkv,
    mom_out,
    mom_gu,
    mom_down,
    gain_first,
    gain_second,
):
    cores = lax.axis_size("head")
    planes = lax.axis_size("zd")
    seq_devices = planes * PLANE
    core = lax.axis_index("head")
    seq_place = lax.axis_index("zd") * PLANE + lax.axis_index("tp")
    half_seqs, stretch_len = inputs.shape[:2]
    tokens = half_seqs * stretch_len
    all_seqs = half_seqs * cores
    seq_length = stretch_len * seq_devices
    reach = -(-WINDOW // stretch_len)
    key_len = (reach + 1) * stretch_len
    qkv_rows, qkv_cols = w_qkv.shape[1:]
    out_rows, out_cols = w_out.shape[1:]
    gu_rows = w_gu.shape[1]
    ff_block = w_down.shape[1]
    share = FF // (cores * PLANE)
    half_planes = planes // cores
    gain_cols = norm_gains.shape[-1]
    gain_len = gain_cols * seq_devices
    lanes = -(-gain_cols // 128) * 128

    packet = jnp.zeros((8, lanes), f32)
    packet = packet.at[:LAYERS, :gain_cols].set(norm_gains[:, 0].astype(bf16).astype(f32))
    packet = packet.at[LAYERS, 0].set(jnp.sum(valid_mask.astype(f32)))
    gu_pieces, *attn_weights, packets = start(w_qkv, w_out, 0, 0, w_gu, packet)
    gu_pieces = gu_pieces[:, : LAYERS * gu_rows].reshape(cores * PLANE, LAYERS, gu_rows, share)
    packets = packets.reshape(cores, seq_devices, 8, lanes)
    valid_count = jnp.sum(packets[:, :, LAYERS, 0])
    gain_rows = [
        packets[:, :, layer, :gain_cols].reshape(cores, gain_len) for layer in range(LAYERS)
    ]

    def ffn_weights(layer, after):
        pieces, rows = gu_pieces, w_down
        if after is not None:
            pieces, rows, after = lax.optimization_barrier((pieces, rows, after))
        pieces, rows = pieces[:, layer], rows[layer : layer + 1].astype(bf16)
        pieces = lax.all_gather(pieces.reshape(2, PLANE * gu_rows, share), "zd", axis=0)
        if PLANE * gu_rows % 16:
            pieces = pieces.transpose(1, 0, 2, 3).reshape(1, 2, D, share)
        return (pieces, lax.all_gather(rows, "zd", axis=1, tiled=True)), after

    full = [ffn_weights(0, None)[0]] + [None] * (LAYERS - 1)

    own_places = seq_place * stretch_len + jnp.arange(stretch_len, dtype=jnp.int32)
    key_places = (seq_place - reach) * stretch_len + jnp.arange(key_len, dtype=jnp.int32)
    cosine_table, sine_table = rope_tables(own_places, HD)
    own_rows = lax.dynamic_slice_in_dim(segments, core * half_seqs, half_seqs, 0)
    own_segments = lax.dynamic_slice_in_dim(own_rows, seq_place * stretch_len, stretch_len, 1)
    padded_segments = jnp.pad(own_rows, ((0, 0), (reach * stretch_len, 0)), constant_values=-1)
    key_segments = lax.dynamic_slice_in_dim(padded_segments, seq_place * stretch_len, key_len, 1)
    spacing = own_places[:, None] - key_places[None, :]
    allowed = (spacing >= 0) & (spacing < WINDOW) & (key_places[None, :] >= 0)
    allowed = allowed[None] & (own_segments[:, :, None] == key_segments[:, None, :])

    hidden = inputs.astype(f32)
    saved = []
    for layer in range(LAYERS):
        w_mixed, w_project = attn_weights
        gain_pack = gain_rows[layer]
        norm_attn = gain_pack[0, :D]
        post_attn = gain_pack[0, D : 2 * D]
        query_gain = gain_pack[0, 2 * D :]
        norm_ffn = gain_pack[1, :D]
        post_ffn = gain_pack[1, D : 2 * D]
        key_gain = gain_pack[1, 2 * D :]
        normed_f, pre_attn_back = jax.vjp(rms_norm, hidden, norm_attn)
        normed = normed_f.astype(bf16)
        mixed_proj = jnp.einsum("bpd,de->bpe", normed, w_mixed, preferred_element_type=f32)
        prepared, prep_back = jax.vjp(
            partial(head_prep, cosine_table=cosine_table, sine_table=sine_table),
            mixed_proj,
            query_gain,
            key_gain,
        )
        query_rows = prepared[0].astype(bf16)
        own_keyvals = prepared[1].astype(bf16)
        earlier = shift(own_keyvals.reshape(tokens, 2 * HD), planes, reach, False, 3 + layer)
        if layer + 1 < LAYERS:
            full[layer + 1], earlier = ffn_weights(layer + 1, earlier)
        earlier = earlier.reshape(reach, half_seqs, stretch_len, 2 * HD)
        ffn_share = full[layer]
        keyvals = jnp.concatenate(
            [earlier[reach - 1 - k] for k in range(reach)] + [own_keyvals], axis=1
        )
        key_tile_rows = keyvals[..., :HD]
        value_tile_rows = keyvals[..., HD:]
        logit_scores = attend_scores(query_rows, key_tile_rows, allowed)
        log_total = jax.nn.logsumexp(logit_scores, axis=-1)
        soft = jnp.exp(logit_scores - log_total[..., None])
        attended = jnp.einsum(
            "zusi,zix->zsux", soft.astype(bf16), value_tile_rows, preferred_element_type=f32
        ).astype(bf16)
        attended_rows = attended.reshape(half_seqs, stretch_len, HEADS * HD)
        projected = jnp.einsum("bpq,qd->bpd", attended_rows, w_project, preferred_element_type=f32)
        branch_out, post_attn_back = jax.vjp(rms_norm, projected, post_attn)
        hidden_half = hidden + branch_out
        normed_f, pre_ffn_back = jax.vjp(rms_norm, hidden_half, norm_ffn)
        normed_ffn = normed_f.astype(bf16).reshape(tokens, D)
        if layer + 1 < LAYERS:
            later_qkv, later_out, attended_rows = lax.optimization_barrier(
                (w_qkv, w_out, attended_rows)
            )
            attn_weights = start(later_qkv, later_out, layer + 1, 2 + 20 * layer)
            normed_ffn, *attn_weights = lax.optimization_barrier((normed_ffn, *attn_weights))
        group_normed, whole_down, down_out = ffn(normed_ffn, ffn_share, 5 + layer)
        full[layer] = (w_mixed, w_project, (ffn_share[0], whole_down))
        down_out = down_out.reshape(half_seqs, stretch_len, D)
        branch_out, post_ffn_back = jax.vjp(rms_norm, down_out, post_ffn)
        hidden = hidden_half + branch_out
        saved.append(
            (
                normed,
                pre_attn_back,
                prep_back,
                query_rows,
                keyvals,
                log_total,
                attended_rows,
                post_attn_back,
                pre_ffn_back,
                group_normed,
                post_ffn_back,
            )
        )

    target_gap = hidden - teacher.astype(f32)
    valid_weight = valid_mask.astype(f32)[:, :, None]
    square_sum = jnp.sum(valid_weight * target_gap * target_gap)
    loss_weight = float(all_seqs * seq_length * D // 4)
    grad_hidden = (
        cotangent.astype(f32)
        + 2.0 * loss_weight / (valid_count * D) * valid_weight * target_gap
    )

    attn_acts = [None] * LAYERS
    down_grads = [None] * LAYERS
    gain_grads = [None] * LAYERS
    gu_sums = [None] * LAYERS
    logit_scale = 1.0 / math.sqrt(HD)
    for layer in reversed(range(LAYERS)):
        (
            normed,
            pre_attn_back,
            prep_back,
            query_rows,
            keyvals,
            log_total,
            attended_rows,
            post_attn_back,
            pre_ffn_back,
            group_normed,
            post_ffn_back,
        ) = saved[layer]
        w_mixed, w_project, ffn_share = full[layer]
        key_tile_rows = keyvals[..., :HD]
        value_tile_rows = keyvals[..., HD:]
        d_down, d_post_ffn = post_ffn_back(grad_hidden)
        d_normed_ffn, *grad_gu, grad_down = ffn(
            d_down.astype(bf16).reshape(tokens, D), ffn_share, 9 + layer, group_normed
        )
        d_normed_ffn = d_normed_ffn.reshape(half_seqs, stretch_len, D)

        down_grads[layer] = lax.psum_scatter(
            grad_down.reshape(planes * ff_block, out_cols), "zd", scatter_dimension=0, tiled=True
        )
        gu_sums[layer] = [
            lax.psum_scatter(g, "zd", scatter_dimension=0, tiled=True) for g in grad_gu
        ]

        d_half, d_norm_ffn = pre_ffn_back(d_normed_ffn)
        d_half = d_half + grad_hidden
        d_projected, d_post_attn = post_attn_back(d_half)
        d_proj_low = d_projected.astype(bf16)
        d_attended = (
            jnp.einsum("bpd,qd->bpq", d_proj_low, w_project, preferred_element_type=f32)
            .astype(bf16)
            .reshape(half_seqs, stretch_len, HEADS, HD)
        )
        logit_scores = attend_scores(query_rows, key_tile_rows, allowed)
        soft = jnp.exp(logit_scores - log_total[..., None])
        d_probs = jnp.einsum(
            "tals,tes->tlae", d_attended, value_tile_rows, preferred_element_type=f32
        )
        row_total = jnp.sum(soft * d_probs, axis=-1, keepdims=True)
        score_gradient = (soft * (d_probs - row_total)).astype(bf16)
        d_queries = (
            jnp.einsum("zusi,zix->zsux", score_gradient, key_tile_rows, preferred_element_type=f32)
            * logit_scale
        )
        d_keys = (
            jnp.einsum("lqkp,lkqf->lpf", score_gradient, query_rows, preferred_element_type=f32)
            * logit_scale
        )
        d_values = jnp.einsum(
            "lqkp,lkqf->lpf", soft.astype(bf16), d_attended, preferred_element_type=f32
        )
        d_keyvals = jnp.concatenate([d_keys, d_values], axis=-1)
        pieces = [
            d_keyvals[:, (reach - k) * stretch_len : (reach - k + 1) * stretch_len]
            for k in range(reach + 1)
        ]
        outgoing = jnp.stack(pieces[1:]).astype(bf16).reshape(reach, tokens, 2 * HD)
        if layer + 1 < LAYERS:
            outgoing, gu_sums[layer + 1], down_grads[layer + 1] = lax.optimization_barrier(
                (outgoing, gu_sums[layer + 1], down_grads[layer + 1])
            )
        incoming = shift(outgoing, planes, reach, True, 17 + layer)
        d_own = pieces[0] + jnp.sum(incoming.astype(f32), axis=0).reshape(
            half_seqs, stretch_len, 2 * HD
        )
        d_mixed, d_query_gain, d_key_gain = prep_back((d_queries, d_own))
        d_mixed_low = d_mixed.astype(bf16)
        d_normed = jnp.einsum("bpe,de->bpd", d_mixed_low, w_mixed, preferred_element_type=f32)
        d_hidden, d_norm_attn = pre_attn_back(d_normed)
        grad_hidden = d_hidden + d_half
        gain_grads[layer] = jnp.stack(
            [
                jnp.concatenate([d_norm_attn, d_post_attn, d_query_gain]),
                jnp.concatenate([d_norm_ffn, d_post_ffn, d_key_gain]),
            ]
        )

        attn_acts[layer] = [
            value.reshape(tokens, -1) for value in (normed, d_mixed_low, attended_rows, d_proj_low)
        ]

    collected = [None] * LAYERS
    for layer in reversed(range(LAYERS)):
        packet = gain_grads[layer].reshape(cores, planes, PLANE, gain_cols).transpose(0, 2, 1, 3)
        packet = jnp.pad(packet[:, :, :, None], [(0, 0)] * 3 + [(0, 7), (0, lanes - gain_cols)])
        packet = packet.at[:, :, :, 1, 0].set(square_sum)
        packet = packet.reshape(cores, PLANE, planes * 8, lanes)
        if layer > 0:
            packet, attn_acts[0][1] = lax.optimization_barrier((packet, attn_acts[0][1]))
        else:
            packet, collected[1:], gu_sums[0] = lax.optimization_barrier(
                (packet, collected[1:], gu_sums[0])
            )
        collected[layer] = collect(attn_acts[layer], packet, 19 + layer)
    grad_qkv, grad_out, packet = (jnp.stack(parts) for parts in zip(*collected))
    grad_qkv, grad_out = grad_qkv[:, :qkv_rows], grad_out[:, :out_rows]
    mse_loss = packet[0, 1, 0] / (valid_count * D)
    gain_grad = packet[:, :1, :gain_cols]

    gu_sums, grad_qkv, down_grads[0] = lax.optimization_barrier(
        (gu_sums, grad_qkv, down_grads[0])
    )
    pieces = jnp.stack([jnp.stack(pair) for pair in zip(*gu_sums)])
    pieces = pieces.reshape(2, LAYERS, PLANE, gu_rows, share).transpose(0, 2, 1, 3, 4)
    pieces = padded(pieces.reshape(2 * PLANE, LAYERS * gu_rows, share))
    (pieces,) = exchange([pieces], GROUP, 15)
    pieces = pieces[:, : LAYERS * gu_rows].astype(f32)
    pieces = pieces.reshape(cores, PLANE, LAYERS, gu_rows, half_planes, ff_block)
    grad_gu = pieces.transpose(2, 3, 0, 4, 1, 5).reshape(LAYERS, gu_rows, FF)
    old_weights = (w_qkv, w_out, w_gu, w_down)
    old_moments = (mom_qkv, mom_out, mom_gu, mom_down)
    gradients = (grad_qkv, grad_out, grad_gu, jnp.stack(down_grads).astype(f32))
    moments = tuple(muon_decay * old_moments[k] + gradients[k] for k in range(4))
    grams = [exact("lrc,lsc->lrs", m, m) for m in moments]
    grams = [
        jnp.sum(
            lax.all_to_all(g[:, None], "head", split_axis=0, concat_axis=1, tiled=True), axis=1
        )
        for g in grams
    ]
    factors = [newton_factor(g) for g in grams]
    others = [lax.ppermute(f, "head", [(0, 1), (1, 0)]) for f in factors]
    factors = [
        jnp.where(core == 0, jnp.concatenate([f, o]), jnp.concatenate([o, f]))
        for f, o in zip(factors, others)
    ]
    new_weights = tuple(
        old_weights[k] * (1.0 - muon_rate * muon_shrink)
        - muon_rate
        * muon_scale
        * math.sqrt(moments[k].shape[-1] * cores)
        * exact("lrs,lsc->lrc", factors[k], moments[k])
        for k in range(4)
    )
    gain_first_new = beta_one * gain_first + (1.0 - beta_one) * gain_grad
    gain_second_new = beta_two * gain_second + (1.0 - beta_two) * gain_grad * gain_grad
    gains_new = norm_gains - adam_rate * (gain_first_new / (1.0 - beta_one**STEP)) / (
        jnp.sqrt(gain_second_new / (1.0 - beta_two**STEP)) + adam_epsilon
    )
    return (
        mse_loss,
        hidden,
        grad_hidden,
        *new_weights,
        *moments,
        gains_new,
        gain_first_new,
        gain_second_new,
    )


def solution(mesh):
    cores, length = mesh.devices.shape
    split = Mesh(mesh.devices.reshape(cores, length // PLANE, PLANE), EVERY)
    stream = P("head", SEQ, None)
    matrix = P(None, SEQ, "head")
    gains = P(None, "head", SEQ)
    return jax.shard_map(
        body,
        mesh=split,
        in_specs=(stream, stream, stream, P(), P("head", SEQ))
        + (matrix,) * 4
        + (gains,)
        + (matrix,) * 4
        + (gains,) * 2,
        out_specs=(P(), stream, stream) + (matrix,) * 8 + (gains,) * 3,
        check_vma=False,
    )
```

```python
from functools import partial
import itertools
import math

import jax
import jax.numpy as jnp
from jax import lax
from jax.experimental import pallas as pl
from jax.experimental.pallas import tpu as pltpu
from jax.sharding import Mesh, PartitionSpec as P

D = 1152
HEADS = 4
HD = 256
FF = 6912
WINDOW = 512
LAYERS = 2
NS_ITERS = 5
STEP = 10
PLANE = 4

norm_eps = 1e-06
rope_base = 10000.0
newton_one = 3.4445
newton_two = -4.775
newton_three = 2.0315
muon_decay = 0.95
muon_rate = 0.15
muon_shrink = 0.01
muon_scale = 0.2
beta_one = 0.9
beta_two = 0.95
adam_rate = 0.7
adam_epsilon = 1e-08
finest_precision = lax.Precision.HIGHEST
MESH = pl.DeviceIdType.MESH
SEQ = ("zd", "tp")
GROUP = ("head", "tp")
EVERY = ("head", "zd", "tp")
bf16 = jnp.bfloat16
f32 = jnp.float32
LIGHT = pl.CostEstimate(flops=1, bytes_accessed=1, transcendentals=0)


def linear(places, sizes):
    index = 0
    for place, size in zip(places, sizes):
        index = index * size + place
    return index


def enter(partners):
    barrier = pltpu.get_barrier_semaphore()
    for partner in partners:
        pl.semaphore_signal(barrier, inc=1, device_id=partner, device_id_type=MESH)
    pl.semaphore_wait(barrier, len(partners))


def exchange_kernel(axes, sizes, count, gather, *refs):
    sources, results = refs[:count], refs[count : 2 * count]
    send_sem, recv_sem, own_sem = refs[2 * count :]
    mine = [lax.axis_index(axis) for axis in axes]
    me = linear(mine, sizes)
    offsets = list(itertools.product(*[range(size) for size in sizes]))[1:]
    partners = []
    for offset in offsets:
        places = [lax.rem(m + o, s) for m, o, s in zip(mine, offset, sizes)]
        partners.append((dict(zip(axes, places)), linear(places, sizes)))
    enter([device for device, _ in partners])
    copies = []
    for step, (device, index) in enumerate(partners):
        for k in range(count):
            copy = pltpu.make_async_remote_copy(
                src_ref=sources[k] if gather else sources[k].at[index],
                dst_ref=results[k].at[me],
                send_sem=send_sem.at[k, step],
                recv_sem=recv_sem.at[k, step],
                device_id=device,
                device_id_type=MESH,
            )
            copy.start()
            copies.append(copy)
    for k in range(count):
        own = pltpu.make_async_copy(
            sources[k] if gather else sources[k].at[me], results[k].at[me], own_sem.at[k]
        )
        own.start()
        copies.append(own)
    for copy in copies:
        copy.wait()


def exchange(arrays, axes, ident, gather=False):
    sizes = tuple(lax.axis_size(axis) for axis in axes)
    members = math.prod(sizes)
    count = len(arrays)
    shapes = [((members,) + a.shape) if gather else a.shape for a in arrays]
    return pl.pallas_call(
        partial(exchange_kernel, axes, sizes, count, gather),
        out_shape=[jax.ShapeDtypeStruct(s, a.dtype) for s, a in zip(shapes, arrays)],
        in_specs=[pl.BlockSpec(memory_space=pl.ANY)] * count,
        out_specs=[pl.BlockSpec(memory_space=pl.ANY)] * count,
        scratch_shapes=[
            pltpu.SemaphoreType.DMA((count, members - 1)),
            pltpu.SemaphoreType.DMA((count, members - 1)),
            pltpu.SemaphoreType.DMA((count,)),
        ],
        cost_estimate=LIGHT,
        compiler_params=pltpu.CompilerParams(collective_id=ident, has_side_effects=True),
    )(*arrays)


class Spread:
    ORDER = ("zd", "tp", "head")

    def __init__(self, sizes, slots, send_sem, recv_sem):
        self.size = dict(zip(EVERY, sizes))
        self.place = {axis: lax.axis_index(axis) for axis in EVERY}
        self.slots, self.send_sem, self.recv_sem = slots, send_sem, recv_sem
        self.held, self.sends, self.number = [(self.place, None)], [], 0

    def partners(self):
        return [
            {axis: lax.rem(self.place[axis] + step, self.size[axis])}
            for axis in self.ORDER
            for step in range(1, self.size[axis])
        ]

    def stage(self, axis):
        arriving = []
        for where, arrivals in self.held:
            while arrivals:
                arrivals.pop().wait_recv()
            for step in range(1, self.size[axis]):
                to = lax.rem(self.place[axis] + step, self.size[axis])
                back = lax.rem(self.place[axis] - step + self.size[axis], self.size[axis])
                landing = []
                for k, slot in enumerate(self.slots):
                    ref = slot.at[tuple(where[name] for name in EVERY)]
                    copy = pltpu.make_async_remote_copy(
                        src_ref=ref,
                        dst_ref=ref,
                        send_sem=self.send_sem.at[k, self.number],
                        recv_sem=self.recv_sem.at[k, self.number],
                        device_id={axis: to},
                        device_id_type=MESH,
                    )
                    copy.start()
                    self.sends.append(copy)
                    landing.append(copy)
                self.number += 1
                arriving.append((dict(where, **{axis: back}), landing))
        self.held = self.held + arriving

    def finish(self):
        for _, arrivals in self.held:
            while arrivals:
                arrivals.pop().wait_recv()
        for copy in self.sends:
            copy.wait_send()


def start_kernel(sizes, layer, first, *refs):
    cores, planes, members = sizes
    if first:
        gu, qkv, out, packet, gu_result, mixed, project, packets = refs[:8]
        qkv_slots, out_slots, packet_slots, send_sem, recv_sem = refs[8:13]
        pieces, gu_send, gu_recv, gu_own = refs[13:]
        slots = [packet_slots, qkv_slots, out_slots]
    else:
        qkv, out, mixed, project, qkv_slots, out_slots, send_sem, recv_sem = refs
        slots = [qkv_slots, out_slots]
    gather = Spread(sizes, slots, send_sem, recv_sem)
    here = tuple(gather.place[name] for name in EVERY)
    core, _, tp = here
    group = []
    for step in range(1, cores * members):
        far = lax.rem(core + step // members, cores), lax.rem(tp + step % members, members)
        group.append((dict(zip(GROUP, far)), linear(far, (cores, members))))
    if first:
        enter(gather.partners() + [device for device, _ in group])
        packet_slots[here] = packet[...]
    else:
        enter(gather.partners())
    for source, slot in ((qkv, qkv_slots), (out, out_slots)):
        rows = source.shape[1]
        slot[here + (slice(0, rows),)] = source[layer].astype(bf16)
        if slot.shape[3] > rows:
            slot[here + (slice(rows, None),)] = jnp.zeros(
                (slot.shape[3] - rows, slot.shape[4]), bf16
            )
    gather.stage("zd")
    moves = []
    if first:
        layers, rows, columns = gu.shape
        block = columns // (planes * members)
        half = planes // cores
        for c in range(cores):
            for j in range(members):
                for i in range(layers):
                    cut = [
                        gu[i, :, pl.ds(((c * half + k) * members + j) * block, block)]
                        for k in range(half)
                    ]
                    value = jnp.concatenate(cut, axis=1) if half > 1 else cut[0]
                    pieces[c * members + j, i * rows : (i + 1) * rows] = value.astype(bf16)
        if pieces.shape[1] > layers * rows:
            for piece in range(cores * members):
                pieces[piece, layers * rows :] = jnp.zeros(
                    (pieces.shape[1] - layers * rows, pieces.shape[2]), bf16
                )
        me = linear((core, tp), (cores, members))
        for step, (device, index) in enumerate(group):
            copy = pltpu.make_async_remote_copy(
                src_ref=pieces.at[index],
                dst_ref=gu_result.at[me],
                send_sem=gu_send.at[step],
                recv_sem=gu_recv.at[step],
                device_id=device,
                device_id_type=MESH,
            )
            copy.start()
            moves.append(copy)
        own = pltpu.make_async_copy(pieces.at[me], gu_result.at[me], gu_own)
        own.start()
        moves.append(own)
    gather.stage("tp")
    gather.stage("head")
    gather.finish()
    for slot, result, rows in ((qkv_slots, mixed, qkv.shape[1]), (out_slots, project, out.shape[1])):
        columns = slot.shape[4]
        for h, z, t in itertools.product(range(cores), range(planes), range(members)):
            row = (z * members + t) * rows
            result[row : row + rows, h * columns : (h + 1) * columns] = slot[h, z, t, :rows]
    if first:
        packets[...] = packet_slots[...]
    for copy in moves:
        copy.wait()


def start(w_qkv, w_out, layer, ident, w_gu=None, packet=None):
    sizes = tuple(lax.axis_size(axis) for axis in EVERY)
    cores, planes, members = sizes
    vmem, dma = pltpu.VMEM, pltpu.SemaphoreType.DMA
    here, there = pl.BlockSpec(memory_space=pltpu.VMEM), pl.BlockSpec(memory_space=pl.ANY)
    shape = jax.ShapeDtypeStruct
    (_, qkv_rows, qkv_cols), (_, out_rows, out_cols) = w_qkv.shape, w_out.shape
    outs = [
        shape((qkv_rows * planes * members, qkv_cols * cores), bf16),
        shape((out_rows * planes * members, out_cols * cores), bf16),
    ]
    slots = [vmem(sizes + (-(-w.shape[1] // 16) * 16, w.shape[2]), bf16) for w in (w_qkv, w_out)]
    count, moves = 2, math.prod(sizes) - 1
    operands, out_specs, extra = [w_qkv, w_out], [here] * 2, []
    if w_gu is not None:
        layers, rows, columns = w_gu.shape
        tall = -(-layers * rows // 16) * 16
        piece = (cores * members, tall, columns // (cores * members))
        operands = [w_gu] + operands + [packet]
        outs = [shape(piece, bf16)] + outs + [shape(sizes + packet.shape, f32)]
        out_specs = [there] + out_specs + [here]
        slots, count = slots + [vmem(sizes + packet.shape, f32)], 3
        extra = [vmem(piece, bf16), dma((cores * members - 1,)), dma((cores * members - 1,)), dma]
    return pl.pallas_call(
        partial(start_kernel, sizes, layer, w_gu is not None),
        out_shape=outs,
        in_specs=[here] * len(operands),
        out_specs=out_specs,
        scratch_shapes=slots + [dma((count, moves))] * 2 + extra,
        cost_estimate=LIGHT,
        compiler_params=pltpu.CompilerParams(
            collective_id=ident, has_side_effects=True, vmem_limit_bytes=48 * 2**20
        ),
    )(*operands)


def by_rows(rows, work, step=16):
    @pl.loop(0, rows // step)
    def _(index):
        work(pl.ds(pl.multiple_of(index * step, step), step))


def collect_kernel(sizes, layers, *refs):
    cores, planes, members = sizes
    acts, packet, results = refs[: 4 * layers], refs[4 * layers], refs[4 * layers + 1 :][:3]
    rest = list(refs[4 * layers + 4 :])
    take = lambda number: [rest.pop(0) for _ in range(number)]
    far, halves = take(4 * layers), take(2 * layers)
    packet_land = rest.pop(0)
    pieces, plane_lands, totals, z_sums, z_lands = (take(3) for _ in range(5))
    act_send, act_recv, packet_send, packet_recv = take(4)
    tp_send, tp_recv, z_send, z_recv = take(4)
    core, zd, tp = (lax.axis_index(axis) for axis in EVERY)
    sibling = {"head": 1 - core}
    enter(
        [sibling]
        + [{"tp": lax.rem(tp + step, members)} for step in range(1, members)]
        + [{"zd": lax.rem(zd + step, planes)} for step in range(1, planes)]
    )
    sends = []

    def send(src, dst, send_sem, recv_sem, device):
        copy = pltpu.make_async_remote_copy(
            src_ref=src,
            dst_ref=dst,
            send_sem=send_sem,
            recv_sem=recv_sem,
            device_id=device,
            device_id_type=MESH,
        )
        copy.start()
        sends.append(copy)
        return copy

    for k in range(2 * layers):
        grad, half = acts[2 * k + 1], halves[k]
        width = half.shape[2]
        for h in range(cores):
            half[h] = grad[:, h * width : (h + 1) * width]
    moves = []
    for k in range(2 * layers):
        moves.append(
            send(acts[2 * k], far[2 * k], act_send.at[2 * k], act_recv.at[2 * k], sibling)
        )
        moves.append(
            send(
                halves[k].at[1 - core],
                far[2 * k + 1],
                act_send.at[2 * k + 1],
                act_recv.at[2 * k + 1],
                sibling,
            )
        )
    gains = send(packet.at[1 - core], packet_land, packet_send, packet_recv, sibling)
    plane_moves, z_moves = {}, {}
    for kind in range(3):
        piece = pieces[kind]
        if kind < 2:
            for layer in range(layers):
                k = 2 * layer + kind
                near = lax.dot_general(
                    acts[2 * k][...], halves[k][core], ALONG, preferred_element_type=f32
                )
                moves[2 * k].wait_recv()
                moves[2 * k + 1].wait_recv()
                value = near + lax.dot_general(
                    far[2 * k][...], far[2 * k + 1][...], ALONG, preferred_element_type=f32
                )
                value = value.astype(bf16)
                rows = value.shape[0] // (planes * members)
                slab = piece.shape[1] // planes
                for z, t in itertools.product(range(planes), range(members)):
                    at = (z * members + t) * rows
                    to = z * slab + layer * rows
                    piece[t, to : to + rows] = value[at : at + rows]
            if slab > layers * rows:
                for z, t in itertools.product(range(planes), range(members)):
                    piece[t, z * slab + layers * rows : (z + 1) * slab] = jnp.zeros(
                        (slab - layers * rows, piece.shape[2]), bf16
                    )
        else:
            gains.wait_recv()
            piece[...] = packet[core] + packet_land[...]
        for step in range(1, members):
            there = lax.rem(tp + step, members)
            plane_moves[kind, step] = send(
                piece.at[there],
                plane_lands[kind].at[step],
                tp_send.at[kind, step],
                tp_recv.at[kind, step],
                {"tp": there},
            )
    for kind in range(3):
        for step in range(1, members):
            plane_moves[kind, step].wait_recv()
        piece, total, land, result = pieces[kind], totals[kind], plane_lands[kind], results[kind]
        stride = 8 if land.dtype == f32 else 16

        def gather_plane(rows):
            value = piece[tp, rows].astype(f32)
            for step in range(1, members):
                value = value + land[step, rows].astype(f32)
            total[rows] = value

        by_rows(total.shape[0], gather_plane, stride)
        height = result.shape[0]
        z_sum = z_sums[kind]
        for step in range(1, planes):
            there = lax.rem(zd + step, planes)

            def round_off(rows):
                at = pl.multiple_of(there * height + rows.start, stride)
                z_sum[step, rows] = total[pl.ds(at, rows.size)].astype(z_sum.dtype)

            by_rows(height, round_off, stride)
            z_moves[kind, step] = send(
                z_sum.at[step],
                z_lands[kind].at[step],
                z_send.at[kind, step],
                z_recv.at[kind, step],
                {"zd": there},
            )
    for kind in range(3):
        for step in range(1, planes):
            z_moves[kind, step].wait_recv()
        total, land, result = totals[kind], z_lands[kind], results[kind]
        height = result.shape[0]
        stride = 8 if land.dtype == f32 else 16

        def gather_z(rows):
            at = pl.multiple_of(zd * height + rows.start, stride)
            value = total[pl.ds(at, rows.size)]
            for step in range(1, planes):
                value = value + land[step, rows].astype(f32)
            result[rows] = value

        by_rows(height, gather_z, stride)
    for copy in sends:
        copy.wait_send()


def collect(acts, packet, ident):
    sizes = tuple(lax.axis_size(axis) for axis in EVERY)
    cores, planes, members = sizes
    layers = len(acts) // 4
    vmem, dma = pltpu.VMEM, pltpu.SemaphoreType.DMA
    tokens = acts[0].shape[0]
    halves = [acts[2 * k + 1].shape[1] // cores for k in range(2 * layers)]
    slabs = []
    for kind in range(2):
        rows = layers * acts[2 * kind].shape[1] // (planes * members)
        slabs.append((-(-rows // 16) * 16, halves[kind], bf16))
    slabs.append((packet.shape[2] // planes, packet.shape[3], f32))
    far = []
    for k in range(2 * layers):
        far += [vmem(acts[2 * k].shape, bf16), vmem((tokens, halves[k]), bf16)]
    scratch = far + [vmem((cores, tokens, width), bf16) for width in halves]
    scratch += [vmem(packet.shape[1:], f32)]
    scratch += [vmem((members, planes * r, c), kind) for r, c, kind in slabs] * 2
    scratch += [vmem((planes * r, c), f32) for r, c, _ in slabs]
    scratch += [vmem((planes, r, c), kind) for r, c, kind in slabs] * 2
    scratch += [dma((4 * layers,))] * 2 + [dma] * 2
    scratch += [dma((3, members))] * 2 + [dma((3, planes))] * 2
    here = pl.BlockSpec(memory_space=pltpu.VMEM)
    return pl.pallas_call(
        partial(collect_kernel, sizes, layers),
        out_shape=[jax.ShapeDtypeStruct((r, c), f32) for r, c, _ in slabs],
        in_specs=[here] * (len(acts) + 1),
        out_specs=[here] * 3,
        scratch_shapes=scratch,
        cost_estimate=LIGHT,
        compiler_params=pltpu.CompilerParams(
            collective_id=ident, has_side_effects=True, vmem_limit_bytes=56 * 2**20
        ),
    )(*acts, packet)


def shift_kernel(planes, reach, back, source, result, send_sem, recv_sem):
    place = linear([lax.axis_index("zd"), lax.axis_index("tp")], (planes, PLANE))
    total = planes * PLANE
    sign = -1 if back else 1
    to, sources = [], []
    for distance in range(1, reach + 1):
        there = lax.rem(place + sign * distance + total, total)
        to.append({"zd": there // PLANE, "tp": lax.rem(there, PLANE)})
        here = lax.rem(place - sign * distance + total, total)
        sources.append({"zd": here // PLANE, "tp": lax.rem(here, PLANE)})
    barrier = pltpu.get_barrier_semaphore()
    for device in to + sources:
        pl.semaphore_signal(barrier, inc=1, device_id=device, device_id_type=MESH)
    pl.semaphore_wait(barrier, 2 * reach)
    copies = []
    for k, device in enumerate(to):
        copy = pltpu.make_async_remote_copy(
            src_ref=source.at[k] if back else source,
            dst_ref=result.at[k],
            send_sem=send_sem.at[k],
            recv_sem=recv_sem.at[k],
            device_id=device,
            device_id_type=MESH,
        )
        copy.start()
        copies.append(copy)
    for copy in copies:
        copy.wait()


def shift(array, planes, reach, back, ident):
    shape = array.shape if back else (reach,) + array.shape
    return pl.pallas_call(
        partial(shift_kernel, planes, reach, back),
        out_shape=jax.ShapeDtypeStruct(shape, array.dtype),
        in_specs=[pl.BlockSpec(memory_space=pl.ANY)],
        out_specs=pl.BlockSpec(memory_space=pl.ANY),
        scratch_shapes=[pltpu.SemaphoreType.DMA((reach,)), pltpu.SemaphoreType.DMA((reach,))],
        cost_estimate=LIGHT,
        compiler_params=pltpu.CompilerParams(collective_id=ident, has_side_effects=True),
    )(array)


GELU_SLOPE = math.sqrt(2.0 / math.pi)
GELU_CUBE = 0.044715
ACROSS = (((1,), (1,)), ((), ()))
ALONG = (((0,), (0,)), ((), ()))


class Plane:
    def __init__(self, own, bufs, sems):
        self.own = own
        self.rows, self.partial, self.other, self.lands, self.sums, self.arrived = bufs
        self.x_send, self.x_recv, self.f_send, self.f_recv = sems[:4]
        self.c_send, self.c_recv, self.p_send, self.p_recv, self.first = sems[4:]
        self.tp = lax.axis_index("tp")
        self.sibling = {"head": 1 - lax.axis_index("head")}

    def member(self, m):
        tp = self.tp
        upper = lax.rem(lax.div(tp, 2) + lax.div(m, 2), 2)
        lower = lax.rem(lax.rem(tp, 2) + lax.rem(m, 2), 2)
        return {"tp": upper * 2 + lower}

    def remote(self, src, dst, send, recv, device):
        return pltpu.make_async_remote_copy(
            src_ref=src,
            dst_ref=dst,
            send_sem=send,
            recv_sem=recv,
            device_id=device,
            device_id_type=MESH,
        )

    def push(self, m):
        return self.remote(
            self.own, self.rows.at[0, m], self.x_send.at[m], self.x_recv.at[m], self.member(m)
        )

    def keep(self):
        return pltpu.make_async_copy(self.own, self.rows.at[0, 0], self.first)

    def forward(self, m):
        return self.remote(
            self.rows.at[0, m],
            self.rows.at[1, m],
            self.f_send.at[m],
            self.f_recv.at[m],
            self.sibling,
        )

    def cross(self, m):
        return self.remote(
            self.other.at[m], self.lands.at[m], self.c_send.at[m], self.c_recv.at[m], self.sibling
        )

    def home(self, m):
        return self.remote(
            self.sums.at[m],
            self.arrived.at[m],
            self.p_send.at[m],
            self.p_recv.at[m],
            self.member(m),
        )

    def begin(self):
        self.keep().start()
        enter([self.sibling] + [self.member(jnp.int32(m)) for m in range(1, PLANE)])
        for m in range(1, PLANE):
            self.push(jnp.int32(m)).start()

    def work(self, compute):
        def settle(m):
            self.cross(m).wait_recv()

            def add(rows):
                value = self.partial[m, rows] + self.lands[m, rows].astype(f32)
                self.sums[m, rows] = value.astype(bf16)

            by_rows(self.partial.shape[1], add)
            self.home(m).start()

        def step(m, carry):
            @pl.when(m == 0)
            def _():
                self.keep().wait()

            @pl.when(m > 0)
            def _():
                self.push(m).wait_recv()

            self.forward(m).start()
            self.partial[m] = compute(0, m)
            self.forward(m).wait_recv()
            self.other[m] = compute(1, m).astype(bf16)
            self.cross(m).start()

            @pl.when(m >= 2)
            def _():
                settle(m - 1)

            return carry

        lax.fori_loop(0, PLANE, step, 0)
        settle(jnp.int32(PLANE - 1))

    def finish(self, result):
        self.cross(jnp.int32(0)).wait_recv()
        for m in range(1, PLANE):
            self.home(jnp.int32(m)).wait_recv()

        def add(rows):
            value = self.partial[0, rows] + self.lands[0, rows].astype(f32)
            for m in range(1, PLANE):
                value = value + self.arrived[m, rows].astype(f32)
            result[rows] = value

        by_rows(result.shape[0], add)
        for m in range(PLANE):
            m = jnp.int32(m)
            self.forward(m).wait_send()
            self.cross(m).wait_send()
        for m in range(1, PLANE):
            m = jnp.int32(m)
            self.push(m).wait_send()
            self.home(m).wait_send()


def gate_up_copies(gu_ref, gate_up, sem):
    blocks = gu_ref.shape[0]
    rows = gate_up.shape[1] // blocks
    return [
        pltpu.make_async_copy(
            gu_ref.at[block, part],
            gate_up.at[part, pl.ds(block * rows, rows)],
            sem.at[2 * block + part],
        )
        for block in range(blocks)
        for part in range(2)
    ]


def ffn_forward_kernel(own, gu_ref, halves_ref, group, saved_down, result, *scratch):
    rows, gate_up, down = scratch[:3]
    plane = Plane(own, (rows,) + scratch[3:8], scratch[8:17])
    weight_sem, group_sem, halves, half_send, half_recv, half_own, save_sem = scratch[17:]
    core = lax.axis_index("head")
    share, width = halves.shape[1:]
    copies = gate_up_copies(gu_ref, gate_up, weight_sem)
    copies.append(
        pltpu.make_async_copy(
            halves_ref.at[0, pl.ds(pl.multiple_of(core * share, 16), share)],
            halves.at[core],
            half_own,
        )
    )
    for copy in copies:
        copy.start()
    plane.begin()
    half = plane.remote(
        halves_ref.at[0, pl.ds(pl.multiple_of((1 - core) * share, 16), share)],
        halves.at[core],
        half_send,
        half_recv,
        plane.sibling,
    )
    half.start()
    for copy in copies:
        copy.wait()
    pltpu.make_async_remote_copy(
        src_ref=halves_ref.at[0, pl.ds(pl.multiple_of((1 - core) * share, 16), share)],
        dst_ref=halves.at[1 - core],
        send_sem=half_send,
        recv_sem=half_recv,
        device_id=plane.sibling,
        device_id_type=MESH,
    ).wait_recv()

    def join(at):
        down[at] = jnp.concatenate([halves[h, at] for h in range(2)], axis=1)

    by_rows(share, join, 32)
    keep_down = pltpu.make_async_copy(down, saved_down, save_sem)
    keep_down.start()

    def compute(side, m):
        tokens = rows[side, m]
        gate = matmul(tokens, gate_up[0])
        up = matmul(tokens, gate_up[1])
        bend = jnp.tanh(GELU_SLOPE * (gate + GELU_CUBE * (gate * gate * gate)))
        inner = (0.5 * gate * (1.0 + bend) * up).astype(bf16)
        return matmul(inner, down[...])

    plane.work(compute)
    save = pltpu.make_async_copy(rows, group, group_sem)
    save.start()
    plane.finish(result)
    save.wait()
    keep_down.wait()
    half.wait_send()


def ffn_backward_kernel(
    own, group, gu_ref, down_ref, result, grad_gate, grad_up, grad_down, *scratch
):
    rows, gate_up, down = scratch[:3]
    plane = Plane(own, (rows,) + scratch[3:8], scratch[8:17])
    weight_sem, group_sem, saved, d_gate, d_up, inner = scratch[17:23]
    down_sem, turned, down_halves, half_send, half_recv, half_own = scratch[23:]
    core = lax.axis_index("head")
    copies = gate_up_copies(gu_ref, gate_up, weight_sem)
    copies.append(pltpu.make_async_copy(down_ref, down, down_sem))
    for copy in copies:
        copy.start()
    load = pltpu.make_async_copy(group, saved, group_sem)
    load.start()
    plane.begin()
    for copy in copies:
        copy.wait()
    load.wait()

    def recompute(index, carry):
        side, m = lax.div(index, PLANE), lax.rem(index, PLANE)
        tokens = saved[side, m]
        gate = matmul(tokens, gate_up[0])
        up = matmul(tokens, gate_up[1])
        square = gate * gate
        bend = jnp.tanh(GELU_SLOPE * (gate + GELU_CUBE * (square * gate)))
        half = 0.5 * (1.0 + bend)
        value = gate * half
        slope = half + (0.5 * GELU_SLOPE) * gate * (1.0 - bend * bend) * (
            1.0 + (3.0 * GELU_CUBE) * square
        )
        inner[side, m] = (value * up).astype(bf16)
        d_gate[side, m] = (slope * up).astype(bf16)
        d_up[side, m] = value.astype(bf16)
        return carry

    lax.fori_loop(0, 2 * PLANE, recompute, 0)

    def compute(side, m):
        d_inner = lax.dot_general(rows[side, m], down[...], ACROSS, preferred_element_type=f32)
        gate = (d_inner * d_gate[side, m].astype(f32)).astype(bf16)
        up = (d_inner * d_up[side, m].astype(f32)).astype(bf16)
        d_gate[side, m] = gate
        d_up[side, m] = up
        return lax.dot_general(
            gate, gate_up[0], ACROSS, preferred_element_type=f32
        ) + lax.dot_general(up, gate_up[1], ACROSS, preferred_element_type=f32)

    plane.work(compute)
    width = rows.shape[-1]
    step = width // 3

    def tall(ref, columns=slice(None)):
        value = ref[:, :, :, columns]
        return value.reshape(-1, value.shape[-1])

    @pl.loop(0, 3)
    def _(index):
        at = pl.ds(pl.multiple_of(index * step, step), step)
        tokens = tall(saved, at)
        for target, other in ((grad_gate, d_gate), (grad_up, d_up)):
            target[at] = lax.dot_general(
                tokens, tall(other), ALONG, preferred_element_type=f32
            ).astype(bf16)
        turned[at] = lax.dot_general(
            tall(rows, at), tall(inner), ALONG, preferred_element_type=f32
        ).astype(bf16)

    half_width = down_halves.shape[2]
    for h in range(2):
        down_halves[h] = turned[h * half_width : (h + 1) * half_width].T
    half = plane.remote(
        down_halves.at[1 - core], grad_down.at[core], half_send, half_recv, plane.sibling
    )
    half.start()
    stay = pltpu.make_async_copy(down_halves.at[core], grad_down.at[core], half_own)
    stay.start()
    plane.finish(result)
    half.wait()
    stay.wait()


def ffn(own, weights, ident, group=None):
    gate_up, down = weights
    tokens, width = own.shape
    blocks, _, _, share = gate_up.shape
    vmem, dma = pltpu.VMEM, pltpu.SemaphoreType.DMA
    scratch = [
        vmem((2, PLANE, tokens, width), bf16),
        vmem((2, width, share), bf16),
        vmem((share, width), bf16),
        vmem((PLANE, tokens, width), f32),
    ]
    scratch += [vmem((PLANE, tokens, width), bf16)] * 4
    scratch += [dma((PLANE,))] * 8 + [dma, dma((2 * blocks,)), dma]
    here, there = pl.BlockSpec(memory_space=pltpu.VMEM), pl.BlockSpec(memory_space=pl.ANY)
    shape = jax.ShapeDtypeStruct
    summed = shape((tokens, width), f32)
    if group is None:
        kernel, operands = ffn_forward_kernel, (own, gate_up, down)
        in_specs, out_specs = [here, there, there], [there, there, here]
        out_shape = [
            shape((2, PLANE, tokens, width), bf16),
            shape((share, width), bf16),
            summed,
        ]
        scratch += [vmem((2, share, width // 2), bf16)] + [dma] * 4
    else:
        kernel, operands = ffn_backward_kernel, (own, group, gate_up, down)
        in_specs, out_specs = [here, there, there, there], [here] * 3 + [there]
        out_shape = [
            summed,
            shape((width, share), bf16),
            shape((width, share), bf16),
            shape((2, share, width // 2), bf16),
        ]
        scratch += [vmem((2, PLANE, tokens, width), bf16)]
        scratch += [vmem((2, PLANE, tokens, share), bf16)] * 3
        scratch += [dma, vmem((width, share), bf16), vmem((2, share, width // 2), bf16)]
        scratch += [dma] * 3
    return pl.pallas_call(
        kernel,
        out_shape=out_shape,
        in_specs=in_specs,
        out_specs=out_specs,
        scratch_shapes=scratch,
        cost_estimate=LIGHT,
        compiler_params=pltpu.CompilerParams(
            collective_id=ident, has_side_effects=True, vmem_limit_bytes=60 * 2**20
        ),
    )(*operands)


def exact(left, right, dims=(((1,), (0,)), ((), ()))):
    return lax.dot_general(
        left, right, dims, precision=finest_precision, preferred_element_type=f32
    )


def update_kernel(sizes, *refs):
    cores, planes, members = sizes
    rest = list(refs)
    take = lambda number: [rest.pop(0) for _ in range(number)]
    plain = [take(cores) for _ in range(3)]
    sides = [take(2) for _ in range(cores)]
    moments_in, weights_in, weights_out, moments_out = (take(4) for _ in range(4))
    moment, weight, gram, land, factor = (take(4) for _ in range(5))
    pieces, arrived = take(2)
    load_sem, store_sem, gram_send, gram_recv, factor_send, factor_recv = take(6)
    gu_send, gu_recv, gu_own = take(3)
    core, _, tp = (lax.axis_index(axis) for axis in EVERY)
    sibling = {"head": 1 - core}
    order = (0, 1, 3, 2)
    loads = {}
    for k in range(4):
        for part, source, target in ((0, moments_in, moment), (1, weights_in, weight)):
            copy = pltpu.make_async_copy(source[k], target[k], load_sem.at[part, k])
            copy.start()
            loads[part, k] = copy
    group = []
    for step in range(1, cores * members):
        far = lax.rem(core + step // members, cores), lax.rem(tp + step % members, members)
        group.append((dict(zip(GROUP, far)), linear(far, (cores, members))))
    enter([device for device, _ in group])
    rows = moment[2].shape[1]
    for part in range(cores):
        for j in range(members):
            for layer in range(cores):
                pieces[part * members + j, layer * rows : (layer + 1) * rows] = sides[layer][part][
                    j * rows : (j + 1) * rows
                ]
    if pieces.shape[1] > cores * rows:
        for piece in range(cores * members):
            pieces[piece, cores * rows :] = jnp.zeros(
                (pieces.shape[1] - cores * rows, pieces.shape[2]), bf16
            )
    me = linear((core, tp), (cores, members))
    moves, stores = [], []

    def send(src, dst, send_sem, recv_sem, device):
        copy = pltpu.make_async_remote_copy(
            src_ref=src,
            dst_ref=dst,
            send_sem=send_sem,
            recv_sem=recv_sem,
            device_id=device,
            device_id_type=MESH,
        )
        copy.start()
        return copy

    for step, (device, index) in enumerate(group):
        moves.append(
            send(pieces.at[index], arrived.at[me], gu_send.at[step], gu_recv.at[step], device)
        )
    own = pltpu.make_async_copy(pieces.at[me], arrived.at[me], gu_own)
    own.start()

    def store(part, k):
        source, target = (moment, moments_out) if part == 0 else (weight, weights_out)
        copy = pltpu.make_async_copy(source[k], target[k], store_sem.at[part, k])
        copy.start()
        stores.append(copy)

    def gram_of(k):
        def one(layer, carry):
            gram[k][layer] = exact(moment[k][layer], moment[k][layer], ACROSS)
            return carry

        lax.fori_loop(0, cores, one, 0)
        return send(
            gram[k].at[1 - core], land[k], gram_send.at[k], gram_recv.at[k], sibling
        )

    def unit(size):
        down = lax.broadcasted_iota(jnp.int32, (size, size), 0)
        return (down == lax.broadcasted_iota(jnp.int32, (size, size), 1)).astype(f32)

    def orthogonal(members_of):
        for k in members_of:
            total = gram[k][core] + land[k][...]
            one = unit(total.shape[0])
            trace = jnp.sum(jnp.sum(total * one, axis=1, keepdims=True), axis=0, keepdims=True)
            scale = 1.0 / (jnp.sqrt(trace) + 1e-07)
            land[k][...] = total * (scale * scale)
            factor[k][core] = one * scale

        def polynomial(present):
            square = exact(present, present)
            return newton_one * unit(present.shape[0]) + newton_two * present + (
                newton_three * square
            )

        def step(_, carry):
            for k in members_of:
                present = land[k][...]
                poly = polynomial(present)
                factor[k][core] = exact(poly, factor[k][core])
                land[k][...] = exact(exact(poly, present), poly)
            return carry

        lax.fori_loop(0, NS_ITERS - 1, step, 0)
        for k in members_of:
            factor[k][core] = exact(polynomial(land[k][...]), factor[k][core])
        return [
            send(factor[k].at[core], factor[k].at[core], factor_send.at[k], factor_recv.at[k], sibling)
            for k in members_of
        ]

    def apply(k):
        columns = weight[k].shape[2] * cores
        rate = muon_rate * muon_scale * math.sqrt(columns)

        def one(layer, carry):
            weight[k][layer] = weight[k][layer] * (1.0 - muon_rate * muon_shrink) - rate * exact(
                factor[k][layer], moment[k][layer]
            )
            return carry

        lax.fori_loop(0, cores, one, 0)
        store(1, k)

    def arrive(copies):
        for copy in copies:
            copy.wait_recv()

    sent = []
    for index, k in enumerate(order[:3]):
        loads[0, k].wait()
        height = moment[k].shape[1]
        for layer in range(cores):
            moment[k][layer] = muon_decay * moment[k][layer] + plain[index][layer][:height].astype(
                f32
            )
        store(0, k)
        sent.append(gram_of(k))
    arrive(sent)
    crossed = orthogonal(order[:3])
    sent += crossed
    own.wait()
    for copy in moves:
        copy.wait_recv()
    loads[0, 2].wait()
    half = planes // cores
    block = arrived.shape[2] // half
    for layer in range(cores):
        cut = [
            arrived[
                c * members + j,
                layer * rows : (layer + 1) * rows,
                k * block : (k + 1) * block,
            ].astype(f32)
            for c in range(cores)
            for k in range(half)
            for j in range(members)
        ]
        moment[2][layer] = muon_decay * moment[2][layer] + jnp.concatenate(cut, axis=1)
    store(0, 2)
    last = gram_of(2)
    sent.append(last)
    arrive(crossed)
    for k in range(4):
        loads[1, k].wait()
    for k in order[:3]:
        apply(k)
    arrive([last])
    crossed = orthogonal(order[3:])
    sent += crossed
    arrive(crossed)
    apply(2)
    for copy in moves + sent:
        copy.wait_send()
    for copy in stores:
        copy.wait()


def update(gradients, sides, moments, weights, ident):
    sizes = tuple(lax.axis_size(axis) for axis in EVERY)
    cores, planes, members = sizes
    vmem, dma = pltpu.VMEM, pltpu.SemaphoreType.DMA
    layers, rows, columns = moments[2].shape
    piece = (
        cores * members,
        -(-layers * rows // 16) * 16,
        columns // (cores * members),
    )
    shapes = [m.shape for m in moments]
    square = [(s[1], s[1]) for s in shapes]
    scratch = [vmem(s, f32) for s in shapes] * 2
    scratch += [vmem((layers,) + s, f32) for s in square]
    scratch += [vmem(s, f32) for s in square]
    scratch += [vmem((layers,) + s, f32) for s in square]
    scratch += [vmem(piece, bf16)] * 2
    scratch += [dma((2, 4))] * 2 + [dma((4,))] * 4
    scratch += [dma((cores * members - 1,))] * 2 + [dma]
    here, there = pl.BlockSpec(memory_space=pltpu.VMEM), pl.BlockSpec(memory_space=pl.ANY)
    operands = sum(gradients, []) + sum(sides, [])
    return pl.pallas_call(
        partial(update_kernel, sizes),
        out_shape=[jax.ShapeDtypeStruct(s, f32) for s in shapes] * 2,
        in_specs=[here] * len(operands) + [there] * 8,
        out_specs=[there] * 8,
        scratch_shapes=scratch,
        compiler_params=pltpu.CompilerParams(
            collective_id=ident, has_side_effects=True, vmem_limit_bytes=56 * 2**20
        ),
    )(*operands, *moments, *weights)


def padded(array, multiple=16):
    extra = -array.shape[-2] % multiple
    if extra == 0:
        return array
    return jnp.pad(array, [(0, 0)] * (array.ndim - 2) + [(0, extra), (0, 0)])


def rms_norm(values, norm_gain):
    return (
        values * lax.rsqrt(jnp.mean(values * values, axis=-1, keepdims=True) + norm_eps) * norm_gain
    )


def rope_tables(positions, head_dim):
    half_dim = head_dim // 2
    frequency = jnp.exp(
        jnp.arange(half_dim, dtype=jnp.float32) * (-2.0 * math.log(rope_base) / head_dim)
    )
    angles = positions.astype(jnp.float32)[:, None] * frequency[None, :]
    return (jnp.cos(angles), jnp.sin(angles))


def rotate(values, cosine_table, sine_table):
    half_dim = values.shape[-1] // 2
    lower_half = values[..., :half_dim]
    upper_half = values[..., half_dim:]
    return jnp.concatenate(
        [
            lower_half * cosine_table - upper_half * sine_table,
            upper_half * cosine_table + lower_half * sine_table,
        ],
        axis=-1,
    )


def head_prep(mixed_proj, query_gain, key_gain, cosine_table, sine_table):
    seq_rows = mixed_proj.shape[0]
    place_rows = mixed_proj.shape[1]
    queries = mixed_proj[..., : HEADS * HD].reshape(seq_rows, place_rows, HEADS, HD)
    key_heads = mixed_proj[..., HEADS * HD : HEADS * HD + HD]
    values = mixed_proj[..., HEADS * HD + HD :]
    queries = rotate(
        rms_norm(queries, query_gain), cosine_table[:, None, :], sine_table[:, None, :]
    )
    key_heads = rotate(rms_norm(key_heads, key_gain), cosine_table, sine_table)
    return (queries, jnp.concatenate([key_heads, values], axis=-1))


def attend_scores(query_rows, key_tile_rows, allowed):
    logit_scores = jnp.einsum(
        "tals,tes->tlae", query_rows, key_tile_rows, preferred_element_type=jnp.float32
    ) * (1.0 / math.sqrt(HD))
    return jnp.where(allowed[:, None], logit_scores, -jnp.inf)


def matmul(left, right):
    return jnp.dot(left, right, preferred_element_type=f32)


def body(
    inputs,
    cotangent,
    teacher,
    segments,
    valid_mask,
    w_qkv,
    w_out,
    w_gu,
    w_down,
    norm_gains,
    mom_qkv,
    mom_out,
    mom_gu,
    mom_down,
    gain_first,
    gain_second,
):
    cores = lax.axis_size("head")
    planes = lax.axis_size("zd")
    seq_devices = planes * PLANE
    core = lax.axis_index("head")
    seq_place = lax.axis_index("zd") * PLANE + lax.axis_index("tp")
    half_seqs, stretch_len = inputs.shape[:2]
    tokens = half_seqs * stretch_len
    all_seqs = half_seqs * cores
    seq_length = stretch_len * seq_devices
    reach = -(-WINDOW // stretch_len)
    key_len = (reach + 1) * stretch_len
    qkv_rows, qkv_cols = w_qkv.shape[1:]
    out_rows, out_cols = w_out.shape[1:]
    gu_rows = w_gu.shape[1]
    ff_block = w_down.shape[1]
    share = FF // (cores * PLANE)
    half_planes = planes // cores
    gain_cols = norm_gains.shape[-1]
    gain_len = gain_cols * seq_devices
    lanes = -(-gain_cols // 128) * 128

    packet = jnp.zeros((8, lanes), f32)
    packet = packet.at[:LAYERS, :gain_cols].set(norm_gains[:, 0].astype(bf16).astype(f32))
    packet = packet.at[LAYERS, 0].set(jnp.sum(valid_mask.astype(f32)))
    gu_pieces, *attn_weights, packets = start(w_qkv, w_out, 0, 0, w_gu, packet)
    gu_pieces = gu_pieces[:, : LAYERS * gu_rows].reshape(cores * PLANE, LAYERS, gu_rows, share)
    packets = packets.reshape(cores, seq_devices, 8, lanes)
    valid_count = jnp.sum(packets[:, :, LAYERS, 0])
    gain_rows = [
        packets[:, :, layer, :gain_cols].reshape(cores, gain_len) for layer in range(LAYERS)
    ]

    def ffn_weights(layer, after):
        pieces, rows = gu_pieces, w_down
        if after is not None:
            pieces, rows, after = lax.optimization_barrier((pieces, rows, after))
        pieces, rows = pieces[:, layer], rows[layer : layer + 1].astype(bf16)
        pieces = lax.all_gather(pieces.reshape(2, PLANE * gu_rows, share), "zd", axis=0)
        if PLANE * gu_rows % 16:
            pieces = pieces.transpose(1, 0, 2, 3).reshape(1, 2, D, share)
        return (pieces, lax.all_gather(rows, "zd", axis=1, tiled=True)), after

    full = [ffn_weights(0, None)[0]] + [None] * (LAYERS - 1)

    own_places = seq_place * stretch_len + jnp.arange(stretch_len, dtype=jnp.int32)
    key_places = (seq_place - reach) * stretch_len + jnp.arange(key_len, dtype=jnp.int32)
    cosine_table, sine_table = rope_tables(own_places, HD)
    own_rows = lax.dynamic_slice_in_dim(segments, core * half_seqs, half_seqs, 0)
    own_segments = lax.dynamic_slice_in_dim(own_rows, seq_place * stretch_len, stretch_len, 1)
    padded_segments = jnp.pad(own_rows, ((0, 0), (reach * stretch_len, 0)), constant_values=-1)
    key_segments = lax.dynamic_slice_in_dim(padded_segments, seq_place * stretch_len, key_len, 1)
    spacing = own_places[:, None] - key_places[None, :]
    allowed = (spacing >= 0) & (spacing < WINDOW) & (key_places[None, :] >= 0)
    allowed = allowed[None] & (own_segments[:, :, None] == key_segments[:, None, :])

    hidden = inputs.astype(f32)
    saved = []
    for layer in range(LAYERS):
        w_mixed, w_project = attn_weights
        gain_pack = gain_rows[layer]
        norm_attn = gain_pack[0, :D]
        post_attn = gain_pack[0, D : 2 * D]
        query_gain = gain_pack[0, 2 * D :]
        norm_ffn = gain_pack[1, :D]
        post_ffn = gain_pack[1, D : 2 * D]
        key_gain = gain_pack[1, 2 * D :]
        normed_f, pre_attn_back = jax.vjp(rms_norm, hidden, norm_attn)
        normed = normed_f.astype(bf16)
        mixed_proj = jnp.einsum("bpd,de->bpe", normed, w_mixed, preferred_element_type=f32)
        prepared, prep_back = jax.vjp(
            partial(head_prep, cosine_table=cosine_table, sine_table=sine_table),
            mixed_proj,
            query_gain,
            key_gain,
        )
        query_rows = prepared[0].astype(bf16)
        own_keyvals = prepared[1].astype(bf16)
        earlier = shift(own_keyvals.reshape(tokens, 2 * HD), planes, reach, False, 3 + layer)
        if layer + 1 < LAYERS:
            full[layer + 1], earlier = ffn_weights(layer + 1, earlier)
        earlier = earlier.reshape(reach, half_seqs, stretch_len, 2 * HD)
        ffn_share = full[layer]
        keyvals = jnp.concatenate(
            [earlier[reach - 1 - k] for k in range(reach)] + [own_keyvals], axis=1
        )
        key_tile_rows = keyvals[..., :HD]
        value_tile_rows = keyvals[..., HD:]
        logit_scores = attend_scores(query_rows, key_tile_rows, allowed)
        log_total = jax.nn.logsumexp(logit_scores, axis=-1)
        soft = jnp.exp(logit_scores - log_total[..., None])
        attended = jnp.einsum(
            "zusi,zix->zsux", soft.astype(bf16), value_tile_rows, preferred_element_type=f32
        ).astype(bf16)
        attended_rows = attended.reshape(half_seqs, stretch_len, HEADS * HD)
        projected = jnp.einsum("bpq,qd->bpd", attended_rows, w_project, preferred_element_type=f32)
        branch_out, post_attn_back = jax.vjp(rms_norm, projected, post_attn)
        hidden_half = hidden + branch_out
        normed_f, pre_ffn_back = jax.vjp(rms_norm, hidden_half, norm_ffn)
        normed_ffn = normed_f.astype(bf16).reshape(tokens, D)
        if layer + 1 < LAYERS:
            later_qkv, later_out, attended_rows = lax.optimization_barrier(
                (w_qkv, w_out, attended_rows)
            )
            attn_weights = start(later_qkv, later_out, layer + 1, 2 + 20 * layer)
            normed_ffn, *attn_weights = lax.optimization_barrier((normed_ffn, *attn_weights))
        group_normed, whole_down, down_out = ffn(normed_ffn, ffn_share, 5 + layer)
        full[layer] = (w_mixed, w_project, (ffn_share[0], whole_down))
        down_out = down_out.reshape(half_seqs, stretch_len, D)
        branch_out, post_ffn_back = jax.vjp(rms_norm, down_out, post_ffn)
        hidden = hidden_half + branch_out
        saved.append(
            (
                normed,
                pre_attn_back,
                prep_back,
                query_rows,
                keyvals,
                log_total,
                attended_rows,
                post_attn_back,
                pre_ffn_back,
                group_normed,
                post_ffn_back,
            )
        )

    target_gap = hidden - teacher.astype(f32)
    valid_weight = valid_mask.astype(f32)[:, :, None]
    square_sum = jnp.sum(valid_weight * target_gap * target_gap)
    loss_weight = float(all_seqs * seq_length * D // 4)
    grad_hidden = (
        cotangent.astype(f32)
        + 2.0 * loss_weight / (valid_count * D) * valid_weight * target_gap
    )

    attn_acts = [None] * LAYERS
    down_grads = [None] * LAYERS
    gain_grads = [None] * LAYERS
    gu_sums = [None] * LAYERS
    logit_scale = 1.0 / math.sqrt(HD)
    for layer in reversed(range(LAYERS)):
        (
            normed,
            pre_attn_back,
            prep_back,
            query_rows,
            keyvals,
            log_total,
            attended_rows,
            post_attn_back,
            pre_ffn_back,
            group_normed,
            post_ffn_back,
        ) = saved[layer]
        w_mixed, w_project, ffn_share = full[layer]
        key_tile_rows = keyvals[..., :HD]
        value_tile_rows = keyvals[..., HD:]
        d_down, d_post_ffn = post_ffn_back(grad_hidden)
        d_normed_ffn, *grad_gu, grad_down = ffn(
            d_down.astype(bf16).reshape(tokens, D), ffn_share, 9 + layer, group_normed
        )
        d_normed_ffn = d_normed_ffn.reshape(half_seqs, stretch_len, D)

        down_grads[layer] = lax.psum_scatter(
            grad_down.reshape(planes * ff_block, out_cols), "zd", scatter_dimension=0, tiled=True
        )
        gu_sums[layer] = [
            lax.psum_scatter(g, "zd", scatter_dimension=0, tiled=True) for g in grad_gu
        ]

        d_half, d_norm_ffn = pre_ffn_back(d_normed_ffn)
        d_half = d_half + grad_hidden
        d_projected, d_post_attn = post_attn_back(d_half)
        d_proj_low = d_projected.astype(bf16)
        d_attended = (
            jnp.einsum("bpd,qd->bpq", d_proj_low, w_project, preferred_element_type=f32)
            .astype(bf16)
            .reshape(half_seqs, stretch_len, HEADS, HD)
        )
        logit_scores = attend_scores(query_rows, key_tile_rows, allowed)
        soft = jnp.exp(logit_scores - log_total[..., None])
        d_probs = jnp.einsum(
            "tals,tes->tlae", d_attended, value_tile_rows, preferred_element_type=f32
        )
        row_total = jnp.sum(soft * d_probs, axis=-1, keepdims=True)
        score_gradient = (soft * (d_probs - row_total)).astype(bf16)
        d_queries = (
            jnp.einsum("zusi,zix->zsux", score_gradient, key_tile_rows, preferred_element_type=f32)
            * logit_scale
        )
        d_keys = (
            jnp.einsum("lqkp,lkqf->lpf", score_gradient, query_rows, preferred_element_type=f32)
            * logit_scale
        )
        d_values = jnp.einsum(
            "lqkp,lkqf->lpf", soft.astype(bf16), d_attended, preferred_element_type=f32
        )
        d_keyvals = jnp.concatenate([d_keys, d_values], axis=-1)
        pieces = [
            d_keyvals[:, (reach - k) * stretch_len : (reach - k + 1) * stretch_len]
            for k in range(reach + 1)
        ]
        outgoing = jnp.stack(pieces[1:]).astype(bf16).reshape(reach, tokens, 2 * HD)
        if layer + 1 < LAYERS:
            outgoing, gu_sums[layer + 1], down_grads[layer + 1] = lax.optimization_barrier(
                (outgoing, gu_sums[layer + 1], down_grads[layer + 1])
            )
        incoming = shift(outgoing, planes, reach, True, 17 + layer)
        d_own = pieces[0] + jnp.sum(incoming.astype(f32), axis=0).reshape(
            half_seqs, stretch_len, 2 * HD
        )
        d_mixed, d_query_gain, d_key_gain = prep_back((d_queries, d_own))
        d_mixed_low = d_mixed.astype(bf16)
        d_normed = jnp.einsum("bpe,de->bpd", d_mixed_low, w_mixed, preferred_element_type=f32)
        d_hidden, d_norm_attn = pre_attn_back(d_normed)
        grad_hidden = d_hidden + d_half
        gain_grads[layer] = jnp.stack(
            [
                jnp.concatenate([d_norm_attn, d_post_attn, d_query_gain]),
                jnp.concatenate([d_norm_ffn, d_post_ffn, d_key_gain]),
            ]
        )

        attn_acts[layer] = [
            value.reshape(tokens, -1) for value in (normed, d_mixed_low, attended_rows, d_proj_low)
        ]

    collected = [None] * LAYERS
    for layer in reversed(range(LAYERS)):
        packet = gain_grads[layer].reshape(cores, planes, PLANE, gain_cols).transpose(0, 2, 1, 3)
        packet = jnp.pad(packet[:, :, :, None], [(0, 0)] * 3 + [(0, 7), (0, lanes - gain_cols)])
        packet = packet.at[:, :, :, 1, 0].set(square_sum)
        packet = packet.reshape(cores, PLANE, planes * 8, lanes)
        if layer > 0:
            packet, attn_acts[0][1] = lax.optimization_barrier((packet, attn_acts[0][1]))
        else:
            packet, collected[1:], gu_sums[0] = lax.optimization_barrier(
                (packet, collected[1:], gu_sums[0])
            )
        collected[layer] = collect(attn_acts[layer], packet, 19 + layer)
    grad_qkv, grad_out, packet = (list(parts) for parts in zip(*collected))
    packet = jnp.stack(packet)
    mse_loss = packet[0, 1, 0] / (valid_count * D)
    gain_grad = packet[:, :1, :gain_cols]

    outcome = update(
        [grad_qkv, grad_out, down_grads],
        [list(pair) for pair in gu_sums],
        (mom_qkv, mom_out, mom_gu, mom_down),
        (w_qkv, w_out, w_gu, w_down),
        15,
    )
    new_weights, moments = outcome[:4], outcome[4:]
    gain_first_new = beta_one * gain_first + (1.0 - beta_one) * gain_grad
    gain_second_new = beta_two * gain_second + (1.0 - beta_two) * gain_grad * gain_grad
    gains_new = norm_gains - adam_rate * (gain_first_new / (1.0 - beta_one**STEP)) / (
        jnp.sqrt(gain_second_new / (1.0 - beta_two**STEP)) + adam_epsilon
    )
    return (
        mse_loss,
        hidden,
        grad_hidden,
        *new_weights,
        *moments,
        gains_new,
        gain_first_new,
        gain_second_new,
    )


def solution(mesh):
    cores, length = mesh.devices.shape
    split = Mesh(mesh.devices.reshape(cores, length // PLANE, PLANE), EVERY)
    stream = P("head", SEQ, None)
    matrix = P(None, SEQ, "head")
    gains = P(None, "head", SEQ)
    return jax.shard_map(
        body,
        mesh=split,
        in_specs=(stream, stream, stream, P(), P("head", SEQ))
        + (matrix,) * 4
        + (gains,)
        + (matrix,) * 4
        + (gains,) * 2,
        out_specs=(P(), stream, stream) + (matrix,) * 8 + (gains,) * 3,
        check_vma=False,
    )
```

```python
from functools import partial
import itertools
import math

import jax
import jax.numpy as jnp
from jax import lax
from jax.experimental import pallas as pl
from jax.experimental.pallas import tpu as pltpu
from jax.sharding import Mesh, PartitionSpec as P

D = 1152
HEADS = 4
HD = 256
FF = 6912
WINDOW = 512
LAYERS = 2
NS_ITERS = 5
STEP = 10
PLANE = 4

norm_eps = 1e-06
rope_base = 10000.0
newton_one = 3.4445
newton_two = -4.775
newton_three = 2.0315
muon_decay = 0.95
muon_rate = 0.15
muon_shrink = 0.01
muon_scale = 0.2
beta_one = 0.9
beta_two = 0.95
adam_rate = 0.7
adam_epsilon = 1e-08
finest_precision = lax.Precision.HIGHEST
MESH = pl.DeviceIdType.MESH
SEQ = ("zd", "tp")
GROUP = ("head", "tp")
EVERY = ("head", "zd", "tp")
bf16 = jnp.bfloat16
f32 = jnp.float32
LIGHT = pl.CostEstimate(flops=1, bytes_accessed=1, transcendentals=0)


def linear(places, sizes):
    index = 0
    for place, size in zip(places, sizes):
        index = index * size + place
    return index


def enter(partners):
    barrier = pltpu.get_barrier_semaphore()
    for partner in partners:
        pl.semaphore_signal(barrier, inc=1, device_id=partner, device_id_type=MESH)
    pl.semaphore_wait(barrier, len(partners))


class Spread:
    ORDER = ("zd", "tp", "head")

    def __init__(self, sizes, slots, send_sem, recv_sem):
        self.size = dict(zip(EVERY, sizes))
        self.place = {axis: lax.axis_index(axis) for axis in EVERY}
        self.slots, self.send_sem, self.recv_sem = slots, send_sem, recv_sem
        self.held, self.sends, self.number = [(self.place, None)], [], 0

    def partners(self):
        return [
            {axis: lax.rem(self.place[axis] + step, self.size[axis])}
            for axis in self.ORDER
            for step in range(1, self.size[axis])
        ]

    def stage(self, axis):
        arriving = []
        for where, arrivals in self.held:
            while arrivals:
                arrivals.pop().wait_recv()
            for step in range(1, self.size[axis]):
                to = lax.rem(self.place[axis] + step, self.size[axis])
                back = lax.rem(self.place[axis] - step + self.size[axis], self.size[axis])
                landing = []
                for k, slot in enumerate(self.slots):
                    ref = slot.at[tuple(where[name] for name in EVERY)]
                    copy = pltpu.make_async_remote_copy(
                        src_ref=ref,
                        dst_ref=ref,
                        send_sem=self.send_sem.at[k, self.number],
                        recv_sem=self.recv_sem.at[k, self.number],
                        device_id={axis: to},
                        device_id_type=MESH,
                    )
                    copy.start()
                    self.sends.append(copy)
                    landing.append(copy)
                self.number += 1
                arriving.append((dict(where, **{axis: back}), landing))
        self.held = self.held + arriving

    def finish(self):
        for _, arrivals in self.held:
            while arrivals:
                arrivals.pop().wait_recv()
        for copy in self.sends:
            copy.wait_send()


def start_kernel(sizes, layer, first, tiled, *refs):
    cores, planes, members = sizes
    if tiled:
        down, refs = refs[0], refs[1:]
        down_low, down_send, down_recv, down_own, refs = *refs[-4:], refs[:-4]
        count = 4 if first else 2
        down_result, refs = refs[count], refs[:count] + refs[count + 1 :]
    if first:
        gu, qkv, out, packet, gu_result, mixed, project, packets = refs[:8]
        qkv_slots, out_slots, packet_slots, send_sem, recv_sem = refs[8:13]
        pieces, gu_send, gu_recv, gu_own = refs[13:]
        slots = [packet_slots, qkv_slots, out_slots]
    else:
        qkv, out, mixed, project, qkv_slots, out_slots, send_sem, recv_sem = refs
        slots = [qkv_slots, out_slots]
    gather = Spread(sizes, slots, send_sem, recv_sem)
    here = tuple(gather.place[name] for name in EVERY)
    core, _, tp = here
    group = []
    for step in range(1, cores * members):
        far = lax.rem(core + step // members, cores), lax.rem(tp + step % members, members)
        group.append((dict(zip(GROUP, far)), linear(far, (cores, members))))
    if first:
        enter(gather.partners() + [device for device, _ in group])
        packet_slots[here] = packet[...]
    else:
        enter(gather.partners())
    for source, slot in ((qkv, qkv_slots), (out, out_slots)):
        rows = source.shape[1]
        slot[here + (slice(0, rows),)] = source[layer].astype(bf16)
        if slot.shape[3] > rows:
            slot[here + (slice(rows, None),)] = jnp.zeros(
                (slot.shape[3] - rows, slot.shape[4]), bf16
            )
    gather.stage("zd")
    moves = []
    if tiled:
        down_low[...] = down[layer].astype(bf16)
        zd = gather.place["zd"]
        for step in range(1, planes):
            copy = pltpu.make_async_remote_copy(
                src_ref=down_low,
                dst_ref=down_result.at[zd],
                send_sem=down_send.at[step],
                recv_sem=down_recv.at[step],
                device_id={"zd": lax.rem(zd + step, planes)},
                device_id_type=MESH,
            )
            copy.start()
            moves.append(copy)
        own = pltpu.make_async_copy(down_low, down_result.at[zd], down_own)
        own.start()
        moves.append(own)
    if first:
        layers, rows, columns = gu.shape
        block = columns // (planes * members)
        half = planes // cores
        for c in range(cores):
            for j in range(members):
                for i in range(layers):
                    cut = [
                        gu[i, :, pl.ds(((c * half + k) * members + j) * block, block)]
                        for k in range(half)
                    ]
                    value = jnp.concatenate(cut, axis=1) if half > 1 else cut[0]
                    pieces[c * members + j, i * rows : (i + 1) * rows] = value.astype(bf16)
        if pieces.shape[1] > layers * rows:
            for piece in range(cores * members):
                pieces[piece, layers * rows :] = jnp.zeros(
                    (pieces.shape[1] - layers * rows, pieces.shape[2]), bf16
                )
        me = linear((core, tp), (cores, members))
        for step, (device, index) in enumerate(group):
            copy = pltpu.make_async_remote_copy(
                src_ref=pieces.at[index],
                dst_ref=gu_result.at[me],
                send_sem=gu_send.at[step],
                recv_sem=gu_recv.at[step],
                device_id=device,
                device_id_type=MESH,
            )
            copy.start()
            moves.append(copy)
        own = pltpu.make_async_copy(pieces.at[me], gu_result.at[me], gu_own)
        own.start()
        moves.append(own)
    gather.stage("tp")
    gather.stage("head")
    gather.finish()
    for slot, result, rows in ((qkv_slots, mixed, qkv.shape[1]), (out_slots, project, out.shape[1])):
        columns = slot.shape[4]
        for h, z, t in itertools.product(range(cores), range(planes), range(members)):
            row = (z * members + t) * rows
            result[row : row + rows, h * columns : (h + 1) * columns] = slot[h, z, t, :rows]
    if first:
        packets[...] = packet_slots[...]
    for copy in moves:
        copy.wait()


def start(w_qkv, w_out, w_down, layer, ident, w_gu=None, packet=None):
    sizes = tuple(lax.axis_size(axis) for axis in EVERY)
    cores, planes, members = sizes
    vmem, dma = pltpu.VMEM, pltpu.SemaphoreType.DMA
    here, there = pl.BlockSpec(memory_space=pltpu.VMEM), pl.BlockSpec(memory_space=pl.ANY)
    shape = jax.ShapeDtypeStruct
    (_, qkv_rows, qkv_cols), (_, out_rows, out_cols) = w_qkv.shape, w_out.shape
    outs = [
        shape((qkv_rows * planes * members, qkv_cols * cores), bf16),
        shape((out_rows * planes * members, out_cols * cores), bf16),
    ]
    slots = [vmem(sizes + (-(-w.shape[1] // 16) * 16, w.shape[2]), bf16) for w in (w_qkv, w_out)]
    count, moves = 2, math.prod(sizes) - 1
    operands, out_specs, extra = [w_qkv, w_out], [here] * 2, []
    if w_gu is not None:
        layers, rows, columns = w_gu.shape
        tall = -(-layers * rows // 16) * 16
        piece = (cores * members, tall, columns // (cores * members))
        operands = [w_gu] + operands + [packet]
        outs = [shape(piece, bf16)] + outs + [shape(sizes + packet.shape, f32)]
        out_specs = [there] + out_specs + [here]
        slots, count = slots + [vmem(sizes + packet.shape, f32)], 3
        extra = [vmem(piece, bf16), dma((cores * members - 1,)), dma((cores * members - 1,)), dma]
    tiled = w_down.shape[1] % 16 == 0
    if tiled:
        _, rows, columns = w_down.shape
        operands = [w_down] + operands
        outs = [shape((planes, rows, columns), bf16)] + outs
        out_specs = [there] + out_specs
        extra += [vmem((rows, columns), bf16), dma((planes,)), dma((planes,)), dma]
    return pl.pallas_call(
        partial(start_kernel, sizes, layer, w_gu is not None, tiled),
        out_shape=outs,
        in_specs=[here] * len(operands),
        out_specs=out_specs,
        scratch_shapes=slots + [dma((count, moves))] * 2 + extra,
        cost_estimate=LIGHT,
        compiler_params=pltpu.CompilerParams(
            collective_id=ident, has_side_effects=True, vmem_limit_bytes=48 * 2**20
        ),
    )(*operands)


def by_rows(rows, work, step=16):
    @pl.loop(0, rows // step)
    def _(index):
        work(pl.ds(pl.multiple_of(index * step, step), step))


def collect_kernel(sizes, layers, *refs):
    cores, planes, members = sizes
    acts, packet, results = refs[: 4 * layers], refs[4 * layers], refs[4 * layers + 1 :][:3]
    rest = list(refs[4 * layers + 4 :])
    take = lambda number: [rest.pop(0) for _ in range(number)]
    far, halves = take(4 * layers), take(2 * layers)
    packet_land = rest.pop(0)
    pieces, plane_lands, totals, z_sums, z_lands = (take(3) for _ in range(5))
    act_send, act_recv, packet_send, packet_recv = take(4)
    tp_send, tp_recv, z_send, z_recv = take(4)
    core, zd, tp = (lax.axis_index(axis) for axis in EVERY)
    sibling = {"head": 1 - core}
    enter(
        [sibling]
        + [{"tp": lax.rem(tp + step, members)} for step in range(1, members)]
        + [{"zd": lax.rem(zd + step, planes)} for step in range(1, planes)]
    )
    sends = []

    def send(src, dst, send_sem, recv_sem, device):
        copy = pltpu.make_async_remote_copy(
            src_ref=src,
            dst_ref=dst,
            send_sem=send_sem,
            recv_sem=recv_sem,
            device_id=device,
            device_id_type=MESH,
        )
        copy.start()
        sends.append(copy)
        return copy

    for k in range(2 * layers):
        grad, half = acts[2 * k + 1], halves[k]
        width = half.shape[2]
        for h in range(cores):
            half[h] = grad[:, h * width : (h + 1) * width]
    moves = []
    for k in range(2 * layers):
        moves.append(
            send(acts[2 * k], far[2 * k], act_send.at[2 * k], act_recv.at[2 * k], sibling)
        )
        moves.append(
            send(
                halves[k].at[1 - core],
                far[2 * k + 1],
                act_send.at[2 * k + 1],
                act_recv.at[2 * k + 1],
                sibling,
            )
        )
    gains = send(packet.at[1 - core], packet_land, packet_send, packet_recv, sibling)
    plane_moves, z_moves = {}, {}
    for kind in range(3):
        piece = pieces[kind]
        if kind < 2:
            for layer in range(layers):
                k = 2 * layer + kind
                near = lax.dot_general(
                    acts[2 * k][...], halves[k][core], ALONG, preferred_element_type=f32
                )
                moves[2 * k].wait_recv()
                moves[2 * k + 1].wait_recv()
                value = near + lax.dot_general(
                    far[2 * k][...], far[2 * k + 1][...], ALONG, preferred_element_type=f32
                )
                value = value.astype(bf16)
                rows = value.shape[0] // (planes * members)
                slab = piece.shape[1] // planes
                for z, t in itertools.product(range(planes), range(members)):
                    at = (z * members + t) * rows
                    to = z * slab + layer * rows
                    piece[t, to : to + rows] = value[at : at + rows]
            if slab > layers * rows:
                for z, t in itertools.product(range(planes), range(members)):
                    piece[t, z * slab + layers * rows : (z + 1) * slab] = jnp.zeros(
                        (slab - layers * rows, piece.shape[2]), bf16
                    )
        else:
            gains.wait_recv()
            piece[...] = packet[core] + packet_land[...]
        for step in range(1, members):
            there = lax.rem(tp + step, members)
            plane_moves[kind, step] = send(
                piece.at[there],
                plane_lands[kind].at[step],
                tp_send.at[kind, step],
                tp_recv.at[kind, step],
                {"tp": there},
            )
    for kind in range(3):
        for step in range(1, members):
            plane_moves[kind, step].wait_recv()
        piece, total, land, result = pieces[kind], totals[kind], plane_lands[kind], results[kind]
        stride = 8 if land.dtype == f32 else 16

        def gather_plane(rows):
            value = piece[tp, rows].astype(f32)
            for step in range(1, members):
                value = value + land[step, rows].astype(f32)
            total[rows] = value

        by_rows(total.shape[0], gather_plane, stride)
        height = result.shape[0]
        z_sum = z_sums[kind]
        for step in range(1, planes):
            there = lax.rem(zd + step, planes)

            def round_off(rows):
                at = pl.multiple_of(there * height + rows.start, stride)
                z_sum[step, rows] = total[pl.ds(at, rows.size)].astype(z_sum.dtype)

            by_rows(height, round_off, stride)
            z_moves[kind, step] = send(
                z_sum.at[step],
                z_lands[kind].at[step],
                z_send.at[kind, step],
                z_recv.at[kind, step],
                {"zd": there},
            )
    for kind in range(3):
        for step in range(1, planes):
            z_moves[kind, step].wait_recv()
        total, land, result = totals[kind], z_lands[kind], results[kind]
        height = result.shape[0]
        stride = 8 if land.dtype == f32 else 16

        def gather_z(rows):
            at = pl.multiple_of(zd * height + rows.start, stride)
            value = total[pl.ds(at, rows.size)]
            for step in range(1, planes):
                value = value + land[step, rows].astype(f32)
            result[rows] = value

        by_rows(height, gather_z, stride)
    for copy in sends:
        copy.wait_send()


def collect(acts, packet, ident):
    sizes = tuple(lax.axis_size(axis) for axis in EVERY)
    cores, planes, members = sizes
    layers = len(acts) // 4
    vmem, dma = pltpu.VMEM, pltpu.SemaphoreType.DMA
    tokens = acts[0].shape[0]
    halves = [acts[2 * k + 1].shape[1] // cores for k in range(2 * layers)]
    slabs = []
    for kind in range(2):
        rows = layers * acts[2 * kind].shape[1] // (planes * members)
        slabs.append((-(-rows // 16) * 16, halves[kind], bf16))
    slabs.append((packet.shape[2] // planes, packet.shape[3], f32))
    far = []
    for k in range(2 * layers):
        far += [vmem(acts[2 * k].shape, bf16), vmem((tokens, halves[k]), bf16)]
    scratch = far + [vmem((cores, tokens, width), bf16) for width in halves]
    scratch += [vmem(packet.shape[1:], f32)]
    scratch += [vmem((members, planes * r, c), kind) for r, c, kind in slabs] * 2
    scratch += [vmem((planes * r, c), f32) for r, c, _ in slabs]
    scratch += [vmem((planes, r, c), kind) for r, c, kind in slabs] * 2
    scratch += [dma((4 * layers,))] * 2 + [dma] * 2
    scratch += [dma((3, members))] * 2 + [dma((3, planes))] * 2
    here = pl.BlockSpec(memory_space=pltpu.VMEM)
    return pl.pallas_call(
        partial(collect_kernel, sizes, layers),
        out_shape=[jax.ShapeDtypeStruct((r, c), f32) for r, c, _ in slabs],
        in_specs=[here] * (len(acts) + 1),
        out_specs=[here] * 3,
        scratch_shapes=scratch,
        cost_estimate=LIGHT,
        compiler_params=pltpu.CompilerParams(
            collective_id=ident, has_side_effects=True, vmem_limit_bytes=56 * 2**20
        ),
    )(*acts, packet)


def neighbours(planes, reach, sign):
    total = planes * PLANE
    place = linear([lax.axis_index("zd"), lax.axis_index("tp")], (planes, PLANE))

    def at(distance):
        there = lax.rem(place + distance + total, total)
        return {"zd": lax.div(there, PLANE), "tp": lax.rem(there, PLANE)}

    steps = range(1, reach + 1)
    return [at(sign * step) for step in steps], [at(-sign * step) for step in steps]


def inverse_rms(values):
    return lax.rsqrt(jnp.mean(values * values, axis=-1, keepdims=True) + norm_eps)


def rms_back(gradient, values, gain):
    inverse = inverse_rms(values)
    scaled = gradient * gain
    shared = jnp.mean(scaled * values, axis=-1, keepdims=True) * (inverse * inverse)
    return inverse * (scaled - values * shared), jnp.sum(
        gradient * values * inverse, axis=0, keepdims=True
    )


def turn(values, cosine, sine):
    half = values.shape[-1] // 2
    lower, upper = values[:, :half], values[:, half:]
    return jnp.concatenate(
        [lower * cosine - upper * sine, upper * cosine + lower * sine], axis=-1
    )


def soft_rows(query, keys, bias):
    scores = lax.dot_general(query, keys, ACROSS, preferred_element_type=f32)
    scores = scores * (1.0 / math.sqrt(HD)) + bias
    raised = jnp.exp(scores - jnp.max(scores, axis=-1, keepdims=True))
    return raised / jnp.sum(raised, axis=-1, keepdims=True)


def attn_forward_kernel(planes, reach, chained, *refs):
    rest = list(refs)
    take = lambda number: [rest.pop(0) for _ in range(number)]
    if chained:
        base, down, before = take(3)
    else:
        (base,) = take(1)
    w_mixed, w_project, gains, cosine, sine, bias = take(6)
    hidden, normed, mixed, queries, keyvals_out = take(5)
    attended, projected, hidden_half, normed_ffn = take(4)
    keyvals, send_sem, recv_sem, save_sem = take(4)
    seqs, stretch, key_len = bias.shape
    devices, sources = neighbours(planes, reach, 1)
    enter(devices + sources)
    value = base[...].astype(f32)
    if chained:
        late = down[...]
        value = value + late * inverse_rms(late) * before[1:2, D : 2 * D]
    hidden[...] = value
    low = (value * inverse_rms(value) * gains[0:1, :D]).astype(bf16)
    normed[...] = low
    mixed[...] = matmul(low, w_mixed[...])
    key = mixed[:, HEADS * HD : HEADS * HD + HD]
    key = turn(key * inverse_rms(key) * gains[1:2, 2 * D :], cosine[...], sine[...]).astype(bf16)
    late_values = mixed[:, HEADS * HD + HD :].astype(bf16)
    copies = []
    for i in range(seqs):
        rows = slice(i * stretch, (i + 1) * stretch)
        keyvals[i, reach * stretch :, :HD] = key[rows]
        keyvals[i, reach * stretch :, HD:] = late_values[rows]
        for step, device in enumerate(devices):
            copy = pltpu.make_async_remote_copy(
                src_ref=keyvals.at[i, pl.ds(reach * stretch, stretch)],
                dst_ref=keyvals.at[i, pl.ds((reach - 1 - step) * stretch, stretch)],
                send_sem=send_sem.at[i, step],
                recv_sem=recv_sem.at[i, step],
                device_id=device,
                device_id_type=MESH,
            )
            copy.start()
            copies.append(copy)
    for h in range(HEADS):
        columns = slice(h * HD, (h + 1) * HD)
        query = mixed[:, columns]
        query = turn(query * inverse_rms(query) * gains[0:1, 2 * D :], cosine[...], sine[...])
        queries[:, columns] = query.astype(bf16)
    for copy in copies:
        copy.wait_recv()
    save = pltpu.make_async_copy(keyvals, keyvals_out, save_sem)
    save.start()
    for i in range(seqs):
        rows = slice(i * stretch, (i + 1) * stretch)
        for h in range(HEADS):
            columns = slice(h * HD, (h + 1) * HD)
            soft = soft_rows(queries[rows, columns], keyvals[i, :, :HD], bias[i])
            attended[rows, columns] = matmul(soft.astype(bf16), keyvals[i, :, HD:]).astype(bf16)
    out = matmul(attended[...], w_project[...])
    projected[...] = out
    half = hidden[...] + out * inverse_rms(out) * gains[0:1, D : 2 * D]
    hidden_half[...] = half
    normed_ffn[...] = (half * inverse_rms(half) * gains[1:2, :D]).astype(bf16)
    for copy in copies:
        copy.wait_send()
    save.wait()


def attn_forward(base, weights, gains, tables, bias, planes, reach, ident, earlier=None):
    tokens = base.shape[0]
    seqs, _, key_len = bias.shape
    shape = jax.ShapeDtypeStruct
    operands = [base] + list(earlier or []) + list(weights) + [gains, *tables, bias]
    here, there = pl.BlockSpec(memory_space=pltpu.VMEM), pl.BlockSpec(memory_space=pl.ANY)
    dma = pltpu.SemaphoreType.DMA
    return pl.pallas_call(
        partial(attn_forward_kernel, planes, reach, earlier is not None),
        out_shape=[
            shape((tokens, D), f32),
            shape((tokens, D), bf16),
            shape((tokens, weights[0].shape[1]), f32),
            shape((tokens, HEADS * HD), bf16),
            shape((seqs, key_len, 2 * HD), bf16),
            shape((tokens, HEADS * HD), bf16),
            shape((tokens, D), f32),
            shape((tokens, D), f32),
            shape((tokens, D), bf16),
        ],
        in_specs=[here] * len(operands),
        out_specs=[here] * 4 + [there] + [here] * 4,
        scratch_shapes=[
            pltpu.VMEM((seqs, key_len, 2 * HD), bf16),
            dma((seqs, reach)),
            dma((seqs, reach)),
            dma,
        ],
        compiler_params=pltpu.CompilerParams(
            collective_id=ident, has_side_effects=True, vmem_limit_bytes=56 * 2**20
        ),
    )(*operands)


def attn_backward_kernel(planes, reach, chained, *refs):
    rest = list(refs)
    take = lambda number: [rest.pop(0) for _ in range(number)]
    d_ffn, above, hidden, mixed, queries, keyvals, projected, hidden_half = take(8)
    w_mixed, w_project, gains, cosine, sine, bias = take(6)
    if chained:
        down, before = take(2)
    grad, d_mixed, d_projected, gain_grads = take(4)
    if chained:
        d_down, d_post = take(2)
    d_keyvals, outgoing, incoming, d_attended, send_sem, recv_sem = take(6)
    seqs, stretch, key_len = bias.shape
    devices, sources = neighbours(planes, reach, -1)
    enter(devices + sources)
    scale = 1.0 / math.sqrt(HD)
    part, gain_row = rms_back(d_ffn[...], hidden_half[...], gains[1:2, :D])
    gain_grads[1:2, :D] = gain_row
    gain_grads[1:2, D : 2 * D] = jnp.zeros((1, D), f32)
    grad[...] = part + above[...]
    part, gain_row = rms_back(grad[...], projected[...], gains[0:1, D : 2 * D])
    gain_grads[0:1, D : 2 * D] = gain_row
    low = part.astype(bf16)
    d_projected[...] = low
    d_attended[...] = lax.dot_general(
        low, w_project[...], ACROSS, preferred_element_type=f32
    ).astype(bf16)
    query_gain = jnp.zeros((1, HD), f32)
    for i in range(seqs):
        rows = slice(i * stretch, (i + 1) * stretch)
        d_keys = d_values = None
        for h in range(HEADS):
            columns = slice(h * HD, (h + 1) * HD)
            query, d_out = queries[rows, columns], d_attended[rows, columns]
            keys, values = keyvals[i, :, :HD], keyvals[i, :, HD:]
            soft = soft_rows(query, keys, bias[i])
            d_soft = lax.dot_general(d_out, values, ACROSS, preferred_element_type=f32)
            total = jnp.sum(soft * d_soft, axis=-1, keepdims=True)
            d_scores = (soft * (d_soft - total)).astype(bf16)
            key_part = lax.dot_general(d_scores, query, ALONG, preferred_element_type=f32)
            value_part = lax.dot_general(
                soft.astype(bf16), d_out, ALONG, preferred_element_type=f32
            )
            d_keys = key_part if d_keys is None else d_keys + key_part
            d_values = value_part if d_values is None else d_values + value_part
            d_query = matmul(d_scores, keys) * scale
            d_query = turn(d_query, cosine[rows], -sine[rows])
            part, gain_row = rms_back(d_query, mixed[rows, columns], gains[0:1, 2 * D :])
            query_gain = query_gain + gain_row
            d_mixed[rows, columns] = part.astype(bf16)
        d_keyvals[i, :, :HD] = d_keys * scale
        d_keyvals[i, :, HD:] = d_values
    gain_grads[0:1, 2 * D :] = query_gain
    outgoing[...] = d_keyvals[:, : reach * stretch].astype(bf16)
    copies = []
    for i in range(seqs):
        for step, device in enumerate(devices):
            copy = pltpu.make_async_remote_copy(
                src_ref=outgoing.at[i, pl.ds((reach - 1 - step) * stretch, stretch)],
                dst_ref=incoming.at[i, step],
                send_sem=send_sem.at[i, step],
                recv_sem=recv_sem.at[i, step],
                device_id=device,
                device_id_type=MESH,
            )
            copy.start()
            copies.append(copy)
    for copy in copies:
        copy.wait_recv()
    key_gain = jnp.zeros((1, HD), f32)
    for i in range(seqs):
        rows = slice(i * stretch, (i + 1) * stretch)
        own = d_keyvals[i, reach * stretch :]
        for step in range(reach):
            own = own + incoming[i, step].astype(f32)
        d_key = turn(own[:, :HD], cosine[rows], -sine[rows])
        part, gain_row = rms_back(
            d_key, mixed[rows, HEADS * HD : HEADS * HD + HD], gains[1:2, 2 * D :]
        )
        key_gain = key_gain + gain_row
        d_mixed[rows, HEADS * HD : HEADS * HD + HD] = part.astype(bf16)
        d_mixed[rows, HEADS * HD + HD :] = own[:, HD:].astype(bf16)
    gain_grads[1:2, 2 * D :] = key_gain
    d_normed = lax.dot_general(d_mixed[...], w_mixed[...], ACROSS, preferred_element_type=f32)
    part, gain_row = rms_back(d_normed, hidden[...], gains[0:1, :D])
    gain_grads[0:1, :D] = gain_row
    grad[...] = grad[...] + part
    if chained:
        part, gain_row = rms_back(grad[...], down[...], before[1:2, D : 2 * D])
        d_down[...] = part.astype(bf16)
        d_post[...] = gain_row
    for copy in copies:
        copy.wait_send()


def attn_backward(
    d_ffn, above, kept, weights, gains, tables, bias, planes, reach, ident, earlier=None
):
    tokens = above.shape[0]
    seqs, stretch, key_len = bias.shape
    shape = jax.ShapeDtypeStruct
    operands = [d_ffn, above, *kept, *weights, gains, *tables, bias] + list(earlier or [])
    outs = [
        shape((tokens, D), f32),
        shape((tokens, weights[0].shape[1]), bf16),
        shape((tokens, D), bf16),
        shape(gains.shape, f32),
    ]
    if earlier is not None:
        outs += [shape((tokens, D), bf16), shape((1, D), f32)]
    here = pl.BlockSpec(memory_space=pltpu.VMEM)
    vmem, dma = pltpu.VMEM, pltpu.SemaphoreType.DMA
    return pl.pallas_call(
        partial(attn_backward_kernel, planes, reach, earlier is not None),
        out_shape=outs,
        in_specs=[here] * len(operands),
        out_specs=[here] * len(outs),
        scratch_shapes=[
            vmem((seqs, key_len, 2 * HD), f32),
            vmem((seqs, reach * stretch, 2 * HD), bf16),
            vmem((seqs, reach, stretch, 2 * HD), bf16),
            vmem((tokens, HEADS * HD), bf16),
            dma((seqs, reach)),
            dma((seqs, reach)),
        ],
        compiler_params=pltpu.CompilerParams(
            collective_id=ident, has_side_effects=True, vmem_limit_bytes=56 * 2**20
        ),
    )(*operands)


GELU_SLOPE = math.sqrt(2.0 / math.pi)
GELU_CUBE = 0.044715
ACROSS = (((1,), (1,)), ((), ()))
ALONG = (((0,), (0,)), ((), ()))


class Plane:
    def __init__(self, own, bufs, sems):
        self.own = own
        self.rows, self.partial, self.other, self.lands, self.sums, self.arrived = bufs
        self.x_send, self.x_recv, self.f_send, self.f_recv = sems[:4]
        self.c_send, self.c_recv, self.p_send, self.p_recv, self.first = sems[4:]
        self.tp = lax.axis_index("tp")
        self.sibling = {"head": 1 - lax.axis_index("head")}

    def member(self, m):
        tp = self.tp
        upper = lax.rem(lax.div(tp, 2) + lax.div(m, 2), 2)
        lower = lax.rem(lax.rem(tp, 2) + lax.rem(m, 2), 2)
        return {"tp": upper * 2 + lower}

    def remote(self, src, dst, send, recv, device):
        return pltpu.make_async_remote_copy(
            src_ref=src,
            dst_ref=dst,
            send_sem=send,
            recv_sem=recv,
            device_id=device,
            device_id_type=MESH,
        )

    def push(self, m):
        return self.remote(
            self.own, self.rows.at[0, m], self.x_send.at[m], self.x_recv.at[m], self.member(m)
        )

    def keep(self):
        return pltpu.make_async_copy(self.own, self.rows.at[0, 0], self.first)

    def forward(self, m):
        return self.remote(
            self.rows.at[0, m],
            self.rows.at[1, m],
            self.f_send.at[m],
            self.f_recv.at[m],
            self.sibling,
        )

    def cross(self, m):
        return self.remote(
            self.other.at[m], self.lands.at[m], self.c_send.at[m], self.c_recv.at[m], self.sibling
        )

    def home(self, m):
        return self.remote(
            self.sums.at[m],
            self.arrived.at[m],
            self.p_send.at[m],
            self.p_recv.at[m],
            self.member(m),
        )

    def begin(self):
        self.keep().start()
        enter([self.sibling] + [self.member(jnp.int32(m)) for m in range(1, PLANE)])
        for m in range(1, PLANE):
            self.push(jnp.int32(m)).start()

    def work(self, compute):
        def settle(m):
            self.cross(m).wait_recv()

            def add(rows):
                value = self.partial[m, rows] + self.lands[m, rows].astype(f32)
                self.sums[m, rows] = value.astype(bf16)

            by_rows(self.partial.shape[1], add)
            self.home(m).start()

        def step(m, carry):
            @pl.when(m == 0)
            def _():
                self.keep().wait()

            @pl.when(m > 0)
            def _():
                self.push(m).wait_recv()

            self.forward(m).start()
            self.partial[m] = compute(0, m)
            self.forward(m).wait_recv()
            self.other[m] = compute(1, m).astype(bf16)
            self.cross(m).start()

            @pl.when(m >= 2)
            def _():
                settle(m - 1)

            return carry

        lax.fori_loop(0, PLANE, step, 0)
        settle(jnp.int32(PLANE - 1))

    def finish(self, result):
        self.cross(jnp.int32(0)).wait_recv()
        for m in range(1, PLANE):
            self.home(jnp.int32(m)).wait_recv()

        def add(rows):
            value = self.partial[0, rows] + self.lands[0, rows].astype(f32)
            for m in range(1, PLANE):
                value = value + self.arrived[m, rows].astype(f32)
            result[rows] = value

        by_rows(result.shape[0], add)
        for m in range(PLANE):
            m = jnp.int32(m)
            self.forward(m).wait_send()
            self.cross(m).wait_send()
        for m in range(1, PLANE):
            m = jnp.int32(m)
            self.push(m).wait_send()
            self.home(m).wait_send()


def gate_up_copies(gu_ref, gate_up, sem):
    blocks = gu_ref.shape[0]
    rows = gate_up.shape[1] // blocks
    return [
        pltpu.make_async_copy(
            gu_ref.at[block, part],
            gate_up.at[part, pl.ds(block * rows, rows)],
            sem.at[2 * block + part],
        )
        for block in range(blocks)
        for part in range(2)
    ]


def ffn_forward_kernel(own, gu_ref, halves_ref, group, saved_down, result, *scratch):
    rows, gate_up, down = scratch[:3]
    plane = Plane(own, (rows,) + scratch[3:8], scratch[8:17])
    weight_sem, group_sem, halves, half_send, half_recv, half_own, save_sem = scratch[17:]
    core = lax.axis_index("head")
    share, width = halves.shape[1:]
    copies = gate_up_copies(gu_ref, gate_up, weight_sem)
    copies.append(
        pltpu.make_async_copy(
            halves_ref.at[0, pl.ds(pl.multiple_of(core * share, 16), share)],
            halves.at[core],
            half_own,
        )
    )
    for copy in copies:
        copy.start()
    plane.begin()
    half = plane.remote(
        halves_ref.at[0, pl.ds(pl.multiple_of((1 - core) * share, 16), share)],
        halves.at[core],
        half_send,
        half_recv,
        plane.sibling,
    )
    half.start()
    for copy in copies:
        copy.wait()
    pltpu.make_async_remote_copy(
        src_ref=halves_ref.at[0, pl.ds(pl.multiple_of((1 - core) * share, 16), share)],
        dst_ref=halves.at[1 - core],
        send_sem=half_send,
        recv_sem=half_recv,
        device_id=plane.sibling,
        device_id_type=MESH,
    ).wait_recv()

    def join(at):
        down[at] = jnp.concatenate([halves[h, at] for h in range(2)], axis=1)

    by_rows(share, join, 32)
    keep_down = pltpu.make_async_copy(down, saved_down, save_sem)
    keep_down.start()

    def compute(side, m):
        tokens = rows[side, m]
        gate = matmul(tokens, gate_up[0])
        up = matmul(tokens, gate_up[1])
        bend = jnp.tanh(GELU_SLOPE * (gate + GELU_CUBE * (gate * gate * gate)))
        inner = (0.5 * gate * (1.0 + bend) * up).astype(bf16)
        return matmul(inner, down[...])

    plane.work(compute)
    save = pltpu.make_async_copy(rows, group, group_sem)
    save.start()
    plane.finish(result)
    save.wait()
    keep_down.wait()
    half.wait_send()


def ffn_backward_kernel(
    own, group, gu_ref, down_ref, result, grad_gate, grad_up, grad_down, *scratch
):
    rows, gate_up, down = scratch[:3]
    plane = Plane(own, (rows,) + scratch[3:8], scratch[8:17])
    weight_sem, group_sem, saved, d_gate, d_up, inner = scratch[17:23]
    down_sem, turned, down_halves, half_send, half_recv, half_own = scratch[23:]
    core = lax.axis_index("head")
    copies = gate_up_copies(gu_ref, gate_up, weight_sem)
    copies.append(pltpu.make_async_copy(down_ref, down, down_sem))
    for copy in copies:
        copy.start()
    load = pltpu.make_async_copy(group, saved, group_sem)
    load.start()
    plane.begin()
    for copy in copies:
        copy.wait()
    load.wait()

    def recompute(index, carry):
        side, m = lax.div(index, PLANE), lax.rem(index, PLANE)
        tokens = saved[side, m]
        gate = matmul(tokens, gate_up[0])
        up = matmul(tokens, gate_up[1])
        square = gate * gate
        bend = jnp.tanh(GELU_SLOPE * (gate + GELU_CUBE * (square * gate)))
        half = 0.5 * (1.0 + bend)
        value = gate * half
        slope = half + (0.5 * GELU_SLOPE) * gate * (1.0 - bend * bend) * (
            1.0 + (3.0 * GELU_CUBE) * square
        )
        inner[side, m] = (value * up).astype(bf16)
        d_gate[side, m] = (slope * up).astype(bf16)
        d_up[side, m] = value.astype(bf16)
        return carry

    lax.fori_loop(0, 2 * PLANE, recompute, 0)

    def compute(side, m):
        d_inner = lax.dot_general(rows[side, m], down[...], ACROSS, preferred_element_type=f32)
        gate = (d_inner * d_gate[side, m].astype(f32)).astype(bf16)
        up = (d_inner * d_up[side, m].astype(f32)).astype(bf16)
        d_gate[side, m] = gate
        d_up[side, m] = up
        return lax.dot_general(
            gate, gate_up[0], ACROSS, preferred_element_type=f32
        ) + lax.dot_general(up, gate_up[1], ACROSS, preferred_element_type=f32)

    plane.work(compute)
    width = rows.shape[-1]
    step = width // 3

    def tall(ref, columns=slice(None)):
        value = ref[:, :, :, columns]
        return value.reshape(-1, value.shape[-1])

    @pl.loop(0, 3)
    def _(index):
        at = pl.ds(pl.multiple_of(index * step, step), step)
        tokens = tall(saved, at)
        for target, other in ((grad_gate, d_gate), (grad_up, d_up)):
            target[at] = lax.dot_general(
                tokens, tall(other), ALONG, preferred_element_type=f32
            ).astype(bf16)
        turned[at] = lax.dot_general(
            tall(rows, at), tall(inner), ALONG, preferred_element_type=f32
        ).astype(bf16)

    half_width = down_halves.shape[2]
    for h in range(2):
        down_halves[h] = turned[h * half_width : (h + 1) * half_width].T
    half = plane.remote(
        down_halves.at[1 - core], grad_down.at[core], half_send, half_recv, plane.sibling
    )
    half.start()
    stay = pltpu.make_async_copy(down_halves.at[core], grad_down.at[core], half_own)
    stay.start()
    plane.finish(result)
    half.wait()
    stay.wait()


def ffn(own, weights, ident, group=None):
    gate_up, down = weights
    tokens, width = own.shape
    blocks, _, _, share = gate_up.shape
    vmem, dma = pltpu.VMEM, pltpu.SemaphoreType.DMA
    scratch = [
        vmem((2, PLANE, tokens, width), bf16),
        vmem((2, width, share), bf16),
        vmem((share, width), bf16),
        vmem((PLANE, tokens, width), f32),
    ]
    scratch += [vmem((PLANE, tokens, width), bf16)] * 4
    scratch += [dma((PLANE,))] * 8 + [dma, dma((2 * blocks,)), dma]
    here, there = pl.BlockSpec(memory_space=pltpu.VMEM), pl.BlockSpec(memory_space=pl.ANY)
    shape = jax.ShapeDtypeStruct
    summed = shape((tokens, width), f32)
    if group is None:
        kernel, operands = ffn_forward_kernel, (own, gate_up, down)
        in_specs, out_specs = [here, there, there], [there, there, here]
        out_shape = [
            shape((2, PLANE, tokens, width), bf16),
            shape((share, width), bf16),
            summed,
        ]
        scratch += [vmem((2, share, width // 2), bf16)] + [dma] * 4
    else:
        kernel, operands = ffn_backward_kernel, (own, group, gate_up, down)
        in_specs, out_specs = [here, there, there, there], [here] * 3 + [there]
        out_shape = [
            summed,
            shape((width, share), bf16),
            shape((width, share), bf16),
            shape((2, share, width // 2), bf16),
        ]
        scratch += [vmem((2, PLANE, tokens, width), bf16)]
        scratch += [vmem((2, PLANE, tokens, share), bf16)] * 3
        scratch += [dma, vmem((width, share), bf16), vmem((2, share, width // 2), bf16)]
        scratch += [dma] * 3
    return pl.pallas_call(
        kernel,
        out_shape=out_shape,
        in_specs=in_specs,
        out_specs=out_specs,
        scratch_shapes=scratch,
        cost_estimate=LIGHT,
        compiler_params=pltpu.CompilerParams(
            collective_id=ident, has_side_effects=True, vmem_limit_bytes=60 * 2**20
        ),
    )(*operands)


def exact(left, right, dims=(((1,), (0,)), ((), ()))):
    return lax.dot_general(
        left, right, dims, precision=finest_precision, preferred_element_type=f32
    )


def update_kernel(sizes, *refs):
    cores, planes, members = sizes
    rest = list(refs)
    take = lambda number: [rest.pop(0) for _ in range(number)]
    plain = [take(cores) for _ in range(3)]
    sides = [take(2) for _ in range(cores)]
    moments_in, weights_in, weights_out, moments_out = (take(4) for _ in range(4))
    moment, weight, gram, land, factor = (take(4) for _ in range(5))
    pieces, arrived = take(2)
    load_sem, store_sem, gram_send, gram_recv, factor_send, factor_recv = take(6)
    gu_send, gu_recv, gu_own = take(3)
    core, _, tp = (lax.axis_index(axis) for axis in EVERY)
    sibling = {"head": 1 - core}
    order = (0, 1, 3, 2)
    loads = {}
    for k in range(4):
        for part, source, target in ((0, moments_in, moment), (1, weights_in, weight)):
            copy = pltpu.make_async_copy(source[k], target[k], load_sem.at[part, k])
            copy.start()
            loads[part, k] = copy
    group = []
    for step in range(1, cores * members):
        far = lax.rem(core + step // members, cores), lax.rem(tp + step % members, members)
        group.append((dict(zip(GROUP, far)), linear(far, (cores, members))))
    enter([device for device, _ in group])
    rows = moment[2].shape[1]
    for part in range(cores):
        for j in range(members):
            for layer in range(cores):
                pieces[part * members + j, layer * rows : (layer + 1) * rows] = sides[layer][part][
                    j * rows : (j + 1) * rows
                ]
    if pieces.shape[1] > cores * rows:
        for piece in range(cores * members):
            pieces[piece, cores * rows :] = jnp.zeros(
                (pieces.shape[1] - cores * rows, pieces.shape[2]), bf16
            )
    me = linear((core, tp), (cores, members))
    moves, stores = [], []

    def send(src, dst, send_sem, recv_sem, device):
        copy = pltpu.make_async_remote_copy(
            src_ref=src,
            dst_ref=dst,
            send_sem=send_sem,
            recv_sem=recv_sem,
            device_id=device,
            device_id_type=MESH,
        )
        copy.start()
        return copy

    for step, (device, index) in enumerate(group):
        moves.append(
            send(pieces.at[index], arrived.at[me], gu_send.at[step], gu_recv.at[step], device)
        )
    own = pltpu.make_async_copy(pieces.at[me], arrived.at[me], gu_own)
    own.start()

    def store(part, k):
        source, target = (moment, moments_out) if part == 0 else (weight, weights_out)
        copy = pltpu.make_async_copy(source[k], target[k], store_sem.at[part, k])
        copy.start()
        stores.append(copy)

    def gram_of(k):
        def one(layer, carry):
            gram[k][layer] = exact(moment[k][layer], moment[k][layer], ACROSS)
            return carry

        lax.fori_loop(0, cores, one, 0)
        return send(
            gram[k].at[1 - core], land[k], gram_send.at[k], gram_recv.at[k], sibling
        )

    def unit(size):
        down = lax.broadcasted_iota(jnp.int32, (size, size), 0)
        return (down == lax.broadcasted_iota(jnp.int32, (size, size), 1)).astype(f32)

    def orthogonal(members_of):
        for k in members_of:
            total = gram[k][core] + land[k][...]
            one = unit(total.shape[0])
            trace = jnp.sum(jnp.sum(total * one, axis=1, keepdims=True), axis=0, keepdims=True)
            scale = 1.0 / (jnp.sqrt(trace) + 1e-07)
            land[k][...] = total * (scale * scale)
            factor[k][core] = one * scale

        def polynomial(present):
            square = exact(present, present)
            return newton_one * unit(present.shape[0]) + newton_two * present + (
                newton_three * square
            )

        def step(_, carry):
            for k in members_of:
                present = land[k][...]
                poly = polynomial(present)
                factor[k][core] = exact(poly, factor[k][core])
                land[k][...] = exact(exact(poly, present), poly)
            return carry

        lax.fori_loop(0, NS_ITERS - 1, step, 0)
        for k in members_of:
            factor[k][core] = exact(polynomial(land[k][...]), factor[k][core])
        return [
            send(factor[k].at[core], factor[k].at[core], factor_send.at[k], factor_recv.at[k], sibling)
            for k in members_of
        ]

    def apply(k):
        columns = weight[k].shape[2] * cores
        rate = muon_rate * muon_scale * math.sqrt(columns)

        def one(layer, carry):
            weight[k][layer] = weight[k][layer] * (1.0 - muon_rate * muon_shrink) - rate * exact(
                factor[k][layer], moment[k][layer]
            )
            return carry

        lax.fori_loop(0, cores, one, 0)
        store(1, k)

    def arrive(copies):
        for copy in copies:
            copy.wait_recv()

    sent = []
    for index, k in enumerate(order[:3]):
        loads[0, k].wait()
        height = moment[k].shape[1]
        for layer in range(cores):
            moment[k][layer] = muon_decay * moment[k][layer] + plain[index][layer][:height].astype(
                f32
            )
        store(0, k)
        sent.append(gram_of(k))
    arrive(sent)
    crossed = orthogonal(order[:3])
    sent += crossed
    own.wait()
    for copy in moves:
        copy.wait_recv()
    loads[0, 2].wait()
    half = planes // cores
    block = arrived.shape[2] // half
    for layer in range(cores):
        cut = [
            arrived[
                c * members + j,
                layer * rows : (layer + 1) * rows,
                k * block : (k + 1) * block,
            ].astype(f32)
            for c in range(cores)
            for k in range(half)
            for j in range(members)
        ]
        moment[2][layer] = muon_decay * moment[2][layer] + jnp.concatenate(cut, axis=1)
    store(0, 2)
    last = gram_of(2)
    sent.append(last)
    arrive(crossed)
    for k in range(4):
        loads[1, k].wait()
    for k in order[:3]:
        apply(k)
    arrive([last])
    crossed = orthogonal(order[3:])
    sent += crossed
    arrive(crossed)
    apply(2)
    for copy in moves + sent:
        copy.wait_send()
    for copy in stores:
        copy.wait()


def update(gradients, sides, moments, weights, ident):
    sizes = tuple(lax.axis_size(axis) for axis in EVERY)
    cores, planes, members = sizes
    vmem, dma = pltpu.VMEM, pltpu.SemaphoreType.DMA
    layers, rows, columns = moments[2].shape
    piece = (
        cores * members,
        -(-layers * rows // 16) * 16,
        columns // (cores * members),
    )
    shapes = [m.shape for m in moments]
    square = [(s[1], s[1]) for s in shapes]
    scratch = [vmem(s, f32) for s in shapes] * 2
    scratch += [vmem((layers,) + s, f32) for s in square]
    scratch += [vmem(s, f32) for s in square]
    scratch += [vmem((layers,) + s, f32) for s in square]
    scratch += [vmem(piece, bf16)] * 2
    scratch += [dma((2, 4))] * 2 + [dma((4,))] * 4
    scratch += [dma((cores * members - 1,))] * 2 + [dma]
    here, there = pl.BlockSpec(memory_space=pltpu.VMEM), pl.BlockSpec(memory_space=pl.ANY)
    operands = sum(gradients, []) + sum(sides, [])
    return pl.pallas_call(
        partial(update_kernel, sizes),
        out_shape=[jax.ShapeDtypeStruct(s, f32) for s in shapes] * 2,
        in_specs=[here] * len(operands) + [there] * 8,
        out_specs=[there] * 8,
        scratch_shapes=scratch,
        compiler_params=pltpu.CompilerParams(
            collective_id=ident, has_side_effects=True, vmem_limit_bytes=56 * 2**20
        ),
    )(*operands, *moments, *weights)


def padded(array, multiple=16):
    extra = -array.shape[-2] % multiple
    if extra == 0:
        return array
    return jnp.pad(array, [(0, 0)] * (array.ndim - 2) + [(0, extra), (0, 0)])


def rms_norm(values, norm_gain):
    return (
        values * lax.rsqrt(jnp.mean(values * values, axis=-1, keepdims=True) + norm_eps) * norm_gain
    )


def rope_tables(positions, head_dim):
    half_dim = head_dim // 2
    frequency = jnp.exp(
        jnp.arange(half_dim, dtype=jnp.float32) * (-2.0 * math.log(rope_base) / head_dim)
    )
    angles = positions.astype(jnp.float32)[:, None] * frequency[None, :]
    return (jnp.cos(angles), jnp.sin(angles))


def matmul(left, right):
    return jnp.dot(left, right, preferred_element_type=f32)


def body(
    inputs,
    cotangent,
    teacher,
    segments,
    valid_mask,
    w_qkv,
    w_out,
    w_gu,
    w_down,
    norm_gains,
    mom_qkv,
    mom_out,
    mom_gu,
    mom_down,
    gain_first,
    gain_second,
):
    cores = lax.axis_size("head")
    planes = lax.axis_size("zd")
    seq_devices = planes * PLANE
    core = lax.axis_index("head")
    seq_place = lax.axis_index("zd") * PLANE + lax.axis_index("tp")
    half_seqs, stretch_len = inputs.shape[:2]
    tokens = half_seqs * stretch_len
    all_seqs = half_seqs * cores
    seq_length = stretch_len * seq_devices
    reach = -(-WINDOW // stretch_len)
    key_len = (reach + 1) * stretch_len
    qkv_rows, qkv_cols = w_qkv.shape[1:]
    out_rows, out_cols = w_out.shape[1:]
    gu_rows = w_gu.shape[1]
    ff_block = w_down.shape[1]
    share = FF // (cores * PLANE)
    half_planes = planes // cores
    gain_cols = norm_gains.shape[-1]
    gain_len = gain_cols * seq_devices
    lanes = -(-gain_cols // 128) * 128

    packet = jnp.zeros((8, lanes), f32)
    packet = packet.at[:LAYERS, :gain_cols].set(norm_gains[:, 0].astype(bf16).astype(f32))
    packet = packet.at[LAYERS, 0].set(jnp.sum(valid_mask.astype(f32)))
    *gathered_down, gu_pieces, w_mixed, w_project, packets = start(
        w_qkv, w_out, w_down, 0, 0, w_gu, packet
    )
    attn_weights = [w_mixed, w_project]
    gu_pieces = gu_pieces[:, : LAYERS * gu_rows].reshape(cores * PLANE, LAYERS, gu_rows, share)
    packets = packets.reshape(cores, seq_devices, 8, lanes)
    valid_count = jnp.sum(packets[:, :, LAYERS, 0])
    gain_rows = [
        packets[:, :, layer, :gain_cols].reshape(cores, gain_len) for layer in range(LAYERS)
    ]

    def gate_up_rows(layer):
        pieces = gu_pieces[:, layer].reshape(2, PLANE * gu_rows, share)
        pieces = lax.all_gather(pieces, "zd", axis=0)
        if PLANE * gu_rows % 16:
            pieces = pieces.transpose(1, 0, 2, 3).reshape(1, 2, D, share)
        return pieces

    def down_rows(layer, gathered):
        if gathered:
            return gathered[0].reshape(1, planes * ff_block, out_cols)
        rows = w_down[layer : layer + 1].astype(bf16)
        return lax.all_gather(rows, "zd", axis=1, tiled=True)

    full = [(gate_up_rows(0), down_rows(0, gathered_down))] + [None] * (LAYERS - 1)

    own_places = seq_place * stretch_len + jnp.arange(stretch_len, dtype=jnp.int32)
    key_places = (seq_place - reach) * stretch_len + jnp.arange(key_len, dtype=jnp.int32)
    cosine_table, sine_table = rope_tables(own_places, HD)
    own_rows = lax.dynamic_slice_in_dim(segments, core * half_seqs, half_seqs, 0)
    own_segments = lax.dynamic_slice_in_dim(own_rows, seq_place * stretch_len, stretch_len, 1)
    padded_segments = jnp.pad(own_rows, ((0, 0), (reach * stretch_len, 0)), constant_values=-1)
    key_segments = lax.dynamic_slice_in_dim(padded_segments, seq_place * stretch_len, key_len, 1)
    spacing = own_places[:, None] - key_places[None, :]
    allowed = (spacing >= 0) & (spacing < WINDOW) & (key_places[None, :] >= 0)
    allowed = allowed[None] & (own_segments[:, :, None] == key_segments[:, None, :])

    tables = [jnp.tile(t, (half_seqs, 1)) for t in (cosine_table, sine_table)]
    bias = jnp.where(allowed, 0.0, -1e30).astype(f32)

    saved, previous = [], None
    base = inputs.reshape(tokens, D)
    for layer in range(LAYERS):
        weights = list(attn_weights)
        hidden, normed, mixed, queries, keyvals, attended, projected, half, normed_ffn = attn_forward(
            base, weights, gain_rows[layer], tables, bias, planes, reach, 3 + layer, previous
        )
        ffn_share = full[layer]
        if layer + 1 < LAYERS:
            gu_pieces, later_qkv, later_out, later_down, attended = lax.optimization_barrier(
                (gu_pieces, w_qkv, w_out, w_down, attended)
            )
            *gathered_down, w_mixed, w_project = start(
                later_qkv, later_out, later_down, layer + 1, 2 + 20 * layer
            )
            attn_weights = [w_mixed, w_project]
            full[layer + 1] = (gate_up_rows(layer + 1), down_rows(layer + 1, gathered_down))
            normed_ffn, *attn_weights = lax.optimization_barrier((normed_ffn, *attn_weights))
        group_normed, whole_down, down_out = ffn(normed_ffn, ffn_share, 5 + layer)
        full[layer] = (weights, (ffn_share[0], whole_down))
        saved.append(
            (
                [hidden, mixed, queries, keyvals, projected, half],
                [normed, attended],
                group_normed,
                down_out,
            )
        )
        base, previous = half, (down_out, gain_rows[layer])

    output, post_ffn_back = jax.vjp(rms_norm, down_out, gain_rows[-1][1, D : 2 * D])
    output = base + output
    target_gap = output - teacher.reshape(tokens, D).astype(f32)
    valid_weight = valid_mask.astype(f32).reshape(tokens, 1)
    square_sum = jnp.sum(valid_weight * target_gap * target_gap)
    loss_weight = float(all_seqs * seq_length * D // 4)
    grad_hidden = (
        cotangent.reshape(tokens, D).astype(f32)
        + 2.0 * loss_weight / (valid_count * D) * valid_weight * target_gap
    )
    d_down, d_post_ffn = post_ffn_back(grad_hidden)
    d_down, d_post_ffn = d_down.astype(bf16), d_post_ffn[None]

    attn_acts = [None] * LAYERS
    down_grads = [None] * LAYERS
    gain_grads = [None] * LAYERS
    gu_sums = [None] * LAYERS
    for layer in reversed(range(LAYERS)):
        kept, (normed, attended), group_normed, _ = saved[layer]
        weights, ffn_share = full[layer]
        d_normed_ffn, *grad_gu, grad_down = ffn(d_down, ffn_share, 9 + layer, group_normed)
        down_grads[layer] = lax.psum_scatter(
            grad_down.reshape(planes * ff_block, out_cols), "zd", scatter_dimension=0, tiled=True
        )
        gu_sums[layer] = [
            lax.psum_scatter(g, "zd", scatter_dimension=0, tiled=True) for g in grad_gu
        ]
        earlier = (saved[layer - 1][3], gain_rows[layer - 1]) if layer > 0 else None
        grad_hidden, d_mixed, d_projected, gain_grads[layer], *d_rest = attn_backward(
            d_normed_ffn,
            grad_hidden,
            kept,
            weights,
            gain_rows[layer],
            tables,
            bias,
            planes,
            reach,
            17 + layer,
            earlier,
        )
        gain_grads[layer] = gain_grads[layer].at[1:, D : 2 * D].set(d_post_ffn)
        if layer > 0:
            d_down, d_post_ffn = d_rest
        attn_acts[layer] = [normed, d_mixed, attended, d_projected]
    attn_acts[0][1], gu_sums[1:], down_grads[1:] = lax.optimization_barrier(
        (attn_acts[0][1], gu_sums[1:], down_grads[1:])
    )

    collected = [None] * LAYERS
    for layer in reversed(range(LAYERS)):
        packet = gain_grads[layer].reshape(cores, planes, PLANE, gain_cols).transpose(0, 2, 1, 3)
        packet = jnp.pad(packet[:, :, :, None], [(0, 0)] * 3 + [(0, 7), (0, lanes - gain_cols)])
        packet = packet.at[:, :, :, 1, 0].set(square_sum)
        packet = packet.reshape(cores, PLANE, planes * 8, lanes)
        if layer > 0:
            packet, attn_acts[0][1] = lax.optimization_barrier((packet, attn_acts[0][1]))
        else:
            packet, collected[1:], gu_sums[0] = lax.optimization_barrier(
                (packet, collected[1:], gu_sums[0])
            )
        collected[layer] = collect(attn_acts[layer], packet, 19 + layer)
    grad_qkv, grad_out, packet = (list(parts) for parts in zip(*collected))
    packet = jnp.stack(packet)
    mse_loss = packet[0, 1, 0] / (valid_count * D)
    gain_grad = packet[:, :1, :gain_cols]

    outcome = update(
        [grad_qkv, grad_out, down_grads],
        [list(pair) for pair in gu_sums],
        (mom_qkv, mom_out, mom_gu, mom_down),
        (w_qkv, w_out, w_gu, w_down),
        15,
    )
    new_weights, moments = outcome[:4], outcome[4:]
    gain_first_new = beta_one * gain_first + (1.0 - beta_one) * gain_grad
    gain_second_new = beta_two * gain_second + (1.0 - beta_two) * gain_grad * gain_grad
    gains_new = norm_gains - adam_rate * (gain_first_new / (1.0 - beta_one**STEP)) / (
        jnp.sqrt(gain_second_new / (1.0 - beta_two**STEP)) + adam_epsilon
    )
    return (
        mse_loss,
        output.reshape(inputs.shape),
        grad_hidden.reshape(inputs.shape),
        *new_weights,
        *moments,
        gains_new,
        gain_first_new,
        gain_second_new,
    )


def solution(mesh):
    cores, length = mesh.devices.shape
    split = Mesh(mesh.devices.reshape(cores, length // PLANE, PLANE), EVERY)
    stream = P("head", SEQ, None)
    matrix = P(None, SEQ, "head")
    gains = P(None, "head", SEQ)
    return jax.shard_map(
        body,
        mesh=split,
        in_specs=(stream, stream, stream, P(), P("head", SEQ))
        + (matrix,) * 4
        + (gains,)
        + (matrix,) * 4
        + (gains,) * 2,
        out_specs=(P(), stream, stream) + (matrix,) * 8 + (gains,) * 3,
        check_vma=False,
    )
```

```python
from functools import partial
import itertools
import math

import jax
import jax.numpy as jnp
from jax import lax
from jax.experimental import pallas as pl
from jax.experimental.pallas import tpu as pltpu
from jax.sharding import Mesh, PartitionSpec as P

D = 1152
HEADS = 4
HD = 256
FF = 6912
WINDOW = 512
LAYERS = 2
NS_ITERS = 5
STEP = 10
PLANE = 4

norm_eps = 1e-06
rope_base = 10000.0
newton_one = 3.4445
newton_two = -4.775
newton_three = 2.0315
muon_decay = 0.95
muon_rate = 0.15
muon_shrink = 0.01
muon_scale = 0.2
beta_one = 0.9
beta_two = 0.95
adam_rate = 0.7
adam_epsilon = 1e-08
finest_precision = lax.Precision.HIGHEST
MESH = pl.DeviceIdType.MESH
SEQ = ("zd", "tp")
GROUP = ("head", "tp")
EVERY = ("head", "zd", "tp")
bf16 = jnp.bfloat16
f32 = jnp.float32
LIGHT = pl.CostEstimate(flops=1, bytes_accessed=1, transcendentals=0)


def linear(places, sizes):
    index = 0
    for place, size in zip(places, sizes):
        index = index * size + place
    return index


def enter(partners):
    barrier = pltpu.get_barrier_semaphore()
    for partner in partners:
        pl.semaphore_signal(barrier, inc=1, device_id=partner, device_id_type=MESH)
    pl.semaphore_wait(barrier, len(partners))


class Spread:
    ORDER = ("zd", "tp", "head")

    def __init__(self, sizes, slots, send_sem, recv_sem, whole_z=False):
        self.size = dict(zip(EVERY, sizes))
        self.place = {axis: lax.axis_index(axis) for axis in EVERY}
        self.slots, self.send_sem, self.recv_sem = slots, send_sem, recv_sem
        self.held, self.sends, self.number = [(self.place, None)], [], 0
        if whole_z:
            self.held = [(dict(self.place, zd=z), None) for z in range(self.size["zd"])]
            self.ORDER = self.ORDER[1:]

    def partners(self):
        return [
            {axis: lax.rem(self.place[axis] + step, self.size[axis])}
            for axis in self.ORDER
            for step in range(1, self.size[axis])
        ]

    def stage(self, axis):
        arriving = []
        for where, arrivals in self.held:
            while arrivals:
                arrivals.pop().wait_recv()
            for step in range(1, self.size[axis]):
                to = lax.rem(self.place[axis] + step, self.size[axis])
                back = lax.rem(self.place[axis] - step + self.size[axis], self.size[axis])
                landing = []
                for k, slot in enumerate(self.slots):
                    ref = slot.at[tuple(where[name] for name in EVERY)]
                    copy = pltpu.make_async_remote_copy(
                        src_ref=ref,
                        dst_ref=ref,
                        send_sem=self.send_sem.at[k, self.number],
                        recv_sem=self.recv_sem.at[k, self.number],
                        device_id={axis: to},
                        device_id_type=MESH,
                    )
                    copy.start()
                    self.sends.append(copy)
                    landing.append(copy)
                self.number += 1
                arriving.append((dict(where, **{axis: back}), landing))
        self.held = self.held + arriving

    def finish(self):
        for _, arrivals in self.held:
            while arrivals:
                arrivals.pop().wait_recv()
        for copy in self.sends:
            copy.wait_send()


def start_kernel(sizes, tiled, *refs):
    cores, planes, members = sizes
    rest = list(refs)
    take = lambda number: [rest.pop(0) for _ in range(number)]
    gu, qkv, out, packet = take(4)
    down = take(1)[0] if tiled else None
    gu_result, mixed, project, packets, qkv_later, out_later = take(6)
    down_result = take(1)[0] if tiled else None
    packet_slots, qkv_slots, out_slots, send_sem, recv_sem = take(5)
    pieces, gu_send, gu_recv, gu_own, later_send, later_recv = take(6)
    qkv_low, out_low, later_own = take(3)
    gather = Spread(sizes, [packet_slots, qkv_slots, out_slots], send_sem, recv_sem)
    here = tuple(gather.place[name] for name in EVERY)
    core, zd, tp = here
    group = []
    for step in range(1, cores * members):
        far = lax.rem(core + step // members, cores), lax.rem(tp + step % members, members)
        group.append((dict(zip(GROUP, far)), linear(far, (cores, members))))
    enter(gather.partners() + [device for device, _ in group])
    packet_slots[here] = packet[...]

    def place_rows(source, layer, slot, index):
        rows = source.shape[1]
        slot[index + (slice(0, rows),)] = source[layer].astype(bf16)
        if slot.shape[-2] > rows:
            slot[index + (slice(rows, slot.shape[-2]),)] = jnp.zeros(
                (slot.shape[-2] - rows, slot.shape[-1]), bf16
            )

    for source, slot in ((qkv, qkv_slots), (out, out_slots)):
        place_rows(source, 0, slot, here)
    gather.stage("zd")
    moves = []

    def along_z(source, target, sends, recvs):
        for step in range(1, planes):
            copy = pltpu.make_async_remote_copy(
                src_ref=source,
                dst_ref=target,
                send_sem=sends.at[step],
                recv_sem=recvs.at[step],
                device_id={"zd": lax.rem(zd + step, planes)},
                device_id_type=MESH,
            )
            copy.start()
            moves.append(copy)

    for k, (source, low, slot) in enumerate(
        ((qkv, qkv_low, qkv_later), (out, out_low, out_later))
    ):
        for layer in range(1, source.shape[0]):
            place_rows(source, layer, low, (layer - 1,))
            target = slot.at[layer - 1, zd]
            along_z(
                low.at[layer - 1], target, later_send.at[k, layer], later_recv.at[k, layer]
            )
            own = pltpu.make_async_copy(low.at[layer - 1], target, later_own.at[k, layer])
            own.start()
            moves.append(own)
    if tiled:
        down_low, down_send, down_recv, down_own = take(4)
        down_low[...] = down[0].astype(bf16)
        along_z(down_low, down_result.at[zd], down_send, down_recv)
        own = pltpu.make_async_copy(down_low, down_result.at[zd], down_own)
        own.start()
        moves.append(own)
    layers, rows, columns = gu.shape
    block = columns // (planes * members)
    half = planes // cores
    for c in range(cores):
        for j in range(members):
            for i in range(layers):
                cut = [
                    gu[i, :, pl.ds(((c * half + k) * members + j) * block, block)]
                    for k in range(half)
                ]
                value = jnp.concatenate(cut, axis=1) if half > 1 else cut[0]
                pieces[c * members + j, i * rows : (i + 1) * rows] = value.astype(bf16)
    if pieces.shape[1] > layers * rows:
        for piece in range(cores * members):
            pieces[piece, layers * rows :] = jnp.zeros(
                (pieces.shape[1] - layers * rows, pieces.shape[2]), bf16
            )
    me = linear((core, tp), (cores, members))
    for step, (device, index) in enumerate(group):
        copy = pltpu.make_async_remote_copy(
            src_ref=pieces.at[index],
            dst_ref=gu_result.at[me],
            send_sem=gu_send.at[step],
            recv_sem=gu_recv.at[step],
            device_id=device,
            device_id_type=MESH,
        )
        copy.start()
        moves.append(copy)
    own = pltpu.make_async_copy(pieces.at[me], gu_result.at[me], gu_own)
    own.start()
    moves.append(own)
    gather.stage("tp")
    gather.stage("head")
    gather.finish()
    side_by_side(sizes, (qkv_slots, out_slots), (mixed, project))
    packets[...] = packet_slots[...]
    for copy in moves:
        copy.wait()


def side_by_side(sizes, slots, results):
    cores, planes, members = sizes
    for slot, result in zip(slots, results):
        columns = slot.shape[4]
        rows = result.shape[0] // (planes * members)
        for h, z, t in itertools.product(range(cores), range(planes), range(members)):
            row = (z * members + t) * rows
            result[row : row + rows, h * columns : (h + 1) * columns] = slot[h, z, t, :rows]


def later_kernel(sizes, layer, qkv, out, mixed, project, qkv_slots, out_slots, send_sem, recv_sem):
    gather = Spread(sizes, [qkv_slots, out_slots], send_sem, recv_sem, whole_z=True)
    core, _, tp = (gather.place[name] for name in EVERY)
    enter(gather.partners())
    for source, slot in ((qkv, qkv_slots), (out, out_slots)):
        for z in range(sizes[1]):
            slot[core, z, tp] = source[layer - 1, z]
    gather.stage("tp")
    gather.stage("head")
    gather.finish()
    side_by_side(sizes, (qkv_slots, out_slots), (mixed, project))


def whole_shapes(sizes, tall, matrices):
    slots = [pltpu.VMEM(sizes + (t, w.shape[2]), bf16) for t, w in zip(tall, matrices)]
    outs = [
        jax.ShapeDtypeStruct((w.shape[1] * sizes[1] * sizes[2], w.shape[2] * sizes[0]), bf16)
        for w in matrices
    ]
    return slots, outs


def start(w_gu, w_qkv, w_out, w_down, packet, ident):
    sizes = tuple(lax.axis_size(axis) for axis in EVERY)
    cores, planes, members = sizes
    vmem, dma = pltpu.VMEM, pltpu.SemaphoreType.DMA
    here, there = pl.BlockSpec(memory_space=pltpu.VMEM), pl.BlockSpec(memory_space=pl.ANY)
    shape = jax.ShapeDtypeStruct
    tall = [-(-w.shape[1] // 16) * 16 for w in (w_qkv, w_out)]
    slots, outs = whole_shapes(sizes, tall, (w_qkv, w_out))
    layers, rows, columns = w_gu.shape
    piece = (
        cores * members,
        -(-layers * rows // 16) * 16,
        columns // (cores * members),
    )
    later = [
        shape((layers - 1, planes, t, w.shape[2]), bf16) for t, w in zip(tall, (w_qkv, w_out))
    ]
    operands = [w_gu, w_qkv, w_out, packet]
    outs = [shape(piece, bf16)] + outs + [shape(sizes + packet.shape, f32)] + later
    out_specs = [there] + [here] * 3 + [there] * 2
    moves = math.prod(sizes) - 1
    scratch = [vmem(sizes + packet.shape, f32)] + slots + [dma((3, moves))] * 2
    scratch += [vmem(piece, bf16), dma((cores * members - 1,)), dma((cores * members - 1,)), dma]
    scratch += [dma((2, layers, planes))] * 2
    scratch += [
        vmem((layers - 1, t, w.shape[2]), bf16) for t, w in zip(tall, (w_qkv, w_out))
    ] + [dma((2, layers))]
    tiled = w_down.shape[1] % 16 == 0
    if tiled:
        _, rows, columns = w_down.shape
        operands += [w_down]
        outs += [shape((planes, rows, columns), bf16)]
        out_specs += [there]
        scratch += [vmem((rows, columns), bf16), dma((planes,)), dma((planes,)), dma]
    return pl.pallas_call(
        partial(start_kernel, sizes, tiled),
        out_shape=outs,
        in_specs=[here] * len(operands),
        out_specs=out_specs,
        scratch_shapes=scratch,
        compiler_params=pltpu.CompilerParams(
            collective_id=ident, has_side_effects=True, vmem_limit_bytes=56 * 2**20
        ),
    )(*operands)


def later_weights(gathered, w_qkv, w_out, layer, ident):
    sizes = tuple(lax.axis_size(axis) for axis in EVERY)
    slots, outs = whole_shapes(sizes, [g.shape[2] for g in gathered], (w_qkv, w_out))
    here = pl.BlockSpec(memory_space=pltpu.VMEM)
    moves = math.prod(sizes) - sizes[1]
    return pl.pallas_call(
        partial(later_kernel, sizes, layer),
        out_shape=outs,
        in_specs=[here] * 2,
        out_specs=[here] * 2,
        scratch_shapes=slots + [pltpu.SemaphoreType.DMA((2, moves))] * 2,
        compiler_params=pltpu.CompilerParams(
            collective_id=ident, has_side_effects=True, vmem_limit_bytes=48 * 2**20
        ),
    )(*gathered)


def by_rows(rows, work, step=16):
    @pl.loop(0, rows // step)
    def _(index):
        work(pl.ds(pl.multiple_of(index * step, step), step))


def collect_kernel(sizes, layers, tiled, *refs):
    cores, planes, members = sizes
    rest = list(refs)
    take = lambda number: [rest.pop(0) for _ in range(number)]
    acts, packet = take(4 * layers), take(1)[0]
    if tiled:
        (down,) = take(1)
    results = take(3)
    if tiled:
        (down_result,) = take(1)
    far, halves = take(4 * layers), take(2 * layers)
    packet_land = rest.pop(0)
    pieces, plane_lands, totals, z_sums, z_lands = (take(3) for _ in range(5))
    act_send, act_recv, packet_send, packet_recv = take(4)
    tp_send, tp_recv, z_send, z_recv = take(4)
    core, zd, tp = (lax.axis_index(axis) for axis in EVERY)
    sibling = {"head": 1 - core}
    enter(
        [sibling]
        + [{"tp": lax.rem(tp + step, members)} for step in range(1, members)]
        + [{"zd": lax.rem(zd + step, planes)} for step in range(1, planes)]
    )
    sends = []

    def send(src, dst, send_sem, recv_sem, device):
        copy = pltpu.make_async_remote_copy(
            src_ref=src,
            dst_ref=dst,
            send_sem=send_sem,
            recv_sem=recv_sem,
            device_id=device,
            device_id_type=MESH,
        )
        copy.start()
        sends.append(copy)
        return copy

    if tiled:
        down_land, down_send, down_recv, down_own = take(4)
        down_moves = []
        for step in range(1, planes):
            there = lax.rem(zd + step, planes)
            down_moves.append(
                send(
                    down.at[there],
                    down_land.at[step],
                    down_send.at[step],
                    down_recv.at[step],
                    {"zd": there},
                )
            )
        down_stay = pltpu.make_async_copy(down.at[zd], down_land.at[0], down_own)
        down_stay.start()
    for k in range(2 * layers):
        grad, half = acts[2 * k + 1], halves[k]
        width = half.shape[2]
        for h in range(cores):
            half[h] = grad[:, h * width : (h + 1) * width]
    moves = []
    for k in range(2 * layers):
        moves.append(
            send(acts[2 * k], far[2 * k], act_send.at[2 * k], act_recv.at[2 * k], sibling)
        )
        moves.append(
            send(
                halves[k].at[1 - core],
                far[2 * k + 1],
                act_send.at[2 * k + 1],
                act_recv.at[2 * k + 1],
                sibling,
            )
        )
    gains = send(packet.at[1 - core], packet_land, packet_send, packet_recv, sibling)
    plane_moves, z_moves = {}, {}
    for kind in range(3):
        piece = pieces[kind]
        if kind < 2:
            for layer in range(layers):
                k = 2 * layer + kind
                near = lax.dot_general(
                    acts[2 * k][...], halves[k][core], ALONG, preferred_element_type=f32
                )
                moves[2 * k].wait_recv()
                moves[2 * k + 1].wait_recv()
                value = near + lax.dot_general(
                    far[2 * k][...], far[2 * k + 1][...], ALONG, preferred_element_type=f32
                )
                value = value.astype(bf16)
                rows = value.shape[0] // (planes * members)
                slab = piece.shape[1] // planes
                for z, t in itertools.product(range(planes), range(members)):
                    at = (z * members + t) * rows
                    to = z * slab + layer * rows
                    piece[t, to : to + rows] = value[at : at + rows]
            if slab > layers * rows:
                for z, t in itertools.product(range(planes), range(members)):
                    piece[t, z * slab + layers * rows : (z + 1) * slab] = jnp.zeros(
                        (slab - layers * rows, piece.shape[2]), bf16
                    )
        else:
            gains.wait_recv()
            piece[...] = packet[core] + packet_land[...]
        for step in range(1, members):
            there = lax.rem(tp + step, members)
            plane_moves[kind, step] = send(
                piece.at[there],
                plane_lands[kind].at[step],
                tp_send.at[kind, step],
                tp_recv.at[kind, step],
                {"tp": there},
            )
    for kind in range(3):
        for step in range(1, members):
            plane_moves[kind, step].wait_recv()
        piece, total, land, result = pieces[kind], totals[kind], plane_lands[kind], results[kind]
        stride = 8 if land.dtype == f32 else 16

        def gather_plane(rows):
            value = piece[tp, rows].astype(f32)
            for step in range(1, members):
                value = value + land[step, rows].astype(f32)
            total[rows] = value

        by_rows(total.shape[0], gather_plane, stride)
        height = result.shape[0]
        z_sum = z_sums[kind]
        for step in range(1, planes):
            there = lax.rem(zd + step, planes)

            def round_off(rows):
                at = pl.multiple_of(there * height + rows.start, stride)
                z_sum[step, rows] = total[pl.ds(at, rows.size)].astype(z_sum.dtype)

            by_rows(height, round_off, stride)
            z_moves[kind, step] = send(
                z_sum.at[step],
                z_lands[kind].at[step],
                z_send.at[kind, step],
                z_recv.at[kind, step],
                {"zd": there},
            )
    for kind in range(3):
        for step in range(1, planes):
            z_moves[kind, step].wait_recv()
        total, land, result = totals[kind], z_lands[kind], results[kind]
        height = result.shape[0]
        stride = 8 if land.dtype == f32 else 16

        def gather_z(rows):
            at = pl.multiple_of(zd * height + rows.start, stride)
            value = total[pl.ds(at, rows.size)]
            for step in range(1, planes):
                value = value + land[step, rows].astype(f32)
            result[rows] = value

        by_rows(height, gather_z, stride)
    if tiled:
        down_stay.wait()
        for copy in down_moves:
            copy.wait_recv()

        def gather_down(rows):
            value = down_land[0, rows].astype(f32)
            for step in range(1, planes):
                value = value + down_land[step, rows].astype(f32)
            down_result[rows] = value

        by_rows(down_result.shape[0], gather_down)
    for copy in sends:
        copy.wait_send()


def collect(acts, packet, down, ident):
    sizes = tuple(lax.axis_size(axis) for axis in EVERY)
    cores, planes, members = sizes
    layers = len(acts) // 4
    vmem, dma = pltpu.VMEM, pltpu.SemaphoreType.DMA
    tokens = acts[0].shape[0]
    halves = [acts[2 * k + 1].shape[1] // cores for k in range(2 * layers)]
    slabs = []
    for kind in range(2):
        rows = layers * acts[2 * kind].shape[1] // (planes * members)
        slabs.append((-(-rows // 16) * 16, halves[kind], bf16))
    slabs.append((packet.shape[2] // planes, packet.shape[3], f32))
    far = []
    for k in range(2 * layers):
        far += [vmem(acts[2 * k].shape, bf16), vmem((tokens, halves[k]), bf16)]
    scratch = far + [vmem((cores, tokens, width), bf16) for width in halves]
    scratch += [vmem(packet.shape[1:], f32)]
    scratch += [vmem((members, planes * r, c), kind) for r, c, kind in slabs] * 2
    scratch += [vmem((planes * r, c), f32) for r, c, _ in slabs]
    scratch += [vmem((planes, r, c), kind) for r, c, kind in slabs] * 2
    scratch += [dma((4 * layers,))] * 2 + [dma] * 2
    scratch += [dma((3, members))] * 2 + [dma((3, planes))] * 2
    here = pl.BlockSpec(memory_space=pltpu.VMEM)
    operands = [*acts, packet]
    outs = [jax.ShapeDtypeStruct((r, c), f32) for r, c, _ in slabs]
    in_specs = [here] * len(operands)
    if down is not None:
        operands, in_specs = operands + [down], in_specs + [pl.BlockSpec(memory_space=pl.ANY)]
        outs += [jax.ShapeDtypeStruct(down.shape[1:], f32)]
        scratch += [vmem(down.shape, bf16), dma((planes,)), dma((planes,)), dma]
    return pl.pallas_call(
        partial(collect_kernel, sizes, layers, down is not None),
        out_shape=outs,
        in_specs=in_specs,
        out_specs=[here] * len(outs),
        scratch_shapes=scratch,
        cost_estimate=LIGHT,
        compiler_params=pltpu.CompilerParams(
            collective_id=ident, has_side_effects=True, vmem_limit_bytes=56 * 2**20
        ),
    )(*operands)


def neighbours(planes, reach, sign):
    total = planes * PLANE
    place = linear([lax.axis_index("zd"), lax.axis_index("tp")], (planes, PLANE))

    def at(distance):
        there = lax.rem(place + distance + total, total)
        return {"zd": lax.div(there, PLANE), "tp": lax.rem(there, PLANE)}

    steps = range(1, reach + 1)
    return [at(sign * step) for step in steps], [at(-sign * step) for step in steps]


def inverse_rms(values):
    return lax.rsqrt(jnp.mean(values * values, axis=-1, keepdims=True) + norm_eps)


def rms_back(gradient, values, gain):
    inverse = inverse_rms(values)
    scaled = gradient * gain
    shared = jnp.mean(scaled * values, axis=-1, keepdims=True) * (inverse * inverse)
    return inverse * (scaled - values * shared), jnp.sum(
        gradient * values * inverse, axis=0, keepdims=True
    )


def turn(values, cosine, sine):
    half = values.shape[-1] // 2
    lower, upper = values[:, :half], values[:, half:]
    return jnp.concatenate(
        [lower * cosine - upper * sine, upper * cosine + lower * sine], axis=-1
    )


def soft_rows(query, keys, bias):
    scores = lax.dot_general(query, keys, ACROSS, preferred_element_type=f32)
    scores = scores * (1.0 / math.sqrt(HD)) + bias
    raised = jnp.exp(scores - jnp.max(scores, axis=-1, keepdims=True))
    return raised / jnp.sum(raised, axis=-1, keepdims=True)


def attn_forward_kernel(planes, reach, chained, *refs):
    rest = list(refs)
    take = lambda number: [rest.pop(0) for _ in range(number)]
    if chained:
        base, down, before = take(3)
    else:
        (base,) = take(1)
    w_mixed, w_project, gains, cosine, sine, bias = take(6)
    hidden, normed, mixed, queries, keyvals_out = take(5)
    attended, projected, hidden_half, normed_ffn = take(4)
    keyvals, send_sem, recv_sem, save_sem = take(4)
    seqs, stretch, key_len = bias.shape
    devices, sources = neighbours(planes, reach, 1)
    enter(devices + sources)
    value = base[...].astype(f32)
    if chained:
        late = down[...]
        value = value + late * inverse_rms(late) * before[1:2, D : 2 * D]
    hidden[...] = value
    low = (value * inverse_rms(value) * gains[0:1, :D]).astype(bf16)
    normed[...] = low
    mixed[...] = matmul(low, w_mixed[...])
    key = mixed[:, HEADS * HD : HEADS * HD + HD]
    key = turn(key * inverse_rms(key) * gains[1:2, 2 * D :], cosine[...], sine[...]).astype(bf16)
    late_values = mixed[:, HEADS * HD + HD :].astype(bf16)
    copies = []
    for i in range(seqs):
        rows = slice(i * stretch, (i + 1) * stretch)
        keyvals[i, reach * stretch :, :HD] = key[rows]
        keyvals[i, reach * stretch :, HD:] = late_values[rows]
        for step, device in enumerate(devices):
            copy = pltpu.make_async_remote_copy(
                src_ref=keyvals.at[i, pl.ds(reach * stretch, stretch)],
                dst_ref=keyvals.at[i, pl.ds((reach - 1 - step) * stretch, stretch)],
                send_sem=send_sem.at[i, step],
                recv_sem=recv_sem.at[i, step],
                device_id=device,
                device_id_type=MESH,
            )
            copy.start()
            copies.append(copy)
    for h in range(HEADS):
        columns = slice(h * HD, (h + 1) * HD)
        query = mixed[:, columns]
        query = turn(query * inverse_rms(query) * gains[0:1, 2 * D :], cosine[...], sine[...])
        queries[:, columns] = query.astype(bf16)
    for copy in copies:
        copy.wait_recv()
    save = pltpu.make_async_copy(keyvals, keyvals_out, save_sem)
    save.start()
    for i in range(seqs):
        rows = slice(i * stretch, (i + 1) * stretch)
        for h in range(HEADS):
            columns = slice(h * HD, (h + 1) * HD)
            soft = soft_rows(queries[rows, columns], keyvals[i, :, :HD], bias[i])
            attended[rows, columns] = matmul(soft.astype(bf16), keyvals[i, :, HD:]).astype(bf16)
    out = matmul(attended[...], w_project[...])
    projected[...] = out
    half = hidden[...] + out * inverse_rms(out) * gains[0:1, D : 2 * D]
    hidden_half[...] = half
    normed_ffn[...] = (half * inverse_rms(half) * gains[1:2, :D]).astype(bf16)
    for copy in copies:
        copy.wait_send()
    save.wait()


def attn_forward(base, weights, gains, tables, bias, planes, reach, ident, earlier=None):
    tokens = base.shape[0]
    seqs, _, key_len = bias.shape
    shape = jax.ShapeDtypeStruct
    operands = [base] + list(earlier or []) + list(weights) + [gains, *tables, bias]
    here, there = pl.BlockSpec(memory_space=pltpu.VMEM), pl.BlockSpec(memory_space=pl.ANY)
    dma = pltpu.SemaphoreType.DMA
    return pl.pallas_call(
        partial(attn_forward_kernel, planes, reach, earlier is not None),
        out_shape=[
            shape((tokens, D), f32),
            shape((tokens, D), bf16),
            shape((tokens, weights[0].shape[1]), f32),
            shape((tokens, HEADS * HD), bf16),
            shape((seqs, key_len, 2 * HD), bf16),
            shape((tokens, HEADS * HD), bf16),
            shape((tokens, D), f32),
            shape((tokens, D), f32),
            shape((tokens, D), bf16),
        ],
        in_specs=[here] * len(operands),
        out_specs=[here] * 4 + [there] + [here] * 4,
        scratch_shapes=[
            pltpu.VMEM((seqs, key_len, 2 * HD), bf16),
            dma((seqs, reach)),
            dma((seqs, reach)),
            dma,
        ],
        compiler_params=pltpu.CompilerParams(
            collective_id=ident, has_side_effects=True, vmem_limit_bytes=56 * 2**20
        ),
    )(*operands)


def attn_backward_kernel(planes, reach, chained, *refs):
    rest = list(refs)
    take = lambda number: [rest.pop(0) for _ in range(number)]
    d_ffn, above, hidden, mixed, queries, keyvals, projected, hidden_half = take(8)
    w_mixed, w_project, gains, cosine, sine, bias = take(6)
    if chained:
        down, before = take(2)
    grad, d_mixed, d_projected, gain_grads = take(4)
    if chained:
        d_down, d_post = take(2)
    d_keyvals, outgoing, incoming, d_attended, send_sem, recv_sem = take(6)
    seqs, stretch, key_len = bias.shape
    devices, sources = neighbours(planes, reach, -1)
    enter(devices + sources)
    scale = 1.0 / math.sqrt(HD)
    part, gain_row = rms_back(d_ffn[...], hidden_half[...], gains[1:2, :D])
    gain_grads[1:2, :D] = gain_row
    gain_grads[1:2, D : 2 * D] = jnp.zeros((1, D), f32)
    grad[...] = part + above[...]
    part, gain_row = rms_back(grad[...], projected[...], gains[0:1, D : 2 * D])
    gain_grads[0:1, D : 2 * D] = gain_row
    low = part.astype(bf16)
    d_projected[...] = low
    d_attended[...] = lax.dot_general(
        low, w_project[...], ACROSS, preferred_element_type=f32
    ).astype(bf16)
    query_gain = jnp.zeros((1, HD), f32)
    for i in range(seqs):
        rows = slice(i * stretch, (i + 1) * stretch)
        d_keys = d_values = None
        for h in range(HEADS):
            columns = slice(h * HD, (h + 1) * HD)
            query, d_out = queries[rows, columns], d_attended[rows, columns]
            keys, values = keyvals[i, :, :HD], keyvals[i, :, HD:]
            soft = soft_rows(query, keys, bias[i])
            d_soft = lax.dot_general(d_out, values, ACROSS, preferred_element_type=f32)
            total = jnp.sum(soft * d_soft, axis=-1, keepdims=True)
            d_scores = (soft * (d_soft - total)).astype(bf16)
            key_part = lax.dot_general(d_scores, query, ALONG, preferred_element_type=f32)
            value_part = lax.dot_general(
                soft.astype(bf16), d_out, ALONG, preferred_element_type=f32
            )
            d_keys = key_part if d_keys is None else d_keys + key_part
            d_values = value_part if d_values is None else d_values + value_part
            d_query = matmul(d_scores, keys) * scale
            d_query = turn(d_query, cosine[rows], -sine[rows])
            part, gain_row = rms_back(d_query, mixed[rows, columns], gains[0:1, 2 * D :])
            query_gain = query_gain + gain_row
            d_mixed[rows, columns] = part.astype(bf16)
        d_keyvals[i, :, :HD] = d_keys * scale
        d_keyvals[i, :, HD:] = d_values
    gain_grads[0:1, 2 * D :] = query_gain
    outgoing[...] = d_keyvals[:, : reach * stretch].astype(bf16)
    copies = []
    for i in range(seqs):
        for step, device in enumerate(devices):
            copy = pltpu.make_async_remote_copy(
                src_ref=outgoing.at[i, pl.ds((reach - 1 - step) * stretch, stretch)],
                dst_ref=incoming.at[i, step],
                send_sem=send_sem.at[i, step],
                recv_sem=recv_sem.at[i, step],
                device_id=device,
                device_id_type=MESH,
            )
            copy.start()
            copies.append(copy)
    for copy in copies:
        copy.wait_recv()
    key_gain = jnp.zeros((1, HD), f32)
    for i in range(seqs):
        rows = slice(i * stretch, (i + 1) * stretch)
        own = d_keyvals[i, reach * stretch :]
        for step in range(reach):
            own = own + incoming[i, step].astype(f32)
        d_key = turn(own[:, :HD], cosine[rows], -sine[rows])
        part, gain_row = rms_back(
            d_key, mixed[rows, HEADS * HD : HEADS * HD + HD], gains[1:2, 2 * D :]
        )
        key_gain = key_gain + gain_row
        d_mixed[rows, HEADS * HD : HEADS * HD + HD] = part.astype(bf16)
        d_mixed[rows, HEADS * HD + HD :] = own[:, HD:].astype(bf16)
    gain_grads[1:2, 2 * D :] = key_gain
    d_normed = lax.dot_general(d_mixed[...], w_mixed[...], ACROSS, preferred_element_type=f32)
    part, gain_row = rms_back(d_normed, hidden[...], gains[0:1, :D])
    gain_grads[0:1, :D] = gain_row
    grad[...] = grad[...] + part
    if chained:
        part, gain_row = rms_back(grad[...], down[...], before[1:2, D : 2 * D])
        d_down[...] = part.astype(bf16)
        d_post[...] = gain_row
    for copy in copies:
        copy.wait_send()


def attn_backward(
    d_ffn, above, kept, weights, gains, tables, bias, planes, reach, ident, earlier=None
):
    tokens = above.shape[0]
    seqs, stretch, key_len = bias.shape
    shape = jax.ShapeDtypeStruct
    operands = [d_ffn, above, *kept, *weights, gains, *tables, bias] + list(earlier or [])
    outs = [
        shape((tokens, D), f32),
        shape((tokens, weights[0].shape[1]), bf16),
        shape((tokens, D), bf16),
        shape(gains.shape, f32),
    ]
    if earlier is not None:
        outs += [shape((tokens, D), bf16), shape((1, D), f32)]
    here = pl.BlockSpec(memory_space=pltpu.VMEM)
    vmem, dma = pltpu.VMEM, pltpu.SemaphoreType.DMA
    return pl.pallas_call(
        partial(attn_backward_kernel, planes, reach, earlier is not None),
        out_shape=outs,
        in_specs=[here] * len(operands),
        out_specs=[here] * len(outs),
        scratch_shapes=[
            vmem((seqs, key_len, 2 * HD), f32),
            vmem((seqs, reach * stretch, 2 * HD), bf16),
            vmem((seqs, reach, stretch, 2 * HD), bf16),
            vmem((tokens, HEADS * HD), bf16),
            dma((seqs, reach)),
            dma((seqs, reach)),
        ],
        compiler_params=pltpu.CompilerParams(
            collective_id=ident, has_side_effects=True, vmem_limit_bytes=56 * 2**20
        ),
    )(*operands)


GELU_SLOPE = math.sqrt(2.0 / math.pi)
GELU_CUBE = 0.044715
ACROSS = (((1,), (1,)), ((), ()))
ALONG = (((0,), (0,)), ((), ()))


class Plane:
    def __init__(self, own, bufs, sems):
        self.own = own
        self.rows, self.partial, self.other, self.lands, self.sums, self.arrived = bufs
        self.x_send, self.x_recv, self.f_send, self.f_recv = sems[:4]
        self.c_send, self.c_recv, self.p_send, self.p_recv, self.first = sems[4:]
        self.tp = lax.axis_index("tp")
        self.sibling = {"head": 1 - lax.axis_index("head")}

    def member(self, m):
        tp = self.tp
        upper = lax.rem(lax.div(tp, 2) + lax.div(m, 2), 2)
        lower = lax.rem(lax.rem(tp, 2) + lax.rem(m, 2), 2)
        return {"tp": upper * 2 + lower}

    def remote(self, src, dst, send, recv, device):
        return pltpu.make_async_remote_copy(
            src_ref=src,
            dst_ref=dst,
            send_sem=send,
            recv_sem=recv,
            device_id=device,
            device_id_type=MESH,
        )

    def push(self, m):
        return self.remote(
            self.own, self.rows.at[0, m], self.x_send.at[m], self.x_recv.at[m], self.member(m)
        )

    def keep(self):
        return pltpu.make_async_copy(self.own, self.rows.at[0, 0], self.first)

    def forward(self, m):
        return self.remote(
            self.rows.at[0, m],
            self.rows.at[1, m],
            self.f_send.at[m],
            self.f_recv.at[m],
            self.sibling,
        )

    def cross(self, m):
        return self.remote(
            self.other.at[m], self.lands.at[m], self.c_send.at[m], self.c_recv.at[m], self.sibling
        )

    def home(self, m):
        return self.remote(
            self.sums.at[m],
            self.arrived.at[m],
            self.p_send.at[m],
            self.p_recv.at[m],
            self.member(m),
        )

    def begin(self):
        self.keep().start()
        enter([self.sibling] + [self.member(jnp.int32(m)) for m in range(1, PLANE)])
        for m in range(1, PLANE):
            self.push(jnp.int32(m)).start()

    def work(self, compute):
        def settle(m):
            self.cross(m).wait_recv()

            def add(rows):
                value = self.partial[m, rows] + self.lands[m, rows].astype(f32)
                self.sums[m, rows] = value.astype(bf16)

            by_rows(self.partial.shape[1], add)
            self.home(m).start()

        def step(m, carry):
            @pl.when(m == 0)
            def _():
                self.keep().wait()

            @pl.when(m > 0)
            def _():
                self.push(m).wait_recv()

            self.forward(m).start()
            self.partial[m] = compute(0, m)
            self.forward(m).wait_recv()
            self.other[m] = compute(1, m).astype(bf16)
            self.cross(m).start()

            @pl.when(m >= 2)
            def _():
                settle(m - 1)

            return carry

        lax.fori_loop(0, PLANE, step, 0)
        settle(jnp.int32(PLANE - 1))

    def finish(self, result):
        self.cross(jnp.int32(0)).wait_recv()
        for m in range(1, PLANE):
            self.home(jnp.int32(m)).wait_recv()

        def add(rows):
            value = self.partial[0, rows] + self.lands[0, rows].astype(f32)
            for m in range(1, PLANE):
                value = value + self.arrived[m, rows].astype(f32)
            result[rows] = value

        by_rows(result.shape[0], add)
        for m in range(PLANE):
            m = jnp.int32(m)
            self.forward(m).wait_send()
            self.cross(m).wait_send()
        for m in range(1, PLANE):
            m = jnp.int32(m)
            self.push(m).wait_send()
            self.home(m).wait_send()


def gate_up_copies(gu_ref, gate_up, sem):
    blocks = gu_ref.shape[0]
    rows = gate_up.shape[1] // blocks
    return [
        pltpu.make_async_copy(
            gu_ref.at[block, part],
            gate_up.at[part, pl.ds(block * rows, rows)],
            sem.at[2 * block + part],
        )
        for block in range(blocks)
        for part in range(2)
    ]


def ffn_forward_kernel(own, gu_ref, halves_ref, group, saved_down, result, *scratch):
    rows, gate_up, down = scratch[:3]
    plane = Plane(own, (rows,) + scratch[3:8], scratch[8:17])
    weight_sem, group_sem, halves, half_send, half_recv, half_own, save_sem = scratch[17:]
    core = lax.axis_index("head")
    share, width = halves.shape[1:]
    copies = gate_up_copies(gu_ref, gate_up, weight_sem)
    copies.append(
        pltpu.make_async_copy(
            halves_ref.at[0, pl.ds(pl.multiple_of(core * share, 16), share)],
            halves.at[core],
            half_own,
        )
    )
    for copy in copies:
        copy.start()
    plane.begin()
    half = plane.remote(
        halves_ref.at[0, pl.ds(pl.multiple_of((1 - core) * share, 16), share)],
        halves.at[core],
        half_send,
        half_recv,
        plane.sibling,
    )
    half.start()
    for copy in copies:
        copy.wait()
    pltpu.make_async_remote_copy(
        src_ref=halves_ref.at[0, pl.ds(pl.multiple_of((1 - core) * share, 16), share)],
        dst_ref=halves.at[1 - core],
        send_sem=half_send,
        recv_sem=half_recv,
        device_id=plane.sibling,
        device_id_type=MESH,
    ).wait_recv()

    def join(at):
        down[at] = jnp.concatenate([halves[h, at] for h in range(2)], axis=1)

    by_rows(share, join, 32)
    keep_down = pltpu.make_async_copy(down, saved_down, save_sem)
    keep_down.start()

    def compute(side, m):
        tokens = rows[side, m]
        gate = matmul(tokens, gate_up[0])
        up = matmul(tokens, gate_up[1])
        bend = jnp.tanh(GELU_SLOPE * (gate + GELU_CUBE * (gate * gate * gate)))
        inner = (0.5 * gate * (1.0 + bend) * up).astype(bf16)
        return matmul(inner, down[...])

    plane.work(compute)
    save = pltpu.make_async_copy(rows, group, group_sem)
    save.start()
    plane.finish(result)
    save.wait()
    keep_down.wait()
    half.wait_send()


def ffn_backward_kernel(
    own, group, gu_ref, down_ref, result, grad_gate, grad_up, grad_down, *scratch
):
    rows, gate_up, down = scratch[:3]
    plane = Plane(own, (rows,) + scratch[3:8], scratch[8:17])
    weight_sem, group_sem, saved, d_gate, d_up, inner = scratch[17:23]
    down_sem, turned, down_halves, half_send, half_recv, half_own = scratch[23:]
    core = lax.axis_index("head")
    copies = gate_up_copies(gu_ref, gate_up, weight_sem)
    copies.append(pltpu.make_async_copy(down_ref, down, down_sem))
    for copy in copies:
        copy.start()
    load = pltpu.make_async_copy(group, saved, group_sem)
    load.start()
    plane.begin()
    for copy in copies:
        copy.wait()
    load.wait()

    def recompute(index, carry):
        side, m = lax.div(index, PLANE), lax.rem(index, PLANE)
        tokens = saved[side, m]
        gate = matmul(tokens, gate_up[0])
        up = matmul(tokens, gate_up[1])
        square = gate * gate
        bend = jnp.tanh(GELU_SLOPE * (gate + GELU_CUBE * (square * gate)))
        half = 0.5 * (1.0 + bend)
        value = gate * half
        slope = half + (0.5 * GELU_SLOPE) * gate * (1.0 - bend * bend) * (
            1.0 + (3.0 * GELU_CUBE) * square
        )
        inner[side, m] = (value * up).astype(bf16)
        d_gate[side, m] = (slope * up).astype(bf16)
        d_up[side, m] = value.astype(bf16)
        return carry

    lax.fori_loop(0, 2 * PLANE, recompute, 0)

    def compute(side, m):
        d_inner = lax.dot_general(rows[side, m], down[...], ACROSS, preferred_element_type=f32)
        gate = (d_inner * d_gate[side, m].astype(f32)).astype(bf16)
        up = (d_inner * d_up[side, m].astype(f32)).astype(bf16)
        d_gate[side, m] = gate
        d_up[side, m] = up
        return lax.dot_general(
            gate, gate_up[0], ACROSS, preferred_element_type=f32
        ) + lax.dot_general(up, gate_up[1], ACROSS, preferred_element_type=f32)

    plane.work(compute)
    width = rows.shape[-1]
    step = width // 3

    def tall(ref, columns=slice(None)):
        value = ref[:, :, :, columns]
        return value.reshape(-1, value.shape[-1])

    @pl.loop(0, 3)
    def _(index):
        at = pl.ds(pl.multiple_of(index * step, step), step)
        tokens = tall(saved, at)
        for target, other in ((grad_gate, d_gate), (grad_up, d_up)):
            target[at] = lax.dot_general(
                tokens, tall(other), ALONG, preferred_element_type=f32
            ).astype(bf16)
        turned[at] = lax.dot_general(
            tall(rows, at), tall(inner), ALONG, preferred_element_type=f32
        ).astype(bf16)

    half_width = down_halves.shape[2]
    for h in range(2):
        down_halves[h] = turned[h * half_width : (h + 1) * half_width].T
    half = plane.remote(
        down_halves.at[1 - core], grad_down.at[core], half_send, half_recv, plane.sibling
    )
    half.start()
    stay = pltpu.make_async_copy(down_halves.at[core], grad_down.at[core], half_own)
    stay.start()
    plane.finish(result)
    half.wait()
    stay.wait()


def ffn(own, weights, ident, group=None):
    gate_up, down = weights
    tokens, width = own.shape
    blocks, _, _, share = gate_up.shape
    vmem, dma = pltpu.VMEM, pltpu.SemaphoreType.DMA
    scratch = [
        vmem((2, PLANE, tokens, width), bf16),
        vmem((2, width, share), bf16),
        vmem((share, width), bf16),
        vmem((PLANE, tokens, width), f32),
    ]
    scratch += [vmem((PLANE, tokens, width), bf16)] * 4
    scratch += [dma((PLANE,))] * 8 + [dma, dma((2 * blocks,)), dma]
    here, there = pl.BlockSpec(memory_space=pltpu.VMEM), pl.BlockSpec(memory_space=pl.ANY)
    shape = jax.ShapeDtypeStruct
    summed = shape((tokens, width), f32)
    if group is None:
        kernel, operands = ffn_forward_kernel, (own, gate_up, down)
        in_specs, out_specs = [here, there, there], [there, there, here]
        out_shape = [
            shape((2, PLANE, tokens, width), bf16),
            shape((share, width), bf16),
            summed,
        ]
        scratch += [vmem((2, share, width // 2), bf16)] + [dma] * 4
    else:
        kernel, operands = ffn_backward_kernel, (own, group, gate_up, down)
        in_specs, out_specs = [here, there, there, there], [here] * 3 + [there]
        out_shape = [
            summed,
            shape((width, share), bf16),
            shape((width, share), bf16),
            shape((2, share, width // 2), bf16),
        ]
        scratch += [vmem((2, PLANE, tokens, width), bf16)]
        scratch += [vmem((2, PLANE, tokens, share), bf16)] * 3
        scratch += [dma, vmem((width, share), bf16), vmem((2, share, width // 2), bf16)]
        scratch += [dma] * 3
    return pl.pallas_call(
        kernel,
        out_shape=out_shape,
        in_specs=in_specs,
        out_specs=out_specs,
        scratch_shapes=scratch,
        cost_estimate=LIGHT,
        compiler_params=pltpu.CompilerParams(
            collective_id=ident, has_side_effects=True, vmem_limit_bytes=60 * 2**20
        ),
    )(*operands)


def exact(left, right, dims=(((1,), (0,)), ((), ()))):
    return lax.dot_general(
        left, right, dims, precision=finest_precision, preferred_element_type=f32
    )


def update_kernel(sizes, counts, *refs):
    cores, planes, members = sizes
    rest = list(refs)
    take = lambda number: [rest.pop(0) for _ in range(number)]
    plain = [take(number) for number in counts]
    sides = [take(2) for _ in range(cores)]
    moments_in, weights_in, weights_out, moments_out = (take(4) for _ in range(4))
    moment, weight, gram, land, factor = (take(4) for _ in range(5))
    pieces, arrived = take(2)
    load_sem, store_sem, gram_send, gram_recv, factor_send, factor_recv = take(6)
    gu_send, gu_recv, gu_own = take(3)
    core, _, tp = (lax.axis_index(axis) for axis in EVERY)
    sibling = {"head": 1 - core}
    order = (0, 1, 3, 2)
    loads = {}
    for k in range(4):
        for part, source, target in ((0, moments_in, moment), (1, weights_in, weight)):
            copy = pltpu.make_async_copy(source[k], target[k], load_sem.at[part, k])
            copy.start()
            loads[part, k] = copy
    group = []
    for step in range(1, cores * members):
        far = lax.rem(core + step // members, cores), lax.rem(tp + step % members, members)
        group.append((dict(zip(GROUP, far)), linear(far, (cores, members))))
    enter([device for device, _ in group])
    rows = moment[2].shape[1]
    for part in range(cores):
        for j in range(members):
            for layer in range(cores):
                pieces[part * members + j, layer * rows : (layer + 1) * rows] = sides[layer][part][
                    j * rows : (j + 1) * rows
                ]
    if pieces.shape[1] > cores * rows:
        for piece in range(cores * members):
            pieces[piece, cores * rows :] = jnp.zeros(
                (pieces.shape[1] - cores * rows, pieces.shape[2]), bf16
            )
    me = linear((core, tp), (cores, members))
    moves, stores = [], []

    def send(src, dst, send_sem, recv_sem, device):
        copy = pltpu.make_async_remote_copy(
            src_ref=src,
            dst_ref=dst,
            send_sem=send_sem,
            recv_sem=recv_sem,
            device_id=device,
            device_id_type=MESH,
        )
        copy.start()
        return copy

    for step, (device, index) in enumerate(group):
        moves.append(
            send(pieces.at[index], arrived.at[me], gu_send.at[step], gu_recv.at[step], device)
        )
    own = pltpu.make_async_copy(pieces.at[me], arrived.at[me], gu_own)
    own.start()

    def store(part, k):
        source, target = (moment, moments_out) if part == 0 else (weight, weights_out)
        copy = pltpu.make_async_copy(source[k], target[k], store_sem.at[part, k])
        copy.start()
        stores.append(copy)

    def gram_of(k):
        def one(layer, carry):
            gram[k][layer] = exact(moment[k][layer], moment[k][layer], ACROSS)
            return carry

        lax.fori_loop(0, cores, one, 0)
        return send(
            gram[k].at[1 - core], land[k], gram_send.at[k], gram_recv.at[k], sibling
        )

    def unit(size):
        down = lax.broadcasted_iota(jnp.int32, (size, size), 0)
        return (down == lax.broadcasted_iota(jnp.int32, (size, size), 1)).astype(f32)

    def orthogonal(members_of):
        for k in members_of:
            total = gram[k][core] + land[k][...]
            one = unit(total.shape[0])
            trace = jnp.sum(jnp.sum(total * one, axis=1, keepdims=True), axis=0, keepdims=True)
            scale = 1.0 / (jnp.sqrt(trace) + 1e-07)
            land[k][...] = total * (scale * scale)
            factor[k][core] = one * scale

        def polynomial(present):
            square = exact(present, present)
            return newton_one * unit(present.shape[0]) + newton_two * present + (
                newton_three * square
            )

        def step(_, carry):
            for k in members_of:
                present = land[k][...]
                poly = polynomial(present)
                factor[k][core] = exact(poly, factor[k][core])
                land[k][...] = exact(exact(poly, present), poly)
            return carry

        lax.fori_loop(0, NS_ITERS - 1, step, 0)
        for k in members_of:
            factor[k][core] = exact(polynomial(land[k][...]), factor[k][core])
        return [
            send(factor[k].at[core], factor[k].at[core], factor_send.at[k], factor_recv.at[k], sibling)
            for k in members_of
        ]

    def apply(k):
        columns = weight[k].shape[2] * cores
        rate = muon_rate * muon_scale * math.sqrt(columns)

        def one(layer, carry):
            weight[k][layer] = weight[k][layer] * (1.0 - muon_rate * muon_shrink) - rate * exact(
                factor[k][layer], moment[k][layer]
            )
            return carry

        lax.fori_loop(0, cores, one, 0)
        store(1, k)

    def arrive(copies):
        for copy in copies:
            copy.wait_recv()

    sent = []
    for index, k in enumerate(order[:3]):
        loads[0, k].wait()
        height = moment[k].shape[1]
        for layer in range(cores):
            if len(plain[index]) == 1:
                gradient = plain[index][0][layer * height : (layer + 1) * height]
            else:
                gradient = plain[index][layer][...].astype(f32)
            moment[k][layer] = muon_decay * moment[k][layer] + gradient
        store(0, k)
        sent.append(gram_of(k))
    arrive(sent)
    crossed = orthogonal(order[:3])
    sent += crossed
    own.wait()
    for copy in moves:
        copy.wait_recv()
    loads[0, 2].wait()
    half = planes // cores
    block = arrived.shape[2] // half
    for layer in range(cores):
        cut = [
            arrived[
                c * members + j,
                layer * rows : (layer + 1) * rows,
                k * block : (k + 1) * block,
            ].astype(f32)
            for c in range(cores)
            for k in range(half)
            for j in range(members)
        ]
        moment[2][layer] = muon_decay * moment[2][layer] + jnp.concatenate(cut, axis=1)
    store(0, 2)
    last = gram_of(2)
    sent.append(last)
    arrive(crossed)
    for k in range(4):
        loads[1, k].wait()
    for k in order[:3]:
        apply(k)
    arrive([last])
    crossed = orthogonal(order[3:])
    sent += crossed
    arrive(crossed)
    apply(2)
    for copy in moves + sent:
        copy.wait_send()
    for copy in stores:
        copy.wait()


def update(gradients, sides, moments, weights, ident):
    sizes = tuple(lax.axis_size(axis) for axis in EVERY)
    cores, planes, members = sizes
    vmem, dma = pltpu.VMEM, pltpu.SemaphoreType.DMA
    layers, rows, columns = moments[2].shape
    piece = (
        cores * members,
        -(-layers * rows // 16) * 16,
        columns // (cores * members),
    )
    shapes = [m.shape for m in moments]
    square = [(s[1], s[1]) for s in shapes]
    scratch = [vmem(s, f32) for s in shapes] * 2
    scratch += [vmem((layers,) + s, f32) for s in square]
    scratch += [vmem(s, f32) for s in square]
    scratch += [vmem((layers,) + s, f32) for s in square]
    scratch += [vmem(piece, bf16)] * 2
    scratch += [dma((2, 4))] * 2 + [dma((4,))] * 4
    scratch += [dma((cores * members - 1,))] * 2 + [dma]
    here, there = pl.BlockSpec(memory_space=pltpu.VMEM), pl.BlockSpec(memory_space=pl.ANY)
    operands = sum(gradients, []) + sum(sides, [])
    return pl.pallas_call(
        partial(update_kernel, sizes, [len(g) for g in gradients]),
        out_shape=[jax.ShapeDtypeStruct(s, f32) for s in shapes] * 2,
        in_specs=[here] * len(operands) + [there] * 8,
        out_specs=[there] * 8,
        scratch_shapes=scratch,
        compiler_params=pltpu.CompilerParams(
            collective_id=ident, has_side_effects=True, vmem_limit_bytes=56 * 2**20
        ),
    )(*operands, *moments, *weights)


def padded(array, multiple=16):
    extra = -array.shape[-2] % multiple
    if extra == 0:
        return array
    return jnp.pad(array, [(0, 0)] * (array.ndim - 2) + [(0, extra), (0, 0)])


def rms_norm(values, norm_gain):
    return (
        values * lax.rsqrt(jnp.mean(values * values, axis=-1, keepdims=True) + norm_eps) * norm_gain
    )


def rope_tables(positions, head_dim):
    half_dim = head_dim // 2
    frequency = jnp.exp(
        jnp.arange(half_dim, dtype=jnp.float32) * (-2.0 * math.log(rope_base) / head_dim)
    )
    angles = positions.astype(jnp.float32)[:, None] * frequency[None, :]
    return (jnp.cos(angles), jnp.sin(angles))


def matmul(left, right):
    return jnp.dot(left, right, preferred_element_type=f32)


def body(
    inputs,
    cotangent,
    teacher,
    segments,
    valid_mask,
    w_qkv,
    w_out,
    w_gu,
    w_down,
    norm_gains,
    mom_qkv,
    mom_out,
    mom_gu,
    mom_down,
    gain_first,
    gain_second,
):
    cores = lax.axis_size("head")
    planes = lax.axis_size("zd")
    seq_devices = planes * PLANE
    core = lax.axis_index("head")
    seq_place = lax.axis_index("zd") * PLANE + lax.axis_index("tp")
    half_seqs, stretch_len = inputs.shape[:2]
    tokens = half_seqs * stretch_len
    all_seqs = half_seqs * cores
    seq_length = stretch_len * seq_devices
    reach = -(-WINDOW // stretch_len)
    key_len = (reach + 1) * stretch_len
    qkv_rows, qkv_cols = w_qkv.shape[1:]
    out_rows, out_cols = w_out.shape[1:]
    gu_rows = w_gu.shape[1]
    ff_block = w_down.shape[1]
    share = FF // (cores * PLANE)
    half_planes = planes // cores
    gain_cols = norm_gains.shape[-1]
    gain_len = gain_cols * seq_devices
    lanes = -(-gain_cols // 128) * 128

    packet = jnp.zeros((8, lanes), f32)
    packet = packet.at[:LAYERS, :gain_cols].set(norm_gains[:, 0].astype(bf16).astype(f32))
    packet = packet.at[LAYERS, 0].set(jnp.sum(valid_mask.astype(f32)))
    gu_pieces, w_mixed, w_project, packets, *later = start(
        w_gu, w_qkv, w_out, w_down, packet, 0
    )
    attn_weights, later, gathered_down = [w_mixed, w_project], later[:2], later[2:]
    gu_pieces = gu_pieces[:, : LAYERS * gu_rows].reshape(cores * PLANE, LAYERS, gu_rows, share)
    packets = packets.reshape(cores, seq_devices, 8, lanes)
    valid_count = jnp.sum(packets[:, :, LAYERS, 0])
    gain_rows = [
        packets[:, :, layer, :gain_cols].reshape(cores, gain_len) for layer in range(LAYERS)
    ]

    def gate_up_rows(layer):
        pieces = gu_pieces[:, layer].reshape(2, PLANE * gu_rows, share)
        pieces = lax.all_gather(pieces, "zd", axis=0)
        if PLANE * gu_rows % 16:
            pieces = pieces.transpose(1, 0, 2, 3).reshape(1, 2, D, share)
        return pieces

    def down_rows(layer, gathered):
        if gathered:
            return gathered[0].reshape(1, planes * ff_block, out_cols)
        rows = w_down[layer : layer + 1].astype(bf16)
        return lax.all_gather(rows, "zd", axis=1, tiled=True)

    full = [(gate_up_rows(0), down_rows(0, gathered_down))] + [None] * (LAYERS - 1)

    own_places = seq_place * stretch_len + jnp.arange(stretch_len, dtype=jnp.int32)
    key_places = (seq_place - reach) * stretch_len + jnp.arange(key_len, dtype=jnp.int32)
    cosine_table, sine_table = rope_tables(own_places, HD)
    own_rows = lax.dynamic_slice_in_dim(segments, core * half_seqs, half_seqs, 0)
    own_segments = lax.dynamic_slice_in_dim(own_rows, seq_place * stretch_len, stretch_len, 1)
    padded_segments = jnp.pad(own_rows, ((0, 0), (reach * stretch_len, 0)), constant_values=-1)
    key_segments = lax.dynamic_slice_in_dim(padded_segments, seq_place * stretch_len, key_len, 1)
    spacing = own_places[:, None] - key_places[None, :]
    allowed = (spacing >= 0) & (spacing < WINDOW) & (key_places[None, :] >= 0)
    allowed = allowed[None] & (own_segments[:, :, None] == key_segments[:, None, :])

    tables = [jnp.tile(t, (half_seqs, 1)) for t in (cosine_table, sine_table)]
    bias = jnp.where(allowed, 0.0, -1e30).astype(f32)

    saved, previous = [], None
    base = inputs.reshape(tokens, D)
    for layer in range(LAYERS):
        weights = list(attn_weights)
        hidden, normed, mixed, queries, keyvals, attended, projected, half, normed_ffn = attn_forward(
            base, weights, gain_rows[layer], tables, bias, planes, reach, 3 + layer, previous
        )
        ffn_share = full[layer]
        if layer + 1 < LAYERS:
            gu_pieces, w_down, later, attended = lax.optimization_barrier(
                (gu_pieces, w_down, later, attended)
            )
            attn_weights = later_weights(later, w_qkv, w_out, layer + 1, 2 + 20 * layer)
            full[layer + 1] = (gate_up_rows(layer + 1), down_rows(layer + 1, []))
            normed_ffn, *attn_weights = lax.optimization_barrier((normed_ffn, *attn_weights))
        group_normed, whole_down, down_out = ffn(normed_ffn, ffn_share, 5 + layer)
        full[layer] = (weights, (ffn_share[0], whole_down))
        saved.append(
            (
                [hidden, mixed, queries, keyvals, projected, half],
                [normed, attended],
                group_normed,
                down_out,
            )
        )
        base, previous = half, (down_out, gain_rows[layer])

    output, post_ffn_back = jax.vjp(rms_norm, down_out, gain_rows[-1][1, D : 2 * D])
    output = base + output
    target_gap = output - teacher.reshape(tokens, D).astype(f32)
    valid_weight = valid_mask.astype(f32).reshape(tokens, 1)
    square_sum = jnp.sum(valid_weight * target_gap * target_gap)
    loss_weight = float(all_seqs * seq_length * D // 4)
    grad_hidden = (
        cotangent.reshape(tokens, D).astype(f32)
        + 2.0 * loss_weight / (valid_count * D) * valid_weight * target_gap
    )
    d_down, d_post_ffn = post_ffn_back(grad_hidden)
    d_down, d_post_ffn = d_down.astype(bf16), d_post_ffn[None]

    tiled = ff_block % 16 == 0
    attn_acts = [None] * LAYERS
    down_grads = [None] * LAYERS
    gain_grads = [None] * LAYERS
    gu_sums = [None] * LAYERS
    for layer in reversed(range(LAYERS)):
        kept, (normed, attended), group_normed, _ = saved[layer]
        weights, ffn_share = full[layer]
        d_normed_ffn, *grad_gu, grad_down = ffn(d_down, ffn_share, 9 + layer, group_normed)
        if layer == 0 and tiled:
            first_down = grad_down.reshape(planes, ff_block, out_cols)
        else:
            down_grads[layer] = lax.psum_scatter(
                grad_down.reshape(planes * ff_block, out_cols),
                "zd",
                scatter_dimension=0,
                tiled=True,
            )
        gu_sums[layer] = [
            lax.psum_scatter(g, "zd", scatter_dimension=0, tiled=True) for g in grad_gu
        ]
        earlier = (saved[layer - 1][3], gain_rows[layer - 1]) if layer > 0 else None
        grad_hidden, d_mixed, d_projected, gain_grads[layer], *d_rest = attn_backward(
            d_normed_ffn,
            grad_hidden,
            kept,
            weights,
            gain_rows[layer],
            tables,
            bias,
            planes,
            reach,
            17 + layer,
            earlier,
        )
        gain_grads[layer] = gain_grads[layer].at[1:, D : 2 * D].set(d_post_ffn)
        if layer > 0:
            d_down, d_post_ffn = d_rest
        attn_acts[layer] = [normed, d_mixed, attended, d_projected]
    attn_acts[0][1], gu_sums[1:], down_grads[1:] = lax.optimization_barrier(
        (attn_acts[0][1], gu_sums[1:], down_grads[1:])
    )

    packet = jnp.stack(gain_grads, axis=1).reshape(cores, LAYERS, planes, PLANE, gain_cols)
    packet = packet.transpose(0, 3, 2, 1, 4)
    packet = jnp.pad(packet, [(0, 0)] * 3 + [(0, 8 - LAYERS), (0, lanes - gain_cols)])
    packet = packet.at[:, :, :, LAYERS, 0].set(square_sum)
    packet = packet.reshape(cores, PLANE, planes * 8, lanes)
    down = first_down if tiled else None
    grad_qkv, grad_out, packet, *summed_down = collect(sum(attn_acts, []), packet, down, 19)
    if tiled:
        (down_grads[0],) = summed_down
    mse_loss = packet[LAYERS, 0] / (valid_count * D)
    gain_grad = packet[:LAYERS, None, :gain_cols]

    outcome = update(
        [[grad_qkv], [grad_out], down_grads],
        [list(pair) for pair in gu_sums],
        (mom_qkv, mom_out, mom_gu, mom_down),
        (w_qkv, w_out, w_gu, w_down),
        15,
    )
    new_weights, moments = outcome[:4], outcome[4:]
    gain_first_new = beta_one * gain_first + (1.0 - beta_one) * gain_grad
    gain_second_new = beta_two * gain_second + (1.0 - beta_two) * gain_grad * gain_grad
    gains_new = norm_gains - adam_rate * (gain_first_new / (1.0 - beta_one**STEP)) / (
        jnp.sqrt(gain_second_new / (1.0 - beta_two**STEP)) + adam_epsilon
    )
    return (
        mse_loss,
        output.reshape(inputs.shape),
        grad_hidden.reshape(inputs.shape),
        *new_weights,
        *moments,
        gains_new,
        gain_first_new,
        gain_second_new,
    )


def solution(mesh):
    cores, length = mesh.devices.shape
    split = Mesh(mesh.devices.reshape(cores, length // PLANE, PLANE), EVERY)
    stream = P("head", SEQ, None)
    matrix = P(None, SEQ, "head")
    gains = P(None, "head", SEQ)
    return jax.shard_map(
        body,
        mesh=split,
        in_specs=(stream, stream, stream, P(), P("head", SEQ))
        + (matrix,) * 4
        + (gains,)
        + (matrix,) * 4
        + (gains,) * 2,
        out_specs=(P(), stream, stream) + (matrix,) * 8 + (gains,) * 3,
        check_vma=False,
    )
```

```python
from functools import partial
import itertools
import math

import jax
import jax.numpy as jnp
from jax import lax
from jax.experimental import pallas as pl
from jax.experimental.pallas import tpu as pltpu
from jax.sharding import Mesh, PartitionSpec as P

D = 1152
HEADS = 4
HD = 256
FF = 6912
WINDOW = 512
LAYERS = 2
NS_ITERS = 5
STEP = 10
PLANE = 4

norm_eps = 1e-06
rope_base = 10000.0
newton_one = 3.4445
newton_two = -4.775
newton_three = 2.0315
muon_decay = 0.95
muon_rate = 0.15
muon_shrink = 0.01
muon_scale = 0.2
beta_one = 0.9
beta_two = 0.95
adam_rate = 0.7
adam_epsilon = 1e-08
finest_precision = lax.Precision.HIGHEST
MESH = pl.DeviceIdType.MESH
SEQ = ("zd", "tp")
GROUP = ("head", "tp")
EVERY = ("head", "zd", "tp")
bf16 = jnp.bfloat16
f32 = jnp.float32
LIGHT = pl.CostEstimate(flops=1, bytes_accessed=1, transcendentals=0)


def linear(places, sizes):
    index = 0
    for place, size in zip(places, sizes):
        index = index * size + place
    return index


def enter(partners):
    barrier = pltpu.get_barrier_semaphore()
    for partner in partners:
        pl.semaphore_signal(barrier, inc=1, device_id=partner, device_id_type=MESH)
    pl.semaphore_wait(barrier, len(partners))


class Spread:
    ORDER = ("zd", "tp", "head")

    def __init__(self, sizes, slots, send_sem, recv_sem, whole_z=False):
        self.size = dict(zip(EVERY, sizes))
        self.place = {axis: lax.axis_index(axis) for axis in EVERY}
        self.slots, self.send_sem, self.recv_sem = slots, send_sem, recv_sem
        self.held, self.sends, self.number = [(self.place, None)], [], 0
        if whole_z:
            self.held = [(dict(self.place, zd=z), None) for z in range(self.size["zd"])]
            self.ORDER = self.ORDER[1:]

    def partners(self):
        return [
            {axis: lax.rem(self.place[axis] + step, self.size[axis])}
            for axis in self.ORDER
            for step in range(1, self.size[axis])
        ]

    def stage(self, axis):
        arriving = []
        for where, arrivals in self.held:
            while arrivals:
                arrivals.pop().wait_recv()
            for step in range(1, self.size[axis]):
                to = lax.rem(self.place[axis] + step, self.size[axis])
                back = lax.rem(self.place[axis] - step + self.size[axis], self.size[axis])
                landing = []
                for k, slot in enumerate(self.slots):
                    ref = slot.at[tuple(where[name] for name in EVERY)]
                    copy = pltpu.make_async_remote_copy(
                        src_ref=ref,
                        dst_ref=ref,
                        send_sem=self.send_sem.at[k, self.number],
                        recv_sem=self.recv_sem.at[k, self.number],
                        device_id={axis: to},
                        device_id_type=MESH,
                    )
                    copy.start()
                    self.sends.append(copy)
                    landing.append(copy)
                self.number += 1
                arriving.append((dict(where, **{axis: back}), landing))
        self.held = self.held + arriving

    def finish(self):
        for _, arrivals in self.held:
            while arrivals:
                arrivals.pop().wait_recv()
        for copy in self.sends:
            copy.wait_send()


def start_kernel(sizes, tiled, *refs):
    cores, planes, members = sizes
    rest = list(refs)
    take = lambda number: [rest.pop(0) for _ in range(number)]
    gu, qkv, out, packet = take(4)
    down = take(1)[0] if tiled else None
    gu_result, mixed, project, packets, qkv_later, out_later = take(6)
    down_result = take(1)[0] if tiled else None
    packet_slots, qkv_slots, out_slots, send_sem, recv_sem = take(5)
    pieces, gu_send, gu_recv, gu_own, later_send, later_recv = take(6)
    qkv_low, out_low, later_own = take(3)
    gather = Spread(sizes, [packet_slots, qkv_slots, out_slots], send_sem, recv_sem)
    here = tuple(gather.place[name] for name in EVERY)
    core, zd, tp = here
    group = []
    for step in range(1, cores * members):
        far = lax.rem(core + step // members, cores), lax.rem(tp + step % members, members)
        group.append((dict(zip(GROUP, far)), linear(far, (cores, members))))
    enter(gather.partners() + [device for device, _ in group])
    packet_slots[here] = packet[...]

    def place_rows(source, layer, slot, index):
        rows = source.shape[1]
        slot[index + (slice(0, rows),)] = source[layer].astype(bf16)
        if slot.shape[-2] > rows:
            slot[index + (slice(rows, slot.shape[-2]),)] = jnp.zeros(
                (slot.shape[-2] - rows, slot.shape[-1]), bf16
            )

    for source, slot in ((qkv, qkv_slots), (out, out_slots)):
        place_rows(source, 0, slot, here)
    gather.stage("zd")
    moves = []

    def along_z(source, target, sends, recvs):
        for step in range(1, planes):
            copy = pltpu.make_async_remote_copy(
                src_ref=source,
                dst_ref=target,
                send_sem=sends.at[step],
                recv_sem=recvs.at[step],
                device_id={"zd": lax.rem(zd + step, planes)},
                device_id_type=MESH,
            )
            copy.start()
            moves.append(copy)

    for k, (source, low, slot) in enumerate(
        ((qkv, qkv_low, qkv_later), (out, out_low, out_later))
    ):
        for layer in range(1, source.shape[0]):
            place_rows(source, layer, low, (layer - 1,))
            target = slot.at[layer - 1, zd]
            along_z(
                low.at[layer - 1], target, later_send.at[k, layer], later_recv.at[k, layer]
            )
            own = pltpu.make_async_copy(low.at[layer - 1], target, later_own.at[k, layer])
            own.start()
            moves.append(own)
    if tiled:
        down_low, down_send, down_recv, down_own = take(4)
        down_low[...] = down[0].astype(bf16)
        along_z(down_low, down_result.at[zd], down_send, down_recv)
        own = pltpu.make_async_copy(down_low, down_result.at[zd], down_own)
        own.start()
        moves.append(own)
    layers, rows, columns = gu.shape
    block = columns // (planes * members)
    half = planes // cores
    for c in range(cores):
        for j in range(members):
            for i in range(layers):
                cut = [
                    gu[i, :, pl.ds(((c * half + k) * members + j) * block, block)]
                    for k in range(half)
                ]
                value = jnp.concatenate(cut, axis=1) if half > 1 else cut[0]
                pieces[c * members + j, i * rows : (i + 1) * rows] = value.astype(bf16)
    if pieces.shape[1] > layers * rows:
        for piece in range(cores * members):
            pieces[piece, layers * rows :] = jnp.zeros(
                (pieces.shape[1] - layers * rows, pieces.shape[2]), bf16
            )
    me = linear((core, tp), (cores, members))
    for step, (device, index) in enumerate(group):
        copy = pltpu.make_async_remote_copy(
            src_ref=pieces.at[index],
            dst_ref=gu_result.at[me],
            send_sem=gu_send.at[step],
            recv_sem=gu_recv.at[step],
            device_id=device,
            device_id_type=MESH,
        )
        copy.start()
        moves.append(copy)
    own = pltpu.make_async_copy(pieces.at[me], gu_result.at[me], gu_own)
    own.start()
    moves.append(own)
    gather.stage("tp")
    gather.stage("head")
    gather.finish()
    side_by_side(sizes, (qkv_slots, out_slots), (mixed, project))
    packets[...] = packet_slots[...]
    for copy in moves:
        copy.wait()


def side_by_side(sizes, slots, results):
    cores, planes, members = sizes
    for slot, result in zip(slots, results):
        columns = slot.shape[4]
        rows = result.shape[0] // (planes * members)
        for h, z, t in itertools.product(range(cores), range(planes), range(members)):
            row = (z * members + t) * rows
            result[row : row + rows, h * columns : (h + 1) * columns] = slot[h, z, t, :rows]


def later_kernel(sizes, layer, qkv, out, mixed, project, qkv_slots, out_slots, send_sem, recv_sem):
    gather = Spread(sizes, [qkv_slots, out_slots], send_sem, recv_sem, whole_z=True)
    core, _, tp = (gather.place[name] for name in EVERY)
    enter(gather.partners())
    for source, slot in ((qkv, qkv_slots), (out, out_slots)):
        for z in range(sizes[1]):
            slot[core, z, tp] = source[layer - 1, z]
    gather.stage("tp")
    gather.stage("head")
    gather.finish()
    side_by_side(sizes, (qkv_slots, out_slots), (mixed, project))


def whole_shapes(sizes, tall, matrices):
    slots = [pltpu.VMEM(sizes + (t, w.shape[2]), bf16) for t, w in zip(tall, matrices)]
    outs = [
        jax.ShapeDtypeStruct((w.shape[1] * sizes[1] * sizes[2], w.shape[2] * sizes[0]), bf16)
        for w in matrices
    ]
    return slots, outs


def start(w_gu, w_qkv, w_out, w_down, packet, ident):
    sizes = tuple(lax.axis_size(axis) for axis in EVERY)
    cores, planes, members = sizes
    vmem, dma = pltpu.VMEM, pltpu.SemaphoreType.DMA
    here, there = pl.BlockSpec(memory_space=pltpu.VMEM), pl.BlockSpec(memory_space=pl.ANY)
    shape = jax.ShapeDtypeStruct
    tall = [-(-w.shape[1] // 16) * 16 for w in (w_qkv, w_out)]
    slots, outs = whole_shapes(sizes, tall, (w_qkv, w_out))
    layers, rows, columns = w_gu.shape
    piece = (
        cores * members,
        -(-layers * rows // 16) * 16,
        columns // (cores * members),
    )
    later = [
        shape((layers - 1, planes, t, w.shape[2]), bf16) for t, w in zip(tall, (w_qkv, w_out))
    ]
    operands = [w_gu, w_qkv, w_out, packet]
    outs = [shape(piece, bf16)] + outs + [shape(sizes + packet.shape, f32)] + later
    out_specs = [there] + [here] * 3 + [there] * 2
    moves = math.prod(sizes) - 1
    scratch = [vmem(sizes + packet.shape, f32)] + slots + [dma((3, moves))] * 2
    scratch += [vmem(piece, bf16), dma((cores * members - 1,)), dma((cores * members - 1,)), dma]
    scratch += [dma((2, layers, planes))] * 2
    scratch += [
        vmem((layers - 1, t, w.shape[2]), bf16) for t, w in zip(tall, (w_qkv, w_out))
    ] + [dma((2, layers))]
    tiled = w_down.shape[1] % 16 == 0
    if tiled:
        _, rows, columns = w_down.shape
        operands += [w_down]
        outs += [shape((planes, rows, columns), bf16)]
        out_specs += [there]
        scratch += [vmem((rows, columns), bf16), dma((planes,)), dma((planes,)), dma]
    return pl.pallas_call(
        partial(start_kernel, sizes, tiled),
        out_shape=outs,
        in_specs=[here] * len(operands),
        out_specs=out_specs,
        scratch_shapes=scratch,
        compiler_params=pltpu.CompilerParams(
            collective_id=ident, has_side_effects=True, vmem_limit_bytes=56 * 2**20
        ),
    )(*operands)


def later_weights(gathered, w_qkv, w_out, layer, ident):
    sizes = tuple(lax.axis_size(axis) for axis in EVERY)
    slots, outs = whole_shapes(sizes, [g.shape[2] for g in gathered], (w_qkv, w_out))
    here = pl.BlockSpec(memory_space=pltpu.VMEM)
    moves = math.prod(sizes) - sizes[1]
    return pl.pallas_call(
        partial(later_kernel, sizes, layer),
        out_shape=outs,
        in_specs=[here] * 2,
        out_specs=[here] * 2,
        scratch_shapes=slots + [pltpu.SemaphoreType.DMA((2, moves))] * 2,
        compiler_params=pltpu.CompilerParams(
            collective_id=ident, has_side_effects=True, vmem_limit_bytes=48 * 2**20
        ),
    )(*gathered)


def by_rows(rows, work, step=16):
    @pl.loop(0, rows // step)
    def _(index):
        work(pl.ds(pl.multiple_of(index * step, step), step))


def collect_kernel(sizes, layers, tiled, *refs):
    cores, planes, members = sizes
    rest = list(refs)
    take = lambda number: [rest.pop(0) for _ in range(number)]
    acts, packet = take(4 * layers), take(1)[0]
    if tiled:
        (down,) = take(1)
    results = take(3)
    if tiled:
        (down_result,) = take(1)
    far, halves = take(4 * layers), take(2 * layers)
    packet_land = rest.pop(0)
    pieces, plane_lands, totals, z_sums, z_lands = (take(3) for _ in range(5))
    act_send, act_recv, packet_send, packet_recv = take(4)
    tp_send, tp_recv, z_send, z_recv = take(4)
    core, zd, tp = (lax.axis_index(axis) for axis in EVERY)
    sibling = {"head": 1 - core}
    enter(
        [sibling]
        + [{"tp": lax.rem(tp + step, members)} for step in range(1, members)]
        + [{"zd": lax.rem(zd + step, planes)} for step in range(1, planes)]
    )
    sends = []

    def send(src, dst, send_sem, recv_sem, device):
        copy = pltpu.make_async_remote_copy(
            src_ref=src,
            dst_ref=dst,
            send_sem=send_sem,
            recv_sem=recv_sem,
            device_id=device,
            device_id_type=MESH,
        )
        copy.start()
        sends.append(copy)
        return copy

    if tiled:
        down_land, down_send, down_recv, down_own = take(4)
        down_moves = []
        for step in range(1, planes):
            there = lax.rem(zd + step, planes)
            down_moves.append(
                send(
                    down.at[there],
                    down_land.at[step],
                    down_send.at[step],
                    down_recv.at[step],
                    {"zd": there},
                )
            )
        down_stay = pltpu.make_async_copy(down.at[zd], down_land.at[0], down_own)
        down_stay.start()
    for k in range(2 * layers):
        grad, half = acts[2 * k + 1], halves[k]
        width = half.shape[2]
        for h in range(cores):
            half[h] = grad[:, h * width : (h + 1) * width]
    moves = []
    for k in range(2 * layers):
        moves.append(
            send(acts[2 * k], far[2 * k], act_send.at[2 * k], act_recv.at[2 * k], sibling)
        )
        moves.append(
            send(
                halves[k].at[1 - core],
                far[2 * k + 1],
                act_send.at[2 * k + 1],
                act_recv.at[2 * k + 1],
                sibling,
            )
        )
    gains = send(packet.at[1 - core], packet_land, packet_send, packet_recv, sibling)
    plane_moves, z_moves = {}, {}
    for kind in range(3):
        piece = pieces[kind]
        if kind < 2:
            for layer in range(layers):
                k = 2 * layer + kind
                near = lax.dot_general(
                    acts[2 * k][...], halves[k][core], ALONG, preferred_element_type=f32
                )
                moves[2 * k].wait_recv()
                moves[2 * k + 1].wait_recv()
                value = near + lax.dot_general(
                    far[2 * k][...], far[2 * k + 1][...], ALONG, preferred_element_type=f32
                )
                value = value.astype(bf16)
                rows = value.shape[0] // (planes * members)
                slab = piece.shape[1] // planes
                for z, t in itertools.product(range(planes), range(members)):
                    at = (z * members + t) * rows
                    to = z * slab + layer * rows
                    piece[t, to : to + rows] = value[at : at + rows]
            if slab > layers * rows:
                for z, t in itertools.product(range(planes), range(members)):
                    piece[t, z * slab + layers * rows : (z + 1) * slab] = jnp.zeros(
                        (slab - layers * rows, piece.shape[2]), bf16
                    )
        else:
            gains.wait_recv()
            piece[...] = packet[core] + packet_land[...]
        for step in range(1, members):
            there = lax.rem(tp + step, members)
            plane_moves[kind, step] = send(
                piece.at[there],
                plane_lands[kind].at[step],
                tp_send.at[kind, step],
                tp_recv.at[kind, step],
                {"tp": there},
            )
    for kind in range(3):
        for step in range(1, members):
            plane_moves[kind, step].wait_recv()
        piece, total, land, result = pieces[kind], totals[kind], plane_lands[kind], results[kind]
        stride = 8 if land.dtype == f32 else 16

        def gather_plane(rows):
            value = piece[tp, rows].astype(f32)
            for step in range(1, members):
                value = value + land[step, rows].astype(f32)
            total[rows] = value

        by_rows(total.shape[0], gather_plane, stride)
        height = result.shape[0]
        z_sum = z_sums[kind]
        for step in range(1, planes):
            there = lax.rem(zd + step, planes)

            def round_off(rows):
                at = pl.multiple_of(there * height + rows.start, stride)
                z_sum[step, rows] = total[pl.ds(at, rows.size)].astype(z_sum.dtype)

            by_rows(height, round_off, stride)
            z_moves[kind, step] = send(
                z_sum.at[step],
                z_lands[kind].at[step],
                z_send.at[kind, step],
                z_recv.at[kind, step],
                {"zd": there},
            )
    for kind in range(3):
        for step in range(1, planes):
            z_moves[kind, step].wait_recv()
        total, land, result = totals[kind], z_lands[kind], results[kind]
        height = result.shape[0]
        stride = 8 if land.dtype == f32 else 16

        def gather_z(rows):
            at = pl.multiple_of(zd * height + rows.start, stride)
            value = total[pl.ds(at, rows.size)]
            for step in range(1, planes):
                value = value + land[step, rows].astype(f32)
            result[rows] = value

        by_rows(height, gather_z, stride)
    if tiled:
        down_stay.wait()
        for copy in down_moves:
            copy.wait_recv()

        def gather_down(rows):
            value = down_land[0, rows].astype(f32)
            for step in range(1, planes):
                value = value + down_land[step, rows].astype(f32)
            down_result[rows] = value

        by_rows(down_result.shape[0], gather_down)
    for copy in sends:
        copy.wait_send()


def collect(acts, packet, down, ident):
    sizes = tuple(lax.axis_size(axis) for axis in EVERY)
    cores, planes, members = sizes
    layers = len(acts) // 4
    vmem, dma = pltpu.VMEM, pltpu.SemaphoreType.DMA
    tokens = acts[0].shape[0]
    halves = [acts[2 * k + 1].shape[1] // cores for k in range(2 * layers)]
    slabs = []
    for kind in range(2):
        rows = layers * acts[2 * kind].shape[1] // (planes * members)
        slabs.append((-(-rows // 16) * 16, halves[kind], bf16))
    slabs.append((packet.shape[2] // planes, packet.shape[3], f32))
    far = []
    for k in range(2 * layers):
        far += [vmem(acts[2 * k].shape, bf16), vmem((tokens, halves[k]), bf16)]
    scratch = far + [vmem((cores, tokens, width), bf16) for width in halves]
    scratch += [vmem(packet.shape[1:], f32)]
    scratch += [vmem((members, planes * r, c), kind) for r, c, kind in slabs] * 2
    scratch += [vmem((planes * r, c), f32) for r, c, _ in slabs]
    scratch += [vmem((planes, r, c), kind) for r, c, kind in slabs] * 2
    scratch += [dma((4 * layers,))] * 2 + [dma] * 2
    scratch += [dma((3, members))] * 2 + [dma((3, planes))] * 2
    here = pl.BlockSpec(memory_space=pltpu.VMEM)
    operands = [*acts, packet]
    outs = [jax.ShapeDtypeStruct((r, c), f32) for r, c, _ in slabs]
    in_specs = [here] * len(operands)
    if down is not None:
        operands, in_specs = operands + [down], in_specs + [pl.BlockSpec(memory_space=pl.ANY)]
        outs += [jax.ShapeDtypeStruct(down.shape[1:], f32)]
        scratch += [vmem(down.shape, bf16), dma((planes,)), dma((planes,)), dma]
    return pl.pallas_call(
        partial(collect_kernel, sizes, layers, down is not None),
        out_shape=outs,
        in_specs=in_specs,
        out_specs=[here] * len(outs),
        scratch_shapes=scratch,
        cost_estimate=LIGHT,
        compiler_params=pltpu.CompilerParams(
            collective_id=ident, has_side_effects=True, vmem_limit_bytes=56 * 2**20
        ),
    )(*operands)


def neighbours(planes, reach, sign):
    total = planes * PLANE
    place = linear([lax.axis_index("zd"), lax.axis_index("tp")], (planes, PLANE))

    def at(distance):
        there = lax.rem(place + distance + total, total)
        return {"zd": lax.div(there, PLANE), "tp": lax.rem(there, PLANE)}

    steps = range(1, reach + 1)
    return [at(sign * step) for step in steps], [at(-sign * step) for step in steps]


def inverse_rms(values):
    return lax.rsqrt(jnp.mean(values * values, axis=-1, keepdims=True) + norm_eps)


def rms_back(gradient, values, gain):
    inverse = inverse_rms(values)
    scaled = gradient * gain
    shared = jnp.mean(scaled * values, axis=-1, keepdims=True) * (inverse * inverse)
    return inverse * (scaled - values * shared), jnp.sum(
        gradient * values * inverse, axis=0, keepdims=True
    )


def turn(values, cosine, sine):
    half = values.shape[-1] // 2
    lower, upper = values[:, :half], values[:, half:]
    return jnp.concatenate(
        [lower * cosine - upper * sine, upper * cosine + lower * sine], axis=-1
    )


def soft_rows(query, keys, bias):
    scores = lax.dot_general(query, keys, ACROSS, preferred_element_type=f32)
    scores = scores * (1.0 / math.sqrt(HD)) + bias
    raised = jnp.exp(scores - jnp.max(scores, axis=-1, keepdims=True))
    return raised / jnp.sum(raised, axis=-1, keepdims=True)


def attn_forward_kernel(planes, reach, chained, *refs):
    rest = list(refs)
    take = lambda number: [rest.pop(0) for _ in range(number)]
    if chained:
        base, down, before = take(3)
    else:
        (base,) = take(1)
    w_mixed, w_project, gains, cosine, sine, bias = take(6)
    hidden, normed, mixed, queries, keyvals_out = take(5)
    attended, projected, hidden_half, normed_ffn = take(4)
    keyvals, send_sem, recv_sem, save_sem = take(4)
    seqs, stretch, key_len = bias.shape
    devices, sources = neighbours(planes, reach, 1)
    enter(devices + sources)
    value = base[...].astype(f32)
    if chained:
        late = down[...]
        value = value + late * inverse_rms(late) * before[1:2, D : 2 * D]
    hidden[...] = value
    low = (value * inverse_rms(value) * gains[0:1, :D]).astype(bf16)
    normed[...] = low
    mixed[...] = matmul(low, w_mixed[...])
    key = mixed[:, HEADS * HD : HEADS * HD + HD]
    key = turn(key * inverse_rms(key) * gains[1:2, 2 * D :], cosine[...], sine[...]).astype(bf16)
    late_values = mixed[:, HEADS * HD + HD :].astype(bf16)
    copies = []
    for i in range(seqs):
        rows = slice(i * stretch, (i + 1) * stretch)
        keyvals[i, reach * stretch :, :HD] = key[rows]
        keyvals[i, reach * stretch :, HD:] = late_values[rows]
        for step, device in enumerate(devices):
            copy = pltpu.make_async_remote_copy(
                src_ref=keyvals.at[i, pl.ds(reach * stretch, stretch)],
                dst_ref=keyvals.at[i, pl.ds((reach - 1 - step) * stretch, stretch)],
                send_sem=send_sem.at[i, step],
                recv_sem=recv_sem.at[i, step],
                device_id=device,
                device_id_type=MESH,
            )
            copy.start()
            copies.append(copy)
    for h in range(HEADS):
        columns = slice(h * HD, (h + 1) * HD)
        query = mixed[:, columns]
        query = turn(query * inverse_rms(query) * gains[0:1, 2 * D :], cosine[...], sine[...])
        queries[:, columns] = query.astype(bf16)
    for copy in copies:
        copy.wait_recv()
    save = pltpu.make_async_copy(keyvals, keyvals_out, save_sem)
    save.start()
    for i in range(seqs):
        rows = slice(i * stretch, (i + 1) * stretch)
        for h in range(HEADS):
            columns = slice(h * HD, (h + 1) * HD)
            soft = soft_rows(queries[rows, columns], keyvals[i, :, :HD], bias[i])
            attended[rows, columns] = matmul(soft.astype(bf16), keyvals[i, :, HD:]).astype(bf16)
    out = matmul(attended[...], w_project[...])
    projected[...] = out
    half = hidden[...] + out * inverse_rms(out) * gains[0:1, D : 2 * D]
    hidden_half[...] = half
    normed_ffn[...] = (half * inverse_rms(half) * gains[1:2, :D]).astype(bf16)
    for copy in copies:
        copy.wait_send()
    save.wait()


def attn_forward(base, weights, gains, tables, bias, planes, reach, ident, earlier=None):
    tokens = base.shape[0]
    seqs, _, key_len = bias.shape
    shape = jax.ShapeDtypeStruct
    operands = [base] + list(earlier or []) + list(weights) + [gains, *tables, bias]
    here, there = pl.BlockSpec(memory_space=pltpu.VMEM), pl.BlockSpec(memory_space=pl.ANY)
    dma = pltpu.SemaphoreType.DMA
    return pl.pallas_call(
        partial(attn_forward_kernel, planes, reach, earlier is not None),
        out_shape=[
            shape((tokens, D), f32),
            shape((tokens, D), bf16),
            shape((tokens, weights[0].shape[1]), f32),
            shape((tokens, HEADS * HD), bf16),
            shape((seqs, key_len, 2 * HD), bf16),
            shape((tokens, HEADS * HD), bf16),
            shape((tokens, D), f32),
            shape((tokens, D), f32),
            shape((tokens, D), bf16),
        ],
        in_specs=[here] * len(operands),
        out_specs=[here] * 4 + [there] + [here] * 4,
        scratch_shapes=[
            pltpu.VMEM((seqs, key_len, 2 * HD), bf16),
            dma((seqs, reach)),
            dma((seqs, reach)),
            dma,
        ],
        compiler_params=pltpu.CompilerParams(
            collective_id=ident, has_side_effects=True, vmem_limit_bytes=56 * 2**20
        ),
    )(*operands)


def attn_backward_kernel(planes, reach, chained, *refs):
    rest = list(refs)
    take = lambda number: [rest.pop(0) for _ in range(number)]
    d_ffn, above, hidden, mixed, queries, keyvals, projected, hidden_half = take(8)
    w_mixed, w_project, gains, cosine, sine, bias = take(6)
    if chained:
        down, before = take(2)
    grad, d_mixed, d_projected, gain_grads = take(4)
    if chained:
        d_down, d_post = take(2)
    d_keyvals, outgoing, incoming, d_attended, send_sem, recv_sem = take(6)
    seqs, stretch, key_len = bias.shape
    devices, sources = neighbours(planes, reach, -1)
    enter(devices + sources)
    scale = 1.0 / math.sqrt(HD)
    part, gain_row = rms_back(d_ffn[...], hidden_half[...], gains[1:2, :D])
    gain_grads[1:2, :D] = gain_row
    gain_grads[1:2, D : 2 * D] = jnp.zeros((1, D), f32)
    grad[...] = part + above[...]
    part, gain_row = rms_back(grad[...], projected[...], gains[0:1, D : 2 * D])
    gain_grads[0:1, D : 2 * D] = gain_row
    low = part.astype(bf16)
    d_projected[...] = low
    d_attended[...] = lax.dot_general(
        low, w_project[...], ACROSS, preferred_element_type=f32
    ).astype(bf16)
    query_gain = jnp.zeros((1, HD), f32)
    for i in range(seqs):
        rows = slice(i * stretch, (i + 1) * stretch)
        d_keys = d_values = None
        for h in range(HEADS):
            columns = slice(h * HD, (h + 1) * HD)
            query, d_out = queries[rows, columns], d_attended[rows, columns]
            keys, values = keyvals[i, :, :HD], keyvals[i, :, HD:]
            soft = soft_rows(query, keys, bias[i])
            d_soft = lax.dot_general(d_out, values, ACROSS, preferred_element_type=f32)
            total = jnp.sum(soft * d_soft, axis=-1, keepdims=True)
            d_scores = (soft * (d_soft - total)).astype(bf16)
            key_part = lax.dot_general(d_scores, query, ALONG, preferred_element_type=f32)
            value_part = lax.dot_general(
                soft.astype(bf16), d_out, ALONG, preferred_element_type=f32
            )
            d_keys = key_part if d_keys is None else d_keys + key_part
            d_values = value_part if d_values is None else d_values + value_part
            d_query = matmul(d_scores, keys) * scale
            d_query = turn(d_query, cosine[rows], -sine[rows])
            part, gain_row = rms_back(d_query, mixed[rows, columns], gains[0:1, 2 * D :])
            query_gain = query_gain + gain_row
            d_mixed[rows, columns] = part.astype(bf16)
        d_keyvals[i, :, :HD] = d_keys * scale
        d_keyvals[i, :, HD:] = d_values
    gain_grads[0:1, 2 * D :] = query_gain
    outgoing[...] = d_keyvals[:, : reach * stretch].astype(bf16)
    copies = []
    for i in range(seqs):
        for step, device in enumerate(devices):
            copy = pltpu.make_async_remote_copy(
                src_ref=outgoing.at[i, pl.ds((reach - 1 - step) * stretch, stretch)],
                dst_ref=incoming.at[i, step],
                send_sem=send_sem.at[i, step],
                recv_sem=recv_sem.at[i, step],
                device_id=device,
                device_id_type=MESH,
            )
            copy.start()
            copies.append(copy)
    for copy in copies:
        copy.wait_recv()
    key_gain = jnp.zeros((1, HD), f32)
    for i in range(seqs):
        rows = slice(i * stretch, (i + 1) * stretch)
        own = d_keyvals[i, reach * stretch :]
        for step in range(reach):
            own = own + incoming[i, step].astype(f32)
        d_key = turn(own[:, :HD], cosine[rows], -sine[rows])
        part, gain_row = rms_back(
            d_key, mixed[rows, HEADS * HD : HEADS * HD + HD], gains[1:2, 2 * D :]
        )
        key_gain = key_gain + gain_row
        d_mixed[rows, HEADS * HD : HEADS * HD + HD] = part.astype(bf16)
        d_mixed[rows, HEADS * HD + HD :] = own[:, HD:].astype(bf16)
    gain_grads[1:2, 2 * D :] = key_gain
    d_normed = lax.dot_general(d_mixed[...], w_mixed[...], ACROSS, preferred_element_type=f32)
    part, gain_row = rms_back(d_normed, hidden[...], gains[0:1, :D])
    gain_grads[0:1, :D] = gain_row
    grad[...] = grad[...] + part
    if chained:
        part, gain_row = rms_back(grad[...], down[...], before[1:2, D : 2 * D])
        d_down[...] = part.astype(bf16)
        d_post[...] = gain_row
    for copy in copies:
        copy.wait_send()


def attn_backward(
    d_ffn, above, kept, weights, gains, tables, bias, planes, reach, ident, earlier=None
):
    tokens = above.shape[0]
    seqs, stretch, key_len = bias.shape
    shape = jax.ShapeDtypeStruct
    operands = [d_ffn, above, *kept, *weights, gains, *tables, bias] + list(earlier or [])
    outs = [
        shape((tokens, D), f32),
        shape((tokens, weights[0].shape[1]), bf16),
        shape((tokens, D), bf16),
        shape(gains.shape, f32),
    ]
    if earlier is not None:
        outs += [shape((tokens, D), bf16), shape((1, D), f32)]
    here = pl.BlockSpec(memory_space=pltpu.VMEM)
    vmem, dma = pltpu.VMEM, pltpu.SemaphoreType.DMA
    return pl.pallas_call(
        partial(attn_backward_kernel, planes, reach, earlier is not None),
        out_shape=outs,
        in_specs=[here] * len(operands),
        out_specs=[here] * len(outs),
        scratch_shapes=[
            vmem((seqs, key_len, 2 * HD), f32),
            vmem((seqs, reach * stretch, 2 * HD), bf16),
            vmem((seqs, reach, stretch, 2 * HD), bf16),
            vmem((tokens, HEADS * HD), bf16),
            dma((seqs, reach)),
            dma((seqs, reach)),
        ],
        compiler_params=pltpu.CompilerParams(
            collective_id=ident, has_side_effects=True, vmem_limit_bytes=56 * 2**20
        ),
    )(*operands)


GELU_SLOPE = math.sqrt(2.0 / math.pi)
GELU_CUBE = 0.044715
ACROSS = (((1,), (1,)), ((), ()))
ALONG = (((0,), (0,)), ((), ()))


class Plane:
    def __init__(self, own, bufs, sems):
        self.own = own
        self.rows, self.partial, self.other, self.lands, self.sums, self.arrived = bufs
        self.x_send, self.x_recv, self.f_send, self.f_recv = sems[:4]
        self.c_send, self.c_recv, self.p_send, self.p_recv, self.first = sems[4:]
        self.tp = lax.axis_index("tp")
        self.sibling = {"head": 1 - lax.axis_index("head")}

    def member(self, m):
        tp = self.tp
        upper = lax.rem(lax.div(tp, 2) + lax.div(m, 2), 2)
        lower = lax.rem(lax.rem(tp, 2) + lax.rem(m, 2), 2)
        return {"tp": upper * 2 + lower}

    def remote(self, src, dst, send, recv, device):
        return pltpu.make_async_remote_copy(
            src_ref=src,
            dst_ref=dst,
            send_sem=send,
            recv_sem=recv,
            device_id=device,
            device_id_type=MESH,
        )

    def push(self, m):
        return self.remote(
            self.own, self.rows.at[0, m], self.x_send.at[m], self.x_recv.at[m], self.member(m)
        )

    def keep(self):
        return pltpu.make_async_copy(self.own, self.rows.at[0, 0], self.first)

    def forward(self, m):
        return self.remote(
            self.rows.at[0, m],
            self.rows.at[1, m],
            self.f_send.at[m],
            self.f_recv.at[m],
            self.sibling,
        )

    def cross(self, m):
        return self.remote(
            self.other.at[m], self.lands.at[m], self.c_send.at[m], self.c_recv.at[m], self.sibling
        )

    def home(self, m):
        return self.remote(
            self.sums.at[m],
            self.arrived.at[m],
            self.p_send.at[m],
            self.p_recv.at[m],
            self.member(m),
        )

    def begin(self, others=()):
        self.keep().start()
        enter([self.sibling, *others] + [self.member(jnp.int32(m)) for m in range(1, PLANE)])
        for m in range(1, PLANE):
            self.push(jnp.int32(m)).start()

    def work(self, compute):
        def settle(m):
            self.cross(m).wait_recv()

            def add(rows):
                value = self.partial[m, rows] + self.lands[m, rows].astype(f32)
                self.sums[m, rows] = value.astype(bf16)

            by_rows(self.partial.shape[1], add)
            self.home(m).start()

        def step(m, carry):
            @pl.when(m == 0)
            def _():
                self.keep().wait()

            @pl.when(m > 0)
            def _():
                self.push(m).wait_recv()

            self.forward(m).start()
            self.partial[m] = compute(0, m)
            self.forward(m).wait_recv()
            self.other[m] = compute(1, m).astype(bf16)
            self.cross(m).start()

            @pl.when(m >= 2)
            def _():
                settle(m - 1)

            return carry

        lax.fori_loop(0, PLANE, step, 0)
        settle(jnp.int32(PLANE - 1))

    def finish(self, result):
        self.cross(jnp.int32(0)).wait_recv()
        for m in range(1, PLANE):
            self.home(jnp.int32(m)).wait_recv()

        def add(rows):
            value = self.partial[0, rows] + self.lands[0, rows].astype(f32)
            for m in range(1, PLANE):
                value = value + self.arrived[m, rows].astype(f32)
            result[rows] = value

        by_rows(result.shape[0], add)
        for m in range(PLANE):
            m = jnp.int32(m)
            self.forward(m).wait_send()
            self.cross(m).wait_send()
        for m in range(1, PLANE):
            m = jnp.int32(m)
            self.push(m).wait_send()
            self.home(m).wait_send()


class Aside:
    def __init__(self, refs):
        self.source, self.result, self.send_sem, self.recv_sem, self.own_sem = refs
        self.planes = self.result.shape[0]
        self.zd = lax.axis_index("zd")
        self.copies = []

    def partners(self):
        return [{"zd": lax.rem(self.zd + s, self.planes)} for s in range(1, self.planes)]

    def block(self, plane):
        return self.source if len(self.source.shape) == 2 else self.source.at[plane]

    def start(self):
        for step in range(1, self.planes):
            there = lax.rem(self.zd + step, self.planes)
            self.copies.append(
                pltpu.make_async_remote_copy(
                    src_ref=self.block(there),
                    dst_ref=self.result.at[self.zd],
                    send_sem=self.send_sem.at[step],
                    recv_sem=self.recv_sem.at[step],
                    device_id={"zd": there},
                    device_id_type=MESH,
                )
            )
        self.copies.append(
            pltpu.make_async_copy(self.block(self.zd), self.result.at[self.zd], self.own_sem)
        )
        for copy in self.copies:
            copy.start()

    def finish(self):
        for copy in self.copies:
            copy.wait()


def with_aside(kernel, inputs, outputs):
    def whole(*refs):
        ins, outs = refs[: inputs + 1], refs[inputs + 1 : inputs + outputs + 2]
        scratch = refs[inputs + outputs + 2 :]
        aside = Aside((ins[-1], outs[-1], *scratch[-3:]))
        kernel(*ins[:-1], *outs[:-1], *scratch[:-3], aside=aside)

    return whole


def gate_up_copies(gu_ref, gate_up, sem):
    blocks = gu_ref.shape[0]
    rows = gate_up.shape[1] // blocks
    return [
        pltpu.make_async_copy(
            gu_ref.at[block, part],
            gate_up.at[part, pl.ds(block * rows, rows)],
            sem.at[2 * block + part],
        )
        for block in range(blocks)
        for part in range(2)
    ]


def ffn_forward_kernel(
    own, gu_ref, halves_ref, group, saved_down, result, *scratch, aside=None
):
    rows, gate_up, down = scratch[:3]
    plane = Plane(own, (rows,) + scratch[3:8], scratch[8:17])
    weight_sem, group_sem, halves, half_send, half_recv, half_own, save_sem = scratch[17:]
    core = lax.axis_index("head")
    share, width = halves.shape[1:]
    copies = gate_up_copies(gu_ref, gate_up, weight_sem)
    copies.append(
        pltpu.make_async_copy(
            halves_ref.at[0, pl.ds(pl.multiple_of(core * share, 16), share)],
            halves.at[core],
            half_own,
        )
    )
    for copy in copies:
        copy.start()
    plane.begin(aside.partners() if aside else ())
    if aside:
        aside.start()
    half = plane.remote(
        halves_ref.at[0, pl.ds(pl.multiple_of((1 - core) * share, 16), share)],
        halves.at[core],
        half_send,
        half_recv,
        plane.sibling,
    )
    half.start()
    for copy in copies:
        copy.wait()
    pltpu.make_async_remote_copy(
        src_ref=halves_ref.at[0, pl.ds(pl.multiple_of((1 - core) * share, 16), share)],
        dst_ref=halves.at[1 - core],
        send_sem=half_send,
        recv_sem=half_recv,
        device_id=plane.sibling,
        device_id_type=MESH,
    ).wait_recv()

    def join(at):
        down[at] = jnp.concatenate([halves[h, at] for h in range(2)], axis=1)

    by_rows(share, join, 32)
    keep_down = pltpu.make_async_copy(down, saved_down, save_sem)
    keep_down.start()

    def compute(side, m):
        tokens = rows[side, m]
        gate = matmul(tokens, gate_up[0])
        up = matmul(tokens, gate_up[1])
        bend = jnp.tanh(GELU_SLOPE * (gate + GELU_CUBE * (gate * gate * gate)))
        inner = (0.5 * gate * (1.0 + bend) * up).astype(bf16)
        return matmul(inner, down[...])

    plane.work(compute)
    save = pltpu.make_async_copy(rows, group, group_sem)
    save.start()
    plane.finish(result)
    save.wait()
    keep_down.wait()
    half.wait_send()
    if aside:
        aside.finish()


def ffn_backward_kernel(
    own, group, gu_ref, down_ref, result, grad_gate, grad_up, grad_down, *scratch, aside=None
):
    rows, gate_up, down = scratch[:3]
    plane = Plane(own, (rows,) + scratch[3:8], scratch[8:17])
    weight_sem, group_sem, saved, d_gate, d_up, inner = scratch[17:23]
    down_sem, turned, down_halves, half_send, half_recv, half_own = scratch[23:]
    core = lax.axis_index("head")
    copies = gate_up_copies(gu_ref, gate_up, weight_sem)
    copies.append(pltpu.make_async_copy(down_ref, down, down_sem))
    for copy in copies:
        copy.start()
    load = pltpu.make_async_copy(group, saved, group_sem)
    load.start()
    plane.begin(aside.partners() if aside else ())
    if aside:
        aside.start()
    for copy in copies:
        copy.wait()
    load.wait()

    def recompute(index, carry):
        side, m = lax.div(index, PLANE), lax.rem(index, PLANE)
        tokens = saved[side, m]
        gate = matmul(tokens, gate_up[0])
        up = matmul(tokens, gate_up[1])
        square = gate * gate
        bend = jnp.tanh(GELU_SLOPE * (gate + GELU_CUBE * (square * gate)))
        half = 0.5 * (1.0 + bend)
        value = gate * half
        slope = half + (0.5 * GELU_SLOPE) * gate * (1.0 - bend * bend) * (
            1.0 + (3.0 * GELU_CUBE) * square
        )
        inner[side, m] = (value * up).astype(bf16)
        d_gate[side, m] = (slope * up).astype(bf16)
        d_up[side, m] = value.astype(bf16)
        return carry

    lax.fori_loop(0, 2 * PLANE, recompute, 0)

    def compute(side, m):
        d_inner = lax.dot_general(rows[side, m], down[...], ACROSS, preferred_element_type=f32)
        gate = (d_inner * d_gate[side, m].astype(f32)).astype(bf16)
        up = (d_inner * d_up[side, m].astype(f32)).astype(bf16)
        d_gate[side, m] = gate
        d_up[side, m] = up
        return lax.dot_general(
            gate, gate_up[0], ACROSS, preferred_element_type=f32
        ) + lax.dot_general(up, gate_up[1], ACROSS, preferred_element_type=f32)

    plane.work(compute)
    width = rows.shape[-1]
    step = width // 3

    def tall(ref, columns=slice(None)):
        value = ref[:, :, :, columns]
        return value.reshape(-1, value.shape[-1])

    @pl.loop(0, 3)
    def _(index):
        at = pl.ds(pl.multiple_of(index * step, step), step)
        tokens = tall(saved, at)
        for target, other in ((grad_gate, d_gate), (grad_up, d_up)):
            target[at] = lax.dot_general(
                tokens, tall(other), ALONG, preferred_element_type=f32
            ).astype(bf16)
        turned[at] = lax.dot_general(
            tall(rows, at), tall(inner), ALONG, preferred_element_type=f32
        ).astype(bf16)

    half_width = down_halves.shape[2]
    for h in range(2):
        down_halves[h] = turned[h * half_width : (h + 1) * half_width].T
    half = plane.remote(
        down_halves.at[1 - core], grad_down.at[core], half_send, half_recv, plane.sibling
    )
    half.start()
    stay = pltpu.make_async_copy(down_halves.at[core], grad_down.at[core], half_own)
    stay.start()
    plane.finish(result)
    half.wait()
    stay.wait()
    if aside:
        aside.finish()


def ffn(own, weights, ident, group=None, aside=None, planes=None):
    gate_up, down = weights
    tokens, width = own.shape
    blocks, _, _, share = gate_up.shape
    vmem, dma = pltpu.VMEM, pltpu.SemaphoreType.DMA
    scratch = [
        vmem((2, PLANE, tokens, width), bf16),
        vmem((2, width, share), bf16),
        vmem((share, width), bf16),
        vmem((PLANE, tokens, width), f32),
    ]
    scratch += [vmem((PLANE, tokens, width), bf16)] * 4
    scratch += [dma((PLANE,))] * 8 + [dma, dma((2 * blocks,)), dma]
    here, there = pl.BlockSpec(memory_space=pltpu.VMEM), pl.BlockSpec(memory_space=pl.ANY)
    shape = jax.ShapeDtypeStruct
    summed = shape((tokens, width), f32)
    if group is None:
        kernel, operands = ffn_forward_kernel, (own, gate_up, down)
        in_specs, out_specs = [here, there, there], [there, there, here]
        out_shape = [
            shape((2, PLANE, tokens, width), bf16),
            shape((share, width), bf16),
            summed,
        ]
        scratch += [vmem((2, share, width // 2), bf16)] + [dma] * 4
    else:
        kernel, operands = ffn_backward_kernel, (own, group, gate_up, down)
        in_specs, out_specs = [here, there, there, there], [here] * 3 + [there]
        out_shape = [
            summed,
            shape((width, share), bf16),
            shape((width, share), bf16),
            shape((2, share, width // 2), bf16),
        ]
        scratch += [vmem((2, PLANE, tokens, width), bf16)]
        scratch += [vmem((2, PLANE, tokens, share), bf16)] * 3
        scratch += [dma, vmem((width, share), bf16), vmem((2, share, width // 2), bf16)]
        scratch += [dma] * 3
    if aside is not None:
        kernel = with_aside(kernel, len(operands), len(out_shape))
        operands, in_specs = [*operands, aside], in_specs + [there]
        out_shape = out_shape + [shape((planes,) + aside.shape[-2:], bf16)]
        out_specs = out_specs + [there]
        scratch += [dma((planes,)), dma((planes,)), dma]
    return pl.pallas_call(
        kernel,
        out_shape=out_shape,
        in_specs=in_specs,
        out_specs=out_specs,
        scratch_shapes=scratch,
        cost_estimate=LIGHT,
        compiler_params=pltpu.CompilerParams(
            collective_id=ident, has_side_effects=True, vmem_limit_bytes=60 * 2**20
        ),
    )(*operands)


def exact(left, right, dims=(((1,), (0,)), ((), ()))):
    return lax.dot_general(
        left, right, dims, precision=finest_precision, preferred_element_type=f32
    )


def update_kernel(sizes, counts, *refs):
    cores, planes, members = sizes
    rest = list(refs)
    take = lambda number: [rest.pop(0) for _ in range(number)]
    number = len(counts) or 1
    plain = [take(parts) for parts in counts]
    sides = [] if counts else [take(2) for _ in range(cores)]
    moments_in, weights_in, weights_out, moments_out = (take(number) for _ in range(4))
    moment, weight, gram, land, factor = (take(number) for _ in range(5))
    load_sem, store_sem, gram_send, gram_recv, factor_send, factor_recv = take(6)
    core, _, tp = (lax.axis_index(axis) for axis in EVERY)
    sibling = {"head": 1 - core}
    every = range(number)
    loads = {}
    for k in every:
        for part, source, target in ((0, moments_in, moment), (1, weights_in, weight)):
            copy = pltpu.make_async_copy(source[k], target[k], load_sem.at[part, k])
            copy.start()
            loads[part, k] = copy
    if counts:
        enter([sibling])
    else:
        pieces, arrived, gu_send, gu_recv, gu_own = take(5)
        group = []
        for step in range(1, cores * members):
            far = lax.rem(core + step // members, cores), lax.rem(tp + step % members, members)
            group.append((dict(zip(GROUP, far)), linear(far, (cores, members))))
        enter([device for device, _ in group])
        rows = moment[0].shape[1]
        for part in range(cores):
            for j in range(members):
                for layer in range(cores):
                    pieces[part * members + j, layer * rows : (layer + 1) * rows] = sides[layer][
                        part
                    ][j * rows : (j + 1) * rows]
        if pieces.shape[1] > cores * rows:
            for piece in range(cores * members):
                pieces[piece, cores * rows :] = jnp.zeros(
                    (pieces.shape[1] - cores * rows, pieces.shape[2]), bf16
                )
        me = linear((core, tp), (cores, members))
    moves, stores = [], []

    def send(src, dst, send_sem, recv_sem, device):
        copy = pltpu.make_async_remote_copy(
            src_ref=src,
            dst_ref=dst,
            send_sem=send_sem,
            recv_sem=recv_sem,
            device_id=device,
            device_id_type=MESH,
        )
        copy.start()
        return copy

    if not counts:
        for step, (device, index) in enumerate(group):
            moves.append(
                send(pieces.at[index], arrived.at[me], gu_send.at[step], gu_recv.at[step], device)
            )
        own = pltpu.make_async_copy(pieces.at[me], arrived.at[me], gu_own)
        own.start()

    def store(part, k):
        source, target = (moment, moments_out) if part == 0 else (weight, weights_out)
        copy = pltpu.make_async_copy(source[k], target[k], store_sem.at[part, k])
        copy.start()
        stores.append(copy)

    def gram_of(k):
        def one(layer, carry):
            gram[k][layer] = exact(moment[k][layer], moment[k][layer], ACROSS)
            return carry

        lax.fori_loop(0, cores, one, 0)
        return send(
            gram[k].at[1 - core], land[k], gram_send.at[k], gram_recv.at[k], sibling
        )

    def unit(size):
        down = lax.broadcasted_iota(jnp.int32, (size, size), 0)
        return (down == lax.broadcasted_iota(jnp.int32, (size, size), 1)).astype(f32)

    def orthogonal(members_of):
        for k in members_of:
            total = gram[k][core] + land[k][...]
            one = unit(total.shape[0])
            trace = jnp.sum(jnp.sum(total * one, axis=1, keepdims=True), axis=0, keepdims=True)
            scale = 1.0 / (jnp.sqrt(trace) + 1e-07)
            land[k][...] = total * (scale * scale)
            factor[k][core] = one * scale

        def polynomial(present):
            square = exact(present, present)
            return newton_one * unit(present.shape[0]) + newton_two * present + (
                newton_three * square
            )

        def step(_, carry):
            for k in members_of:
                present = land[k][...]
                poly = polynomial(present)
                factor[k][core] = exact(poly, factor[k][core])
                land[k][...] = exact(exact(poly, present), poly)
            return carry

        lax.fori_loop(0, NS_ITERS - 1, step, 0)
        for k in members_of:
            factor[k][core] = exact(polynomial(land[k][...]), factor[k][core])
        return [
            send(factor[k].at[core], factor[k].at[core], factor_send.at[k], factor_recv.at[k], sibling)
            for k in members_of
        ]

    def apply(k):
        columns = weight[k].shape[2] * cores
        rate = muon_rate * muon_scale * math.sqrt(columns)

        def one(layer, carry):
            weight[k][layer] = weight[k][layer] * (1.0 - muon_rate * muon_shrink) - rate * exact(
                factor[k][layer], moment[k][layer]
            )
            return carry

        lax.fori_loop(0, cores, one, 0)
        store(1, k)

    def arrive(copies):
        for copy in copies:
            copy.wait_recv()

    if not counts:
        own.wait()
        for copy in moves:
            copy.wait_recv()
        half = planes // cores
        block = arrived.shape[2] // half
    sent = []
    for k in every:
        loads[0, k].wait()
        height = moment[k].shape[1]
        for layer in range(cores):
            if not counts:
                cut = [
                    arrived[
                        c * members + j,
                        layer * rows : (layer + 1) * rows,
                        i * block : (i + 1) * block,
                    ].astype(f32)
                    for c in range(cores)
                    for i in range(half)
                    for j in range(members)
                ]
                gradient = jnp.concatenate(cut, axis=1)
            elif len(plain[k]) == 1:
                gradient = plain[k][0][layer * height : (layer + 1) * height]
            elif len(plain[k][layer].shape) == 3:
                gradient = plain[k][layer][0].astype(f32)
                for plane in range(1, planes):
                    gradient = gradient + plain[k][layer][plane].astype(f32)
            else:
                gradient = plain[k][layer][...].astype(f32)
            moment[k][layer] = muon_decay * moment[k][layer] + gradient
        store(0, k)
        sent.append(gram_of(k))
    arrive(sent)
    crossed = orthogonal(every)
    sent += crossed
    arrive(crossed)
    for k in every:
        loads[1, k].wait()
        apply(k)
    for copy in moves + sent:
        copy.wait_send()
    for copy in stores:
        copy.wait()


def update(gradients, sides, moments, weights, ident):
    sizes = tuple(lax.axis_size(axis) for axis in EVERY)
    cores, planes, members = sizes
    vmem, dma = pltpu.VMEM, pltpu.SemaphoreType.DMA
    number = len(moments)
    shapes = [m.shape for m in moments]
    square = [(s[1], s[1]) for s in shapes]
    scratch = [vmem(s, f32) for s in shapes] * 2
    scratch += [vmem((cores,) + s, f32) for s in square]
    scratch += [vmem(s, f32) for s in square]
    scratch += [vmem((cores,) + s, f32) for s in square]
    scratch += [dma((2, number))] * 2 + [dma((number,))] * 4
    if not gradients:
        layers, rows, columns = shapes[0]
        piece = (
            cores * members,
            -(-layers * rows // 16) * 16,
            columns // (cores * members),
        )
        scratch += [vmem(piece, bf16)] * 2 + [dma((cores * members - 1,))] * 2 + [dma]
    here, there = pl.BlockSpec(memory_space=pltpu.VMEM), pl.BlockSpec(memory_space=pl.ANY)
    operands = sum(gradients, []) + sum(sides, [])
    return pl.pallas_call(
        partial(update_kernel, sizes, [len(g) for g in gradients]),
        out_shape=[jax.ShapeDtypeStruct(s, f32) for s in shapes] * 2,
        in_specs=[here] * len(operands) + [there] * (2 * number),
        out_specs=[there] * (2 * number),
        scratch_shapes=scratch,
        compiler_params=pltpu.CompilerParams(
            collective_id=ident, has_side_effects=True, vmem_limit_bytes=56 * 2**20
        ),
    )(*operands, *moments, *weights)


def padded(array, multiple=16):
    extra = -array.shape[-2] % multiple
    if extra == 0:
        return array
    return jnp.pad(array, [(0, 0)] * (array.ndim - 2) + [(0, extra), (0, 0)])


def rms_norm(values, norm_gain):
    return (
        values * lax.rsqrt(jnp.mean(values * values, axis=-1, keepdims=True) + norm_eps) * norm_gain
    )


def rope_tables(positions, head_dim):
    half_dim = head_dim // 2
    frequency = jnp.exp(
        jnp.arange(half_dim, dtype=jnp.float32) * (-2.0 * math.log(rope_base) / head_dim)
    )
    angles = positions.astype(jnp.float32)[:, None] * frequency[None, :]
    return (jnp.cos(angles), jnp.sin(angles))


def matmul(left, right):
    return jnp.dot(left, right, preferred_element_type=f32)


def body(
    inputs,
    cotangent,
    teacher,
    segments,
    valid_mask,
    w_qkv,
    w_out,
    w_gu,
    w_down,
    norm_gains,
    mom_qkv,
    mom_out,
    mom_gu,
    mom_down,
    gain_first,
    gain_second,
):
    cores = lax.axis_size("head")
    planes = lax.axis_size("zd")
    seq_devices = planes * PLANE
    core = lax.axis_index("head")
    seq_place = lax.axis_index("zd") * PLANE + lax.axis_index("tp")
    half_seqs, stretch_len = inputs.shape[:2]
    tokens = half_seqs * stretch_len
    all_seqs = half_seqs * cores
    seq_length = stretch_len * seq_devices
    reach = -(-WINDOW // stretch_len)
    key_len = (reach + 1) * stretch_len
    qkv_rows, qkv_cols = w_qkv.shape[1:]
    out_rows, out_cols = w_out.shape[1:]
    gu_rows = w_gu.shape[1]
    ff_block = w_down.shape[1]
    share = FF // (cores * PLANE)
    half_planes = planes // cores
    gain_cols = norm_gains.shape[-1]
    gain_len = gain_cols * seq_devices
    lanes = -(-gain_cols // 128) * 128

    packet = jnp.zeros((8, lanes), f32)
    packet = packet.at[:LAYERS, :gain_cols].set(norm_gains[:, 0].astype(bf16).astype(f32))
    packet = packet.at[LAYERS, 0].set(jnp.sum(valid_mask.astype(f32)))
    gu_pieces, w_mixed, w_project, packets, *later = start(
        w_gu, w_qkv, w_out, w_down, packet, 0
    )
    attn_weights, later, gathered_down = [w_mixed, w_project], later[:2], later[2:]
    gu_pieces = gu_pieces[:, : LAYERS * gu_rows].reshape(cores * PLANE, LAYERS, gu_rows, share)
    packets = packets.reshape(cores, seq_devices, 8, lanes)
    valid_count = jnp.sum(packets[:, :, LAYERS, 0])
    gain_rows = [
        packets[:, :, layer, :gain_cols].reshape(cores, gain_len) for layer in range(LAYERS)
    ]

    tiled = ff_block % 16 == 0

    def gate_up_rows(layer):
        pieces = gu_pieces[:, layer].reshape(2, PLANE * gu_rows, share)
        pieces = lax.all_gather(pieces, "zd", axis=0)
        if PLANE * gu_rows % 16:
            pieces = pieces.transpose(1, 0, 2, 3).reshape(1, 2, D, share)
        return pieces

    def down_rows(layer, gathered):
        if gathered:
            return gathered[0].reshape(1, planes * ff_block, out_cols)
        rows = w_down[layer : layer + 1].astype(bf16)
        return lax.all_gather(rows, "zd", axis=1, tiled=True)

    full = [(gate_up_rows(0), down_rows(0, gathered_down))] + [None] * (LAYERS - 1)

    own_places = seq_place * stretch_len + jnp.arange(stretch_len, dtype=jnp.int32)
    key_places = (seq_place - reach) * stretch_len + jnp.arange(key_len, dtype=jnp.int32)
    cosine_table, sine_table = rope_tables(own_places, HD)
    own_rows = lax.dynamic_slice_in_dim(segments, core * half_seqs, half_seqs, 0)
    own_segments = lax.dynamic_slice_in_dim(own_rows, seq_place * stretch_len, stretch_len, 1)
    padded_segments = jnp.pad(own_rows, ((0, 0), (reach * stretch_len, 0)), constant_values=-1)
    key_segments = lax.dynamic_slice_in_dim(padded_segments, seq_place * stretch_len, key_len, 1)
    spacing = own_places[:, None] - key_places[None, :]
    allowed = (spacing >= 0) & (spacing < WINDOW) & (key_places[None, :] >= 0)
    allowed = allowed[None] & (own_segments[:, :, None] == key_segments[:, None, :])

    tables = [jnp.tile(t, (half_seqs, 1)) for t in (cosine_table, sine_table)]
    bias = jnp.where(allowed, 0.0, -1e30).astype(f32)

    saved, previous = [], None
    base = inputs.reshape(tokens, D)
    for layer in range(LAYERS):
        weights = list(attn_weights)
        hidden, normed, mixed, queries, keyvals, attended, projected, half, normed_ffn = attn_forward(
            base, weights, gain_rows[layer], tables, bias, planes, reach, 3 + layer, previous
        )
        ffn_share = full[layer]
        if layer + 1 < LAYERS:
            gu_pieces, w_down, later, attended = lax.optimization_barrier(
                (gu_pieces, w_down, later, attended)
            )
            attn_weights = later_weights(later, w_qkv, w_out, layer + 1, 2 + 20 * layer)
            later_gate_up = gate_up_rows(layer + 1)
            normed_ffn, *attn_weights = lax.optimization_barrier((normed_ffn, *attn_weights))
        later_down = None
        if layer + 1 < LAYERS and tiled:
            later_down = w_down[layer + 1].astype(bf16)
        group_normed, whole_down, down_out, *gathered_down = ffn(
            normed_ffn, ffn_share, 5 + layer, None, later_down, planes
        )
        if layer + 1 < LAYERS:
            full[layer + 1] = (later_gate_up, down_rows(layer + 1, gathered_down))
        full[layer] = (weights, (ffn_share[0], whole_down))
        saved.append(
            (
                [hidden, mixed, queries, keyvals, projected, half],
                [normed, attended],
                group_normed,
                down_out,
            )
        )
        base, previous = half, (down_out, gain_rows[layer])

    output, post_ffn_back = jax.vjp(rms_norm, down_out, gain_rows[-1][1, D : 2 * D])
    output = base + output
    target_gap = output - teacher.reshape(tokens, D).astype(f32)
    valid_weight = valid_mask.astype(f32).reshape(tokens, 1)
    square_sum = jnp.sum(valid_weight * target_gap * target_gap)
    loss_weight = float(all_seqs * seq_length * D // 4)
    grad_hidden = (
        cotangent.reshape(tokens, D).astype(f32)
        + 2.0 * loss_weight / (valid_count * D) * valid_weight * target_gap
    )
    d_down, d_post_ffn = post_ffn_back(grad_hidden)
    d_down, d_post_ffn = d_down.astype(bf16), d_post_ffn[None]

    attn_acts = [None] * LAYERS
    down_grads = [None] * LAYERS
    gain_grads = [None] * LAYERS
    gu_sums = [None] * LAYERS
    for layer in reversed(range(LAYERS)):
        kept, (normed, attended), group_normed, _ = saved[layer]
        weights, ffn_share = full[layer]
        aside = later_down if tiled and layer + 1 < LAYERS else None
        d_normed_ffn, *grad_gu, grad_down = ffn(
            d_down, ffn_share, 9 + layer, group_normed, aside, planes
        )
        if aside is not None:
            *grad_gu, grad_down, down_grads[layer + 1] = *grad_gu, grad_down
        if tiled:
            later_down = grad_down.reshape(planes, ff_block, out_cols)
        else:
            down_grads[layer] = lax.psum_scatter(
                grad_down.reshape(planes * ff_block, out_cols),
                "zd",
                scatter_dimension=0,
                tiled=True,
            )
        gu_sums[layer] = [
            lax.psum_scatter(g, "zd", scatter_dimension=0, tiled=True) for g in grad_gu
        ]
        earlier = (saved[layer - 1][3], gain_rows[layer - 1]) if layer > 0 else None
        grad_hidden, d_mixed, d_projected, gain_grads[layer], *d_rest = attn_backward(
            d_normed_ffn,
            grad_hidden,
            kept,
            weights,
            gain_rows[layer],
            tables,
            bias,
            planes,
            reach,
            17 + layer,
            earlier,
        )
        gain_grads[layer] = gain_grads[layer].at[1:, D : 2 * D].set(d_post_ffn)
        if layer > 0:
            d_down, d_post_ffn = d_rest
        attn_acts[layer] = [normed, d_mixed, attended, d_projected]
    attn_acts[0][1], gu_sums[1:], down_grads[1:] = lax.optimization_barrier(
        (attn_acts[0][1], gu_sums[1:], down_grads[1:])
    )

    packet = jnp.stack(gain_grads, axis=1).reshape(cores, LAYERS, planes, PLANE, gain_cols)
    packet = packet.transpose(0, 3, 2, 1, 4)
    packet = jnp.pad(packet, [(0, 0)] * 3 + [(0, 8 - LAYERS), (0, lanes - gain_cols)])
    packet = packet.at[:, :, :, LAYERS, 0].set(square_sum)
    packet = packet.reshape(cores, PLANE, planes * 8, lanes)
    down = later_down if tiled else None
    grad_qkv, grad_out, packet, *summed_down = collect(sum(attn_acts, []), packet, down, 19)
    if tiled:
        (down_grads[0],) = summed_down
    mse_loss = packet[LAYERS, 0] / (valid_count * D)
    gain_grad = packet[:LAYERS, None, :gain_cols]

    new_qkv, new_out, new_down, moment_qkv, moment_out, moment_down = update(
        [[grad_qkv], [grad_out], down_grads],
        [],
        (mom_qkv, mom_out, mom_down),
        (w_qkv, w_out, w_down),
        15,
    )
    gu_sums, new_qkv = lax.optimization_barrier((gu_sums, new_qkv))
    new_gu, moment_gu = update([], [list(pair) for pair in gu_sums], (mom_gu,), (w_gu,), 16)
    new_weights = (new_qkv, new_out, new_gu, new_down)
    moments = (moment_qkv, moment_out, moment_gu, moment_down)
    gain_first_new = beta_one * gain_first + (1.0 - beta_one) * gain_grad
    gain_second_new = beta_two * gain_second + (1.0 - beta_two) * gain_grad * gain_grad
    gains_new = norm_gains - adam_rate * (gain_first_new / (1.0 - beta_one**STEP)) / (
        jnp.sqrt(gain_second_new / (1.0 - beta_two**STEP)) + adam_epsilon
    )
    return (
        mse_loss,
        output.reshape(inputs.shape),
        grad_hidden.reshape(inputs.shape),
        *new_weights,
        *moments,
        gains_new,
        gain_first_new,
        gain_second_new,
    )


def solution(mesh):
    cores, length = mesh.devices.shape
    split = Mesh(mesh.devices.reshape(cores, length // PLANE, PLANE), EVERY)
    stream = P("head", SEQ, None)
    matrix = P(None, SEQ, "head")
    gains = P(None, "head", SEQ)
    return jax.shard_map(
        body,
        mesh=split,
        in_specs=(stream, stream, stream, P(), P("head", SEQ))
        + (matrix,) * 4
        + (gains,)
        + (matrix,) * 4
        + (gains,) * 2,
        out_specs=(P(), stream, stream) + (matrix,) * 8 + (gains,) * 3,
        check_vma=False,
    )
```

```python
from functools import partial
import itertools
import math

import jax
import jax.numpy as jnp
from jax import lax
from jax.experimental import pallas as pl
from jax.experimental.pallas import tpu as pltpu
from jax.sharding import Mesh, PartitionSpec as P

D = 1152
HEADS = 4
HD = 256
FF = 6912
WINDOW = 512
LAYERS = 2
NS_ITERS = 5
STEP = 10
PLANE = 4

norm_eps = 1e-06
rope_base = 10000.0
newton_one = 3.4445
newton_two = -4.775
newton_three = 2.0315
muon_decay = 0.95
muon_rate = 0.15
muon_shrink = 0.01
muon_scale = 0.2
beta_one = 0.9
beta_two = 0.95
adam_rate = 0.7
adam_epsilon = 1e-08
finest_precision = lax.Precision.HIGHEST
MESH = pl.DeviceIdType.MESH
SEQ = ("zd", "tp")
GROUP = ("head", "tp")
EVERY = ("head", "zd", "tp")
bf16 = jnp.bfloat16
f32 = jnp.float32
LIGHT = pl.CostEstimate(flops=1, bytes_accessed=1, transcendentals=0)


def linear(places, sizes):
    index = 0
    for place, size in zip(places, sizes):
        index = index * size + place
    return index


def enter(partners):
    barrier = pltpu.get_barrier_semaphore()
    for partner in partners:
        pl.semaphore_signal(barrier, inc=1, device_id=partner, device_id_type=MESH)
    pl.semaphore_wait(barrier, len(partners))


class Spread:
    ORDER = ("zd", "tp", "head")

    def __init__(self, sizes, slots, send_sem, recv_sem, whole_z=False):
        self.size = dict(zip(EVERY, sizes))
        self.place = {axis: lax.axis_index(axis) for axis in EVERY}
        self.slots, self.send_sem, self.recv_sem = slots, send_sem, recv_sem
        self.held, self.sends, self.number = [(self.place, None)], [], 0
        if whole_z:
            self.held = [(dict(self.place, zd=z), None) for z in range(self.size["zd"])]
            self.ORDER = self.ORDER[1:]

    def partners(self):
        return [
            {axis: lax.rem(self.place[axis] + step, self.size[axis])}
            for axis in self.ORDER
            for step in range(1, self.size[axis])
        ]

    def stage(self, axis):
        arriving = []
        for where, arrivals in self.held:
            while arrivals:
                arrivals.pop().wait_recv()
            for step in range(1, self.size[axis]):
                to = lax.rem(self.place[axis] + step, self.size[axis])
                back = lax.rem(self.place[axis] - step + self.size[axis], self.size[axis])
                landing = []
                for k, slot in enumerate(self.slots):
                    ref = slot.at[tuple(where[name] for name in EVERY)]
                    copy = pltpu.make_async_remote_copy(
                        src_ref=ref,
                        dst_ref=ref,
                        send_sem=self.send_sem.at[k, self.number],
                        recv_sem=self.recv_sem.at[k, self.number],
                        device_id={axis: to},
                        device_id_type=MESH,
                    )
                    copy.start()
                    self.sends.append(copy)
                    landing.append(copy)
                self.number += 1
                arriving.append((dict(where, **{axis: back}), landing))
        self.held = self.held + arriving

    def finish(self):
        for _, arrivals in self.held:
            while arrivals:
                arrivals.pop().wait_recv()
        for copy in self.sends:
            copy.wait_send()


def start_kernel(sizes, *refs):
    cores, planes, members = sizes
    rest = list(refs)
    take = lambda number: [rest.pop(0) for _ in range(number)]
    gu, qkv, out, packet = take(4)
    gu_result, mixed, project, packets, qkv_later, out_later = take(6)
    packet_slots, qkv_slots, out_slots, send_sem, recv_sem = take(5)
    pieces, gu_send, gu_recv, gu_own, later_send, later_recv = take(6)
    qkv_low, out_low, later_own = take(3)
    gather = Spread(sizes, [packet_slots, qkv_slots, out_slots], send_sem, recv_sem)
    here = tuple(gather.place[name] for name in EVERY)
    core, zd, tp = here
    group = []
    for step in range(1, cores * members):
        far = lax.rem(core + step // members, cores), lax.rem(tp + step % members, members)
        group.append((dict(zip(GROUP, far)), linear(far, (cores, members))))
    enter(gather.partners() + [device for device, _ in group])
    packet_slots[here] = packet[...]

    def place_rows(source, layer, slot, index):
        rows = source.shape[1]
        slot[index + (slice(0, rows),)] = source[layer].astype(bf16)
        if slot.shape[-2] > rows:
            slot[index + (slice(rows, slot.shape[-2]),)] = jnp.zeros(
                (slot.shape[-2] - rows, slot.shape[-1]), bf16
            )

    for source, slot in ((qkv, qkv_slots), (out, out_slots)):
        place_rows(source, 0, slot, here)
    gather.stage("zd")
    moves = []

    def along_z(source, target, sends, recvs):
        for step in range(1, planes):
            copy = pltpu.make_async_remote_copy(
                src_ref=source,
                dst_ref=target,
                send_sem=sends.at[step],
                recv_sem=recvs.at[step],
                device_id={"zd": lax.rem(zd + step, planes)},
                device_id_type=MESH,
            )
            copy.start()
            moves.append(copy)

    for k, (source, low, slot) in enumerate(
        ((qkv, qkv_low, qkv_later), (out, out_low, out_later))
    ):
        for layer in range(1, source.shape[0]):
            place_rows(source, layer, low, (layer - 1,))
            target = slot.at[layer - 1, zd]
            along_z(
                low.at[layer - 1], target, later_send.at[k, layer], later_recv.at[k, layer]
            )
            own = pltpu.make_async_copy(low.at[layer - 1], target, later_own.at[k, layer])
            own.start()
            moves.append(own)
    layers, rows, columns = gu.shape
    block = columns // (planes * members)
    half = planes // cores
    for c in range(cores):
        for j in range(members):
            for i in range(layers):
                cut = [
                    gu[i, :, pl.ds(((c * half + k) * members + j) * block, block)]
                    for k in range(half)
                ]
                value = jnp.concatenate(cut, axis=1) if half > 1 else cut[0]
                pieces[c * members + j, i * rows : (i + 1) * rows] = value.astype(bf16)
    if pieces.shape[1] > layers * rows:
        for piece in range(cores * members):
            pieces[piece, layers * rows :] = jnp.zeros(
                (pieces.shape[1] - layers * rows, pieces.shape[2]), bf16
            )
    me = linear((core, tp), (cores, members))
    for step, (device, index) in enumerate(group):
        copy = pltpu.make_async_remote_copy(
            src_ref=pieces.at[index],
            dst_ref=gu_result.at[me],
            send_sem=gu_send.at[step],
            recv_sem=gu_recv.at[step],
            device_id=device,
            device_id_type=MESH,
        )
        copy.start()
        moves.append(copy)
    own = pltpu.make_async_copy(pieces.at[me], gu_result.at[me], gu_own)
    own.start()
    moves.append(own)
    gather.stage("tp")
    gather.stage("head")
    gather.finish()
    side_by_side(sizes, (qkv_slots, out_slots), (mixed, project))
    packets[...] = packet_slots[...]
    for copy in moves:
        copy.wait()


def side_by_side(sizes, slots, results):
    cores, planes, members = sizes
    for slot, result in zip(slots, results):
        columns = slot.shape[4]
        rows = result.shape[0] // (planes * members)
        for h, z, t in itertools.product(range(cores), range(planes), range(members)):
            row = (z * members + t) * rows
            result[row : row + rows, h * columns : (h + 1) * columns] = slot[h, z, t, :rows]


def later_kernel(sizes, layer, qkv, out, mixed, project, qkv_slots, out_slots, send_sem, recv_sem):
    gather = Spread(sizes, [qkv_slots, out_slots], send_sem, recv_sem, whole_z=True)
    core, _, tp = (gather.place[name] for name in EVERY)
    enter(gather.partners())
    for source, slot in ((qkv, qkv_slots), (out, out_slots)):
        for z in range(sizes[1]):
            slot[core, z, tp] = source[layer - 1, z]
    gather.stage("tp")
    gather.stage("head")
    gather.finish()
    side_by_side(sizes, (qkv_slots, out_slots), (mixed, project))


def whole_shapes(sizes, tall, matrices):
    slots = [pltpu.VMEM(sizes + (t, w.shape[2]), bf16) for t, w in zip(tall, matrices)]
    outs = [
        jax.ShapeDtypeStruct((w.shape[1] * sizes[1] * sizes[2], w.shape[2] * sizes[0]), bf16)
        for w in matrices
    ]
    return slots, outs


def start(w_gu, w_qkv, w_out, packet, ident):
    sizes = tuple(lax.axis_size(axis) for axis in EVERY)
    cores, planes, members = sizes
    vmem, dma = pltpu.VMEM, pltpu.SemaphoreType.DMA
    here, there = pl.BlockSpec(memory_space=pltpu.VMEM), pl.BlockSpec(memory_space=pl.ANY)
    shape = jax.ShapeDtypeStruct
    tall = [-(-w.shape[1] // 16) * 16 for w in (w_qkv, w_out)]
    slots, outs = whole_shapes(sizes, tall, (w_qkv, w_out))
    layers, rows, columns = w_gu.shape
    piece = (
        cores * members,
        -(-layers * rows // 16) * 16,
        columns // (cores * members),
    )
    later = [
        shape((layers - 1, planes, t, w.shape[2]), bf16) for t, w in zip(tall, (w_qkv, w_out))
    ]
    operands = [w_gu, w_qkv, w_out, packet]
    outs = [shape(piece, bf16)] + outs + [shape(sizes + packet.shape, f32)] + later
    out_specs = [there] + [here] * 3 + [there] * 2
    moves = math.prod(sizes) - 1
    scratch = [vmem(sizes + packet.shape, f32)] + slots + [dma((3, moves))] * 2
    scratch += [vmem(piece, bf16), dma((cores * members - 1,)), dma((cores * members - 1,)), dma]
    scratch += [dma((2, layers, planes))] * 2
    scratch += [
        vmem((layers - 1, t, w.shape[2]), bf16) for t, w in zip(tall, (w_qkv, w_out))
    ] + [dma((2, layers))]
    return pl.pallas_call(
        partial(start_kernel, sizes),
        out_shape=outs,
        in_specs=[here] * len(operands),
        out_specs=out_specs,
        scratch_shapes=scratch,
        compiler_params=pltpu.CompilerParams(
            collective_id=ident, has_side_effects=True, vmem_limit_bytes=56 * 2**20
        ),
    )(*operands)


def later_weights(gathered, w_qkv, w_out, layer, ident):
    sizes = tuple(lax.axis_size(axis) for axis in EVERY)
    slots, outs = whole_shapes(sizes, [g.shape[2] for g in gathered], (w_qkv, w_out))
    here = pl.BlockSpec(memory_space=pltpu.VMEM)
    moves = math.prod(sizes) - sizes[1]
    return pl.pallas_call(
        partial(later_kernel, sizes, layer),
        out_shape=outs,
        in_specs=[here] * 2,
        out_specs=[here] * 2,
        scratch_shapes=slots + [pltpu.SemaphoreType.DMA((2, moves))] * 2,
        compiler_params=pltpu.CompilerParams(
            collective_id=ident, has_side_effects=True, vmem_limit_bytes=48 * 2**20
        ),
    )(*gathered)


def by_rows(rows, work, step=16):
    @pl.loop(0, rows // step)
    def _(index):
        work(pl.ds(pl.multiple_of(index * step, step), step))


def collect_kernel(sizes, layers, tiled, *refs):
    cores, planes, members = sizes
    rest = list(refs)
    take = lambda number: [rest.pop(0) for _ in range(number)]
    acts, packet = take(4 * layers), take(1)[0]
    if tiled:
        (down,) = take(1)
    results = take(3)
    if tiled:
        (down_result,) = take(1)
    far, halves = take(4 * layers), take(2 * layers)
    packet_land = rest.pop(0)
    pieces, plane_lands, totals, z_sums, z_lands = (take(3) for _ in range(5))
    act_send, act_recv, packet_send, packet_recv = take(4)
    tp_send, tp_recv, z_send, z_recv = take(4)
    core, zd, tp = (lax.axis_index(axis) for axis in EVERY)
    sibling = {"head": 1 - core}
    enter(
        [sibling]
        + [{"tp": lax.rem(tp + step, members)} for step in range(1, members)]
        + [{"zd": lax.rem(zd + step, planes)} for step in range(1, planes)]
    )
    sends = []

    def send(src, dst, send_sem, recv_sem, device):
        copy = pltpu.make_async_remote_copy(
            src_ref=src,
            dst_ref=dst,
            send_sem=send_sem,
            recv_sem=recv_sem,
            device_id=device,
            device_id_type=MESH,
        )
        copy.start()
        sends.append(copy)
        return copy

    if tiled:
        down_land, down_send, down_recv, down_own = take(4)
        down_moves = []
        for step in range(1, planes):
            there = lax.rem(zd + step, planes)
            down_moves.append(
                send(
                    down.at[there],
                    down_land.at[step],
                    down_send.at[step],
                    down_recv.at[step],
                    {"zd": there},
                )
            )
        down_stay = pltpu.make_async_copy(down.at[zd], down_land.at[0], down_own)
        down_stay.start()
    for k in range(2 * layers):
        grad, half = acts[2 * k + 1], halves[k]
        width = half.shape[2]
        for h in range(cores):
            half[h] = grad[:, h * width : (h + 1) * width]
    moves = []
    for k in range(2 * layers):
        moves.append(
            send(acts[2 * k], far[2 * k], act_send.at[2 * k], act_recv.at[2 * k], sibling)
        )
        moves.append(
            send(
                halves[k].at[1 - core],
                far[2 * k + 1],
                act_send.at[2 * k + 1],
                act_recv.at[2 * k + 1],
                sibling,
            )
        )
    gains = send(packet.at[1 - core], packet_land, packet_send, packet_recv, sibling)
    plane_moves, z_moves = {}, {}
    for kind in range(3):
        piece = pieces[kind]
        if kind < 2:
            for layer in range(layers):
                k = 2 * layer + kind
                near = lax.dot_general(
                    acts[2 * k][...], halves[k][core], ALONG, preferred_element_type=f32
                )
                moves[2 * k].wait_recv()
                moves[2 * k + 1].wait_recv()
                value = near + lax.dot_general(
                    far[2 * k][...], far[2 * k + 1][...], ALONG, preferred_element_type=f32
                )
                value = value.astype(bf16)
                rows = value.shape[0] // (planes * members)
                slab = piece.shape[1] // planes
                for z, t in itertools.product(range(planes), range(members)):
                    at = (z * members + t) * rows
                    to = z * slab + layer * rows
                    piece[t, to : to + rows] = value[at : at + rows]
            if slab > layers * rows:
                for z, t in itertools.product(range(planes), range(members)):
                    piece[t, z * slab + layers * rows : (z + 1) * slab] = jnp.zeros(
                        (slab - layers * rows, piece.shape[2]), bf16
                    )
        else:
            gains.wait_recv()
            piece[...] = packet[core] + packet_land[...]
        for step in range(1, members):
            there = lax.rem(tp + step, members)
            plane_moves[kind, step] = send(
                piece.at[there],
                plane_lands[kind].at[step],
                tp_send.at[kind, step],
                tp_recv.at[kind, step],
                {"tp": there},
            )
    for kind in range(3):
        for step in range(1, members):
            plane_moves[kind, step].wait_recv()
        piece, total, land, result = pieces[kind], totals[kind], plane_lands[kind], results[kind]
        stride = 8 if land.dtype == f32 else 16

        def gather_plane(rows):
            value = piece[tp, rows].astype(f32)
            for step in range(1, members):
                value = value + land[step, rows].astype(f32)
            total[rows] = value

        by_rows(total.shape[0], gather_plane, stride)
        height = result.shape[0]
        z_sum = z_sums[kind]
        for step in range(1, planes):
            there = lax.rem(zd + step, planes)

            def round_off(rows):
                at = pl.multiple_of(there * height + rows.start, stride)
                z_sum[step, rows] = total[pl.ds(at, rows.size)].astype(z_sum.dtype)

            by_rows(height, round_off, stride)
            z_moves[kind, step] = send(
                z_sum.at[step],
                z_lands[kind].at[step],
                z_send.at[kind, step],
                z_recv.at[kind, step],
                {"zd": there},
            )
    for kind in range(3):
        for step in range(1, planes):
            z_moves[kind, step].wait_recv()
        total, land, result = totals[kind], z_lands[kind], results[kind]
        height = result.shape[0]
        stride = 8 if land.dtype == f32 else 16

        def gather_z(rows):
            at = pl.multiple_of(zd * height + rows.start, stride)
            value = total[pl.ds(at, rows.size)]
            for step in range(1, planes):
                value = value + land[step, rows].astype(f32)
            result[rows] = value

        by_rows(height, gather_z, stride)
    if tiled:
        down_stay.wait()
        for copy in down_moves:
            copy.wait_recv()

        def gather_down(rows):
            value = down_land[0, rows].astype(f32)
            for step in range(1, planes):
                value = value + down_land[step, rows].astype(f32)
            down_result[rows] = value

        by_rows(down_result.shape[0], gather_down)
    for copy in sends:
        copy.wait_send()


def collect(acts, packet, down, ident):
    sizes = tuple(lax.axis_size(axis) for axis in EVERY)
    cores, planes, members = sizes
    layers = len(acts) // 4
    vmem, dma = pltpu.VMEM, pltpu.SemaphoreType.DMA
    tokens = acts[0].shape[0]
    halves = [acts[2 * k + 1].shape[1] // cores for k in range(2 * layers)]
    slabs = []
    for kind in range(2):
        rows = layers * acts[2 * kind].shape[1] // (planes * members)
        slabs.append((-(-rows // 16) * 16, halves[kind], bf16))
    slabs.append((packet.shape[2] // planes, packet.shape[3], f32))
    far = []
    for k in range(2 * layers):
        far += [vmem(acts[2 * k].shape, bf16), vmem((tokens, halves[k]), bf16)]
    scratch = far + [vmem((cores, tokens, width), bf16) for width in halves]
    scratch += [vmem(packet.shape[1:], f32)]
    scratch += [vmem((members, planes * r, c), kind) for r, c, kind in slabs] * 2
    scratch += [vmem((planes * r, c), f32) for r, c, _ in slabs]
    scratch += [vmem((planes, r, c), kind) for r, c, kind in slabs] * 2
    scratch += [dma((4 * layers,))] * 2 + [dma] * 2
    scratch += [dma((3, members))] * 2 + [dma((3, planes))] * 2
    here = pl.BlockSpec(memory_space=pltpu.VMEM)
    operands = [*acts, packet]
    outs = [jax.ShapeDtypeStruct((r, c), f32) for r, c, _ in slabs]
    in_specs = [here] * len(operands)
    if down is not None:
        operands, in_specs = operands + [down], in_specs + [pl.BlockSpec(memory_space=pl.ANY)]
        outs += [jax.ShapeDtypeStruct(down.shape[1:], f32)]
        scratch += [vmem(down.shape, bf16), dma((planes,)), dma((planes,)), dma]
    return pl.pallas_call(
        partial(collect_kernel, sizes, layers, down is not None),
        out_shape=outs,
        in_specs=in_specs,
        out_specs=[here] * len(outs),
        scratch_shapes=scratch,
        cost_estimate=LIGHT,
        compiler_params=pltpu.CompilerParams(
            collective_id=ident, has_side_effects=True, vmem_limit_bytes=56 * 2**20
        ),
    )(*operands)


def neighbours(planes, reach, sign):
    total = planes * PLANE
    place = linear([lax.axis_index("zd"), lax.axis_index("tp")], (planes, PLANE))

    def at(distance):
        there = lax.rem(place + distance + total, total)
        return {"zd": lax.div(there, PLANE), "tp": lax.rem(there, PLANE)}

    steps = range(1, reach + 1)
    return [at(sign * step) for step in steps], [at(-sign * step) for step in steps]


def inverse_rms(values):
    return lax.rsqrt(jnp.mean(values * values, axis=-1, keepdims=True) + norm_eps)


def rms_back(gradient, values, gain):
    inverse = inverse_rms(values)
    scaled = gradient * gain
    shared = jnp.mean(scaled * values, axis=-1, keepdims=True) * (inverse * inverse)
    return inverse * (scaled - values * shared), jnp.sum(
        gradient * values * inverse, axis=0, keepdims=True
    )


def turn(values, cosine, sine):
    half = values.shape[-1] // 2
    lower, upper = values[:, :half], values[:, half:]
    return jnp.concatenate(
        [lower * cosine - upper * sine, upper * cosine + lower * sine], axis=-1
    )


def soft_rows(query, keys, bias):
    scores = lax.dot_general(query, keys, ACROSS, preferred_element_type=f32)
    scores = scores * (1.0 / math.sqrt(HD)) + bias
    raised = jnp.exp(scores - jnp.max(scores, axis=-1, keepdims=True))
    return raised / jnp.sum(raised, axis=-1, keepdims=True)


def attn_forward_kernel(planes, reach, chained, *refs):
    rest = list(refs)
    take = lambda number: [rest.pop(0) for _ in range(number)]
    if chained:
        base, down, before = take(3)
    else:
        (base,) = take(1)
    w_mixed, w_project, gains, cosine, sine, bias = take(6)
    hidden, normed, mixed, queries, keyvals_out = take(5)
    attended, projected, hidden_half, normed_ffn = take(4)
    keyvals, send_sem, recv_sem, save_sem = take(4)
    seqs, stretch, key_len = bias.shape
    devices, sources = neighbours(planes, reach, 1)
    enter(devices + sources)
    value = base[...].astype(f32)
    if chained:
        late = down[...]
        value = value + late * inverse_rms(late) * before[1:2, D : 2 * D]
    hidden[...] = value
    low = (value * inverse_rms(value) * gains[0:1, :D]).astype(bf16)
    normed[...] = low
    mixed[...] = matmul(low, w_mixed[...])
    key = mixed[:, HEADS * HD : HEADS * HD + HD]
    key = turn(key * inverse_rms(key) * gains[1:2, 2 * D :], cosine[...], sine[...]).astype(bf16)
    late_values = mixed[:, HEADS * HD + HD :].astype(bf16)
    copies = []
    for i in range(seqs):
        rows = slice(i * stretch, (i + 1) * stretch)
        keyvals[i, reach * stretch :, :HD] = key[rows]
        keyvals[i, reach * stretch :, HD:] = late_values[rows]
        for step, device in enumerate(devices):
            copy = pltpu.make_async_remote_copy(
                src_ref=keyvals.at[i, pl.ds(reach * stretch, stretch)],
                dst_ref=keyvals.at[i, pl.ds((reach - 1 - step) * stretch, stretch)],
                send_sem=send_sem.at[i, step],
                recv_sem=recv_sem.at[i, step],
                device_id=device,
                device_id_type=MESH,
            )
            copy.start()
            copies.append(copy)
    for h in range(HEADS):
        columns = slice(h * HD, (h + 1) * HD)
        query = mixed[:, columns]
        query = turn(query * inverse_rms(query) * gains[0:1, 2 * D :], cosine[...], sine[...])
        queries[:, columns] = query.astype(bf16)
    for copy in copies:
        copy.wait_recv()
    save = pltpu.make_async_copy(keyvals, keyvals_out, save_sem)
    save.start()
    for i in range(seqs):
        rows = slice(i * stretch, (i + 1) * stretch)
        for h in range(HEADS):
            columns = slice(h * HD, (h + 1) * HD)
            soft = soft_rows(queries[rows, columns], keyvals[i, :, :HD], bias[i])
            attended[rows, columns] = matmul(soft.astype(bf16), keyvals[i, :, HD:]).astype(bf16)
    out = matmul(attended[...], w_project[...])
    projected[...] = out
    half = hidden[...] + out * inverse_rms(out) * gains[0:1, D : 2 * D]
    hidden_half[...] = half
    normed_ffn[...] = (half * inverse_rms(half) * gains[1:2, :D]).astype(bf16)
    for copy in copies:
        copy.wait_send()
    save.wait()


def attn_forward(base, weights, gains, tables, bias, planes, reach, ident, earlier=None):
    tokens = base.shape[0]
    seqs, _, key_len = bias.shape
    shape = jax.ShapeDtypeStruct
    operands = [base] + list(earlier or []) + list(weights) + [gains, *tables, bias]
    here, there = pl.BlockSpec(memory_space=pltpu.VMEM), pl.BlockSpec(memory_space=pl.ANY)
    dma = pltpu.SemaphoreType.DMA
    return pl.pallas_call(
        partial(attn_forward_kernel, planes, reach, earlier is not None),
        out_shape=[
            shape((tokens, D), f32),
            shape((tokens, D), bf16),
            shape((tokens, weights[0].shape[1]), f32),
            shape((tokens, HEADS * HD), bf16),
            shape((seqs, key_len, 2 * HD), bf16),
            shape((tokens, HEADS * HD), bf16),
            shape((tokens, D), f32),
            shape((tokens, D), f32),
            shape((tokens, D), bf16),
        ],
        in_specs=[here] * len(operands),
        out_specs=[here] * 4 + [there] + [here] * 4,
        scratch_shapes=[
            pltpu.VMEM((seqs, key_len, 2 * HD), bf16),
            dma((seqs, reach)),
            dma((seqs, reach)),
            dma,
        ],
        compiler_params=pltpu.CompilerParams(
            collective_id=ident, has_side_effects=True, vmem_limit_bytes=56 * 2**20
        ),
    )(*operands)


def attn_backward_kernel(planes, reach, chained, *refs):
    rest = list(refs)
    take = lambda number: [rest.pop(0) for _ in range(number)]
    d_ffn, above, hidden, mixed, queries, keyvals, projected, hidden_half = take(8)
    w_mixed, w_project, gains, cosine, sine, bias = take(6)
    if chained:
        down, before = take(2)
    grad, d_mixed, d_projected, gain_grads = take(4)
    if chained:
        d_down, d_post = take(2)
    d_keyvals, outgoing, incoming, d_attended, send_sem, recv_sem = take(6)
    seqs, stretch, key_len = bias.shape
    devices, sources = neighbours(planes, reach, -1)
    enter(devices + sources)
    scale = 1.0 / math.sqrt(HD)
    part, gain_row = rms_back(d_ffn[...], hidden_half[...], gains[1:2, :D])
    gain_grads[1:2, :D] = gain_row
    gain_grads[1:2, D : 2 * D] = jnp.zeros((1, D), f32)
    grad[...] = part + above[...]
    part, gain_row = rms_back(grad[...], projected[...], gains[0:1, D : 2 * D])
    gain_grads[0:1, D : 2 * D] = gain_row
    low = part.astype(bf16)
    d_projected[...] = low
    d_attended[...] = lax.dot_general(
        low, w_project[...], ACROSS, preferred_element_type=f32
    ).astype(bf16)
    query_gain = jnp.zeros((1, HD), f32)
    for i in range(seqs):
        rows = slice(i * stretch, (i + 1) * stretch)
        d_keys = d_values = None
        for h in range(HEADS):
            columns = slice(h * HD, (h + 1) * HD)
            query, d_out = queries[rows, columns], d_attended[rows, columns]
            keys, values = keyvals[i, :, :HD], keyvals[i, :, HD:]
            soft = soft_rows(query, keys, bias[i])
            d_soft = lax.dot_general(d_out, values, ACROSS, preferred_element_type=f32)
            total = jnp.sum(soft * d_soft, axis=-1, keepdims=True)
            d_scores = (soft * (d_soft - total)).astype(bf16)
            key_part = lax.dot_general(d_scores, query, ALONG, preferred_element_type=f32)
            value_part = lax.dot_general(
                soft.astype(bf16), d_out, ALONG, preferred_element_type=f32
            )
            d_keys = key_part if d_keys is None else d_keys + key_part
            d_values = value_part if d_values is None else d_values + value_part
            d_query = matmul(d_scores, keys) * scale
            d_query = turn(d_query, cosine[rows], -sine[rows])
            part, gain_row = rms_back(d_query, mixed[rows, columns], gains[0:1, 2 * D :])
            query_gain = query_gain + gain_row
            d_mixed[rows, columns] = part.astype(bf16)
        d_keyvals[i, :, :HD] = d_keys * scale
        d_keyvals[i, :, HD:] = d_values
    gain_grads[0:1, 2 * D :] = query_gain
    outgoing[...] = d_keyvals[:, : reach * stretch].astype(bf16)
    copies = []
    for i in range(seqs):
        for step, device in enumerate(devices):
            copy = pltpu.make_async_remote_copy(
                src_ref=outgoing.at[i, pl.ds((reach - 1 - step) * stretch, stretch)],
                dst_ref=incoming.at[i, step],
                send_sem=send_sem.at[i, step],
                recv_sem=recv_sem.at[i, step],
                device_id=device,
                device_id_type=MESH,
            )
            copy.start()
            copies.append(copy)
    for copy in copies:
        copy.wait_recv()
    key_gain = jnp.zeros((1, HD), f32)
    for i in range(seqs):
        rows = slice(i * stretch, (i + 1) * stretch)
        own = d_keyvals[i, reach * stretch :]
        for step in range(reach):
            own = own + incoming[i, step].astype(f32)
        d_key = turn(own[:, :HD], cosine[rows], -sine[rows])
        part, gain_row = rms_back(
            d_key, mixed[rows, HEADS * HD : HEADS * HD + HD], gains[1:2, 2 * D :]
        )
        key_gain = key_gain + gain_row
        d_mixed[rows, HEADS * HD : HEADS * HD + HD] = part.astype(bf16)
        d_mixed[rows, HEADS * HD + HD :] = own[:, HD:].astype(bf16)
    gain_grads[1:2, 2 * D :] = key_gain
    d_normed = lax.dot_general(d_mixed[...], w_mixed[...], ACROSS, preferred_element_type=f32)
    part, gain_row = rms_back(d_normed, hidden[...], gains[0:1, :D])
    gain_grads[0:1, :D] = gain_row
    grad[...] = grad[...] + part
    if chained:
        part, gain_row = rms_back(grad[...], down[...], before[1:2, D : 2 * D])
        d_down[...] = part.astype(bf16)
        d_post[...] = gain_row
    for copy in copies:
        copy.wait_send()


def attn_backward(
    d_ffn, above, kept, weights, gains, tables, bias, planes, reach, ident, earlier=None
):
    tokens = above.shape[0]
    seqs, stretch, key_len = bias.shape
    shape = jax.ShapeDtypeStruct
    operands = [d_ffn, above, *kept, *weights, gains, *tables, bias] + list(earlier or [])
    outs = [
        shape((tokens, D), f32),
        shape((tokens, weights[0].shape[1]), bf16),
        shape((tokens, D), bf16),
        shape(gains.shape, f32),
    ]
    if earlier is not None:
        outs += [shape((tokens, D), bf16), shape((1, D), f32)]
    here = pl.BlockSpec(memory_space=pltpu.VMEM)
    vmem, dma = pltpu.VMEM, pltpu.SemaphoreType.DMA
    return pl.pallas_call(
        partial(attn_backward_kernel, planes, reach, earlier is not None),
        out_shape=outs,
        in_specs=[here] * len(operands),
        out_specs=[here] * len(outs),
        scratch_shapes=[
            vmem((seqs, key_len, 2 * HD), f32),
            vmem((seqs, reach * stretch, 2 * HD), bf16),
            vmem((seqs, reach, stretch, 2 * HD), bf16),
            vmem((tokens, HEADS * HD), bf16),
            dma((seqs, reach)),
            dma((seqs, reach)),
        ],
        compiler_params=pltpu.CompilerParams(
            collective_id=ident, has_side_effects=True, vmem_limit_bytes=56 * 2**20
        ),
    )(*operands)


GELU_SLOPE = math.sqrt(2.0 / math.pi)
GELU_CUBE = 0.044715
ACROSS = (((1,), (1,)), ((), ()))
ALONG = (((0,), (0,)), ((), ()))


class Plane:
    def __init__(self, own, bufs, sems):
        self.own = own
        self.rows, self.partial, self.other, self.lands, self.sums, self.arrived = bufs
        self.x_send, self.x_recv, self.f_send, self.f_recv = sems[:4]
        self.c_send, self.c_recv, self.p_send, self.p_recv, self.first = sems[4:]
        self.tp = lax.axis_index("tp")
        self.sibling = {"head": 1 - lax.axis_index("head")}

    def member(self, m):
        tp = self.tp
        upper = lax.rem(lax.div(tp, 2) + lax.div(m, 2), 2)
        lower = lax.rem(lax.rem(tp, 2) + lax.rem(m, 2), 2)
        return {"tp": upper * 2 + lower}

    def remote(self, src, dst, send, recv, device):
        return pltpu.make_async_remote_copy(
            src_ref=src,
            dst_ref=dst,
            send_sem=send,
            recv_sem=recv,
            device_id=device,
            device_id_type=MESH,
        )

    def push(self, m):
        return self.remote(
            self.own, self.rows.at[0, m], self.x_send.at[m], self.x_recv.at[m], self.member(m)
        )

    def keep(self):
        return pltpu.make_async_copy(self.own, self.rows.at[0, 0], self.first)

    def forward(self, m):
        return self.remote(
            self.rows.at[0, m],
            self.rows.at[1, m],
            self.f_send.at[m],
            self.f_recv.at[m],
            self.sibling,
        )

    def cross(self, m):
        return self.remote(
            self.other.at[m], self.lands.at[m], self.c_send.at[m], self.c_recv.at[m], self.sibling
        )

    def home(self, m):
        return self.remote(
            self.sums.at[m],
            self.arrived.at[m],
            self.p_send.at[m],
            self.p_recv.at[m],
            self.member(m),
        )

    def begin(self):
        self.keep().start()
        enter([self.sibling] + [self.member(jnp.int32(m)) for m in range(1, PLANE)])
        for m in range(1, PLANE - 1):
            self.push(jnp.int32(m)).start()

    def push_far(self):
        for near in range(1, PLANE - 1):
            self.push(jnp.int32(near)).wait_send()
        self.push(jnp.int32(PLANE - 1)).start()

    def work(self, compute, sent_far=False):
        def settle(m):
            self.cross(m).wait_recv()

            def add(rows):
                value = self.partial[m, rows] + self.lands[m, rows].astype(f32)
                self.sums[m, rows] = value.astype(bf16)

            by_rows(self.partial.shape[1], add)
            self.home(m).start()

        def step(m, carry):
            @pl.when(m == 0)
            def _():
                self.keep().wait()

            @pl.when(m > 0)
            def _():
                self.push(m).wait_recv()

            self.forward(m).start()
            self.partial[m] = compute(0, m)
            self.forward(m).wait_recv()
            self.other[m] = compute(1, m).astype(bf16)
            self.cross(m).start()

            if not sent_far:

                @pl.when(m == 0)
                def _():
                    self.push_far()

            @pl.when(m >= 2)
            def _():
                settle(m - 1)

            return carry

        lax.fori_loop(0, PLANE, step, 0)
        settle(jnp.int32(PLANE - 1))

    def finish(self, result):
        self.cross(jnp.int32(0)).wait_recv()
        for m in range(1, PLANE):
            self.home(jnp.int32(m)).wait_recv()

        def add(rows):
            value = self.partial[0, rows] + self.lands[0, rows].astype(f32)
            for m in range(1, PLANE):
                value = value + self.arrived[m, rows].astype(f32)
            result[rows] = value

        by_rows(result.shape[0], add)
        for m in range(PLANE):
            m = jnp.int32(m)
            self.forward(m).wait_send()
            self.cross(m).wait_send()
        self.push(jnp.int32(PLANE - 1)).wait_send()
        for m in range(1, PLANE):
            self.home(jnp.int32(m)).wait_send()


def gate_up_copies(gu_ref, gate_up, sem):
    blocks = gu_ref.shape[0]
    rows = gate_up.shape[1] // blocks
    return [
        pltpu.make_async_copy(
            gu_ref.at[block, part],
            gate_up.at[part, pl.ds(block * rows, rows)],
            sem.at[2 * block + part],
        )
        for block in range(blocks)
        for part in range(2)
    ]


def ffn_forward_kernel(own, gu_ref, halves_ref, group, saved_down, result, *scratch):
    rows, gate_up, down = scratch[:3]
    plane = Plane(own, (rows,) + scratch[3:8], scratch[8:17])
    weight_sem, group_sem, halves, half_send, half_recv, half_own, save_sem = scratch[17:]
    core = lax.axis_index("head")
    share, width = halves.shape[1:]
    copies = gate_up_copies(gu_ref, gate_up, weight_sem)
    copies.append(
        pltpu.make_async_copy(
            halves_ref.at[0, pl.ds(pl.multiple_of(core * share, 16), share)],
            halves.at[core],
            half_own,
        )
    )
    for copy in copies:
        copy.start()
    plane.begin()
    half = plane.remote(
        halves_ref.at[0, pl.ds(pl.multiple_of((1 - core) * share, 16), share)],
        halves.at[core],
        half_send,
        half_recv,
        plane.sibling,
    )
    half.start()
    for copy in copies:
        copy.wait()
    pltpu.make_async_remote_copy(
        src_ref=halves_ref.at[0, pl.ds(pl.multiple_of((1 - core) * share, 16), share)],
        dst_ref=halves.at[1 - core],
        send_sem=half_send,
        recv_sem=half_recv,
        device_id=plane.sibling,
        device_id_type=MESH,
    ).wait_recv()

    def join(at):
        down[at] = jnp.concatenate([halves[h, at] for h in range(2)], axis=1)

    by_rows(share, join, 32)
    keep_down = pltpu.make_async_copy(down, saved_down, save_sem)
    keep_down.start()

    def compute(side, m):
        tokens = rows[side, m]
        gate = matmul(tokens, gate_up[0])
        up = matmul(tokens, gate_up[1])
        bend = jnp.tanh(GELU_SLOPE * (gate + GELU_CUBE * (gate * gate * gate)))
        inner = (0.5 * gate * (1.0 + bend) * up).astype(bf16)
        return matmul(inner, down[...])

    plane.work(compute)
    save = pltpu.make_async_copy(rows, group, group_sem)
    save.start()
    plane.finish(result)
    save.wait()
    keep_down.wait()
    half.wait_send()


def ffn_backward_kernel(
    own, group, gu_ref, down_ref, result, grad_gate, grad_up, grad_down, *scratch
):
    rows, gate_up, down = scratch[:3]
    plane = Plane(own, (rows,) + scratch[3:8], scratch[8:17])
    weight_sem, group_sem, saved, d_gate, d_up, inner = scratch[17:23]
    down_sem, turned, down_halves, half_send, half_recv, half_own = scratch[23:]
    core = lax.axis_index("head")
    copies = gate_up_copies(gu_ref, gate_up, weight_sem)
    copies.append(pltpu.make_async_copy(down_ref, down, down_sem))
    for copy in copies:
        copy.start()
    load = pltpu.make_async_copy(group, saved, group_sem)
    load.start()
    plane.begin()
    for copy in copies:
        copy.wait()
    load.wait()

    def recompute(index, carry):
        side, m = lax.div(index, PLANE), lax.rem(index, PLANE)
        tokens = saved[side, m]
        gate = matmul(tokens, gate_up[0])
        up = matmul(tokens, gate_up[1])
        square = gate * gate
        bend = jnp.tanh(GELU_SLOPE * (gate + GELU_CUBE * (square * gate)))
        half = 0.5 * (1.0 + bend)
        value = gate * half
        slope = half + (0.5 * GELU_SLOPE) * gate * (1.0 - bend * bend) * (
            1.0 + (3.0 * GELU_CUBE) * square
        )
        inner[side, m] = (value * up).astype(bf16)
        d_gate[side, m] = (slope * up).astype(bf16)
        d_up[side, m] = value.astype(bf16)
        return carry

    lax.fori_loop(0, PLANE, recompute, 0)
    plane.push_far()
    lax.fori_loop(PLANE, 2 * PLANE, recompute, 0)

    def compute(side, m):
        d_inner = lax.dot_general(rows[side, m], down[...], ACROSS, preferred_element_type=f32)
        gate = (d_inner * d_gate[side, m].astype(f32)).astype(bf16)
        up = (d_inner * d_up[side, m].astype(f32)).astype(bf16)
        d_gate[side, m] = gate
        d_up[side, m] = up
        return lax.dot_general(
            gate, gate_up[0], ACROSS, preferred_element_type=f32
        ) + lax.dot_general(up, gate_up[1], ACROSS, preferred_element_type=f32)

    plane.work(compute, sent_far=True)
    width = rows.shape[-1]
    step = width // 3

    def tall(ref, columns=slice(None)):
        value = ref[:, :, :, columns]
        return value.reshape(-1, value.shape[-1])

    @pl.loop(0, 3)
    def _(index):
        at = pl.ds(pl.multiple_of(index * step, step), step)
        tokens = tall(saved, at)
        for target, other in ((grad_gate, d_gate), (grad_up, d_up)):
            target[at] = lax.dot_general(
                tokens, tall(other), ALONG, preferred_element_type=f32
            ).astype(bf16)
        turned[at] = lax.dot_general(
            tall(rows, at), tall(inner), ALONG, preferred_element_type=f32
        ).astype(bf16)

    half_width = down_halves.shape[2]
    for h in range(2):
        down_halves[h] = turned[h * half_width : (h + 1) * half_width].T
    half = plane.remote(
        down_halves.at[1 - core], grad_down.at[core], half_send, half_recv, plane.sibling
    )
    half.start()
    stay = pltpu.make_async_copy(down_halves.at[core], grad_down.at[core], half_own)
    stay.start()
    plane.finish(result)
    half.wait()
    stay.wait()


def ffn(own, weights, ident, group=None):
    gate_up, down = weights
    tokens, width = own.shape
    blocks, _, _, share = gate_up.shape
    vmem, dma = pltpu.VMEM, pltpu.SemaphoreType.DMA
    scratch = [
        vmem((2, PLANE, tokens, width), bf16),
        vmem((2, width, share), bf16),
        vmem((share, width), bf16),
        vmem((PLANE, tokens, width), f32),
    ]
    scratch += [vmem((PLANE, tokens, width), bf16)] * 4
    scratch += [dma((PLANE,))] * 8 + [dma, dma((2 * blocks,)), dma]
    here, there = pl.BlockSpec(memory_space=pltpu.VMEM), pl.BlockSpec(memory_space=pl.ANY)
    shape = jax.ShapeDtypeStruct
    summed = shape((tokens, width), f32)
    if group is None:
        kernel, operands = ffn_forward_kernel, (own, gate_up, down)
        in_specs, out_specs = [here, there, there], [there, there, here]
        out_shape = [
            shape((2, PLANE, tokens, width), bf16),
            shape((share, width), bf16),
            summed,
        ]
        scratch += [vmem((2, share, width // 2), bf16)] + [dma] * 4
    else:
        kernel, operands = ffn_backward_kernel, (own, group, gate_up, down)
        in_specs, out_specs = [here, there, there, there], [here] * 3 + [there]
        out_shape = [
            summed,
            shape((width, share), bf16),
            shape((width, share), bf16),
            shape((2, share, width // 2), bf16),
        ]
        scratch += [vmem((2, PLANE, tokens, width), bf16)]
        scratch += [vmem((2, PLANE, tokens, share), bf16)] * 3
        scratch += [dma, vmem((width, share), bf16), vmem((2, share, width // 2), bf16)]
        scratch += [dma] * 3
    return pl.pallas_call(
        kernel,
        out_shape=out_shape,
        in_specs=in_specs,
        out_specs=out_specs,
        scratch_shapes=scratch,
        cost_estimate=LIGHT,
        compiler_params=pltpu.CompilerParams(
            collective_id=ident, has_side_effects=True, vmem_limit_bytes=60 * 2**20
        ),
    )(*operands)


def exact(left, right, dims=(((1,), (0,)), ((), ()))):
    return lax.dot_general(
        left, right, dims, precision=finest_precision, preferred_element_type=f32
    )


def update_kernel(sizes, counts, *refs):
    cores, planes, members = sizes
    rest = list(refs)
    take = lambda number: [rest.pop(0) for _ in range(number)]
    plain = [take(number) for number in counts]
    sides = [take(2) for _ in range(cores)]
    moments_in, weights_in, weights_out, moments_out = (take(4) for _ in range(4))
    moment, weight, gram, land, factor = (take(4) for _ in range(5))
    pieces, arrived = take(2)
    load_sem, store_sem, gram_send, gram_recv, factor_send, factor_recv = take(6)
    gu_send, gu_recv, gu_own = take(3)
    core, _, tp = (lax.axis_index(axis) for axis in EVERY)
    sibling = {"head": 1 - core}
    order = (0, 1, 3, 2)
    loads = {}
    for k in range(4):
        for part, source, target in ((0, moments_in, moment), (1, weights_in, weight)):
            copy = pltpu.make_async_copy(source[k], target[k], load_sem.at[part, k])
            copy.start()
            loads[part, k] = copy
    group = []
    for step in range(1, cores * members):
        far = lax.rem(core + step // members, cores), lax.rem(tp + step % members, members)
        group.append((dict(zip(GROUP, far)), linear(far, (cores, members))))
    enter([device for device, _ in group])
    rows = moment[2].shape[1]
    for part in range(cores):
        for j in range(members):
            for layer in range(cores):
                pieces[part * members + j, layer * rows : (layer + 1) * rows] = sides[layer][part][
                    j * rows : (j + 1) * rows
                ]
    if pieces.shape[1] > cores * rows:
        for piece in range(cores * members):
            pieces[piece, cores * rows :] = jnp.zeros(
                (pieces.shape[1] - cores * rows, pieces.shape[2]), bf16
            )
    me = linear((core, tp), (cores, members))
    moves, stores = [], []

    def send(src, dst, send_sem, recv_sem, device):
        copy = pltpu.make_async_remote_copy(
            src_ref=src,
            dst_ref=dst,
            send_sem=send_sem,
            recv_sem=recv_sem,
            device_id=device,
            device_id_type=MESH,
        )
        copy.start()
        return copy

    for step, (device, index) in enumerate(group):
        moves.append(
            send(pieces.at[index], arrived.at[me], gu_send.at[step], gu_recv.at[step], device)
        )
    own = pltpu.make_async_copy(pieces.at[me], arrived.at[me], gu_own)
    own.start()

    def store(part, k):
        source, target = (moment, moments_out) if part == 0 else (weight, weights_out)
        copy = pltpu.make_async_copy(source[k], target[k], store_sem.at[part, k])
        copy.start()
        stores.append(copy)

    def gram_of(k):
        def one(layer, carry):
            gram[k][layer] = exact(moment[k][layer], moment[k][layer], ACROSS)
            return carry

        lax.fori_loop(0, cores, one, 0)
        return send(
            gram[k].at[1 - core], land[k], gram_send.at[k], gram_recv.at[k], sibling
        )

    def unit(size):
        down = lax.broadcasted_iota(jnp.int32, (size, size), 0)
        return (down == lax.broadcasted_iota(jnp.int32, (size, size), 1)).astype(f32)

    def orthogonal(members_of):
        for k in members_of:
            total = gram[k][core] + land[k][...]
            one = unit(total.shape[0])
            trace = jnp.sum(jnp.sum(total * one, axis=1, keepdims=True), axis=0, keepdims=True)
            scale = 1.0 / (jnp.sqrt(trace) + 1e-07)
            land[k][...] = total * (scale * scale)
            factor[k][core] = one * scale

        def polynomial(present):
            square = exact(present, present)
            return newton_one * unit(present.shape[0]) + newton_two * present + (
                newton_three * square
            )

        def step(_, carry):
            for k in members_of:
                present = land[k][...]
                poly = polynomial(present)
                factor[k][core] = exact(poly, factor[k][core])
                land[k][...] = exact(exact(poly, present), poly)
            return carry

        lax.fori_loop(0, NS_ITERS - 1, step, 0)
        for k in members_of:
            factor[k][core] = exact(polynomial(land[k][...]), factor[k][core])
        return [
            send(factor[k].at[core], factor[k].at[core], factor_send.at[k], factor_recv.at[k], sibling)
            for k in members_of
        ]

    def apply(k):
        columns = weight[k].shape[2] * cores
        rate = muon_rate * muon_scale * math.sqrt(columns)

        def one(layer, carry):
            weight[k][layer] = weight[k][layer] * (1.0 - muon_rate * muon_shrink) - rate * exact(
                factor[k][layer], moment[k][layer]
            )
            return carry

        lax.fori_loop(0, cores, one, 0)
        store(1, k)

    def arrive(copies):
        for copy in copies:
            copy.wait_recv()

    sent = []
    for index, k in enumerate(order[:3]):
        loads[0, k].wait()
        height = moment[k].shape[1]
        for layer in range(cores):
            if len(plain[index]) == 1:
                gradient = plain[index][0][layer * height : (layer + 1) * height]
            else:
                gradient = plain[index][layer][...].astype(f32)
            moment[k][layer] = muon_decay * moment[k][layer] + gradient
        store(0, k)
        sent.append(gram_of(k))
    arrive(sent)
    crossed = orthogonal(order[:3])
    sent += crossed
    own.wait()
    for copy in moves:
        copy.wait_recv()
    loads[0, 2].wait()
    half = planes // cores
    block = arrived.shape[2] // half
    for layer in range(cores):
        cut = [
            arrived[
                c * members + j,
                layer * rows : (layer + 1) * rows,
                k * block : (k + 1) * block,
            ].astype(f32)
            for c in range(cores)
            for k in range(half)
            for j in range(members)
        ]
        moment[2][layer] = muon_decay * moment[2][layer] + jnp.concatenate(cut, axis=1)
    store(0, 2)
    last = gram_of(2)
    sent.append(last)
    arrive(crossed)
    for k in range(4):
        loads[1, k].wait()
    for k in order[:3]:
        apply(k)
    arrive([last])
    crossed = orthogonal(order[3:])
    sent += crossed
    arrive(crossed)
    apply(2)
    for copy in moves + sent:
        copy.wait_send()
    for copy in stores:
        copy.wait()


def update(gradients, sides, moments, weights, ident):
    sizes = tuple(lax.axis_size(axis) for axis in EVERY)
    cores, planes, members = sizes
    vmem, dma = pltpu.VMEM, pltpu.SemaphoreType.DMA
    layers, rows, columns = moments[2].shape
    piece = (
        cores * members,
        -(-layers * rows // 16) * 16,
        columns // (cores * members),
    )
    shapes = [m.shape for m in moments]
    square = [(s[1], s[1]) for s in shapes]
    scratch = [vmem(s, f32) for s in shapes] * 2
    scratch += [vmem((layers,) + s, f32) for s in square]
    scratch += [vmem(s, f32) for s in square]
    scratch += [vmem((layers,) + s, f32) for s in square]
    scratch += [vmem(piece, bf16)] * 2
    scratch += [dma((2, 4))] * 2 + [dma((4,))] * 4
    scratch += [dma((cores * members - 1,))] * 2 + [dma]
    here, there = pl.BlockSpec(memory_space=pltpu.VMEM), pl.BlockSpec(memory_space=pl.ANY)
    operands = sum(gradients, []) + sum(sides, [])
    return pl.pallas_call(
        partial(update_kernel, sizes, [len(g) for g in gradients]),
        out_shape=[jax.ShapeDtypeStruct(s, f32) for s in shapes] * 2,
        in_specs=[here] * len(operands) + [there] * 8,
        out_specs=[there] * 8,
        scratch_shapes=scratch,
        compiler_params=pltpu.CompilerParams(
            collective_id=ident, has_side_effects=True, vmem_limit_bytes=56 * 2**20
        ),
    )(*operands, *moments, *weights)


def padded(array, multiple=16):
    extra = -array.shape[-2] % multiple
    if extra == 0:
        return array
    return jnp.pad(array, [(0, 0)] * (array.ndim - 2) + [(0, extra), (0, 0)])


def rms_norm(values, norm_gain):
    return (
        values * lax.rsqrt(jnp.mean(values * values, axis=-1, keepdims=True) + norm_eps) * norm_gain
    )


def rope_tables(positions, head_dim):
    half_dim = head_dim // 2
    frequency = jnp.exp(
        jnp.arange(half_dim, dtype=jnp.float32) * (-2.0 * math.log(rope_base) / head_dim)
    )
    angles = positions.astype(jnp.float32)[:, None] * frequency[None, :]
    return (jnp.cos(angles), jnp.sin(angles))


def matmul(left, right):
    return jnp.dot(left, right, preferred_element_type=f32)


def body(
    inputs,
    cotangent,
    teacher,
    segments,
    valid_mask,
    w_qkv,
    w_out,
    w_gu,
    w_down,
    norm_gains,
    mom_qkv,
    mom_out,
    mom_gu,
    mom_down,
    gain_first,
    gain_second,
):
    cores = lax.axis_size("head")
    planes = lax.axis_size("zd")
    seq_devices = planes * PLANE
    core = lax.axis_index("head")
    seq_place = lax.axis_index("zd") * PLANE + lax.axis_index("tp")
    half_seqs, stretch_len = inputs.shape[:2]
    tokens = half_seqs * stretch_len
    all_seqs = half_seqs * cores
    seq_length = stretch_len * seq_devices
    reach = -(-WINDOW // stretch_len)
    key_len = (reach + 1) * stretch_len
    qkv_rows, qkv_cols = w_qkv.shape[1:]
    out_rows, out_cols = w_out.shape[1:]
    gu_rows = w_gu.shape[1]
    ff_block = w_down.shape[1]
    share = FF // (cores * PLANE)
    half_planes = planes // cores
    gain_cols = norm_gains.shape[-1]
    gain_len = gain_cols * seq_devices
    lanes = -(-gain_cols // 128) * 128

    packet = jnp.zeros((8, lanes), f32)
    packet = packet.at[:LAYERS, :gain_cols].set(norm_gains[:, 0].astype(bf16).astype(f32))
    packet = packet.at[LAYERS, 0].set(jnp.sum(valid_mask.astype(f32)))
    gu_pieces, w_mixed, w_project, packets, *later = start(
        w_gu, w_qkv, w_out, packet, 0
    )
    attn_weights = [w_mixed, w_project]
    gu_pieces = gu_pieces[:, : LAYERS * gu_rows].reshape(cores * PLANE, LAYERS, gu_rows, share)
    packets = packets.reshape(cores, seq_devices, 8, lanes)
    valid_count = jnp.sum(packets[:, :, LAYERS, 0])
    gain_rows = [
        packets[:, :, layer, :gain_cols].reshape(cores, gain_len) for layer in range(LAYERS)
    ]

    def gate_up_rows(layer):
        pieces = gu_pieces[:, layer].reshape(2, PLANE * gu_rows, share)
        pieces = lax.all_gather(pieces, "zd", axis=0)
        if PLANE * gu_rows % 16:
            pieces = pieces.transpose(1, 0, 2, 3).reshape(1, 2, D, share)
        return pieces

    def down_rows(layer):
        rows = w_down[layer : layer + 1].astype(bf16)
        return lax.all_gather(rows, "zd", axis=1, tiled=True)

    full = [(gate_up_rows(0), down_rows(0))] + [None] * (LAYERS - 1)

    own_places = seq_place * stretch_len + jnp.arange(stretch_len, dtype=jnp.int32)
    key_places = (seq_place - reach) * stretch_len + jnp.arange(key_len, dtype=jnp.int32)
    cosine_table, sine_table = rope_tables(own_places, HD)
    own_rows = lax.dynamic_slice_in_dim(segments, core * half_seqs, half_seqs, 0)
    own_segments = lax.dynamic_slice_in_dim(own_rows, seq_place * stretch_len, stretch_len, 1)
    padded_segments = jnp.pad(own_rows, ((0, 0), (reach * stretch_len, 0)), constant_values=-1)
    key_segments = lax.dynamic_slice_in_dim(padded_segments, seq_place * stretch_len, key_len, 1)
    spacing = own_places[:, None] - key_places[None, :]
    allowed = (spacing >= 0) & (spacing < WINDOW) & (key_places[None, :] >= 0)
    allowed = allowed[None] & (own_segments[:, :, None] == key_segments[:, None, :])

    tables = [jnp.tile(t, (half_seqs, 1)) for t in (cosine_table, sine_table)]
    bias = jnp.where(allowed, 0.0, -1e30).astype(f32)

    saved, previous = [], None
    base = inputs.reshape(tokens, D)
    for layer in range(LAYERS):
        weights = list(attn_weights)
        hidden, normed, mixed, queries, keyvals, attended, projected, half, normed_ffn = attn_forward(
            base, weights, gain_rows[layer], tables, bias, planes, reach, 3 + layer, previous
        )
        ffn_share = full[layer]
        if layer + 1 < LAYERS:
            gu_pieces, w_down, later, attended = lax.optimization_barrier(
                (gu_pieces, w_down, later, attended)
            )
            attn_weights = later_weights(later, w_qkv, w_out, layer + 1, 2 + 20 * layer)
            full[layer + 1] = (gate_up_rows(layer + 1), down_rows(layer + 1))
            normed_ffn, *attn_weights = lax.optimization_barrier((normed_ffn, *attn_weights))
        group_normed, whole_down, down_out = ffn(normed_ffn, ffn_share, 5 + layer)
        full[layer] = (weights, (ffn_share[0], whole_down))
        saved.append(
            (
                [hidden, mixed, queries, keyvals, projected, half],
                [normed, attended],
                group_normed,
                down_out,
            )
        )
        base, previous = half, (down_out, gain_rows[layer])

    output, post_ffn_back = jax.vjp(rms_norm, down_out, gain_rows[-1][1, D : 2 * D])
    output = base + output
    target_gap = output - teacher.reshape(tokens, D).astype(f32)
    valid_weight = valid_mask.astype(f32).reshape(tokens, 1)
    square_sum = jnp.sum(valid_weight * target_gap * target_gap)
    loss_weight = float(all_seqs * seq_length * D // 4)
    grad_hidden = (
        cotangent.reshape(tokens, D).astype(f32)
        + 2.0 * loss_weight / (valid_count * D) * valid_weight * target_gap
    )
    d_down, d_post_ffn = post_ffn_back(grad_hidden)
    d_down, d_post_ffn = d_down.astype(bf16), d_post_ffn[None]

    tiled = ff_block % 16 == 0
    attn_acts = [None] * LAYERS
    down_grads = [None] * LAYERS
    gain_grads = [None] * LAYERS
    gu_sums = [None] * LAYERS
    for layer in reversed(range(LAYERS)):
        kept, (normed, attended), group_normed, _ = saved[layer]
        weights, ffn_share = full[layer]
        d_normed_ffn, *grad_gu, grad_down = ffn(d_down, ffn_share, 9 + layer, group_normed)
        if layer == 0 and tiled:
            first_down = grad_down.reshape(planes, ff_block, out_cols)
        else:
            down_grads[layer] = lax.psum_scatter(
                grad_down.reshape(planes * ff_block, out_cols),
                "zd",
                scatter_dimension=0,
                tiled=True,
            )
        gu_sums[layer] = [
            lax.psum_scatter(g, "zd", scatter_dimension=0, tiled=True) for g in grad_gu
        ]
        earlier = (saved[layer - 1][3], gain_rows[layer - 1]) if layer > 0 else None
        grad_hidden, d_mixed, d_projected, gain_grads[layer], *d_rest = attn_backward(
            d_normed_ffn,
            grad_hidden,
            kept,
            weights,
            gain_rows[layer],
            tables,
            bias,
            planes,
            reach,
            17 + layer,
            earlier,
        )
        gain_grads[layer] = gain_grads[layer].at[1:, D : 2 * D].set(d_post_ffn)
        if layer > 0:
            d_down, d_post_ffn = d_rest
        attn_acts[layer] = [normed, d_mixed, attended, d_projected]
    attn_acts[0][1], gu_sums[1:], down_grads[1:] = lax.optimization_barrier(
        (attn_acts[0][1], gu_sums[1:], down_grads[1:])
    )

    packet = jnp.stack(gain_grads, axis=1).reshape(cores, LAYERS, planes, PLANE, gain_cols)
    packet = packet.transpose(0, 3, 2, 1, 4)
    packet = jnp.pad(packet, [(0, 0)] * 3 + [(0, 8 - LAYERS), (0, lanes - gain_cols)])
    packet = packet.at[:, :, :, LAYERS, 0].set(square_sum)
    packet = packet.reshape(cores, PLANE, planes * 8, lanes)
    down = first_down if tiled else None
    grad_qkv, grad_out, packet, *summed_down = collect(sum(attn_acts, []), packet, down, 19)
    if tiled:
        (down_grads[0],) = summed_down
    mse_loss = packet[LAYERS, 0] / (valid_count * D)
    gain_grad = packet[:LAYERS, None, :gain_cols]

    outcome = update(
        [[grad_qkv], [grad_out], down_grads],
        [list(pair) for pair in gu_sums],
        (mom_qkv, mom_out, mom_gu, mom_down),
        (w_qkv, w_out, w_gu, w_down),
        15,
    )
    new_weights, moments = outcome[:4], outcome[4:]
    gain_first_new = beta_one * gain_first + (1.0 - beta_one) * gain_grad
    gain_second_new = beta_two * gain_second + (1.0 - beta_two) * gain_grad * gain_grad
    gains_new = norm_gains - adam_rate * (gain_first_new / (1.0 - beta_one**STEP)) / (
        jnp.sqrt(gain_second_new / (1.0 - beta_two**STEP)) + adam_epsilon
    )
    return (
        mse_loss,
        output.reshape(inputs.shape),
        grad_hidden.reshape(inputs.shape),
        *new_weights,
        *moments,
        gains_new,
        gain_first_new,
        gain_second_new,
    )


def solution(mesh):
    cores, length = mesh.devices.shape
    split = Mesh(mesh.devices.reshape(cores, length // PLANE, PLANE), EVERY)
    stream = P("head", SEQ, None)
    matrix = P(None, SEQ, "head")
    gains = P(None, "head", SEQ)
    return jax.shard_map(
        body,
        mesh=split,
        in_specs=(stream, stream, stream, P(), P("head", SEQ))
        + (matrix,) * 4
        + (gains,)
        + (matrix,) * 4
        + (gains,) * 2,
        out_specs=(P(), stream, stream) + (matrix,) * 8 + (gains,) * 3,
        check_vma=False,
    )
```

```python
from functools import partial
import itertools
import math

import jax
import jax.numpy as jnp
from jax import lax
from jax.experimental import pallas as pl
from jax.experimental.pallas import tpu as pltpu
from jax.sharding import Mesh, PartitionSpec as P

D = 1152
HEADS = 4
HD = 256
FF = 6912
WINDOW = 512
LAYERS = 2
NS_ITERS = 5
STEP = 10
PLANE = 4

norm_eps = 1e-06
rope_base = 10000.0
newton_one = 3.4445
newton_two = -4.775
newton_three = 2.0315
muon_decay = 0.95
muon_rate = 0.15
muon_shrink = 0.01
muon_scale = 0.2
beta_one = 0.9
beta_two = 0.95
adam_rate = 0.7
adam_epsilon = 1e-08
finest_precision = lax.Precision.HIGHEST
MESH = pl.DeviceIdType.MESH
SEQ = ("zd", "tp")
GROUP = ("head", "tp")
EVERY = ("head", "zd", "tp")
bf16 = jnp.bfloat16
f32 = jnp.float32
LIGHT = pl.CostEstimate(flops=1, bytes_accessed=1, transcendentals=0)


def linear(places, sizes):
    index = 0
    for place, size in zip(places, sizes):
        index = index * size + place
    return index


def enter(partners):
    barrier = pltpu.get_barrier_semaphore()
    for partner in partners:
        pl.semaphore_signal(barrier, inc=1, device_id=partner, device_id_type=MESH)
    pl.semaphore_wait(barrier, len(partners))


class Spread:
    ORDER = ("zd", "tp", "head")

    def __init__(self, sizes, slots, send_sem, recv_sem, whole_z=False):
        self.size = dict(zip(EVERY, sizes))
        self.place = {axis: lax.axis_index(axis) for axis in EVERY}
        self.slots, self.send_sem, self.recv_sem = slots, send_sem, recv_sem
        self.held, self.sends, self.number = [(self.place, None)], [], 0
        if whole_z:
            self.held = [(dict(self.place, zd=z), None) for z in range(self.size["zd"])]
            self.ORDER = self.ORDER[1:]

    def partners(self):
        return [
            {axis: lax.rem(self.place[axis] + step, self.size[axis])}
            for axis in self.ORDER
            for step in range(1, self.size[axis])
        ]

    def stage(self, axis):
        arriving = []
        for where, arrivals in self.held:
            while arrivals:
                arrivals.pop().wait_recv()
            for step in range(1, self.size[axis]):
                to = lax.rem(self.place[axis] + step, self.size[axis])
                back = lax.rem(self.place[axis] - step + self.size[axis], self.size[axis])
                landing = []
                for k, slot in enumerate(self.slots):
                    ref = slot.at[tuple(where[name] for name in EVERY)]
                    copy = pltpu.make_async_remote_copy(
                        src_ref=ref,
                        dst_ref=ref,
                        send_sem=self.send_sem.at[k, self.number],
                        recv_sem=self.recv_sem.at[k, self.number],
                        device_id={axis: to},
                        device_id_type=MESH,
                    )
                    copy.start()
                    self.sends.append(copy)
                    landing.append(copy)
                self.number += 1
                arriving.append((dict(where, **{axis: back}), landing))
        self.held = self.held + arriving

    def finish(self):
        for _, arrivals in self.held:
            while arrivals:
                arrivals.pop().wait_recv()
        for copy in self.sends:
            copy.wait_send()


def start_kernel(sizes, *refs):
    cores, planes, members = sizes
    rest = list(refs)
    take = lambda number: [rest.pop(0) for _ in range(number)]
    gu, qkv, out, packet = take(4)
    gu_result, mixed, project, packets, qkv_later, out_later = take(6)
    packet_slots, qkv_slots, out_slots, send_sem, recv_sem = take(5)
    pieces, gu_send, gu_recv, gu_own, later_send, later_recv = take(6)
    qkv_low, out_low, later_own = take(3)
    gather = Spread(sizes, [packet_slots, qkv_slots, out_slots], send_sem, recv_sem)
    here = tuple(gather.place[name] for name in EVERY)
    core, zd, tp = here
    group = []
    for step in range(1, cores * members):
        far = lax.rem(core + step // members, cores), lax.rem(tp + step % members, members)
        group.append((dict(zip(GROUP, far)), linear(far, (cores, members))))
    enter(gather.partners() + [device for device, _ in group])
    packet_slots[here] = packet[...]

    def place_rows(source, layer, slot, index):
        rows = source.shape[1]
        slot[index + (slice(0, rows),)] = source[layer].astype(bf16)
        if slot.shape[-2] > rows:
            slot[index + (slice(rows, slot.shape[-2]),)] = jnp.zeros(
                (slot.shape[-2] - rows, slot.shape[-1]), bf16
            )

    for source, slot in ((qkv, qkv_slots), (out, out_slots)):
        place_rows(source, 0, slot, here)
    gather.stage("zd")
    moves = []

    def along_z(source, target, sends, recvs):
        for step in range(1, planes):
            copy = pltpu.make_async_remote_copy(
                src_ref=source,
                dst_ref=target,
                send_sem=sends.at[step],
                recv_sem=recvs.at[step],
                device_id={"zd": lax.rem(zd + step, planes)},
                device_id_type=MESH,
            )
            copy.start()
            moves.append(copy)

    for k, (source, low, slot) in enumerate(
        ((qkv, qkv_low, qkv_later), (out, out_low, out_later))
    ):
        for layer in range(1, source.shape[0]):
            place_rows(source, layer, low, (layer - 1,))
            target = slot.at[layer - 1, zd]
            along_z(
                low.at[layer - 1], target, later_send.at[k, layer], later_recv.at[k, layer]
            )
            own = pltpu.make_async_copy(low.at[layer - 1], target, later_own.at[k, layer])
            own.start()
            moves.append(own)
    layers, rows, columns = gu.shape
    block = columns // (planes * members)
    half = planes // cores
    for c in range(cores):
        for j in range(members):
            for i in range(layers):
                cut = [
                    gu[i, :, pl.ds(((c * half + k) * members + j) * block, block)]
                    for k in range(half)
                ]
                value = jnp.concatenate(cut, axis=1) if half > 1 else cut[0]
                pieces[c * members + j, i * rows : (i + 1) * rows] = value.astype(bf16)
    if pieces.shape[1] > layers * rows:
        for piece in range(cores * members):
            pieces[piece, layers * rows :] = jnp.zeros(
                (pieces.shape[1] - layers * rows, pieces.shape[2]), bf16
            )
    me = linear((core, tp), (cores, members))
    for step, (device, index) in enumerate(group):
        copy = pltpu.make_async_remote_copy(
            src_ref=pieces.at[index],
            dst_ref=gu_result.at[me],
            send_sem=gu_send.at[step],
            recv_sem=gu_recv.at[step],
            device_id=device,
            device_id_type=MESH,
        )
        copy.start()
        moves.append(copy)
    own = pltpu.make_async_copy(pieces.at[me], gu_result.at[me], gu_own)
    own.start()
    moves.append(own)
    gather.stage("tp")
    gather.stage("head")
    gather.finish()
    side_by_side(sizes, (qkv_slots, out_slots), (mixed, project))
    packets[...] = packet_slots[...]
    for copy in moves:
        copy.wait()


def side_by_side(sizes, slots, results):
    cores, planes, members = sizes
    for slot, result in zip(slots, results):
        columns = slot.shape[4]
        rows = result.shape[0] // (planes * members)
        for h, z, t in itertools.product(range(cores), range(planes), range(members)):
            row = (z * members + t) * rows
            result[row : row + rows, h * columns : (h + 1) * columns] = slot[h, z, t, :rows]


def later_kernel(sizes, layer, qkv, out, mixed, project, qkv_slots, out_slots, send_sem, recv_sem):
    gather = Spread(sizes, [qkv_slots, out_slots], send_sem, recv_sem, whole_z=True)
    core, _, tp = (gather.place[name] for name in EVERY)
    enter(gather.partners())
    for source, slot in ((qkv, qkv_slots), (out, out_slots)):
        for z in range(sizes[1]):
            slot[core, z, tp] = source[layer - 1, z]
    gather.stage("tp")
    gather.stage("head")
    gather.finish()
    side_by_side(sizes, (qkv_slots, out_slots), (mixed, project))


def whole_shapes(sizes, tall, matrices):
    slots = [pltpu.VMEM(sizes + (t, w.shape[2]), bf16) for t, w in zip(tall, matrices)]
    outs = [
        jax.ShapeDtypeStruct((w.shape[1] * sizes[1] * sizes[2], w.shape[2] * sizes[0]), bf16)
        for w in matrices
    ]
    return slots, outs


def start(w_gu, w_qkv, w_out, packet, ident):
    sizes = tuple(lax.axis_size(axis) for axis in EVERY)
    cores, planes, members = sizes
    vmem, dma = pltpu.VMEM, pltpu.SemaphoreType.DMA
    here, there = pl.BlockSpec(memory_space=pltpu.VMEM), pl.BlockSpec(memory_space=pl.ANY)
    shape = jax.ShapeDtypeStruct
    tall = [-(-w.shape[1] // 16) * 16 for w in (w_qkv, w_out)]
    slots, outs = whole_shapes(sizes, tall, (w_qkv, w_out))
    layers, rows, columns = w_gu.shape
    piece = (
        cores * members,
        -(-layers * rows // 16) * 16,
        columns // (cores * members),
    )
    later = [
        shape((layers - 1, planes, t, w.shape[2]), bf16) for t, w in zip(tall, (w_qkv, w_out))
    ]
    operands = [w_gu, w_qkv, w_out, packet]
    outs = [shape(piece, bf16)] + outs + [shape(sizes + packet.shape, f32)] + later
    out_specs = [there] + [here] * 3 + [there] * 2
    moves = math.prod(sizes) - 1
    scratch = [vmem(sizes + packet.shape, f32)] + slots + [dma((3, moves))] * 2
    scratch += [vmem(piece, bf16), dma((cores * members - 1,)), dma((cores * members - 1,)), dma]
    scratch += [dma((2, layers, planes))] * 2
    scratch += [
        vmem((layers - 1, t, w.shape[2]), bf16) for t, w in zip(tall, (w_qkv, w_out))
    ] + [dma((2, layers))]
    return pl.pallas_call(
        partial(start_kernel, sizes),
        out_shape=outs,
        in_specs=[here] * len(operands),
        out_specs=out_specs,
        scratch_shapes=scratch,
        compiler_params=pltpu.CompilerParams(
            collective_id=ident, has_side_effects=True, vmem_limit_bytes=56 * 2**20
        ),
    )(*operands)


def later_weights(gathered, w_qkv, w_out, layer, ident):
    sizes = tuple(lax.axis_size(axis) for axis in EVERY)
    slots, outs = whole_shapes(sizes, [g.shape[2] for g in gathered], (w_qkv, w_out))
    here = pl.BlockSpec(memory_space=pltpu.VMEM)
    moves = math.prod(sizes) - sizes[1]
    return pl.pallas_call(
        partial(later_kernel, sizes, layer),
        out_shape=outs,
        in_specs=[here] * 2,
        out_specs=[here] * 2,
        scratch_shapes=slots + [pltpu.SemaphoreType.DMA((2, moves))] * 2,
        compiler_params=pltpu.CompilerParams(
            collective_id=ident, has_side_effects=True, vmem_limit_bytes=48 * 2**20
        ),
    )(*gathered)


def by_rows(rows, work, step=16):
    @pl.loop(0, rows // step)
    def _(index):
        work(pl.ds(pl.multiple_of(index * step, step), step))


def collect_kernel(sizes, layers, tiled, *refs):
    cores, planes, members = sizes
    rest = list(refs)
    take = lambda number: [rest.pop(0) for _ in range(number)]
    acts, packet = take(4 * layers), take(1)[0]
    if tiled:
        (down,) = take(1)
    results = take(3)
    if tiled:
        (down_result,) = take(1)
    far, halves = take(4 * layers), take(2 * layers)
    packet_land = rest.pop(0)
    pieces, plane_lands, totals, z_sums, z_lands = (take(3) for _ in range(5))
    act_send, act_recv, packet_send, packet_recv = take(4)
    tp_send, tp_recv, z_send, z_recv = take(4)
    core, zd, tp = (lax.axis_index(axis) for axis in EVERY)
    sibling = {"head": 1 - core}
    enter(
        [sibling]
        + [{"tp": lax.rem(tp + step, members)} for step in range(1, members)]
        + [{"zd": lax.rem(zd + step, planes)} for step in range(1, planes)]
    )
    sends = []

    def send(src, dst, send_sem, recv_sem, device):
        copy = pltpu.make_async_remote_copy(
            src_ref=src,
            dst_ref=dst,
            send_sem=send_sem,
            recv_sem=recv_sem,
            device_id=device,
            device_id_type=MESH,
        )
        copy.start()
        sends.append(copy)
        return copy

    if tiled:
        down_land, down_send, down_recv, down_own = take(4)
        down_moves = []
        for step in range(1, planes):
            there = lax.rem(zd + step, planes)
            down_moves.append(
                send(
                    down.at[there],
                    down_land.at[step],
                    down_send.at[step],
                    down_recv.at[step],
                    {"zd": there},
                )
            )
        down_stay = pltpu.make_async_copy(down.at[zd], down_land.at[0], down_own)
        down_stay.start()
    for k in range(2 * layers):
        grad, half = acts[2 * k + 1], halves[k]
        width = half.shape[2]
        for h in range(cores):
            half[h] = grad[:, h * width : (h + 1) * width]
    moves = []
    for k in range(2 * layers):
        moves.append(
            send(acts[2 * k], far[2 * k], act_send.at[2 * k], act_recv.at[2 * k], sibling)
        )
        moves.append(
            send(
                halves[k].at[1 - core],
                far[2 * k + 1],
                act_send.at[2 * k + 1],
                act_recv.at[2 * k + 1],
                sibling,
            )
        )
    gains = send(packet.at[1 - core], packet_land, packet_send, packet_recv, sibling)
    plane_moves, z_moves = {}, {}
    for kind in range(3):
        piece = pieces[kind]
        if kind < 2:
            for layer in range(layers):
                k = 2 * layer + kind
                near = lax.dot_general(
                    acts[2 * k][...], halves[k][core], ALONG, preferred_element_type=f32
                )
                moves[2 * k].wait_recv()
                moves[2 * k + 1].wait_recv()
                value = near + lax.dot_general(
                    far[2 * k][...], far[2 * k + 1][...], ALONG, preferred_element_type=f32
                )
                value = value.astype(bf16)
                rows = value.shape[0] // (planes * members)
                slab = piece.shape[1] // planes
                for z, t in itertools.product(range(planes), range(members)):
                    at = (z * members + t) * rows
                    to = z * slab + layer * rows
                    piece[t, to : to + rows] = value[at : at + rows]
            if slab > layers * rows:
                for z, t in itertools.product(range(planes), range(members)):
                    piece[t, z * slab + layers * rows : (z + 1) * slab] = jnp.zeros(
                        (slab - layers * rows, piece.shape[2]), bf16
                    )
        else:
            gains.wait_recv()
            piece[...] = packet[core] + packet_land[...]
        for step in range(1, members):
            there = lax.rem(tp + step, members)
            plane_moves[kind, step] = send(
                piece.at[there],
                plane_lands[kind].at[step],
                tp_send.at[kind, step],
                tp_recv.at[kind, step],
                {"tp": there},
            )
    for kind in range(3):
        for step in range(1, members):
            plane_moves[kind, step].wait_recv()
        piece, total, land, result = pieces[kind], totals[kind], plane_lands[kind], results[kind]
        stride = 8 if land.dtype == f32 else 16

        def gather_plane(rows):
            value = piece[tp, rows].astype(f32)
            for step in range(1, members):
                value = value + land[step, rows].astype(f32)
            total[rows] = value

        by_rows(total.shape[0], gather_plane, stride)
        height = result.shape[0]
        z_sum = z_sums[kind]
        for step in range(1, planes):
            there = lax.rem(zd + step, planes)

            def round_off(rows):
                at = pl.multiple_of(there * height + rows.start, stride)
                z_sum[step, rows] = total[pl.ds(at, rows.size)].astype(z_sum.dtype)

            by_rows(height, round_off, stride)
            z_moves[kind, step] = send(
                z_sum.at[step],
                z_lands[kind].at[step],
                z_send.at[kind, step],
                z_recv.at[kind, step],
                {"zd": there},
            )
    for kind in range(3):
        for step in range(1, planes):
            z_moves[kind, step].wait_recv()
        total, land, result = totals[kind], z_lands[kind], results[kind]
        height = result.shape[0]
        stride = 8 if land.dtype == f32 else 16

        def gather_z(rows):
            at = pl.multiple_of(zd * height + rows.start, stride)
            value = total[pl.ds(at, rows.size)]
            for step in range(1, planes):
                value = value + land[step, rows].astype(f32)
            result[rows] = value

        by_rows(height, gather_z, stride)
    if tiled:
        down_stay.wait()
        for copy in down_moves:
            copy.wait_recv()

        def gather_down(rows):
            value = down_land[0, rows].astype(f32)
            for step in range(1, planes):
                value = value + down_land[step, rows].astype(f32)
            down_result[rows] = value

        by_rows(down_result.shape[0], gather_down)
    for copy in sends:
        copy.wait_send()


def collect(acts, packet, down, ident):
    sizes = tuple(lax.axis_size(axis) for axis in EVERY)
    cores, planes, members = sizes
    layers = len(acts) // 4
    vmem, dma = pltpu.VMEM, pltpu.SemaphoreType.DMA
    tokens = acts[0].shape[0]
    halves = [acts[2 * k + 1].shape[1] // cores for k in range(2 * layers)]
    slabs = []
    for kind in range(2):
        rows = layers * acts[2 * kind].shape[1] // (planes * members)
        slabs.append((-(-rows // 16) * 16, halves[kind], bf16))
    slabs.append((packet.shape[2] // planes, packet.shape[3], f32))
    far = []
    for k in range(2 * layers):
        far += [vmem(acts[2 * k].shape, bf16), vmem((tokens, halves[k]), bf16)]
    scratch = far + [vmem((cores, tokens, width), bf16) for width in halves]
    scratch += [vmem(packet.shape[1:], f32)]
    scratch += [vmem((members, planes * r, c), kind) for r, c, kind in slabs] * 2
    scratch += [vmem((planes * r, c), f32) for r, c, _ in slabs]
    scratch += [vmem((planes, r, c), kind) for r, c, kind in slabs] * 2
    scratch += [dma((4 * layers,))] * 2 + [dma] * 2
    scratch += [dma((3, members))] * 2 + [dma((3, planes))] * 2
    here = pl.BlockSpec(memory_space=pltpu.VMEM)
    operands = [*acts, packet]
    outs = [jax.ShapeDtypeStruct((r, c), f32) for r, c, _ in slabs]
    in_specs = [here] * len(operands)
    if down is not None:
        operands, in_specs = operands + [down], in_specs + [pl.BlockSpec(memory_space=pl.ANY)]
        outs += [jax.ShapeDtypeStruct(down.shape[1:], f32)]
        scratch += [vmem(down.shape, bf16), dma((planes,)), dma((planes,)), dma]
    return pl.pallas_call(
        partial(collect_kernel, sizes, layers, down is not None),
        out_shape=outs,
        in_specs=in_specs,
        out_specs=[here] * len(outs),
        scratch_shapes=scratch,
        cost_estimate=LIGHT,
        compiler_params=pltpu.CompilerParams(
            collective_id=ident, has_side_effects=True, vmem_limit_bytes=56 * 2**20
        ),
    )(*operands)


def neighbours(planes, reach, sign):
    total = planes * PLANE
    place = linear([lax.axis_index("zd"), lax.axis_index("tp")], (planes, PLANE))

    def at(distance):
        there = lax.rem(place + distance + total, total)
        return {"zd": lax.div(there, PLANE), "tp": lax.rem(there, PLANE)}

    steps = range(1, reach + 1)
    return [at(sign * step) for step in steps], [at(-sign * step) for step in steps]


def inverse_rms(values):
    return lax.rsqrt(jnp.mean(values * values, axis=-1, keepdims=True) + norm_eps)


def rms_back(gradient, values, gain):
    inverse = inverse_rms(values)
    scaled = gradient * gain
    shared = jnp.mean(scaled * values, axis=-1, keepdims=True) * (inverse * inverse)
    return inverse * (scaled - values * shared), jnp.sum(
        gradient * values * inverse, axis=0, keepdims=True
    )


def turn(values, cosine, sine):
    half = values.shape[-1] // 2
    lower, upper = values[:, :half], values[:, half:]
    return jnp.concatenate(
        [lower * cosine - upper * sine, upper * cosine + lower * sine], axis=-1
    )


def soft_rows(query, keys, bias):
    scores = lax.dot_general(query, keys, ACROSS, preferred_element_type=f32)
    scores = scores * (1.0 / math.sqrt(HD)) + bias
    raised = jnp.exp(scores - jnp.max(scores, axis=-1, keepdims=True))
    return raised / jnp.sum(raised, axis=-1, keepdims=True)


def attn_forward_kernel(planes, reach, chained, *refs):
    rest = list(refs)
    take = lambda number: [rest.pop(0) for _ in range(number)]
    if chained:
        base, down, before = take(3)
    else:
        (base,) = take(1)
    w_mixed, w_project, gains, cosine, sine, bias = take(6)
    hidden, normed, mixed, queries, keyvals_out = take(5)
    attended, projected, hidden_half, normed_ffn = take(4)
    keyvals, send_sem, recv_sem, save_sem = take(4)
    seqs, stretch, key_len = bias.shape
    devices, sources = neighbours(planes, reach, 1)
    enter(devices + sources)
    value = base[...].astype(f32)
    if chained:
        late = down[...]
        value = value + late * inverse_rms(late) * before[1:2, D : 2 * D]
    hidden[...] = value
    low = (value * inverse_rms(value) * gains[0:1, :D]).astype(bf16)
    normed[...] = low
    mixed[...] = matmul(low, w_mixed[...])
    key = mixed[:, HEADS * HD : HEADS * HD + HD]
    key = turn(key * inverse_rms(key) * gains[1:2, 2 * D :], cosine[...], sine[...]).astype(bf16)
    late_values = mixed[:, HEADS * HD + HD :].astype(bf16)
    copies = []
    for i in range(seqs):
        rows = slice(i * stretch, (i + 1) * stretch)
        keyvals[i, reach * stretch :, :HD] = key[rows]
        keyvals[i, reach * stretch :, HD:] = late_values[rows]
        for step, device in enumerate(devices):
            copy = pltpu.make_async_remote_copy(
                src_ref=keyvals.at[i, pl.ds(reach * stretch, stretch)],
                dst_ref=keyvals.at[i, pl.ds((reach - 1 - step) * stretch, stretch)],
                send_sem=send_sem.at[i, step],
                recv_sem=recv_sem.at[i, step],
                device_id=device,
                device_id_type=MESH,
            )
            copy.start()
            copies.append(copy)
    for h in range(HEADS):
        columns = slice(h * HD, (h + 1) * HD)
        query = mixed[:, columns]
        query = turn(query * inverse_rms(query) * gains[0:1, 2 * D :], cosine[...], sine[...])
        queries[:, columns] = query.astype(bf16)
    for copy in copies:
        copy.wait_recv()
    save = pltpu.make_async_copy(keyvals, keyvals_out, save_sem)
    save.start()
    for i in range(seqs):
        rows = slice(i * stretch, (i + 1) * stretch)
        for h in range(HEADS):
            columns = slice(h * HD, (h + 1) * HD)
            soft = soft_rows(queries[rows, columns], keyvals[i, :, :HD], bias[i])
            attended[rows, columns] = matmul(soft.astype(bf16), keyvals[i, :, HD:]).astype(bf16)
    out = matmul(attended[...], w_project[...])
    projected[...] = out
    half = hidden[...] + out * inverse_rms(out) * gains[0:1, D : 2 * D]
    hidden_half[...] = half
    normed_ffn[...] = (half * inverse_rms(half) * gains[1:2, :D]).astype(bf16)
    for copy in copies:
        copy.wait_send()
    save.wait()


def attn_forward(base, weights, gains, tables, bias, planes, reach, ident, earlier=None):
    tokens = base.shape[0]
    seqs, _, key_len = bias.shape
    shape = jax.ShapeDtypeStruct
    operands = [base] + list(earlier or []) + list(weights) + [gains, *tables, bias]
    here, there = pl.BlockSpec(memory_space=pltpu.VMEM), pl.BlockSpec(memory_space=pl.ANY)
    dma = pltpu.SemaphoreType.DMA
    return pl.pallas_call(
        partial(attn_forward_kernel, planes, reach, earlier is not None),
        out_shape=[
            shape((tokens, D), f32),
            shape((tokens, D), bf16),
            shape((tokens, weights[0].shape[1]), f32),
            shape((tokens, HEADS * HD), bf16),
            shape((seqs, key_len, 2 * HD), bf16),
            shape((tokens, HEADS * HD), bf16),
            shape((tokens, D), f32),
            shape((tokens, D), f32),
            shape((tokens, D), bf16),
        ],
        in_specs=[here] * len(operands),
        out_specs=[here] * 4 + [there] + [here] * 4,
        scratch_shapes=[
            pltpu.VMEM((seqs, key_len, 2 * HD), bf16),
            dma((seqs, reach)),
            dma((seqs, reach)),
            dma,
        ],
        compiler_params=pltpu.CompilerParams(
            collective_id=ident, has_side_effects=True, vmem_limit_bytes=56 * 2**20
        ),
    )(*operands)


def attn_backward_kernel(planes, reach, chained, *refs):
    rest = list(refs)
    take = lambda number: [rest.pop(0) for _ in range(number)]
    d_ffn, above, hidden, mixed, queries, keyvals, projected, hidden_half = take(8)
    w_mixed, w_project, gains, cosine, sine, bias = take(6)
    if chained:
        down, before = take(2)
    grad, d_mixed, d_projected, gain_grads = take(4)
    if chained:
        d_down, d_post = take(2)
    d_keyvals, outgoing, incoming, d_attended, send_sem, recv_sem = take(6)
    seqs, stretch, key_len = bias.shape
    devices, sources = neighbours(planes, reach, -1)
    enter(devices + sources)
    scale = 1.0 / math.sqrt(HD)
    part, gain_row = rms_back(d_ffn[...], hidden_half[...], gains[1:2, :D])
    gain_grads[1:2, :D] = gain_row
    gain_grads[1:2, D : 2 * D] = jnp.zeros((1, D), f32)
    grad[...] = part + above[...]
    part, gain_row = rms_back(grad[...], projected[...], gains[0:1, D : 2 * D])
    gain_grads[0:1, D : 2 * D] = gain_row
    low = part.astype(bf16)
    d_projected[...] = low
    d_attended[...] = lax.dot_general(
        low, w_project[...], ACROSS, preferred_element_type=f32
    ).astype(bf16)
    query_gain = jnp.zeros((1, HD), f32)
    for i in range(seqs):
        rows = slice(i * stretch, (i + 1) * stretch)
        d_keys = d_values = None
        for h in range(HEADS):
            columns = slice(h * HD, (h + 1) * HD)
            query, d_out = queries[rows, columns], d_attended[rows, columns]
            keys, values = keyvals[i, :, :HD], keyvals[i, :, HD:]
            soft = soft_rows(query, keys, bias[i])
            d_soft = lax.dot_general(d_out, values, ACROSS, preferred_element_type=f32)
            total = jnp.sum(soft * d_soft, axis=-1, keepdims=True)
            d_scores = (soft * (d_soft - total)).astype(bf16)
            key_part = lax.dot_general(d_scores, query, ALONG, preferred_element_type=f32)
            value_part = lax.dot_general(
                soft.astype(bf16), d_out, ALONG, preferred_element_type=f32
            )
            d_keys = key_part if d_keys is None else d_keys + key_part
            d_values = value_part if d_values is None else d_values + value_part
            d_query = matmul(d_scores, keys) * scale
            d_query = turn(d_query, cosine[rows], -sine[rows])
            part, gain_row = rms_back(d_query, mixed[rows, columns], gains[0:1, 2 * D :])
            query_gain = query_gain + gain_row
            d_mixed[rows, columns] = part.astype(bf16)
        d_keyvals[i, :, :HD] = d_keys * scale
        d_keyvals[i, :, HD:] = d_values
    gain_grads[0:1, 2 * D :] = query_gain
    outgoing[...] = d_keyvals[:, : reach * stretch].astype(bf16)
    copies = []
    for i in range(seqs):
        for step, device in enumerate(devices):
            copy = pltpu.make_async_remote_copy(
                src_ref=outgoing.at[i, pl.ds((reach - 1 - step) * stretch, stretch)],
                dst_ref=incoming.at[i, step],
                send_sem=send_sem.at[i, step],
                recv_sem=recv_sem.at[i, step],
                device_id=device,
                device_id_type=MESH,
            )
            copy.start()
            copies.append(copy)
    for copy in copies:
        copy.wait_recv()
    key_gain = jnp.zeros((1, HD), f32)
    for i in range(seqs):
        rows = slice(i * stretch, (i + 1) * stretch)
        own = d_keyvals[i, reach * stretch :]
        for step in range(reach):
            own = own + incoming[i, step].astype(f32)
        d_key = turn(own[:, :HD], cosine[rows], -sine[rows])
        part, gain_row = rms_back(
            d_key, mixed[rows, HEADS * HD : HEADS * HD + HD], gains[1:2, 2 * D :]
        )
        key_gain = key_gain + gain_row
        d_mixed[rows, HEADS * HD : HEADS * HD + HD] = part.astype(bf16)
        d_mixed[rows, HEADS * HD + HD :] = own[:, HD:].astype(bf16)
    gain_grads[1:2, 2 * D :] = key_gain
    d_normed = lax.dot_general(d_mixed[...], w_mixed[...], ACROSS, preferred_element_type=f32)
    part, gain_row = rms_back(d_normed, hidden[...], gains[0:1, :D])
    gain_grads[0:1, :D] = gain_row
    grad[...] = grad[...] + part
    if chained:
        part, gain_row = rms_back(grad[...], down[...], before[1:2, D : 2 * D])
        d_down[...] = part.astype(bf16)
        d_post[...] = gain_row
    for copy in copies:
        copy.wait_send()


def attn_backward(
    d_ffn, above, kept, weights, gains, tables, bias, planes, reach, ident, earlier=None
):
    tokens = above.shape[0]
    seqs, stretch, key_len = bias.shape
    shape = jax.ShapeDtypeStruct
    operands = [d_ffn, above, *kept, *weights, gains, *tables, bias] + list(earlier or [])
    outs = [
        shape((tokens, D), f32),
        shape((tokens, weights[0].shape[1]), bf16),
        shape((tokens, D), bf16),
        shape(gains.shape, f32),
    ]
    if earlier is not None:
        outs += [shape((tokens, D), bf16), shape((1, D), f32)]
    here = pl.BlockSpec(memory_space=pltpu.VMEM)
    vmem, dma = pltpu.VMEM, pltpu.SemaphoreType.DMA
    return pl.pallas_call(
        partial(attn_backward_kernel, planes, reach, earlier is not None),
        out_shape=outs,
        in_specs=[here] * len(operands),
        out_specs=[here] * len(outs),
        scratch_shapes=[
            vmem((seqs, key_len, 2 * HD), f32),
            vmem((seqs, reach * stretch, 2 * HD), bf16),
            vmem((seqs, reach, stretch, 2 * HD), bf16),
            vmem((tokens, HEADS * HD), bf16),
            dma((seqs, reach)),
            dma((seqs, reach)),
        ],
        compiler_params=pltpu.CompilerParams(
            collective_id=ident, has_side_effects=True, vmem_limit_bytes=56 * 2**20
        ),
    )(*operands)


GELU_SLOPE = math.sqrt(2.0 / math.pi)
GELU_CUBE = 0.044715
ACROSS = (((1,), (1,)), ((), ()))
ALONG = (((0,), (0,)), ((), ()))


class Plane:
    def __init__(self, own, bufs, sems):
        self.own = own
        self.rows, self.partial, self.other, self.lands, self.sums, self.arrived = bufs
        self.x_send, self.x_recv, self.f_send, self.f_recv = sems[:4]
        self.c_send, self.c_recv, self.p_send, self.p_recv, self.first = sems[4:]
        self.tp = lax.axis_index("tp")
        self.sibling = {"head": 1 - lax.axis_index("head")}

    def member(self, m):
        tp = self.tp
        upper = lax.rem(lax.div(tp, 2) + lax.div(m, 2), 2)
        lower = lax.rem(lax.rem(tp, 2) + lax.rem(m, 2), 2)
        return {"tp": upper * 2 + lower}

    def remote(self, src, dst, send, recv, device):
        return pltpu.make_async_remote_copy(
            src_ref=src,
            dst_ref=dst,
            send_sem=send,
            recv_sem=recv,
            device_id=device,
            device_id_type=MESH,
        )

    def push(self, m):
        return self.remote(
            self.own, self.rows.at[0, m], self.x_send.at[m], self.x_recv.at[m], self.member(m)
        )

    def keep(self):
        return pltpu.make_async_copy(self.own, self.rows.at[0, 0], self.first)

    def forward(self, m):
        return self.remote(
            self.rows.at[0, m],
            self.rows.at[1, m],
            self.f_send.at[m],
            self.f_recv.at[m],
            self.sibling,
        )

    def cross(self, m):
        return self.remote(
            self.other.at[m], self.lands.at[m], self.c_send.at[m], self.c_recv.at[m], self.sibling
        )

    def home(self, m):
        return self.remote(
            self.sums.at[m],
            self.arrived.at[m],
            self.p_send.at[m],
            self.p_recv.at[m],
            self.member(m),
        )

    def begin(self):
        self.keep().start()
        enter([self.sibling] + [self.member(jnp.int32(m)) for m in range(1, PLANE)])
        for m in range(1, PLANE):
            self.push(jnp.int32(m)).start()

    def work(self, compute):
        def settle(m):
            self.cross(m).wait_recv()

            def add(rows):
                value = self.partial[m, rows] + self.lands[m, rows].astype(f32)
                self.sums[m, rows] = value.astype(bf16)

            by_rows(self.partial.shape[1], add)
            self.home(m).start()

        def step(m, carry):
            @pl.when(m == 0)
            def _():
                self.keep().wait()

            @pl.when(m > 0)
            def _():
                self.push(m).wait_recv()

            self.forward(m).start()
            self.partial[m] = compute(0, m)
            self.forward(m).wait_recv()
            self.other[m] = compute(1, m).astype(bf16)
            self.cross(m).start()

            @pl.when(m >= 2)
            def _():
                settle(m - 1)

            return carry

        lax.fori_loop(0, PLANE, step, 0)
        settle(jnp.int32(PLANE - 1))

    def finish(self, result):
        self.cross(jnp.int32(0)).wait_recv()
        for m in range(1, PLANE):
            self.home(jnp.int32(m)).wait_recv()

        def add(rows):
            value = self.partial[0, rows] + self.lands[0, rows].astype(f32)
            for m in range(1, PLANE):
                value = value + self.arrived[m, rows].astype(f32)
            result[rows] = value

        by_rows(result.shape[0], add)
        for m in range(PLANE):
            m = jnp.int32(m)
            self.forward(m).wait_send()
            self.cross(m).wait_send()
        for m in range(1, PLANE):
            m = jnp.int32(m)
            self.push(m).wait_send()
            self.home(m).wait_send()


def chunks(extent, step=256):
    return [slice(at, min(at + step, extent)) for at in range(0, extent, step)]


def gate_up_copies(gu_ref, gate_up, sem):
    blocks = gu_ref.shape[0]
    rows = gate_up.shape[1] // blocks
    return [
        pltpu.make_async_copy(
            gu_ref.at[block, part],
            gate_up.at[part, pl.ds(block * rows, rows)],
            sem.at[2 * block + part],
        )
        for block in range(blocks)
        for part in range(2)
    ]


def ffn_forward_kernel(own, gu_ref, halves_ref, group, saved_down, result, *scratch):
    rows, gate_up, down = scratch[:3]
    plane = Plane(own, (rows,) + scratch[3:8], scratch[8:17])
    weight_sem, group_sem, halves, half_send, half_recv, half_own, save_sem = scratch[17:]
    core = lax.axis_index("head")
    share, width = halves.shape[1:]
    copies = gate_up_copies(gu_ref, gate_up, weight_sem)
    copies.append(
        pltpu.make_async_copy(
            halves_ref.at[0, pl.ds(pl.multiple_of(core * share, 16), share)],
            halves.at[core],
            half_own,
        )
    )
    for copy in copies:
        copy.start()
    plane.begin()
    half = plane.remote(
        halves_ref.at[0, pl.ds(pl.multiple_of((1 - core) * share, 16), share)],
        halves.at[core],
        half_send,
        half_recv,
        plane.sibling,
    )
    half.start()
    for copy in copies:
        copy.wait()
    pltpu.make_async_remote_copy(
        src_ref=halves_ref.at[0, pl.ds(pl.multiple_of((1 - core) * share, 16), share)],
        dst_ref=halves.at[1 - core],
        send_sem=half_send,
        recv_sem=half_recv,
        device_id=plane.sibling,
        device_id_type=MESH,
    ).wait_recv()

    def join(at):
        down[at] = jnp.concatenate([halves[h, at] for h in range(2)], axis=1)

    by_rows(share, join, 32)
    keep_down = pltpu.make_async_copy(down, saved_down, save_sem)
    keep_down.start()

    def compute(side, m):
        tokens, total = rows[side, m], None
        for columns in chunks(share):
            gate = matmul(tokens, gate_up[0, :, columns])
            up = matmul(tokens, gate_up[1, :, columns])
            bend = jnp.tanh(GELU_SLOPE * (gate + GELU_CUBE * (gate * gate * gate)))
            inner = (0.5 * gate * (1.0 + bend) * up).astype(bf16)
            part = matmul(inner, down[columns])
            total = part if total is None else total + part
        return total

    plane.work(compute)
    save = pltpu.make_async_copy(rows, group, group_sem)
    save.start()
    plane.finish(result)
    save.wait()
    keep_down.wait()
    half.wait_send()


def ffn_backward_kernel(
    own, group, gu_ref, down_ref, result, grad_gu, grad_down, *scratch
):
    rows, gate_up, down = scratch[:3]
    plane = Plane(own, (rows,) + scratch[3:8], scratch[8:17])
    weight_sem, group_sem, saved, d_gate, d_up, inner = scratch[17:23]
    down_sem, turned, down_halves, half_send, half_recv, half_own = scratch[23:29]
    share = down.shape[0]
    core = lax.axis_index("head")
    copies = gate_up_copies(gu_ref, gate_up, weight_sem)
    copies.append(pltpu.make_async_copy(down_ref, down, down_sem))
    for copy in copies:
        copy.start()
    load = pltpu.make_async_copy(group, saved, group_sem)
    load.start()
    plane.begin()
    for copy in copies:
        copy.wait()
    load.wait()

    def recompute(index, carry):
        side, m = lax.div(index, PLANE), lax.rem(index, PLANE)
        tokens = saved[side, m]
        for columns in chunks(share):
            gate = matmul(tokens, gate_up[0, :, columns])
            up = matmul(tokens, gate_up[1, :, columns])
            square = gate * gate
            bend = jnp.tanh(GELU_SLOPE * (gate + GELU_CUBE * (square * gate)))
            half = 0.5 * (1.0 + bend)
            value = gate * half
            slope = half + (0.5 * GELU_SLOPE) * gate * (1.0 - bend * bend) * (
                1.0 + (3.0 * GELU_CUBE) * square
            )
            inner[side, m, :, columns] = (value * up).astype(bf16)
            d_gate[side, m, :, columns] = (slope * up).astype(bf16)
            d_up[side, m, :, columns] = value.astype(bf16)
        return carry

    lax.fori_loop(0, 2 * PLANE, recompute, 0)

    def compute(side, m):
        tokens, total = rows[side, m], None
        for columns in chunks(share):
            d_inner = lax.dot_general(tokens, down[columns], ACROSS, preferred_element_type=f32)
            gate = (d_inner * d_gate[side, m, :, columns].astype(f32)).astype(bf16)
            up = (d_inner * d_up[side, m, :, columns].astype(f32)).astype(bf16)
            d_gate[side, m, :, columns] = gate
            d_up[side, m, :, columns] = up
            part = lax.dot_general(
                gate, gate_up[0, :, columns], ACROSS, preferred_element_type=f32
            ) + lax.dot_general(up, gate_up[1, :, columns], ACROSS, preferred_element_type=f32)
            total = part if total is None else total + part
        return total

    plane.work(compute)
    width = rows.shape[-1]
    step = width // 3

    by_planes = len(grad_gu.shape) == 4
    sides = scratch[29] if by_planes else grad_gu

    def tall(ref, columns=slice(None)):
        value = ref[:, :, :, columns]
        return value.reshape(-1, value.shape[-1])

    @pl.loop(0, 3)
    def _(index):
        at = pl.ds(pl.multiple_of(index * step, step), step)
        tokens = tall(saved, at)
        for part, other in enumerate((d_gate, d_up)):
            sides[part, at] = lax.dot_general(
                tokens, tall(other), ALONG, preferred_element_type=f32
            ).astype(bf16)
        turned[at] = lax.dot_general(
            tall(rows, at), tall(inner), ALONG, preferred_element_type=f32
        ).astype(bf16)

    stores = []
    if by_planes:
        for plane_at in range(grad_gu.shape[0]):
            for part in range(2):
                height = grad_gu.shape[2]
                copy = pltpu.make_async_copy(
                    sides.at[part, pl.ds(plane_at * height, height)],
                    grad_gu.at[plane_at, part],
                    scratch[30].at[2 * plane_at + part],
                )
                copy.start()
                stores.append(copy)
    half_width = down_halves.shape[2]
    for h in range(2):
        down_halves[h] = turned[h * half_width : (h + 1) * half_width].T
    half = plane.remote(
        down_halves.at[1 - core], grad_down.at[core], half_send, half_recv, plane.sibling
    )
    half.start()
    stay = pltpu.make_async_copy(down_halves.at[core], grad_down.at[core], half_own)
    stay.start()
    plane.finish(result)
    half.wait()
    stay.wait()
    for copy in stores:
        copy.wait()


def ffn(own, weights, ident, planes, group=None):
    gate_up, down = weights
    tokens, width = own.shape
    blocks, _, _, share = gate_up.shape
    vmem, dma = pltpu.VMEM, pltpu.SemaphoreType.DMA
    scratch = [
        vmem((2, PLANE, tokens, width), bf16),
        vmem((2, width, share), bf16),
        vmem((share, width), bf16),
        vmem((PLANE, tokens, width), f32),
    ]
    scratch += [vmem((PLANE, tokens, width), bf16)] * 4
    scratch += [dma((PLANE,))] * 8 + [dma, dma((2 * blocks,)), dma]
    here, there = pl.BlockSpec(memory_space=pltpu.VMEM), pl.BlockSpec(memory_space=pl.ANY)
    shape = jax.ShapeDtypeStruct
    summed = shape((tokens, width), f32)
    if group is None:
        kernel, operands = ffn_forward_kernel, (own, gate_up, down)
        in_specs, out_specs = [here, there, there], [there, there, here]
        out_shape = [
            shape((2, PLANE, tokens, width), bf16),
            shape((share, width), bf16),
            summed,
        ]
        scratch += [vmem((2, share, width // 2), bf16)] + [dma] * 4
    else:
        kernel, operands = ffn_backward_kernel, (own, group, gate_up, down)
        by_planes = width // planes % 16 == 0
        sides = (2, width, share)
        in_specs = [here, there, there, there]
        out_specs = [here, there if by_planes else here, there]
        out_shape = [
            summed,
            shape((planes, 2, width // planes, share) if by_planes else sides, bf16),
            shape((2, share, width // 2), bf16),
        ]
        scratch += [vmem((2, PLANE, tokens, width), bf16)]
        scratch += [vmem((2, PLANE, tokens, share), bf16)] * 3
        scratch += [dma, vmem((width, share), bf16), vmem((2, share, width // 2), bf16)]
        scratch += [dma] * 3
        if by_planes:
            scratch += [vmem(sides, bf16), dma((2 * planes,))]
    return pl.pallas_call(
        kernel,
        out_shape=out_shape,
        in_specs=in_specs,
        out_specs=out_specs,
        scratch_shapes=scratch,
        cost_estimate=LIGHT,
        compiler_params=pltpu.CompilerParams(
            collective_id=ident, has_side_effects=True, vmem_limit_bytes=60 * 2**20
        ),
    )(*operands)


def exact(left, right, dims=(((1,), (0,)), ((), ()))):
    return lax.dot_general(
        left, right, dims, precision=finest_precision, preferred_element_type=f32
    )


def update_kernel(sizes, counts, *refs):
    cores, planes, members = sizes
    rest = list(refs)
    take = lambda number: [rest.pop(0) for _ in range(number)]
    plain = [take(number) for number in counts]
    sides = take(cores)
    moments_in, weights_in, weights_out, moments_out = (take(4) for _ in range(4))
    moment, weight, gram, land, factor = (take(4) for _ in range(5))
    pieces, arrived = take(2)
    load_sem, store_sem, gram_send, gram_recv, factor_send, factor_recv = take(6)
    gu_send, gu_recv, gu_own = take(3)
    core, _, tp = (lax.axis_index(axis) for axis in EVERY)
    sibling = {"head": 1 - core}
    order = (0, 1, 3, 2)
    loads = {}
    for k in range(4):
        for part, source, target in ((0, moments_in, moment), (1, weights_in, weight)):
            copy = pltpu.make_async_copy(source[k], target[k], load_sem.at[part, k])
            copy.start()
            loads[part, k] = copy
    group = []
    for step in range(1, cores * members):
        far = lax.rem(core + step // members, cores), lax.rem(tp + step % members, members)
        group.append((dict(zip(GROUP, far)), linear(far, (cores, members))))
    enter([device for device, _ in group])
    rows = moment[2].shape[1]
    for part in range(cores):
        for j in range(members):
            for layer in range(cores):
                at = (part * members + j) * rows
                pieces[part * members + j, layer * rows : (layer + 1) * rows] = sides[layer][
                    at : at + rows
                ]
    if pieces.shape[1] > cores * rows:
        for piece in range(cores * members):
            pieces[piece, cores * rows :] = jnp.zeros(
                (pieces.shape[1] - cores * rows, pieces.shape[2]), bf16
            )
    me = linear((core, tp), (cores, members))
    moves, stores = [], []

    def send(src, dst, send_sem, recv_sem, device):
        copy = pltpu.make_async_remote_copy(
            src_ref=src,
            dst_ref=dst,
            send_sem=send_sem,
            recv_sem=recv_sem,
            device_id=device,
            device_id_type=MESH,
        )
        copy.start()
        return copy

    for step, (device, index) in enumerate(group):
        moves.append(
            send(pieces.at[index], arrived.at[me], gu_send.at[step], gu_recv.at[step], device)
        )
    own = pltpu.make_async_copy(pieces.at[me], arrived.at[me], gu_own)
    own.start()

    def store(part, k):
        source, target = (moment, moments_out) if part == 0 else (weight, weights_out)
        copy = pltpu.make_async_copy(source[k], target[k], store_sem.at[part, k])
        copy.start()
        stores.append(copy)

    def gram_of(k):
        def one(layer, carry):
            gram[k][layer] = exact(moment[k][layer], moment[k][layer], ACROSS)
            return carry

        lax.fori_loop(0, cores, one, 0)
        return send(
            gram[k].at[1 - core], land[k], gram_send.at[k], gram_recv.at[k], sibling
        )

    def unit(size):
        down = lax.broadcasted_iota(jnp.int32, (size, size), 0)
        return (down == lax.broadcasted_iota(jnp.int32, (size, size), 1)).astype(f32)

    def orthogonal(members_of):
        for k in members_of:
            total = gram[k][core] + land[k][...]
            one = unit(total.shape[0])
            trace = jnp.sum(jnp.sum(total * one, axis=1, keepdims=True), axis=0, keepdims=True)
            scale = 1.0 / (jnp.sqrt(trace) + 1e-07)
            land[k][...] = total * (scale * scale)
            factor[k][core] = one * scale

        def polynomial(present):
            square = exact(present, present)
            return newton_one * unit(present.shape[0]) + newton_two * present + (
                newton_three * square
            )

        def step(_, carry):
            for k in members_of:
                present = land[k][...]
                poly = polynomial(present)
                factor[k][core] = exact(poly, factor[k][core])
                land[k][...] = exact(exact(poly, present), poly)
            return carry

        lax.fori_loop(0, NS_ITERS - 1, step, 0)
        for k in members_of:
            factor[k][core] = exact(polynomial(land[k][...]), factor[k][core])
        return [
            send(factor[k].at[core], factor[k].at[core], factor_send.at[k], factor_recv.at[k], sibling)
            for k in members_of
        ]

    def apply(k):
        columns = weight[k].shape[2] * cores
        rate = muon_rate * muon_scale * math.sqrt(columns)

        def one(layer, carry):
            weight[k][layer] = weight[k][layer] * (1.0 - muon_rate * muon_shrink) - rate * exact(
                factor[k][layer], moment[k][layer]
            )
            return carry

        lax.fori_loop(0, cores, one, 0)
        store(1, k)

    def arrive(copies):
        for copy in copies:
            copy.wait_recv()

    sent = []
    for index, k in enumerate(order[:3]):
        loads[0, k].wait()
        height = moment[k].shape[1]
        for layer in range(cores):
            if len(plain[index]) == 1:
                gradient = plain[index][0][layer * height : (layer + 1) * height]
            else:
                gradient = plain[index][layer][...].astype(f32)
            moment[k][layer] = muon_decay * moment[k][layer] + gradient
        store(0, k)
        sent.append(gram_of(k))
    arrive(sent)
    crossed = orthogonal(order[:3])
    sent += crossed
    own.wait()
    for copy in moves:
        copy.wait_recv()
    loads[0, 2].wait()
    half = planes // cores
    block = arrived.shape[2] // half
    for layer in range(cores):
        cut = [
            arrived[
                c * members + j,
                layer * rows : (layer + 1) * rows,
                k * block : (k + 1) * block,
            ].astype(f32)
            for c in range(cores)
            for k in range(half)
            for j in range(members)
        ]
        moment[2][layer] = muon_decay * moment[2][layer] + jnp.concatenate(cut, axis=1)
    store(0, 2)
    last = gram_of(2)
    sent.append(last)
    arrive(crossed)
    for k in range(4):
        loads[1, k].wait()
    for k in order[:3]:
        apply(k)
    arrive([last])
    crossed = orthogonal(order[3:])
    sent += crossed
    arrive(crossed)
    apply(2)
    for copy in moves + sent:
        copy.wait_send()
    for copy in stores:
        copy.wait()


def update(gradients, sides, moments, weights, ident):
    sizes = tuple(lax.axis_size(axis) for axis in EVERY)
    cores, planes, members = sizes
    vmem, dma = pltpu.VMEM, pltpu.SemaphoreType.DMA
    layers, rows, columns = moments[2].shape
    piece = (
        cores * members,
        -(-layers * rows // 16) * 16,
        columns // (cores * members),
    )
    shapes = [m.shape for m in moments]
    square = [(s[1], s[1]) for s in shapes]
    scratch = [vmem(s, f32) for s in shapes] * 2
    scratch += [vmem((layers,) + s, f32) for s in square]
    scratch += [vmem(s, f32) for s in square]
    scratch += [vmem((layers,) + s, f32) for s in square]
    scratch += [vmem(piece, bf16)] * 2
    scratch += [dma((2, 4))] * 2 + [dma((4,))] * 4
    scratch += [dma((cores * members - 1,))] * 2 + [dma]
    here, there = pl.BlockSpec(memory_space=pltpu.VMEM), pl.BlockSpec(memory_space=pl.ANY)
    operands = sum(gradients, []) + sides
    return pl.pallas_call(
        partial(update_kernel, sizes, [len(g) for g in gradients]),
        out_shape=[jax.ShapeDtypeStruct(s, f32) for s in shapes] * 2,
        in_specs=[here] * len(operands) + [there] * 8,
        out_specs=[there] * 8,
        scratch_shapes=scratch,
        compiler_params=pltpu.CompilerParams(
            collective_id=ident, has_side_effects=True, vmem_limit_bytes=56 * 2**20
        ),
    )(*operands, *moments, *weights)


def padded(array, multiple=16):
    extra = -array.shape[-2] % multiple
    if extra == 0:
        return array
    return jnp.pad(array, [(0, 0)] * (array.ndim - 2) + [(0, extra), (0, 0)])


def rms_norm(values, norm_gain):
    return (
        values * lax.rsqrt(jnp.mean(values * values, axis=-1, keepdims=True) + norm_eps) * norm_gain
    )


def rope_tables(positions, head_dim):
    half_dim = head_dim // 2
    frequency = jnp.exp(
        jnp.arange(half_dim, dtype=jnp.float32) * (-2.0 * math.log(rope_base) / head_dim)
    )
    angles = positions.astype(jnp.float32)[:, None] * frequency[None, :]
    return (jnp.cos(angles), jnp.sin(angles))


def matmul(left, right):
    return jnp.dot(left, right, preferred_element_type=f32)


def body(
    inputs,
    cotangent,
    teacher,
    segments,
    valid_mask,
    w_qkv,
    w_out,
    w_gu,
    w_down,
    norm_gains,
    mom_qkv,
    mom_out,
    mom_gu,
    mom_down,
    gain_first,
    gain_second,
):
    cores = lax.axis_size("head")
    planes = lax.axis_size("zd")
    seq_devices = planes * PLANE
    core = lax.axis_index("head")
    seq_place = lax.axis_index("zd") * PLANE + lax.axis_index("tp")
    half_seqs, stretch_len = inputs.shape[:2]
    tokens = half_seqs * stretch_len
    all_seqs = half_seqs * cores
    seq_length = stretch_len * seq_devices
    reach = -(-WINDOW // stretch_len)
    key_len = (reach + 1) * stretch_len
    qkv_rows, qkv_cols = w_qkv.shape[1:]
    out_rows, out_cols = w_out.shape[1:]
    gu_rows = w_gu.shape[1]
    ff_block = w_down.shape[1]
    share = FF // (cores * PLANE)
    half_planes = planes // cores
    gain_cols = norm_gains.shape[-1]
    gain_len = gain_cols * seq_devices
    lanes = -(-gain_cols // 128) * 128

    packet = jnp.zeros((8, lanes), f32)
    packet = packet.at[:LAYERS, :gain_cols].set(norm_gains[:, 0].astype(bf16).astype(f32))
    packet = packet.at[LAYERS, 0].set(jnp.sum(valid_mask.astype(f32)))
    gu_pieces, w_mixed, w_project, packets, *later = start(
        w_gu, w_qkv, w_out, packet, 0
    )
    attn_weights = [w_mixed, w_project]
    gu_pieces = gu_pieces[:, : LAYERS * gu_rows].reshape(cores * PLANE, LAYERS, gu_rows, share)
    packets = packets.reshape(cores, seq_devices, 8, lanes)
    valid_count = jnp.sum(packets[:, :, LAYERS, 0])
    gain_rows = [
        packets[:, :, layer, :gain_cols].reshape(cores, gain_len) for layer in range(LAYERS)
    ]

    def gate_up_rows(layer):
        pieces = gu_pieces[:, layer].reshape(2, PLANE * gu_rows, share)
        pieces = lax.all_gather(pieces, "zd", axis=0)
        if PLANE * gu_rows % 16:
            pieces = pieces.transpose(1, 0, 2, 3).reshape(1, 2, D, share)
        return pieces

    def down_rows(layer):
        rows = w_down[layer : layer + 1].astype(bf16)
        return lax.all_gather(rows, "zd", axis=1, tiled=True)

    full = [(gate_up_rows(0), down_rows(0))] + [None] * (LAYERS - 1)

    own_places = seq_place * stretch_len + jnp.arange(stretch_len, dtype=jnp.int32)
    key_places = (seq_place - reach) * stretch_len + jnp.arange(key_len, dtype=jnp.int32)
    cosine_table, sine_table = rope_tables(own_places, HD)
    own_rows = lax.dynamic_slice_in_dim(segments, core * half_seqs, half_seqs, 0)
    own_segments = lax.dynamic_slice_in_dim(own_rows, seq_place * stretch_len, stretch_len, 1)
    padded_segments = jnp.pad(own_rows, ((0, 0), (reach * stretch_len, 0)), constant_values=-1)
    key_segments = lax.dynamic_slice_in_dim(padded_segments, seq_place * stretch_len, key_len, 1)
    spacing = own_places[:, None] - key_places[None, :]
    allowed = (spacing >= 0) & (spacing < WINDOW) & (key_places[None, :] >= 0)
    allowed = allowed[None] & (own_segments[:, :, None] == key_segments[:, None, :])

    tables = [jnp.tile(t, (half_seqs, 1)) for t in (cosine_table, sine_table)]
    bias = jnp.where(allowed, 0.0, -1e30).astype(f32)

    saved, previous = [], None
    base = inputs.reshape(tokens, D)
    for layer in range(LAYERS):
        weights = list(attn_weights)
        hidden, normed, mixed, queries, keyvals, attended, projected, half, normed_ffn = attn_forward(
            base, weights, gain_rows[layer], tables, bias, planes, reach, 3 + layer, previous
        )
        ffn_share = full[layer]
        if layer + 1 < LAYERS:
            gu_pieces, w_down, later, attended = lax.optimization_barrier(
                (gu_pieces, w_down, later, attended)
            )
            attn_weights = later_weights(later, w_qkv, w_out, layer + 1, 2 + 20 * layer)
            full[layer + 1] = (gate_up_rows(layer + 1), down_rows(layer + 1))
            normed_ffn, *attn_weights = lax.optimization_barrier((normed_ffn, *attn_weights))
        group_normed, whole_down, down_out = ffn(normed_ffn, ffn_share, 5 + layer, planes)
        full[layer] = (weights, (ffn_share[0], whole_down))
        saved.append(
            (
                [hidden, mixed, queries, keyvals, projected, half],
                [normed, attended],
                group_normed,
                down_out,
            )
        )
        base, previous = half, (down_out, gain_rows[layer])

    output, post_ffn_back = jax.vjp(rms_norm, down_out, gain_rows[-1][1, D : 2 * D])
    output = base + output
    target_gap = output - teacher.reshape(tokens, D).astype(f32)
    valid_weight = valid_mask.astype(f32).reshape(tokens, 1)
    square_sum = jnp.sum(valid_weight * target_gap * target_gap)
    loss_weight = float(all_seqs * seq_length * D // 4)
    grad_hidden = (
        cotangent.reshape(tokens, D).astype(f32)
        + 2.0 * loss_weight / (valid_count * D) * valid_weight * target_gap
    )
    d_down, d_post_ffn = post_ffn_back(grad_hidden)
    d_down, d_post_ffn = d_down.astype(bf16), d_post_ffn[None]

    tiled = ff_block % 16 == 0
    attn_acts = [None] * LAYERS
    down_grads = [None] * LAYERS
    gain_grads = [None] * LAYERS
    gu_sums = [None] * LAYERS
    for layer in reversed(range(LAYERS)):
        kept, (normed, attended), group_normed, _ = saved[layer]
        weights, ffn_share = full[layer]
        d_normed_ffn, grad_gu, grad_down = ffn(
            d_down, ffn_share, 9 + layer, planes, group_normed
        )
        if layer == 0 and tiled:
            first_down = grad_down.reshape(planes, ff_block, out_cols)
        else:
            down_grads[layer] = lax.psum_scatter(
                grad_down.reshape(planes * ff_block, out_cols),
                "zd",
                scatter_dimension=0,
                tiled=True,
            )
        if len(grad_gu.shape) == 3:
            grad_gu = grad_gu.reshape(2, planes, PLANE * gu_rows, share).transpose(1, 0, 2, 3)
        gu_sums[layer] = lax.psum_scatter(
            grad_gu.reshape(-1, share), "zd", scatter_dimension=0, tiled=True
        )
        earlier = (saved[layer - 1][3], gain_rows[layer - 1]) if layer > 0 else None
        grad_hidden, d_mixed, d_projected, gain_grads[layer], *d_rest = attn_backward(
            d_normed_ffn,
            grad_hidden,
            kept,
            weights,
            gain_rows[layer],
            tables,
            bias,
            planes,
            reach,
            17 + layer,
            earlier,
        )
        gain_grads[layer] = gain_grads[layer].at[1:, D : 2 * D].set(d_post_ffn)
        if layer > 0:
            d_down, d_post_ffn = d_rest
        attn_acts[layer] = [normed, d_mixed, attended, d_projected]
    attn_acts[0][1], gu_sums[1:], down_grads[1:] = lax.optimization_barrier(
        (attn_acts[0][1], gu_sums[1:], down_grads[1:])
    )

    packet = jnp.stack(gain_grads, axis=1).reshape(cores, LAYERS, planes, PLANE, gain_cols)
    packet = packet.transpose(0, 3, 2, 1, 4)
    packet = jnp.pad(packet, [(0, 0)] * 3 + [(0, 8 - LAYERS), (0, lanes - gain_cols)])
    packet = packet.at[:, :, :, LAYERS, 0].set(square_sum)
    packet = packet.reshape(cores, PLANE, planes * 8, lanes)
    down = first_down if tiled else None
    grad_qkv, grad_out, packet, *summed_down = collect(sum(attn_acts, []), packet, down, 19)
    if tiled:
        (down_grads[0],) = summed_down
    mse_loss = packet[LAYERS, 0] / (valid_count * D)
    gain_grad = packet[:LAYERS, None, :gain_cols]

    outcome = update(
        [[grad_qkv], [grad_out], down_grads],
        gu_sums,
        (mom_qkv, mom_out, mom_gu, mom_down),
        (w_qkv, w_out, w_gu, w_down),
        15,
    )
    new_weights, moments = outcome[:4], outcome[4:]
    gain_first_new = beta_one * gain_first + (1.0 - beta_one) * gain_grad
    gain_second_new = beta_two * gain_second + (1.0 - beta_two) * gain_grad * gain_grad
    gains_new = norm_gains - adam_rate * (gain_first_new / (1.0 - beta_one**STEP)) / (
        jnp.sqrt(gain_second_new / (1.0 - beta_two**STEP)) + adam_epsilon
    )
    return (
        mse_loss,
        output.reshape(inputs.shape),
        grad_hidden.reshape(inputs.shape),
        *new_weights,
        *moments,
        gains_new,
        gain_first_new,
        gain_second_new,
    )


def solution(mesh):
    cores, length = mesh.devices.shape
    split = Mesh(mesh.devices.reshape(cores, length // PLANE, PLANE), EVERY)
    stream = P("head", SEQ, None)
    matrix = P(None, SEQ, "head")
    gains = P(None, "head", SEQ)
    return jax.shard_map(
        body,
        mesh=split,
        in_specs=(stream, stream, stream, P(), P("head", SEQ))
        + (matrix,) * 4
        + (gains,)
        + (matrix,) * 4
        + (gains,) * 2,
        out_specs=(P(), stream, stream) + (matrix,) * 8 + (gains,) * 3,
        check_vma=False,
    )
```

```python
from functools import partial
import itertools
import math

import jax
import jax.numpy as jnp
from jax import lax
from jax.experimental import pallas as pl
from jax.experimental.pallas import tpu as pltpu
from jax.sharding import Mesh, PartitionSpec as P

D = 1152
HEADS = 4
HD = 256
FF = 6912
WINDOW = 512
LAYERS = 2
NS_ITERS = 5
STEP = 10
PLANE = 4

norm_eps = 1e-06
rope_base = 10000.0
newton_one = 3.4445
newton_two = -4.775
newton_three = 2.0315
muon_decay = 0.95
muon_rate = 0.15
muon_shrink = 0.01
muon_scale = 0.2
beta_one = 0.9
beta_two = 0.95
adam_rate = 0.7
adam_epsilon = 1e-08
finest_precision = lax.Precision.HIGHEST
MESH = pl.DeviceIdType.MESH
SEQ = ("zd", "tp")
GROUP = ("head", "tp")
EVERY = ("head", "zd", "tp")
bf16 = jnp.bfloat16
f32 = jnp.float32
LIGHT = pl.CostEstimate(flops=1, bytes_accessed=1, transcendentals=0)


def linear(places, sizes):
    index = 0
    for place, size in zip(places, sizes):
        index = index * size + place
    return index


def enter(partners):
    barrier = pltpu.get_barrier_semaphore()
    for partner in partners:
        pl.semaphore_signal(barrier, inc=1, device_id=partner, device_id_type=MESH)
    pl.semaphore_wait(barrier, len(partners))


class Spread:
    ORDER = ("zd", "tp", "head")

    def __init__(self, sizes, slots, send_sem, recv_sem, whole_z=False):
        self.size = dict(zip(EVERY, sizes))
        self.place = {axis: lax.axis_index(axis) for axis in EVERY}
        self.slots, self.send_sem, self.recv_sem = slots, send_sem, recv_sem
        self.held, self.sends, self.number = [(self.place, None)], [], 0
        if whole_z:
            self.held = [(dict(self.place, zd=z), None) for z in range(self.size["zd"])]
            self.ORDER = self.ORDER[1:]

    def partners(self):
        return [
            {axis: lax.rem(self.place[axis] + step, self.size[axis])}
            for axis in self.ORDER
            for step in range(1, self.size[axis])
        ]

    def stage(self, axis):
        arriving = []
        for where, arrivals in self.held:
            while arrivals:
                arrivals.pop().wait_recv()
            for step in range(1, self.size[axis]):
                to = lax.rem(self.place[axis] + step, self.size[axis])
                back = lax.rem(self.place[axis] - step + self.size[axis], self.size[axis])
                landing = []
                for k, slot in enumerate(self.slots):
                    ref = slot.at[tuple(where[name] for name in EVERY)]
                    copy = pltpu.make_async_remote_copy(
                        src_ref=ref,
                        dst_ref=ref,
                        send_sem=self.send_sem.at[k, self.number],
                        recv_sem=self.recv_sem.at[k, self.number],
                        device_id={axis: to},
                        device_id_type=MESH,
                    )
                    copy.start()
                    self.sends.append(copy)
                    landing.append(copy)
                self.number += 1
                arriving.append((dict(where, **{axis: back}), landing))
        self.held = self.held + arriving

    def finish(self):
        for _, arrivals in self.held:
            while arrivals:
                arrivals.pop().wait_recv()
        for copy in self.sends:
            copy.wait_send()


def start_kernel(sizes, *refs):
    cores, planes, members = sizes
    rest = list(refs)
    take = lambda number: [rest.pop(0) for _ in range(number)]
    gu, qkv, out, packet = take(4)
    gu_result, mixed, project, packets, qkv_later, out_later = take(6)
    packet_slots, qkv_slots, out_slots, send_sem, recv_sem = take(5)
    pieces, gu_send, gu_recv, gu_own, later_send, later_recv = take(6)
    qkv_low, out_low, later_own = take(3)
    gather = Spread(sizes, [packet_slots, qkv_slots, out_slots], send_sem, recv_sem)
    here = tuple(gather.place[name] for name in EVERY)
    core, zd, tp = here
    group = []
    for step in range(1, cores * members):
        far = lax.rem(core + step // members, cores), lax.rem(tp + step % members, members)
        group.append((dict(zip(GROUP, far)), linear(far, (cores, members))))
    enter(gather.partners() + [device for device, _ in group])
    packet_slots[here] = packet[...]

    def place_rows(source, layer, slot, index):
        rows = source.shape[1]
        slot[index + (slice(0, rows),)] = source[layer].astype(bf16)
        if slot.shape[-2] > rows:
            slot[index + (slice(rows, slot.shape[-2]),)] = jnp.zeros(
                (slot.shape[-2] - rows, slot.shape[-1]), bf16
            )

    for source, slot in ((qkv, qkv_slots), (out, out_slots)):
        place_rows(source, 0, slot, here)
    gather.stage("zd")
    moves = []

    def along_z(source, target, sends, recvs):
        for step in range(1, planes):
            copy = pltpu.make_async_remote_copy(
                src_ref=source,
                dst_ref=target,
                send_sem=sends.at[step],
                recv_sem=recvs.at[step],
                device_id={"zd": lax.rem(zd + step, planes)},
                device_id_type=MESH,
            )
            copy.start()
            moves.append(copy)

    for k, (source, low, slot) in enumerate(
        ((qkv, qkv_low, qkv_later), (out, out_low, out_later))
    ):
        for layer in range(1, source.shape[0]):
            place_rows(source, layer, low, (layer - 1,))
            target = slot.at[layer - 1, zd]
            along_z(
                low.at[layer - 1], target, later_send.at[k, layer], later_recv.at[k, layer]
            )
            own = pltpu.make_async_copy(low.at[layer - 1], target, later_own.at[k, layer])
            own.start()
            moves.append(own)
    layers, rows, columns = gu.shape
    block = columns // (planes * members)
    half = planes // cores
    for c in range(cores):
        for j in range(members):
            for i in range(layers):
                cut = [
                    gu[i, :, pl.ds(((c * half + k) * members + j) * block, block)]
                    for k in range(half)
                ]
                value = jnp.concatenate(cut, axis=1) if half > 1 else cut[0]
                pieces[c * members + j, i * rows : (i + 1) * rows] = value.astype(bf16)
    if pieces.shape[1] > layers * rows:
        for piece in range(cores * members):
            pieces[piece, layers * rows :] = jnp.zeros(
                (pieces.shape[1] - layers * rows, pieces.shape[2]), bf16
            )
    me = linear((core, tp), (cores, members))
    for step, (device, index) in enumerate(group):
        copy = pltpu.make_async_remote_copy(
            src_ref=pieces.at[index],
            dst_ref=gu_result.at[me],
            send_sem=gu_send.at[step],
            recv_sem=gu_recv.at[step],
            device_id=device,
            device_id_type=MESH,
        )
        copy.start()
        moves.append(copy)
    own = pltpu.make_async_copy(pieces.at[me], gu_result.at[me], gu_own)
    own.start()
    moves.append(own)
    gather.stage("tp")
    gather.stage("head")
    gather.finish()
    side_by_side(sizes, (qkv_slots, out_slots), (mixed, project))
    packets[...] = packet_slots[...]
    for copy in moves:
        copy.wait()


def side_by_side(sizes, slots, results):
    cores, planes, members = sizes
    for slot, result in zip(slots, results):
        columns = slot.shape[4]
        rows = result.shape[0] // (planes * members)
        for h, z, t in itertools.product(range(cores), range(planes), range(members)):
            row = (z * members + t) * rows
            result[row : row + rows, h * columns : (h + 1) * columns] = slot[h, z, t, :rows]


def later_kernel(sizes, layer, qkv, out, mixed, project, qkv_slots, out_slots, send_sem, recv_sem):
    gather = Spread(sizes, [qkv_slots, out_slots], send_sem, recv_sem, whole_z=True)
    core, _, tp = (gather.place[name] for name in EVERY)
    enter(gather.partners())
    for source, slot in ((qkv, qkv_slots), (out, out_slots)):
        for z in range(sizes[1]):
            slot[core, z, tp] = source[layer - 1, z]
    gather.stage("tp")
    gather.stage("head")
    gather.finish()
    side_by_side(sizes, (qkv_slots, out_slots), (mixed, project))


def whole_shapes(sizes, tall, matrices):
    slots = [pltpu.VMEM(sizes + (t, w.shape[2]), bf16) for t, w in zip(tall, matrices)]
    outs = [
        jax.ShapeDtypeStruct((w.shape[1] * sizes[1] * sizes[2], w.shape[2] * sizes[0]), bf16)
        for w in matrices
    ]
    return slots, outs


def start(w_gu, w_qkv, w_out, packet, ident):
    sizes = tuple(lax.axis_size(axis) for axis in EVERY)
    cores, planes, members = sizes
    vmem, dma = pltpu.VMEM, pltpu.SemaphoreType.DMA
    here, there = pl.BlockSpec(memory_space=pltpu.VMEM), pl.BlockSpec(memory_space=pl.ANY)
    shape = jax.ShapeDtypeStruct
    tall = [-(-w.shape[1] // 16) * 16 for w in (w_qkv, w_out)]
    slots, outs = whole_shapes(sizes, tall, (w_qkv, w_out))
    layers, rows, columns = w_gu.shape
    piece = (
        cores * members,
        -(-layers * rows // 16) * 16,
        columns // (cores * members),
    )
    later = [
        shape((layers - 1, planes, t, w.shape[2]), bf16) for t, w in zip(tall, (w_qkv, w_out))
    ]
    operands = [w_gu, w_qkv, w_out, packet]
    outs = [shape(piece, bf16)] + outs + [shape(sizes + packet.shape, f32)] + later
    out_specs = [there] + [here] * 3 + [there] * 2
    moves = math.prod(sizes) - 1
    scratch = [vmem(sizes + packet.shape, f32)] + slots + [dma((3, moves))] * 2
    scratch += [vmem(piece, bf16), dma((cores * members - 1,)), dma((cores * members - 1,)), dma]
    scratch += [dma((2, layers, planes))] * 2
    scratch += [
        vmem((layers - 1, t, w.shape[2]), bf16) for t, w in zip(tall, (w_qkv, w_out))
    ] + [dma((2, layers))]
    return pl.pallas_call(
        partial(start_kernel, sizes),
        out_shape=outs,
        in_specs=[here] * len(operands),
        out_specs=out_specs,
        scratch_shapes=scratch,
        compiler_params=pltpu.CompilerParams(
            collective_id=ident, has_side_effects=True, vmem_limit_bytes=56 * 2**20
        ),
    )(*operands)


def later_weights(gathered, w_qkv, w_out, layer, ident):
    sizes = tuple(lax.axis_size(axis) for axis in EVERY)
    slots, outs = whole_shapes(sizes, [g.shape[2] for g in gathered], (w_qkv, w_out))
    here = pl.BlockSpec(memory_space=pltpu.VMEM)
    moves = math.prod(sizes) - sizes[1]
    return pl.pallas_call(
        partial(later_kernel, sizes, layer),
        out_shape=outs,
        in_specs=[here] * 2,
        out_specs=[here] * 2,
        scratch_shapes=slots + [pltpu.SemaphoreType.DMA((2, moves))] * 2,
        compiler_params=pltpu.CompilerParams(
            collective_id=ident, has_side_effects=True, vmem_limit_bytes=48 * 2**20
        ),
    )(*gathered)


def by_rows(rows, work, step=16):
    @pl.loop(0, rows // step)
    def _(index):
        work(pl.ds(pl.multiple_of(index * step, step), step))


def collect_kernel(sizes, layers, tiled, *refs):
    cores, planes, members = sizes
    rest = list(refs)
    take = lambda number: [rest.pop(0) for _ in range(number)]
    acts, packet = take(4 * layers), take(1)[0]
    if tiled:
        (down,) = take(1)
    results = take(3)
    if tiled:
        (down_result,) = take(1)
    far, halves = take(4 * layers), take(2 * layers)
    packet_land = rest.pop(0)
    pieces, plane_lands, totals, z_sums, z_lands = (take(3) for _ in range(5))
    act_send, act_recv, packet_send, packet_recv = take(4)
    tp_send, tp_recv, z_send, z_recv = take(4)
    core, zd, tp = (lax.axis_index(axis) for axis in EVERY)
    sibling = {"head": 1 - core}
    enter(
        [sibling]
        + [{"tp": lax.rem(tp + step, members)} for step in range(1, members)]
        + [{"zd": lax.rem(zd + step, planes)} for step in range(1, planes)]
    )
    sends = []

    def send(src, dst, send_sem, recv_sem, device):
        copy = pltpu.make_async_remote_copy(
            src_ref=src,
            dst_ref=dst,
            send_sem=send_sem,
            recv_sem=recv_sem,
            device_id=device,
            device_id_type=MESH,
        )
        copy.start()
        sends.append(copy)
        return copy

    if tiled:
        down_land, down_send, down_recv, down_own = take(4)
        down_moves = []
        for step in range(1, planes):
            there = lax.rem(zd + step, planes)
            down_moves.append(
                send(
                    down.at[there],
                    down_land.at[step],
                    down_send.at[step],
                    down_recv.at[step],
                    {"zd": there},
                )
            )
        down_stay = pltpu.make_async_copy(down.at[zd], down_land.at[0], down_own)
        down_stay.start()
    for k in range(2 * layers):
        grad, half = acts[2 * k + 1], halves[k]
        width = half.shape[2]
        for h in range(cores):
            half[h] = grad[:, h * width : (h + 1) * width]
    moves = []
    for k in range(2 * layers):
        moves.append(
            send(acts[2 * k], far[2 * k], act_send.at[2 * k], act_recv.at[2 * k], sibling)
        )
        moves.append(
            send(
                halves[k].at[1 - core],
                far[2 * k + 1],
                act_send.at[2 * k + 1],
                act_recv.at[2 * k + 1],
                sibling,
            )
        )
    gains = send(packet.at[1 - core], packet_land, packet_send, packet_recv, sibling)
    plane_moves, z_moves = {}, {}
    for kind in range(3):
        piece = pieces[kind]
        if kind < 2:
            for layer in range(layers):
                k = 2 * layer + kind
                near = lax.dot_general(
                    acts[2 * k][...], halves[k][core], ALONG, preferred_element_type=f32
                )
                moves[2 * k].wait_recv()
                moves[2 * k + 1].wait_recv()
                value = near + lax.dot_general(
                    far[2 * k][...], far[2 * k + 1][...], ALONG, preferred_element_type=f32
                )
                value = value.astype(bf16)
                rows = value.shape[0] // (planes * members)
                slab = piece.shape[1] // planes
                for z, t in itertools.product(range(planes), range(members)):
                    at = (z * members + t) * rows
                    to = z * slab + layer * rows
                    piece[t, to : to + rows] = value[at : at + rows]
            if slab > layers * rows:
                for z, t in itertools.product(range(planes), range(members)):
                    piece[t, z * slab + layers * rows : (z + 1) * slab] = jnp.zeros(
                        (slab - layers * rows, piece.shape[2]), bf16
                    )
        else:
            gains.wait_recv()
            piece[...] = packet[core] + packet_land[...]
        for step in range(1, members):
            there = lax.rem(tp + step, members)
            plane_moves[kind, step] = send(
                piece.at[there],
                plane_lands[kind].at[step],
                tp_send.at[kind, step],
                tp_recv.at[kind, step],
                {"tp": there},
            )
    for kind in range(3):
        for step in range(1, members):
            plane_moves[kind, step].wait_recv()
        piece, total, land, result = pieces[kind], totals[kind], plane_lands[kind], results[kind]
        stride = 8 if land.dtype == f32 else 16

        def gather_plane(rows):
            value = piece[tp, rows].astype(f32)
            for step in range(1, members):
                value = value + land[step, rows].astype(f32)
            total[rows] = value

        by_rows(total.shape[0], gather_plane, stride)
        height = result.shape[0]
        z_sum = z_sums[kind]
        for step in range(1, planes):
            there = lax.rem(zd + step, planes)

            def round_off(rows):
                at = pl.multiple_of(there * height + rows.start, stride)
                z_sum[step, rows] = total[pl.ds(at, rows.size)].astype(z_sum.dtype)

            by_rows(height, round_off, stride)
            z_moves[kind, step] = send(
                z_sum.at[step],
                z_lands[kind].at[step],
                z_send.at[kind, step],
                z_recv.at[kind, step],
                {"zd": there},
            )
    for kind in range(3):
        for step in range(1, planes):
            z_moves[kind, step].wait_recv()
        total, land, result = totals[kind], z_lands[kind], results[kind]
        height = result.shape[0]
        stride = 8 if land.dtype == f32 else 16

        def gather_z(rows):
            at = pl.multiple_of(zd * height + rows.start, stride)
            value = total[pl.ds(at, rows.size)]
            for step in range(1, planes):
                value = value + land[step, rows].astype(f32)
            result[rows] = value

        by_rows(height, gather_z, stride)
    if tiled:
        down_stay.wait()
        for copy in down_moves:
            copy.wait_recv()

        def gather_down(rows):
            value = down_land[0, rows].astype(f32)
            for step in range(1, planes):
                value = value + down_land[step, rows].astype(f32)
            down_result[rows] = value

        by_rows(down_result.shape[0], gather_down)
    for copy in sends:
        copy.wait_send()


def collect(acts, packet, down, ident):
    sizes = tuple(lax.axis_size(axis) for axis in EVERY)
    cores, planes, members = sizes
    layers = len(acts) // 4
    vmem, dma = pltpu.VMEM, pltpu.SemaphoreType.DMA
    tokens = acts[0].shape[0]
    halves = [acts[2 * k + 1].shape[1] // cores for k in range(2 * layers)]
    slabs = []
    for kind in range(2):
        rows = layers * acts[2 * kind].shape[1] // (planes * members)
        slabs.append((-(-rows // 16) * 16, halves[kind], bf16))
    slabs.append((packet.shape[2] // planes, packet.shape[3], f32))
    far = []
    for k in range(2 * layers):
        far += [vmem(acts[2 * k].shape, bf16), vmem((tokens, halves[k]), bf16)]
    scratch = far + [vmem((cores, tokens, width), bf16) for width in halves]
    scratch += [vmem(packet.shape[1:], f32)]
    scratch += [vmem((members, planes * r, c), kind) for r, c, kind in slabs] * 2
    scratch += [vmem((planes * r, c), f32) for r, c, _ in slabs]
    scratch += [vmem((planes, r, c), kind) for r, c, kind in slabs] * 2
    scratch += [dma((4 * layers,))] * 2 + [dma] * 2
    scratch += [dma((3, members))] * 2 + [dma((3, planes))] * 2
    here = pl.BlockSpec(memory_space=pltpu.VMEM)
    operands = [*acts, packet]
    outs = [jax.ShapeDtypeStruct((r, c), f32) for r, c, _ in slabs]
    in_specs = [here] * len(operands)
    if down is not None:
        operands, in_specs = operands + [down], in_specs + [pl.BlockSpec(memory_space=pl.ANY)]
        outs += [jax.ShapeDtypeStruct(down.shape[1:], f32)]
        scratch += [vmem(down.shape, bf16), dma((planes,)), dma((planes,)), dma]
    return pl.pallas_call(
        partial(collect_kernel, sizes, layers, down is not None),
        out_shape=outs,
        in_specs=in_specs,
        out_specs=[here] * len(outs),
        scratch_shapes=scratch,
        cost_estimate=LIGHT,
        compiler_params=pltpu.CompilerParams(
            collective_id=ident, has_side_effects=True, vmem_limit_bytes=56 * 2**20
        ),
    )(*operands)


def neighbours(planes, reach, sign):
    total = planes * PLANE
    place = linear([lax.axis_index("zd"), lax.axis_index("tp")], (planes, PLANE))

    def at(distance):
        there = lax.rem(place + distance + total, total)
        return {"zd": lax.div(there, PLANE), "tp": lax.rem(there, PLANE)}

    steps = range(1, reach + 1)
    devices, sources = [at(sign * step) for step in steps], [at(-sign * step) for step in steps]
    above = [place + step < total for step in steps]
    below = [place >= step for step in steps]
    sends, comes = (above, below) if sign > 0 else (below, above)
    return devices, sources, sends, comes


def inverse_rms(values):
    return lax.rsqrt(jnp.mean(values * values, axis=-1, keepdims=True) + norm_eps)


def rms_back(gradient, values, gain):
    inverse = inverse_rms(values)
    scaled = gradient * gain
    shared = jnp.mean(scaled * values, axis=-1, keepdims=True) * (inverse * inverse)
    return inverse * (scaled - values * shared), jnp.sum(
        gradient * values * inverse, axis=0, keepdims=True
    )


def turn(values, cosine, sine):
    half = values.shape[-1] // 2
    lower, upper = values[:, :half], values[:, half:]
    return jnp.concatenate(
        [lower * cosine - upper * sine, upper * cosine + lower * sine], axis=-1
    )


def soft_rows(query, keys, bias):
    scores = lax.dot_general(query, keys, ACROSS, preferred_element_type=f32)
    scores = scores * (1.0 / math.sqrt(HD)) + bias
    raised = jnp.exp(scores - jnp.max(scores, axis=-1, keepdims=True))
    return raised / jnp.sum(raised, axis=-1, keepdims=True)


def attn_forward_kernel(planes, reach, chained, *refs):
    rest = list(refs)
    take = lambda number: [rest.pop(0) for _ in range(number)]
    if chained:
        base, down, before = take(3)
    else:
        (base,) = take(1)
    w_mixed, w_project, gains, cosine, sine, bias = take(6)
    hidden, normed, mixed, queries, keyvals_out = take(5)
    attended, projected, hidden_half, normed_ffn = take(4)
    keyvals, send_sem, recv_sem, save_sem = take(4)
    seqs, stretch, key_len = bias.shape
    devices, sources, sends, comes = neighbours(planes, reach, 1)
    enter(devices + sources)
    value = base[...].astype(f32)
    if chained:
        late = down[...]
        value = value + late * inverse_rms(late) * before[1:2, D : 2 * D]
    hidden[...] = value
    low = (value * inverse_rms(value) * gains[0:1, :D]).astype(bf16)
    normed[...] = low
    mixed[...] = matmul(low, w_mixed[...])
    key = mixed[:, HEADS * HD : HEADS * HD + HD]
    key = turn(key * inverse_rms(key) * gains[1:2, 2 * D :], cosine[...], sine[...]).astype(bf16)
    late_values = mixed[:, HEADS * HD + HD :].astype(bf16)
    copies = []
    for i in range(seqs):
        rows = slice(i * stretch, (i + 1) * stretch)
        keyvals[i, reach * stretch :, :HD] = key[rows]
        keyvals[i, reach * stretch :, HD:] = late_values[rows]
        for step, device in enumerate(devices):
            copy = pltpu.make_async_remote_copy(
                src_ref=keyvals.at[i, pl.ds(reach * stretch, stretch)],
                dst_ref=keyvals.at[i, pl.ds((reach - 1 - step) * stretch, stretch)],
                send_sem=send_sem.at[i, step],
                recv_sem=recv_sem.at[i, step],
                device_id=device,
                device_id_type=MESH,
            )
            pl.when(sends[step])(copy.start)
            copies.append((step, copy))

            @pl.when(jnp.logical_not(comes[step]))
            def _():
                at = (reach - 1 - step) * stretch
                keyvals[i, at : at + stretch] = jnp.zeros((stretch, 2 * HD), bf16)

    for h in range(HEADS):
        columns = slice(h * HD, (h + 1) * HD)
        query = mixed[:, columns]
        query = turn(query * inverse_rms(query) * gains[0:1, 2 * D :], cosine[...], sine[...])
        queries[:, columns] = query.astype(bf16)
    for step, copy in copies:
        pl.when(comes[step])(copy.wait_recv)
    save = pltpu.make_async_copy(keyvals, keyvals_out, save_sem)
    save.start()
    for i in range(seqs):
        rows = slice(i * stretch, (i + 1) * stretch)
        for h in range(HEADS):
            columns = slice(h * HD, (h + 1) * HD)
            soft = soft_rows(queries[rows, columns], keyvals[i, :, :HD], bias[i])
            attended[rows, columns] = matmul(soft.astype(bf16), keyvals[i, :, HD:]).astype(bf16)
    out = matmul(attended[...], w_project[...])
    projected[...] = out
    half = hidden[...] + out * inverse_rms(out) * gains[0:1, D : 2 * D]
    hidden_half[...] = half
    normed_ffn[...] = (half * inverse_rms(half) * gains[1:2, :D]).astype(bf16)
    for step, copy in copies:
        pl.when(sends[step])(copy.wait_send)
    save.wait()


def attn_forward(base, weights, gains, tables, bias, planes, reach, ident, earlier=None):
    tokens = base.shape[0]
    seqs, _, key_len = bias.shape
    shape = jax.ShapeDtypeStruct
    operands = [base] + list(earlier or []) + list(weights) + [gains, *tables, bias]
    here, there = pl.BlockSpec(memory_space=pltpu.VMEM), pl.BlockSpec(memory_space=pl.ANY)
    dma = pltpu.SemaphoreType.DMA
    return pl.pallas_call(
        partial(attn_forward_kernel, planes, reach, earlier is not None),
        out_shape=[
            shape((tokens, D), f32),
            shape((tokens, D), bf16),
            shape((tokens, weights[0].shape[1]), f32),
            shape((tokens, HEADS * HD), bf16),
            shape((seqs, key_len, 2 * HD), bf16),
            shape((tokens, HEADS * HD), bf16),
            shape((tokens, D), f32),
            shape((tokens, D), f32),
            shape((tokens, D), bf16),
        ],
        in_specs=[here] * len(operands),
        out_specs=[here] * 4 + [there] + [here] * 4,
        scratch_shapes=[
            pltpu.VMEM((seqs, key_len, 2 * HD), bf16),
            dma((seqs, reach)),
            dma((seqs, reach)),
            dma,
        ],
        compiler_params=pltpu.CompilerParams(
            collective_id=ident, has_side_effects=True, vmem_limit_bytes=56 * 2**20
        ),
    )(*operands)


def attn_backward_kernel(planes, reach, chained, *refs):
    rest = list(refs)
    take = lambda number: [rest.pop(0) for _ in range(number)]
    d_ffn, above, hidden, mixed, queries, keyvals, projected, hidden_half = take(8)
    w_mixed, w_project, gains, cosine, sine, bias = take(6)
    if chained:
        down, before = take(2)
    grad, d_mixed, d_projected, gain_grads = take(4)
    if chained:
        d_down, d_post = take(2)
    d_keyvals, outgoing, incoming, d_attended, send_sem, recv_sem = take(6)
    seqs, stretch, key_len = bias.shape
    devices, sources, sends, comes = neighbours(planes, reach, -1)
    enter(devices + sources)
    scale = 1.0 / math.sqrt(HD)
    part, gain_row = rms_back(d_ffn[...], hidden_half[...], gains[1:2, :D])
    gain_grads[1:2, :D] = gain_row
    gain_grads[1:2, D : 2 * D] = jnp.zeros((1, D), f32)
    grad[...] = part + above[...]
    part, gain_row = rms_back(grad[...], projected[...], gains[0:1, D : 2 * D])
    gain_grads[0:1, D : 2 * D] = gain_row
    low = part.astype(bf16)
    d_projected[...] = low
    d_attended[...] = lax.dot_general(
        low, w_project[...], ACROSS, preferred_element_type=f32
    ).astype(bf16)
    query_gain = jnp.zeros((1, HD), f32)
    for i in range(seqs):
        rows = slice(i * stretch, (i + 1) * stretch)
        d_keys = d_values = None
        for h in range(HEADS):
            columns = slice(h * HD, (h + 1) * HD)
            query, d_out = queries[rows, columns], d_attended[rows, columns]
            keys, values = keyvals[i, :, :HD], keyvals[i, :, HD:]
            soft = soft_rows(query, keys, bias[i])
            d_soft = lax.dot_general(d_out, values, ACROSS, preferred_element_type=f32)
            total = jnp.sum(soft * d_soft, axis=-1, keepdims=True)
            d_scores = (soft * (d_soft - total)).astype(bf16)
            key_part = lax.dot_general(d_scores, query, ALONG, preferred_element_type=f32)
            value_part = lax.dot_general(
                soft.astype(bf16), d_out, ALONG, preferred_element_type=f32
            )
            d_keys = key_part if d_keys is None else d_keys + key_part
            d_values = value_part if d_values is None else d_values + value_part
            d_query = matmul(d_scores, keys) * scale
            d_query = turn(d_query, cosine[rows], -sine[rows])
            part, gain_row = rms_back(d_query, mixed[rows, columns], gains[0:1, 2 * D :])
            query_gain = query_gain + gain_row
            d_mixed[rows, columns] = part.astype(bf16)
        d_keyvals[i, :, :HD] = d_keys * scale
        d_keyvals[i, :, HD:] = d_values
    gain_grads[0:1, 2 * D :] = query_gain
    outgoing[...] = d_keyvals[:, : reach * stretch].astype(bf16)
    copies = []
    for i in range(seqs):
        for step, device in enumerate(devices):
            copy = pltpu.make_async_remote_copy(
                src_ref=outgoing.at[i, pl.ds((reach - 1 - step) * stretch, stretch)],
                dst_ref=incoming.at[i, step],
                send_sem=send_sem.at[i, step],
                recv_sem=recv_sem.at[i, step],
                device_id=device,
                device_id_type=MESH,
            )
            pl.when(sends[step])(copy.start)
            copies.append((step, copy))

            @pl.when(jnp.logical_not(comes[step]))
            def _():
                incoming[i, step] = jnp.zeros((stretch, 2 * HD), bf16)

    for step, copy in copies:
        pl.when(comes[step])(copy.wait_recv)
    key_gain = jnp.zeros((1, HD), f32)
    for i in range(seqs):
        rows = slice(i * stretch, (i + 1) * stretch)
        own = d_keyvals[i, reach * stretch :]
        for step in range(reach):
            own = own + incoming[i, step].astype(f32)
        d_key = turn(own[:, :HD], cosine[rows], -sine[rows])
        part, gain_row = rms_back(
            d_key, mixed[rows, HEADS * HD : HEADS * HD + HD], gains[1:2, 2 * D :]
        )
        key_gain = key_gain + gain_row
        d_mixed[rows, HEADS * HD : HEADS * HD + HD] = part.astype(bf16)
        d_mixed[rows, HEADS * HD + HD :] = own[:, HD:].astype(bf16)
    gain_grads[1:2, 2 * D :] = key_gain
    d_normed = lax.dot_general(d_mixed[...], w_mixed[...], ACROSS, preferred_element_type=f32)
    part, gain_row = rms_back(d_normed, hidden[...], gains[0:1, :D])
    gain_grads[0:1, :D] = gain_row
    grad[...] = grad[...] + part
    if chained:
        part, gain_row = rms_back(grad[...], down[...], before[1:2, D : 2 * D])
        d_down[...] = part.astype(bf16)
        d_post[...] = gain_row
    for step, copy in copies:
        pl.when(sends[step])(copy.wait_send)


def attn_backward(
    d_ffn, above, kept, weights, gains, tables, bias, planes, reach, ident, earlier=None
):
    tokens = above.shape[0]
    seqs, stretch, key_len = bias.shape
    shape = jax.ShapeDtypeStruct
    operands = [d_ffn, above, *kept, *weights, gains, *tables, bias] + list(earlier or [])
    outs = [
        shape((tokens, D), f32),
        shape((tokens, weights[0].shape[1]), bf16),
        shape((tokens, D), bf16),
        shape(gains.shape, f32),
    ]
    if earlier is not None:
        outs += [shape((tokens, D), bf16), shape((1, D), f32)]
    here = pl.BlockSpec(memory_space=pltpu.VMEM)
    vmem, dma = pltpu.VMEM, pltpu.SemaphoreType.DMA
    return pl.pallas_call(
        partial(attn_backward_kernel, planes, reach, earlier is not None),
        out_shape=outs,
        in_specs=[here] * len(operands),
        out_specs=[here] * len(outs),
        scratch_shapes=[
            vmem((seqs, key_len, 2 * HD), f32),
            vmem((seqs, reach * stretch, 2 * HD), bf16),
            vmem((seqs, reach, stretch, 2 * HD), bf16),
            vmem((tokens, HEADS * HD), bf16),
            dma((seqs, reach)),
            dma((seqs, reach)),
        ],
        compiler_params=pltpu.CompilerParams(
            collective_id=ident, has_side_effects=True, vmem_limit_bytes=56 * 2**20
        ),
    )(*operands)


GELU_SLOPE = math.sqrt(2.0 / math.pi)
GELU_CUBE = 0.044715
ACROSS = (((1,), (1,)), ((), ()))
ALONG = (((0,), (0,)), ((), ()))


class Plane:
    def __init__(self, own, bufs, sems):
        self.own = own
        self.rows, self.partial, self.other, self.lands, self.sums, self.arrived = bufs
        self.x_send, self.x_recv, self.f_send, self.f_recv = sems[:4]
        self.c_send, self.c_recv, self.p_send, self.p_recv, self.first = sems[4:]
        self.tp = lax.axis_index("tp")
        self.sibling = {"head": 1 - lax.axis_index("head")}

    def member(self, m):
        tp = self.tp
        upper = lax.rem(lax.div(tp, 2) + lax.div(m, 2), 2)
        lower = lax.rem(lax.rem(tp, 2) + lax.rem(m, 2), 2)
        return {"tp": upper * 2 + lower}

    def remote(self, src, dst, send, recv, device):
        return pltpu.make_async_remote_copy(
            src_ref=src,
            dst_ref=dst,
            send_sem=send,
            recv_sem=recv,
            device_id=device,
            device_id_type=MESH,
        )

    def push(self, m):
        return self.remote(
            self.own, self.rows.at[0, m], self.x_send.at[m], self.x_recv.at[m], self.member(m)
        )

    def keep(self):
        return pltpu.make_async_copy(self.own, self.rows.at[0, 0], self.first)

    def forward(self, m):
        return self.remote(
            self.rows.at[0, m],
            self.rows.at[1, m],
            self.f_send.at[m],
            self.f_recv.at[m],
            self.sibling,
        )

    def cross(self, m):
        return self.remote(
            self.other.at[m], self.lands.at[m], self.c_send.at[m], self.c_recv.at[m], self.sibling
        )

    def home(self, m):
        return self.remote(
            self.sums.at[m],
            self.arrived.at[m],
            self.p_send.at[m],
            self.p_recv.at[m],
            self.member(m),
        )

    def begin(self):
        self.keep().start()
        enter([self.sibling] + [self.member(jnp.int32(m)) for m in range(1, PLANE)])
        for m in range(1, PLANE):
            self.push(jnp.int32(m)).start()

    def work(self, compute):
        def settle(m):
            self.cross(m).wait_recv()

            def add(rows):
                value = self.partial[m, rows] + self.lands[m, rows].astype(f32)
                self.sums[m, rows] = value.astype(bf16)

            by_rows(self.partial.shape[1], add)
            self.home(m).start()

        def step(m, carry):
            @pl.when(m == 0)
            def _():
                self.keep().wait()

            @pl.when(m > 0)
            def _():
                self.push(m).wait_recv()

            self.forward(m).start()
            self.partial[m] = compute(0, m)
            self.forward(m).wait_recv()
            self.other[m] = compute(1, m).astype(bf16)
            self.cross(m).start()

            @pl.when(m >= 2)
            def _():
                settle(m - 1)

            return carry

        lax.fori_loop(0, PLANE, step, 0)
        settle(jnp.int32(PLANE - 1))

    def finish(self, result):
        self.cross(jnp.int32(0)).wait_recv()
        for m in range(1, PLANE):
            self.home(jnp.int32(m)).wait_recv()

        def add(rows):
            value = self.partial[0, rows] + self.lands[0, rows].astype(f32)
            for m in range(1, PLANE):
                value = value + self.arrived[m, rows].astype(f32)
            result[rows] = value

        by_rows(result.shape[0], add)
        for m in range(PLANE):
            m = jnp.int32(m)
            self.forward(m).wait_send()
            self.cross(m).wait_send()
        for m in range(1, PLANE):
            m = jnp.int32(m)
            self.push(m).wait_send()
            self.home(m).wait_send()


def chunks(extent, step=256):
    return [slice(at, min(at + step, extent)) for at in range(0, extent, step)]


def gate_up_copies(gu_ref, gate_up, sem):
    blocks = gu_ref.shape[0]
    rows = gate_up.shape[1] // blocks
    return [
        pltpu.make_async_copy(
            gu_ref.at[block, part],
            gate_up.at[part, pl.ds(block * rows, rows)],
            sem.at[2 * block + part],
        )
        for block in range(blocks)
        for part in range(2)
    ]


def ffn_forward_kernel(own, gu_ref, halves_ref, group, saved_down, result, *scratch):
    rows, gate_up, down = scratch[:3]
    plane = Plane(own, (rows,) + scratch[3:8], scratch[8:17])
    weight_sem, group_sem, halves, half_send, half_recv, half_own, save_sem = scratch[17:]
    core = lax.axis_index("head")
    share, width = halves.shape[1:]
    copies = gate_up_copies(gu_ref, gate_up, weight_sem)
    copies.append(
        pltpu.make_async_copy(
            halves_ref.at[0, pl.ds(pl.multiple_of(core * share, 16), share)],
            halves.at[core],
            half_own,
        )
    )
    for copy in copies:
        copy.start()
    plane.begin()
    half = plane.remote(
        halves_ref.at[0, pl.ds(pl.multiple_of((1 - core) * share, 16), share)],
        halves.at[core],
        half_send,
        half_recv,
        plane.sibling,
    )
    half.start()
    for copy in copies:
        copy.wait()
    pltpu.make_async_remote_copy(
        src_ref=halves_ref.at[0, pl.ds(pl.multiple_of((1 - core) * share, 16), share)],
        dst_ref=halves.at[1 - core],
        send_sem=half_send,
        recv_sem=half_recv,
        device_id=plane.sibling,
        device_id_type=MESH,
    ).wait_recv()

    def join(at):
        down[at] = jnp.concatenate([halves[h, at] for h in range(2)], axis=1)

    by_rows(share, join, 32)
    keep_down = pltpu.make_async_copy(down, saved_down, save_sem)
    keep_down.start()

    def compute(side, m):
        tokens, total = rows[side, m], None
        for columns in chunks(share):
            gate = matmul(tokens, gate_up[0, :, columns])
            up = matmul(tokens, gate_up[1, :, columns])
            bend = jnp.tanh(GELU_SLOPE * (gate + GELU_CUBE * (gate * gate * gate)))
            inner = (0.5 * gate * (1.0 + bend) * up).astype(bf16)
            part = matmul(inner, down[columns])
            total = part if total is None else total + part
        return total

    plane.work(compute)
    save = pltpu.make_async_copy(rows, group, group_sem)
    save.start()
    plane.finish(result)
    save.wait()
    keep_down.wait()
    half.wait_send()


def ffn_backward_kernel(
    own, group, gu_ref, down_ref, result, grad_gu, grad_down, *scratch
):
    rows, gate_up, down = scratch[:3]
    plane = Plane(own, (rows,) + scratch[3:8], scratch[8:17])
    weight_sem, group_sem, saved, d_gate, d_up, inner = scratch[17:23]
    down_sem, turned, down_halves, half_send, half_recv, half_own = scratch[23:29]
    core = lax.axis_index("head")
    copies = gate_up_copies(gu_ref, gate_up, weight_sem)
    copies.append(pltpu.make_async_copy(down_ref, down, down_sem))
    for copy in copies:
        copy.start()
    load = pltpu.make_async_copy(group, saved, group_sem)
    load.start()
    plane.begin()
    for copy in copies:
        copy.wait()
    load.wait()

    def recompute(index, carry):
        side, m = lax.div(index, PLANE), lax.rem(index, PLANE)
        tokens = saved[side, m]
        gate = matmul(tokens, gate_up[0])
        up = matmul(tokens, gate_up[1])
        square = gate * gate
        bend = jnp.tanh(GELU_SLOPE * (gate + GELU_CUBE * (square * gate)))
        half = 0.5 * (1.0 + bend)
        value = gate * half
        slope = half + (0.5 * GELU_SLOPE) * gate * (1.0 - bend * bend) * (
            1.0 + (3.0 * GELU_CUBE) * square
        )
        inner[side, m] = (value * up).astype(bf16)
        d_gate[side, m] = (slope * up).astype(bf16)
        d_up[side, m] = value.astype(bf16)
        return carry

    lax.fori_loop(0, 2 * PLANE, recompute, 0)

    def compute(side, m):
        d_inner = lax.dot_general(rows[side, m], down[...], ACROSS, preferred_element_type=f32)
        gate = (d_inner * d_gate[side, m].astype(f32)).astype(bf16)
        up = (d_inner * d_up[side, m].astype(f32)).astype(bf16)
        d_gate[side, m] = gate
        d_up[side, m] = up
        return lax.dot_general(
            gate, gate_up[0], ACROSS, preferred_element_type=f32
        ) + lax.dot_general(up, gate_up[1], ACROSS, preferred_element_type=f32)

    plane.work(compute)
    width = rows.shape[-1]
    step = width // 3

    by_planes = len(grad_gu.shape) == 4
    sides = scratch[29] if by_planes else grad_gu

    def tall(ref, columns=slice(None)):
        value = ref[:, :, :, columns]
        return value.reshape(-1, value.shape[-1])

    @pl.loop(0, 3)
    def _(index):
        at = pl.ds(pl.multiple_of(index * step, step), step)
        tokens = tall(saved, at)
        for part, other in enumerate((d_gate, d_up)):
            sides[part, at] = lax.dot_general(
                tokens, tall(other), ALONG, preferred_element_type=f32
            ).astype(bf16)
        turned[at] = lax.dot_general(
            tall(rows, at), tall(inner), ALONG, preferred_element_type=f32
        ).astype(bf16)

    stores = []
    if by_planes:
        for plane_at in range(grad_gu.shape[0]):
            for part in range(2):
                height = grad_gu.shape[2]
                copy = pltpu.make_async_copy(
                    sides.at[part, pl.ds(plane_at * height, height)],
                    grad_gu.at[plane_at, part],
                    scratch[30].at[2 * plane_at + part],
                )
                copy.start()
                stores.append(copy)
    half_width = down_halves.shape[2]
    for h in range(2):
        down_halves[h] = turned[h * half_width : (h + 1) * half_width].T
    half = plane.remote(
        down_halves.at[1 - core], grad_down.at[core], half_send, half_recv, plane.sibling
    )
    half.start()
    stay = pltpu.make_async_copy(down_halves.at[core], grad_down.at[core], half_own)
    stay.start()
    plane.finish(result)
    half.wait()
    stay.wait()
    for copy in stores:
        copy.wait()


def ffn(own, weights, ident, planes, group=None):
    gate_up, down = weights
    tokens, width = own.shape
    blocks, _, _, share = gate_up.shape
    vmem, dma = pltpu.VMEM, pltpu.SemaphoreType.DMA
    scratch = [
        vmem((2, PLANE, tokens, width), bf16),
        vmem((2, width, share), bf16),
        vmem((share, width), bf16),
        vmem((PLANE, tokens, width), f32),
    ]
    scratch += [vmem((PLANE, tokens, width), bf16)] * 4
    scratch += [dma((PLANE,))] * 8 + [dma, dma((2 * blocks,)), dma]
    here, there = pl.BlockSpec(memory_space=pltpu.VMEM), pl.BlockSpec(memory_space=pl.ANY)
    shape = jax.ShapeDtypeStruct
    summed = shape((tokens, width), f32)
    if group is None:
        kernel, operands = ffn_forward_kernel, (own, gate_up, down)
        in_specs, out_specs = [here, there, there], [there, there, here]
        out_shape = [
            shape((2, PLANE, tokens, width), bf16),
            shape((share, width), bf16),
            summed,
        ]
        scratch += [vmem((2, share, width // 2), bf16)] + [dma] * 4
    else:
        kernel, operands = ffn_backward_kernel, (own, group, gate_up, down)
        by_planes = width // planes % 16 == 0
        sides = (2, width, share)
        in_specs = [here, there, there, there]
        out_specs = [here, there if by_planes else here, there]
        out_shape = [
            summed,
            shape((planes, 2, width // planes, share) if by_planes else sides, bf16),
            shape((2, share, width // 2), bf16),
        ]
        scratch += [vmem((2, PLANE, tokens, width), bf16)]
        scratch += [vmem((2, PLANE, tokens, share), bf16)] * 3
        scratch += [dma, vmem((width, share), bf16), vmem((2, share, width // 2), bf16)]
        scratch += [dma] * 3
        if by_planes:
            scratch += [vmem(sides, bf16), dma((2 * planes,))]
    return pl.pallas_call(
        kernel,
        out_shape=out_shape,
        in_specs=in_specs,
        out_specs=out_specs,
        scratch_shapes=scratch,
        cost_estimate=LIGHT,
        compiler_params=pltpu.CompilerParams(
            collective_id=ident, has_side_effects=True, vmem_limit_bytes=60 * 2**20
        ),
    )(*operands)


def exact(left, right, dims=(((1,), (0,)), ((), ()))):
    return lax.dot_general(
        left, right, dims, precision=finest_precision, preferred_element_type=f32
    )


def update_kernel(sizes, counts, *refs):
    cores, planes, members = sizes
    rest = list(refs)
    take = lambda number: [rest.pop(0) for _ in range(number)]
    plain = [take(number) for number in counts]
    sides = take(cores)
    moments_in, weights_in, weights_out, moments_out = (take(4) for _ in range(4))
    moment, weight, gram, land, factor = (take(4) for _ in range(5))
    pieces, arrived = take(2)
    load_sem, store_sem, gram_send, gram_recv, factor_send, factor_recv = take(6)
    gu_send, gu_recv, gu_own = take(3)
    core, _, tp = (lax.axis_index(axis) for axis in EVERY)
    sibling = {"head": 1 - core}
    order = (0, 1, 3, 2)
    loads = {}
    for k in range(4):
        for part, source, target in ((0, moments_in, moment), (1, weights_in, weight)):
            copy = pltpu.make_async_copy(source[k], target[k], load_sem.at[part, k])
            copy.start()
            loads[part, k] = copy
    group = []
    for step in range(1, cores * members):
        far = lax.rem(core + step // members, cores), lax.rem(tp + step % members, members)
        group.append((dict(zip(GROUP, far)), linear(far, (cores, members))))
    enter([device for device, _ in group])
    rows = moment[2].shape[1]
    for part in range(cores):
        for j in range(members):
            for layer in range(cores):
                at = (part * members + j) * rows
                pieces[part * members + j, layer * rows : (layer + 1) * rows] = sides[layer][
                    at : at + rows
                ]
    if pieces.shape[1] > cores * rows:
        for piece in range(cores * members):
            pieces[piece, cores * rows :] = jnp.zeros(
                (pieces.shape[1] - cores * rows, pieces.shape[2]), bf16
            )
    me = linear((core, tp), (cores, members))
    moves, stores = [], []

    def send(src, dst, send_sem, recv_sem, device):
        copy = pltpu.make_async_remote_copy(
            src_ref=src,
            dst_ref=dst,
            send_sem=send_sem,
            recv_sem=recv_sem,
            device_id=device,
            device_id_type=MESH,
        )
        copy.start()
        return copy

    for step, (device, index) in enumerate(group):
        moves.append(
            send(pieces.at[index], arrived.at[me], gu_send.at[step], gu_recv.at[step], device)
        )
    own = pltpu.make_async_copy(pieces.at[me], arrived.at[me], gu_own)
    own.start()

    def store(part, k):
        source, target = (moment, moments_out) if part == 0 else (weight, weights_out)
        copy = pltpu.make_async_copy(source[k], target[k], store_sem.at[part, k])
        copy.start()
        stores.append(copy)

    def gram_of(k):
        def one(layer, carry):
            gram[k][layer] = exact(moment[k][layer], moment[k][layer], ACROSS)
            return carry

        lax.fori_loop(0, cores, one, 0)
        return send(
            gram[k].at[1 - core], land[k], gram_send.at[k], gram_recv.at[k], sibling
        )

    def unit(size):
        down = lax.broadcasted_iota(jnp.int32, (size, size), 0)
        return (down == lax.broadcasted_iota(jnp.int32, (size, size), 1)).astype(f32)

    def orthogonal(members_of):
        for k in members_of:
            total = gram[k][core] + land[k][...]
            one = unit(total.shape[0])
            trace = jnp.sum(jnp.sum(total * one, axis=1, keepdims=True), axis=0, keepdims=True)
            scale = 1.0 / (jnp.sqrt(trace) + 1e-07)
            land[k][...] = total * (scale * scale)
            factor[k][core] = one * scale

        def polynomial(present):
            square = exact(present, present)
            return newton_one * unit(present.shape[0]) + newton_two * present + (
                newton_three * square
            )

        def step(_, carry):
            for k in members_of:
                present = land[k][...]
                poly = polynomial(present)
                factor[k][core] = exact(poly, factor[k][core])
                land[k][...] = exact(exact(poly, present), poly)
            return carry

        lax.fori_loop(0, NS_ITERS - 1, step, 0)
        for k in members_of:
            factor[k][core] = exact(polynomial(land[k][...]), factor[k][core])
        return [
            send(factor[k].at[core], factor[k].at[core], factor_send.at[k], factor_recv.at[k], sibling)
            for k in members_of
        ]

    def apply(k):
        columns = weight[k].shape[2] * cores
        rate = muon_rate * muon_scale * math.sqrt(columns)

        def one(layer, carry):
            weight[k][layer] = weight[k][layer] * (1.0 - muon_rate * muon_shrink) - rate * exact(
                factor[k][layer], moment[k][layer]
            )
            return carry

        lax.fori_loop(0, cores, one, 0)
        store(1, k)

    def arrive(copies):
        for copy in copies:
            copy.wait_recv()

    sent = []
    for index, k in enumerate(order[:3]):
        loads[0, k].wait()
        height = moment[k].shape[1]
        for layer in range(cores):
            if len(plain[index]) == 1:
                gradient = plain[index][0][layer * height : (layer + 1) * height]
            else:
                gradient = plain[index][layer][...].astype(f32)
            moment[k][layer] = muon_decay * moment[k][layer] + gradient
        store(0, k)
        sent.append(gram_of(k))
    arrive(sent)
    crossed = orthogonal(order[:3])
    sent += crossed
    own.wait()
    for copy in moves:
        copy.wait_recv()
    loads[0, 2].wait()
    half = planes // cores
    block = arrived.shape[2] // half
    for layer in range(cores):
        cut = [
            arrived[
                c * members + j,
                layer * rows : (layer + 1) * rows,
                k * block : (k + 1) * block,
            ].astype(f32)
            for c in range(cores)
            for k in range(half)
            for j in range(members)
        ]
        moment[2][layer] = muon_decay * moment[2][layer] + jnp.concatenate(cut, axis=1)
    store(0, 2)
    last = gram_of(2)
    sent.append(last)
    arrive(crossed)
    for k in range(4):
        loads[1, k].wait()
    for k in order[:3]:
        apply(k)
    arrive([last])
    crossed = orthogonal(order[3:])
    sent += crossed
    arrive(crossed)
    apply(2)
    for copy in moves + sent:
        copy.wait_send()
    for copy in stores:
        copy.wait()


def update(gradients, sides, moments, weights, ident):
    sizes = tuple(lax.axis_size(axis) for axis in EVERY)
    cores, planes, members = sizes
    vmem, dma = pltpu.VMEM, pltpu.SemaphoreType.DMA
    layers, rows, columns = moments[2].shape
    piece = (
        cores * members,
        -(-layers * rows // 16) * 16,
        columns // (cores * members),
    )
    shapes = [m.shape for m in moments]
    square = [(s[1], s[1]) for s in shapes]
    scratch = [vmem(s, f32) for s in shapes] * 2
    scratch += [vmem((layers,) + s, f32) for s in square]
    scratch += [vmem(s, f32) for s in square]
    scratch += [vmem((layers,) + s, f32) for s in square]
    scratch += [vmem(piece, bf16)] * 2
    scratch += [dma((2, 4))] * 2 + [dma((4,))] * 4
    scratch += [dma((cores * members - 1,))] * 2 + [dma]
    here, there = pl.BlockSpec(memory_space=pltpu.VMEM), pl.BlockSpec(memory_space=pl.ANY)
    operands = sum(gradients, []) + sides
    return pl.pallas_call(
        partial(update_kernel, sizes, [len(g) for g in gradients]),
        out_shape=[jax.ShapeDtypeStruct(s, f32) for s in shapes] * 2,
        in_specs=[here] * len(operands) + [there] * 8,
        out_specs=[there] * 8,
        scratch_shapes=scratch,
        compiler_params=pltpu.CompilerParams(
            collective_id=ident, has_side_effects=True, vmem_limit_bytes=56 * 2**20
        ),
    )(*operands, *moments, *weights)


def padded(array, multiple=16):
    extra = -array.shape[-2] % multiple
    if extra == 0:
        return array
    return jnp.pad(array, [(0, 0)] * (array.ndim - 2) + [(0, extra), (0, 0)])


def rms_norm(values, norm_gain):
    return (
        values * lax.rsqrt(jnp.mean(values * values, axis=-1, keepdims=True) + norm_eps) * norm_gain
    )


def rope_tables(positions, head_dim):
    half_dim = head_dim // 2
    frequency = jnp.exp(
        jnp.arange(half_dim, dtype=jnp.float32) * (-2.0 * math.log(rope_base) / head_dim)
    )
    angles = positions.astype(jnp.float32)[:, None] * frequency[None, :]
    return (jnp.cos(angles), jnp.sin(angles))


def matmul(left, right):
    return jnp.dot(left, right, preferred_element_type=f32)


def body(
    inputs,
    cotangent,
    teacher,
    segments,
    valid_mask,
    w_qkv,
    w_out,
    w_gu,
    w_down,
    norm_gains,
    mom_qkv,
    mom_out,
    mom_gu,
    mom_down,
    gain_first,
    gain_second,
):
    cores = lax.axis_size("head")
    planes = lax.axis_size("zd")
    seq_devices = planes * PLANE
    core = lax.axis_index("head")
    seq_place = lax.axis_index("zd") * PLANE + lax.axis_index("tp")
    half_seqs, stretch_len = inputs.shape[:2]
    tokens = half_seqs * stretch_len
    all_seqs = half_seqs * cores
    seq_length = stretch_len * seq_devices
    reach = -(-WINDOW // stretch_len)
    key_len = (reach + 1) * stretch_len
    qkv_rows, qkv_cols = w_qkv.shape[1:]
    out_rows, out_cols = w_out.shape[1:]
    gu_rows = w_gu.shape[1]
    ff_block = w_down.shape[1]
    share = FF // (cores * PLANE)
    half_planes = planes // cores
    gain_cols = norm_gains.shape[-1]
    gain_len = gain_cols * seq_devices
    lanes = -(-gain_cols // 128) * 128

    packet = jnp.zeros((8, lanes), f32)
    packet = packet.at[:LAYERS, :gain_cols].set(norm_gains[:, 0].astype(bf16).astype(f32))
    packet = packet.at[LAYERS, 0].set(jnp.sum(valid_mask.astype(f32)))
    gu_pieces, w_mixed, w_project, packets, *later = start(
        w_gu, w_qkv, w_out, packet, 0
    )
    attn_weights = [w_mixed, w_project]
    gu_pieces = gu_pieces[:, : LAYERS * gu_rows].reshape(cores * PLANE, LAYERS, gu_rows, share)
    packets = packets.reshape(cores, seq_devices, 8, lanes)
    valid_count = jnp.sum(packets[:, :, LAYERS, 0])
    gain_rows = [
        packets[:, :, layer, :gain_cols].reshape(cores, gain_len) for layer in range(LAYERS)
    ]

    def gate_up_rows(layer):
        pieces = gu_pieces[:, layer].reshape(2, PLANE * gu_rows, share)
        pieces = lax.all_gather(pieces, "zd", axis=0)
        if PLANE * gu_rows % 16:
            pieces = pieces.transpose(1, 0, 2, 3).reshape(1, 2, D, share)
        return pieces

    def down_rows(layer):
        rows = w_down[layer : layer + 1].astype(bf16)
        return lax.all_gather(rows, "zd", axis=1, tiled=True)

    full = [(gate_up_rows(0), down_rows(0))] + [None] * (LAYERS - 1)

    own_places = seq_place * stretch_len + jnp.arange(stretch_len, dtype=jnp.int32)
    key_places = (seq_place - reach) * stretch_len + jnp.arange(key_len, dtype=jnp.int32)
    cosine_table, sine_table = rope_tables(own_places, HD)
    own_rows = lax.dynamic_slice_in_dim(segments, core * half_seqs, half_seqs, 0)
    own_segments = lax.dynamic_slice_in_dim(own_rows, seq_place * stretch_len, stretch_len, 1)
    padded_segments = jnp.pad(own_rows, ((0, 0), (reach * stretch_len, 0)), constant_values=-1)
    key_segments = lax.dynamic_slice_in_dim(padded_segments, seq_place * stretch_len, key_len, 1)
    spacing = own_places[:, None] - key_places[None, :]
    allowed = (spacing >= 0) & (spacing < WINDOW) & (key_places[None, :] >= 0)
    allowed = allowed[None] & (own_segments[:, :, None] == key_segments[:, None, :])

    tables = [jnp.tile(t, (half_seqs, 1)) for t in (cosine_table, sine_table)]
    bias = jnp.where(allowed, 0.0, -1e30).astype(f32)

    saved, previous = [], None
    base = inputs.reshape(tokens, D)
    for layer in range(LAYERS):
        weights = list(attn_weights)
        hidden, normed, mixed, queries, keyvals, attended, projected, half, normed_ffn = attn_forward(
            base, weights, gain_rows[layer], tables, bias, planes, reach, 3 + layer, previous
        )
        ffn_share = full[layer]
        if layer + 1 < LAYERS:
            gu_pieces, w_down, later, attended = lax.optimization_barrier(
                (gu_pieces, w_down, later, attended)
            )
            attn_weights = later_weights(later, w_qkv, w_out, layer + 1, 2 + 20 * layer)
            full[layer + 1] = (gate_up_rows(layer + 1), down_rows(layer + 1))
            normed_ffn, *attn_weights = lax.optimization_barrier((normed_ffn, *attn_weights))
        group_normed, whole_down, down_out = ffn(normed_ffn, ffn_share, 5 + layer, planes)
        full[layer] = (weights, (ffn_share[0], whole_down))
        saved.append(
            (
                [hidden, mixed, queries, keyvals, projected, half],
                [normed, attended],
                group_normed,
                down_out,
            )
        )
        base, previous = half, (down_out, gain_rows[layer])

    output, post_ffn_back = jax.vjp(rms_norm, down_out, gain_rows[-1][1, D : 2 * D])
    output = base + output
    target_gap = output - teacher.reshape(tokens, D).astype(f32)
    valid_weight = valid_mask.astype(f32).reshape(tokens, 1)
    square_sum = jnp.sum(valid_weight * target_gap * target_gap)
    loss_weight = float(all_seqs * seq_length * D // 4)
    grad_hidden = (
        cotangent.reshape(tokens, D).astype(f32)
        + 2.0 * loss_weight / (valid_count * D) * valid_weight * target_gap
    )
    d_down, d_post_ffn = post_ffn_back(grad_hidden)
    d_down, d_post_ffn = d_down.astype(bf16), d_post_ffn[None]

    tiled = ff_block % 16 == 0
    attn_acts = [None] * LAYERS
    down_grads = [None] * LAYERS
    gain_grads = [None] * LAYERS
    gu_sums = [None] * LAYERS
    for layer in reversed(range(LAYERS)):
        kept, (normed, attended), group_normed, _ = saved[layer]
        weights, ffn_share = full[layer]
        d_normed_ffn, grad_gu, grad_down = ffn(
            d_down, ffn_share, 9 + layer, planes, group_normed
        )
        if layer == 0 and tiled:
            first_down = grad_down.reshape(planes, ff_block, out_cols)
        else:
            down_grads[layer] = lax.psum_scatter(
                grad_down.reshape(planes * ff_block, out_cols),
                "zd",
                scatter_dimension=0,
                tiled=True,
            )
        if len(grad_gu.shape) == 3:
            grad_gu = grad_gu.reshape(2, planes, PLANE * gu_rows, share).transpose(1, 0, 2, 3)
        gu_sums[layer] = lax.psum_scatter(
            grad_gu.reshape(-1, share), "zd", scatter_dimension=0, tiled=True
        )
        earlier = (saved[layer - 1][3], gain_rows[layer - 1]) if layer > 0 else None
        grad_hidden, d_mixed, d_projected, gain_grads[layer], *d_rest = attn_backward(
            d_normed_ffn,
            grad_hidden,
            kept,
            weights,
            gain_rows[layer],
            tables,
            bias,
            planes,
            reach,
            17 + layer,
            earlier,
        )
        gain_grads[layer] = gain_grads[layer].at[1:, D : 2 * D].set(d_post_ffn)
        if layer > 0:
            d_down, d_post_ffn = d_rest
        attn_acts[layer] = [normed, d_mixed, attended, d_projected]
    attn_acts[0][1], gu_sums[1:], down_grads[1:] = lax.optimization_barrier(
        (attn_acts[0][1], gu_sums[1:], down_grads[1:])
    )

    packet = jnp.stack(gain_grads, axis=1).reshape(cores, LAYERS, planes, PLANE, gain_cols)
    packet = packet.transpose(0, 3, 2, 1, 4)
    packet = jnp.pad(packet, [(0, 0)] * 3 + [(0, 8 - LAYERS), (0, lanes - gain_cols)])
    packet = packet.at[:, :, :, LAYERS, 0].set(square_sum)
    packet = packet.reshape(cores, PLANE, planes * 8, lanes)
    down = first_down if tiled else None
    grad_qkv, grad_out, packet, *summed_down = collect(sum(attn_acts, []), packet, down, 19)
    if tiled:
        (down_grads[0],) = summed_down
    mse_loss = packet[LAYERS, 0] / (valid_count * D)
    gain_grad = packet[:LAYERS, None, :gain_cols]

    outcome = update(
        [[grad_qkv], [grad_out], down_grads],
        gu_sums,
        (mom_qkv, mom_out, mom_gu, mom_down),
        (w_qkv, w_out, w_gu, w_down),
        15,
    )
    new_weights, moments = outcome[:4], outcome[4:]
    gain_first_new = beta_one * gain_first + (1.0 - beta_one) * gain_grad
    gain_second_new = beta_two * gain_second + (1.0 - beta_two) * gain_grad * gain_grad
    gains_new = norm_gains - adam_rate * (gain_first_new / (1.0 - beta_one**STEP)) / (
        jnp.sqrt(gain_second_new / (1.0 - beta_two**STEP)) + adam_epsilon
    )
    return (
        mse_loss,
        output.reshape(inputs.shape),
        grad_hidden.reshape(inputs.shape),
        *new_weights,
        *moments,
        gains_new,
        gain_first_new,
        gain_second_new,
    )


def solution(mesh):
    cores, length = mesh.devices.shape
    split = Mesh(mesh.devices.reshape(cores, length // PLANE, PLANE), EVERY)
    stream = P("head", SEQ, None)
    matrix = P(None, SEQ, "head")
    gains = P(None, "head", SEQ)
    return jax.shard_map(
        body,
        mesh=split,
        in_specs=(stream, stream, stream, P(), P("head", SEQ))
        + (matrix,) * 4
        + (gains,)
        + (matrix,) * 4
        + (gains,) * 2,
        out_specs=(P(), stream, stream) + (matrix,) * 8 + (gains,) * 3,
        check_vma=False,
    )
```

```python
from functools import partial
import itertools
import math

import jax
import jax.numpy as jnp
from jax import lax
from jax.experimental import pallas as pl
from jax.experimental.pallas import tpu as pltpu
from jax.sharding import Mesh, PartitionSpec as P

D = 1152
HEADS = 4
HD = 256
FF = 6912
WINDOW = 512
LAYERS = 2
NS_ITERS = 5
STEP = 10
PLANE = 4

norm_eps = 1e-06
rope_base = 10000.0
newton_one = 3.4445
newton_two = -4.775
newton_three = 2.0315
muon_decay = 0.95
muon_rate = 0.15
muon_shrink = 0.01
muon_scale = 0.2
beta_one = 0.9
beta_two = 0.95
adam_rate = 0.7
adam_epsilon = 1e-08
finest_precision = lax.Precision.HIGHEST
MESH = pl.DeviceIdType.MESH
SEQ = ("zd", "tp")
GROUP = ("head", "tp")
EVERY = ("head", "zd", "tp")
bf16 = jnp.bfloat16
f32 = jnp.float32
LIGHT = pl.CostEstimate(flops=1, bytes_accessed=1, transcendentals=0)


def linear(places, sizes):
    index = 0
    for place, size in zip(places, sizes):
        index = index * size + place
    return index


def enter(partners):
    barrier = pltpu.get_barrier_semaphore()
    for partner in partners:
        pl.semaphore_signal(barrier, inc=1, device_id=partner, device_id_type=MESH)
    pl.semaphore_wait(barrier, len(partners))


class Spread:
    ORDER = ("zd", "tp", "head")

    def __init__(self, sizes, slots, send_sem, recv_sem, whole_z=False):
        self.size = dict(zip(EVERY, sizes))
        self.place = {axis: lax.axis_index(axis) for axis in EVERY}
        self.slots, self.send_sem, self.recv_sem = slots, send_sem, recv_sem
        self.held, self.sends, self.number = [(self.place, None)], [], 0
        if whole_z:
            self.held = [(dict(self.place, zd=z), None) for z in range(self.size["zd"])]
            self.ORDER = self.ORDER[1:]

    def partners(self):
        return [
            {axis: lax.rem(self.place[axis] + step, self.size[axis])}
            for axis in self.ORDER
            for step in range(1, self.size[axis])
        ]

    def stage(self, axis):
        arriving = []
        for where, arrivals in self.held:
            while arrivals:
                arrivals.pop().wait_recv()
            for step in range(1, self.size[axis]):
                to = lax.rem(self.place[axis] + step, self.size[axis])
                back = lax.rem(self.place[axis] - step + self.size[axis], self.size[axis])
                landing = []
                for k, slot in enumerate(self.slots):
                    ref = slot.at[tuple(where[name] for name in EVERY)]
                    copy = pltpu.make_async_remote_copy(
                        src_ref=ref,
                        dst_ref=ref,
                        send_sem=self.send_sem.at[k, self.number],
                        recv_sem=self.recv_sem.at[k, self.number],
                        device_id={axis: to},
                        device_id_type=MESH,
                    )
                    copy.start()
                    self.sends.append(copy)
                    landing.append(copy)
                self.number += 1
                arriving.append((dict(where, **{axis: back}), landing))
        self.held = self.held + arriving

    def finish(self):
        for _, arrivals in self.held:
            while arrivals:
                arrivals.pop().wait_recv()
        for copy in self.sends:
            copy.wait_send()


def start_kernel(sizes, *refs):
    cores, planes, members = sizes
    rest = list(refs)
    take = lambda number: [rest.pop(0) for _ in range(number)]
    qkv, out, packet = take(3)
    mixed, project, packets, qkv_later, out_later = take(5)
    packet_slots, qkv_slots, out_slots, send_sem, recv_sem = take(5)
    later_send, later_recv = take(2)
    qkv_low, out_low, later_own = take(3)
    gather = Spread(sizes, [packet_slots, qkv_slots, out_slots], send_sem, recv_sem)
    here = tuple(gather.place[name] for name in EVERY)
    zd = gather.place["zd"]
    enter(gather.partners())
    packet_slots[here] = packet[...]

    def place_rows(source, layer, slot, index):
        rows = source.shape[1]
        slot[index + (slice(0, rows),)] = source[layer].astype(bf16)
        if slot.shape[-2] > rows:
            slot[index + (slice(rows, slot.shape[-2]),)] = jnp.zeros(
                (slot.shape[-2] - rows, slot.shape[-1]), bf16
            )

    for source, slot in ((qkv, qkv_slots), (out, out_slots)):
        place_rows(source, 0, slot, here)
    gather.stage("zd")
    moves = []

    def along_z(source, target, sends, recvs):
        for step in range(1, planes):
            copy = pltpu.make_async_remote_copy(
                src_ref=source,
                dst_ref=target,
                send_sem=sends.at[step],
                recv_sem=recvs.at[step],
                device_id={"zd": lax.rem(zd + step, planes)},
                device_id_type=MESH,
            )
            copy.start()
            moves.append(copy)

    for k, (source, low, slot) in enumerate(
        ((qkv, qkv_low, qkv_later), (out, out_low, out_later))
    ):
        for layer in range(1, source.shape[0]):
            place_rows(source, layer, low, (layer - 1,))
            target = slot.at[layer - 1, zd]
            along_z(
                low.at[layer - 1], target, later_send.at[k, layer], later_recv.at[k, layer]
            )
            own = pltpu.make_async_copy(low.at[layer - 1], target, later_own.at[k, layer])
            own.start()
            moves.append(own)
    gather.stage("tp")
    gather.stage("head")
    gather.finish()
    side_by_side(sizes, (qkv_slots, out_slots), (mixed, project))
    packets[...] = packet_slots[...]
    for copy in moves:
        copy.wait()


def rows_kernel(sizes, gu, gu_result, pieces, gu_send, gu_recv, gu_own):
    cores, planes, members = sizes
    core, _, tp = (lax.axis_index(axis) for axis in EVERY)
    moves = []
    group = []
    for step in range(1, cores * members):
        far = lax.rem(core + step // members, cores), lax.rem(tp + step % members, members)
        group.append((dict(zip(GROUP, far)), linear(far, (cores, members))))
    enter([device for device, _ in group])
    layers, rows, columns = gu.shape
    block = columns // (planes * members)
    half = planes // cores
    for c in range(cores):
        for j in range(members):
            for i in range(layers):
                cut = [
                    gu[i, :, pl.ds(((c * half + k) * members + j) * block, block)]
                    for k in range(half)
                ]
                value = jnp.concatenate(cut, axis=1) if half > 1 else cut[0]
                pieces[c * members + j, i * rows : (i + 1) * rows] = value.astype(bf16)
    if pieces.shape[1] > layers * rows:
        for piece in range(cores * members):
            pieces[piece, layers * rows :] = jnp.zeros(
                (pieces.shape[1] - layers * rows, pieces.shape[2]), bf16
            )
    me = linear((core, tp), (cores, members))
    for step, (device, index) in enumerate(group):
        copy = pltpu.make_async_remote_copy(
            src_ref=pieces.at[index],
            dst_ref=gu_result.at[me],
            send_sem=gu_send.at[step],
            recv_sem=gu_recv.at[step],
            device_id=device,
            device_id_type=MESH,
        )
        copy.start()
        moves.append(copy)
    own = pltpu.make_async_copy(pieces.at[me], gu_result.at[me], gu_own)
    own.start()
    moves.append(own)
    for copy in moves:
        copy.wait()


def exchanged_rows(w_gu, ident):
    sizes = tuple(lax.axis_size(axis) for axis in EVERY)
    cores, _, members = sizes
    vmem, dma = pltpu.VMEM, pltpu.SemaphoreType.DMA
    layers, rows, columns = w_gu.shape
    piece = (
        cores * members,
        -(-layers * rows // 16) * 16,
        columns // (cores * members),
    )
    return pl.pallas_call(
        partial(rows_kernel, sizes),
        out_shape=jax.ShapeDtypeStruct(piece, bf16),
        in_specs=[pl.BlockSpec(memory_space=pltpu.VMEM)],
        out_specs=pl.BlockSpec(memory_space=pl.ANY),
        scratch_shapes=[vmem(piece, bf16)] + [dma((cores * members - 1,))] * 2 + [dma],
        compiler_params=pltpu.CompilerParams(
            collective_id=ident, has_side_effects=True, vmem_limit_bytes=48 * 2**20
        ),
    )(w_gu)


def side_by_side(sizes, slots, results):
    cores, planes, members = sizes
    for slot, result in zip(slots, results):
        columns = slot.shape[4]
        rows = result.shape[0] // (planes * members)
        for h, z, t in itertools.product(range(cores), range(planes), range(members)):
            row = (z * members + t) * rows
            result[row : row + rows, h * columns : (h + 1) * columns] = slot[h, z, t, :rows]


def later_kernel(sizes, layer, qkv, out, mixed, project, qkv_slots, out_slots, send_sem, recv_sem):
    gather = Spread(sizes, [qkv_slots, out_slots], send_sem, recv_sem, whole_z=True)
    core, _, tp = (gather.place[name] for name in EVERY)
    enter(gather.partners())
    for source, slot in ((qkv, qkv_slots), (out, out_slots)):
        for z in range(sizes[1]):
            slot[core, z, tp] = source[layer - 1, z]
    gather.stage("tp")
    gather.stage("head")
    gather.finish()
    side_by_side(sizes, (qkv_slots, out_slots), (mixed, project))


def whole_shapes(sizes, tall, matrices):
    slots = [pltpu.VMEM(sizes + (t, w.shape[2]), bf16) for t, w in zip(tall, matrices)]
    outs = [
        jax.ShapeDtypeStruct((w.shape[1] * sizes[1] * sizes[2], w.shape[2] * sizes[0]), bf16)
        for w in matrices
    ]
    return slots, outs


def start(w_qkv, w_out, packet, ident):
    sizes = tuple(lax.axis_size(axis) for axis in EVERY)
    cores, planes, members = sizes
    vmem, dma = pltpu.VMEM, pltpu.SemaphoreType.DMA
    here, there = pl.BlockSpec(memory_space=pltpu.VMEM), pl.BlockSpec(memory_space=pl.ANY)
    shape = jax.ShapeDtypeStruct
    tall = [-(-w.shape[1] // 16) * 16 for w in (w_qkv, w_out)]
    slots, outs = whole_shapes(sizes, tall, (w_qkv, w_out))
    layers = w_qkv.shape[0]
    later = [
        shape((layers - 1, planes, t, w.shape[2]), bf16) for t, w in zip(tall, (w_qkv, w_out))
    ]
    operands = [w_qkv, w_out, packet]
    outs = outs + [shape(sizes + packet.shape, f32)] + later
    out_specs = [here] * 3 + [there] * 2
    moves = math.prod(sizes) - 1
    scratch = [vmem(sizes + packet.shape, f32)] + slots + [dma((3, moves))] * 2
    scratch += [dma((2, layers, planes))] * 2
    scratch += [
        vmem((layers - 1, t, w.shape[2]), bf16) for t, w in zip(tall, (w_qkv, w_out))
    ] + [dma((2, layers))]
    return pl.pallas_call(
        partial(start_kernel, sizes),
        out_shape=outs,
        in_specs=[here] * len(operands),
        out_specs=out_specs,
        scratch_shapes=scratch,
        compiler_params=pltpu.CompilerParams(
            collective_id=ident, has_side_effects=True, vmem_limit_bytes=56 * 2**20
        ),
    )(*operands)


def later_weights(gathered, w_qkv, w_out, layer, ident):
    sizes = tuple(lax.axis_size(axis) for axis in EVERY)
    slots, outs = whole_shapes(sizes, [g.shape[2] for g in gathered], (w_qkv, w_out))
    here = pl.BlockSpec(memory_space=pltpu.VMEM)
    moves = math.prod(sizes) - sizes[1]
    return pl.pallas_call(
        partial(later_kernel, sizes, layer),
        out_shape=outs,
        in_specs=[here] * 2,
        out_specs=[here] * 2,
        scratch_shapes=slots + [pltpu.SemaphoreType.DMA((2, moves))] * 2,
        compiler_params=pltpu.CompilerParams(
            collective_id=ident, has_side_effects=True, vmem_limit_bytes=48 * 2**20
        ),
    )(*gathered)


def by_rows(rows, work, step=16):
    @pl.loop(0, rows // step)
    def _(index):
        work(pl.ds(pl.multiple_of(index * step, step), step))


def collect_kernel(sizes, layers, tiled, *refs):
    cores, planes, members = sizes
    rest = list(refs)
    take = lambda number: [rest.pop(0) for _ in range(number)]
    acts, packet = take(4 * layers), take(1)[0]
    if tiled:
        (down,) = take(1)
    results = take(3)
    if tiled:
        (down_result,) = take(1)
    far, halves = take(4 * layers), take(2 * layers)
    packet_land = rest.pop(0)
    pieces, plane_lands, totals, z_sums, z_lands = (take(3) for _ in range(5))
    act_send, act_recv, packet_send, packet_recv = take(4)
    tp_send, tp_recv, z_send, z_recv = take(4)
    core, zd, tp = (lax.axis_index(axis) for axis in EVERY)
    sibling = {"head": 1 - core}
    enter(
        [sibling]
        + [{"tp": lax.rem(tp + step, members)} for step in range(1, members)]
        + [{"zd": lax.rem(zd + step, planes)} for step in range(1, planes)]
    )
    sends = []

    def send(src, dst, send_sem, recv_sem, device):
        copy = pltpu.make_async_remote_copy(
            src_ref=src,
            dst_ref=dst,
            send_sem=send_sem,
            recv_sem=recv_sem,
            device_id=device,
            device_id_type=MESH,
        )
        copy.start()
        sends.append(copy)
        return copy

    if tiled:
        down_land, down_send, down_recv, down_own = take(4)
        down_moves = []
        for step in range(1, planes):
            there = lax.rem(zd + step, planes)
            down_moves.append(
                send(
                    down.at[there],
                    down_land.at[step],
                    down_send.at[step],
                    down_recv.at[step],
                    {"zd": there},
                )
            )
        down_stay = pltpu.make_async_copy(down.at[zd], down_land.at[0], down_own)
        down_stay.start()
    for k in range(2 * layers):
        grad, half = acts[2 * k + 1], halves[k]
        width = half.shape[2]
        for h in range(cores):
            half[h] = grad[:, h * width : (h + 1) * width]
    moves = []
    for k in range(2 * layers):
        moves.append(
            send(acts[2 * k], far[2 * k], act_send.at[2 * k], act_recv.at[2 * k], sibling)
        )
        moves.append(
            send(
                halves[k].at[1 - core],
                far[2 * k + 1],
                act_send.at[2 * k + 1],
                act_recv.at[2 * k + 1],
                sibling,
            )
        )
    gains = send(packet.at[1 - core], packet_land, packet_send, packet_recv, sibling)
    plane_moves, z_moves = {}, {}
    for kind in range(3):
        piece = pieces[kind]
        if kind < 2:
            for layer in range(layers):
                k = 2 * layer + kind
                near = lax.dot_general(
                    acts[2 * k][...], halves[k][core], ALONG, preferred_element_type=f32
                )
                moves[2 * k].wait_recv()
                moves[2 * k + 1].wait_recv()
                value = near + lax.dot_general(
                    far[2 * k][...], far[2 * k + 1][...], ALONG, preferred_element_type=f32
                )
                value = value.astype(bf16)
                rows = value.shape[0] // (planes * members)
                slab = piece.shape[1] // planes
                for z, t in itertools.product(range(planes), range(members)):
                    at = (z * members + t) * rows
                    to = z * slab + layer * rows
                    piece[t, to : to + rows] = value[at : at + rows]
            if slab > layers * rows:
                for z, t in itertools.product(range(planes), range(members)):
                    piece[t, z * slab + layers * rows : (z + 1) * slab] = jnp.zeros(
                        (slab - layers * rows, piece.shape[2]), bf16
                    )
        else:
            gains.wait_recv()
            piece[...] = packet[core] + packet_land[...]
        for step in range(1, members):
            there = lax.rem(tp + step, members)
            plane_moves[kind, step] = send(
                piece.at[there],
                plane_lands[kind].at[step],
                tp_send.at[kind, step],
                tp_recv.at[kind, step],
                {"tp": there},
            )
    for kind in range(3):
        for step in range(1, members):
            plane_moves[kind, step].wait_recv()
        piece, total, land, result = pieces[kind], totals[kind], plane_lands[kind], results[kind]
        stride = 8 if land.dtype == f32 else 16

        def gather_plane(rows):
            value = piece[tp, rows].astype(f32)
            for step in range(1, members):
                value = value + land[step, rows].astype(f32)
            total[rows] = value

        by_rows(total.shape[0], gather_plane, stride)
        height = result.shape[0]
        z_sum = z_sums[kind]
        for step in range(1, planes):
            there = lax.rem(zd + step, planes)

            def round_off(rows):
                at = pl.multiple_of(there * height + rows.start, stride)
                z_sum[step, rows] = total[pl.ds(at, rows.size)].astype(z_sum.dtype)

            by_rows(height, round_off, stride)
            z_moves[kind, step] = send(
                z_sum.at[step],
                z_lands[kind].at[step],
                z_send.at[kind, step],
                z_recv.at[kind, step],
                {"zd": there},
            )
    for kind in range(3):
        for step in range(1, planes):
            z_moves[kind, step].wait_recv()
        total, land, result = totals[kind], z_lands[kind], results[kind]
        height = result.shape[0]
        stride = 8 if land.dtype == f32 else 16

        def gather_z(rows):
            at = pl.multiple_of(zd * height + rows.start, stride)
            value = total[pl.ds(at, rows.size)]
            for step in range(1, planes):
                value = value + land[step, rows].astype(f32)
            result[rows] = value

        by_rows(height, gather_z, stride)
    if tiled:
        down_stay.wait()
        for copy in down_moves:
            copy.wait_recv()

        def gather_down(rows):
            value = down_land[0, rows].astype(f32)
            for step in range(1, planes):
                value = value + down_land[step, rows].astype(f32)
            down_result[rows] = value

        by_rows(down_result.shape[0], gather_down)
    for copy in sends:
        copy.wait_send()


def collect(acts, packet, down, ident):
    sizes = tuple(lax.axis_size(axis) for axis in EVERY)
    cores, planes, members = sizes
    layers = len(acts) // 4
    vmem, dma = pltpu.VMEM, pltpu.SemaphoreType.DMA
    tokens = acts[0].shape[0]
    halves = [acts[2 * k + 1].shape[1] // cores for k in range(2 * layers)]
    slabs = []
    for kind in range(2):
        rows = layers * acts[2 * kind].shape[1] // (planes * members)
        slabs.append((-(-rows // 16) * 16, halves[kind], bf16))
    slabs.append((packet.shape[2] // planes, packet.shape[3], f32))
    far = []
    for k in range(2 * layers):
        far += [vmem(acts[2 * k].shape, bf16), vmem((tokens, halves[k]), bf16)]
    scratch = far + [vmem((cores, tokens, width), bf16) for width in halves]
    scratch += [vmem(packet.shape[1:], f32)]
    scratch += [vmem((members, planes * r, c), kind) for r, c, kind in slabs] * 2
    scratch += [vmem((planes * r, c), f32) for r, c, _ in slabs]
    scratch += [vmem((planes, r, c), kind) for r, c, kind in slabs] * 2
    scratch += [dma((4 * layers,))] * 2 + [dma] * 2
    scratch += [dma((3, members))] * 2 + [dma((3, planes))] * 2
    here = pl.BlockSpec(memory_space=pltpu.VMEM)
    operands = [*acts, packet]
    outs = [jax.ShapeDtypeStruct((r, c), f32) for r, c, _ in slabs]
    in_specs = [here] * len(operands)
    if down is not None:
        operands, in_specs = operands + [down], in_specs + [pl.BlockSpec(memory_space=pl.ANY)]
        outs += [jax.ShapeDtypeStruct(down.shape[1:], f32)]
        scratch += [vmem(down.shape, bf16), dma((planes,)), dma((planes,)), dma]
    return pl.pallas_call(
        partial(collect_kernel, sizes, layers, down is not None),
        out_shape=outs,
        in_specs=in_specs,
        out_specs=[here] * len(outs),
        scratch_shapes=scratch,
        cost_estimate=LIGHT,
        compiler_params=pltpu.CompilerParams(
            collective_id=ident, has_side_effects=True, vmem_limit_bytes=56 * 2**20
        ),
    )(*operands)


def neighbours(planes, reach, sign):
    total = planes * PLANE
    place = linear([lax.axis_index("zd"), lax.axis_index("tp")], (planes, PLANE))

    def at(distance):
        there = lax.rem(place + distance + total, total)
        return {"zd": lax.div(there, PLANE), "tp": lax.rem(there, PLANE)}

    steps = range(1, reach + 1)
    devices, sources = [at(sign * step) for step in steps], [at(-sign * step) for step in steps]
    above = [place + step < total for step in steps]
    below = [place >= step for step in steps]
    sends, comes = (above, below) if sign > 0 else (below, above)
    return devices, sources, sends, comes


def inverse_rms(values):
    return lax.rsqrt(jnp.mean(values * values, axis=-1, keepdims=True) + norm_eps)


def rms_back(gradient, values, gain):
    inverse = inverse_rms(values)
    scaled = gradient * gain
    shared = jnp.mean(scaled * values, axis=-1, keepdims=True) * (inverse * inverse)
    return inverse * (scaled - values * shared), jnp.sum(
        gradient * values * inverse, axis=0, keepdims=True
    )


def turn(values, cosine, sine):
    half = values.shape[-1] // 2
    lower, upper = values[:, :half], values[:, half:]
    return jnp.concatenate(
        [lower * cosine - upper * sine, upper * cosine + lower * sine], axis=-1
    )


def soft_rows(query, keys, bias):
    scores = lax.dot_general(query, keys, ACROSS, preferred_element_type=f32)
    scores = scores * (1.0 / math.sqrt(HD)) + bias
    raised = jnp.exp(scores - jnp.max(scores, axis=-1, keepdims=True))
    return raised / jnp.sum(raised, axis=-1, keepdims=True)


def attn_forward_kernel(planes, reach, chained, *refs):
    rest = list(refs)
    take = lambda number: [rest.pop(0) for _ in range(number)]
    if chained:
        base, down, before = take(3)
    else:
        (base,) = take(1)
    w_mixed, w_project, gains, cosine, sine, bias = take(6)
    hidden, normed, mixed, queries, keyvals_out = take(5)
    attended, projected, hidden_half, normed_ffn = take(4)
    keyvals, send_sem, recv_sem, save_sem = take(4)
    seqs, stretch, key_len = bias.shape
    devices, sources, sends, comes = neighbours(planes, reach, 1)
    enter(devices + sources)
    value = base[...].astype(f32)
    if chained:
        late = down[...]
        value = value + late * inverse_rms(late) * before[1:2, D : 2 * D]
    hidden[...] = value
    low = (value * inverse_rms(value) * gains[0:1, :D]).astype(bf16)
    normed[...] = low
    mixed[...] = matmul(low, w_mixed[...])
    key = mixed[:, HEADS * HD : HEADS * HD + HD]
    key = turn(key * inverse_rms(key) * gains[1:2, 2 * D :], cosine[...], sine[...]).astype(bf16)
    late_values = mixed[:, HEADS * HD + HD :].astype(bf16)
    copies = []
    for i in range(seqs):
        rows = slice(i * stretch, (i + 1) * stretch)
        keyvals[i, reach * stretch :, :HD] = key[rows]
        keyvals[i, reach * stretch :, HD:] = late_values[rows]
        for step, device in enumerate(devices):
            copy = pltpu.make_async_remote_copy(
                src_ref=keyvals.at[i, pl.ds(reach * stretch, stretch)],
                dst_ref=keyvals.at[i, pl.ds((reach - 1 - step) * stretch, stretch)],
                send_sem=send_sem.at[i, step],
                recv_sem=recv_sem.at[i, step],
                device_id=device,
                device_id_type=MESH,
            )
            pl.when(sends[step])(copy.start)
            copies.append((step, copy))

            @pl.when(jnp.logical_not(comes[step]))
            def _():
                at = (reach - 1 - step) * stretch
                keyvals[i, at : at + stretch] = jnp.zeros((stretch, 2 * HD), bf16)

    for h in range(HEADS):
        columns = slice(h * HD, (h + 1) * HD)
        query = mixed[:, columns]
        query = turn(query * inverse_rms(query) * gains[0:1, 2 * D :], cosine[...], sine[...])
        queries[:, columns] = query.astype(bf16)
    for step, copy in copies:
        pl.when(comes[step])(copy.wait_recv)
    save = pltpu.make_async_copy(keyvals, keyvals_out, save_sem)
    save.start()
    for i in range(seqs):
        rows = slice(i * stretch, (i + 1) * stretch)
        for h in range(HEADS):
            columns = slice(h * HD, (h + 1) * HD)
            soft = soft_rows(queries[rows, columns], keyvals[i, :, :HD], bias[i])
            attended[rows, columns] = matmul(soft.astype(bf16), keyvals[i, :, HD:]).astype(bf16)
    out = matmul(attended[...], w_project[...])
    projected[...] = out
    half = hidden[...] + out * inverse_rms(out) * gains[0:1, D : 2 * D]
    hidden_half[...] = half
    normed_ffn[...] = (half * inverse_rms(half) * gains[1:2, :D]).astype(bf16)
    for step, copy in copies:
        pl.when(sends[step])(copy.wait_send)
    save.wait()


def attn_forward(base, weights, gains, tables, bias, planes, reach, ident, earlier=None):
    tokens = base.shape[0]
    seqs, _, key_len = bias.shape
    shape = jax.ShapeDtypeStruct
    operands = [base] + list(earlier or []) + list(weights) + [gains, *tables, bias]
    here, there = pl.BlockSpec(memory_space=pltpu.VMEM), pl.BlockSpec(memory_space=pl.ANY)
    dma = pltpu.SemaphoreType.DMA
    return pl.pallas_call(
        partial(attn_forward_kernel, planes, reach, earlier is not None),
        out_shape=[
            shape((tokens, D), f32),
            shape((tokens, D), bf16),
            shape((tokens, weights[0].shape[1]), f32),
            shape((tokens, HEADS * HD), bf16),
            shape((seqs, key_len, 2 * HD), bf16),
            shape((tokens, HEADS * HD), bf16),
            shape((tokens, D), f32),
            shape((tokens, D), f32),
            shape((tokens, D), bf16),
        ],
        in_specs=[here] * len(operands),
        out_specs=[here] * 4 + [there] + [here] * 4,
        scratch_shapes=[
            pltpu.VMEM((seqs, key_len, 2 * HD), bf16),
            dma((seqs, reach)),
            dma((seqs, reach)),
            dma,
        ],
        compiler_params=pltpu.CompilerParams(
            collective_id=ident, has_side_effects=True, vmem_limit_bytes=56 * 2**20
        ),
    )(*operands)


def attn_backward_kernel(planes, reach, chained, *refs):
    rest = list(refs)
    take = lambda number: [rest.pop(0) for _ in range(number)]
    d_ffn, above, hidden, mixed, queries, keyvals, projected, hidden_half = take(8)
    w_mixed, w_project, gains, cosine, sine, bias = take(6)
    if chained:
        down, before = take(2)
    grad, d_mixed, d_projected, gain_grads = take(4)
    if chained:
        d_down, d_post = take(2)
    d_keyvals, outgoing, incoming, d_attended, send_sem, recv_sem = take(6)
    seqs, stretch, key_len = bias.shape
    devices, sources, sends, comes = neighbours(planes, reach, -1)
    enter(devices + sources)
    scale = 1.0 / math.sqrt(HD)
    part, gain_row = rms_back(d_ffn[...], hidden_half[...], gains[1:2, :D])
    gain_grads[1:2, :D] = gain_row
    gain_grads[1:2, D : 2 * D] = jnp.zeros((1, D), f32)
    grad[...] = part + above[...]
    part, gain_row = rms_back(grad[...], projected[...], gains[0:1, D : 2 * D])
    gain_grads[0:1, D : 2 * D] = gain_row
    low = part.astype(bf16)
    d_projected[...] = low
    d_attended[...] = lax.dot_general(
        low, w_project[...], ACROSS, preferred_element_type=f32
    ).astype(bf16)
    query_gain = jnp.zeros((1, HD), f32)
    for i in range(seqs):
        rows = slice(i * stretch, (i + 1) * stretch)
        d_keys = d_values = None
        for h in range(HEADS):
            columns = slice(h * HD, (h + 1) * HD)
            query, d_out = queries[rows, columns], d_attended[rows, columns]
            keys, values = keyvals[i, :, :HD], keyvals[i, :, HD:]
            soft = soft_rows(query, keys, bias[i])
            d_soft = lax.dot_general(d_out, values, ACROSS, preferred_element_type=f32)
            total = jnp.sum(soft * d_soft, axis=-1, keepdims=True)
            d_scores = (soft * (d_soft - total)).astype(bf16)
            key_part = lax.dot_general(d_scores, query, ALONG, preferred_element_type=f32)
            value_part = lax.dot_general(
                soft.astype(bf16), d_out, ALONG, preferred_element_type=f32
            )
            d_keys = key_part if d_keys is None else d_keys + key_part
            d_values = value_part if d_values is None else d_values + value_part
            d_query = matmul(d_scores, keys) * scale
            d_query = turn(d_query, cosine[rows], -sine[rows])
            part, gain_row = rms_back(d_query, mixed[rows, columns], gains[0:1, 2 * D :])
            query_gain = query_gain + gain_row
            d_mixed[rows, columns] = part.astype(bf16)
        d_keyvals[i, :, :HD] = d_keys * scale
        d_keyvals[i, :, HD:] = d_values
    gain_grads[0:1, 2 * D :] = query_gain
    outgoing[...] = d_keyvals[:, : reach * stretch].astype(bf16)
    copies = []
    for i in range(seqs):
        for step, device in enumerate(devices):
            copy = pltpu.make_async_remote_copy(
                src_ref=outgoing.at[i, pl.ds((reach - 1 - step) * stretch, stretch)],
                dst_ref=incoming.at[i, step],
                send_sem=send_sem.at[i, step],
                recv_sem=recv_sem.at[i, step],
                device_id=device,
                device_id_type=MESH,
            )
            pl.when(sends[step])(copy.start)
            copies.append((step, copy))

            @pl.when(jnp.logical_not(comes[step]))
            def _():
                incoming[i, step] = jnp.zeros((stretch, 2 * HD), bf16)

    for step, copy in copies:
        pl.when(comes[step])(copy.wait_recv)
    key_gain = jnp.zeros((1, HD), f32)
    for i in range(seqs):
        rows = slice(i * stretch, (i + 1) * stretch)
        own = d_keyvals[i, reach * stretch :]
        for step in range(reach):
            own = own + incoming[i, step].astype(f32)
        d_key = turn(own[:, :HD], cosine[rows], -sine[rows])
        part, gain_row = rms_back(
            d_key, mixed[rows, HEADS * HD : HEADS * HD + HD], gains[1:2, 2 * D :]
        )
        key_gain = key_gain + gain_row
        d_mixed[rows, HEADS * HD : HEADS * HD + HD] = part.astype(bf16)
        d_mixed[rows, HEADS * HD + HD :] = own[:, HD:].astype(bf16)
    gain_grads[1:2, 2 * D :] = key_gain
    d_normed = lax.dot_general(d_mixed[...], w_mixed[...], ACROSS, preferred_element_type=f32)
    part, gain_row = rms_back(d_normed, hidden[...], gains[0:1, :D])
    gain_grads[0:1, :D] = gain_row
    grad[...] = grad[...] + part
    if chained:
        part, gain_row = rms_back(grad[...], down[...], before[1:2, D : 2 * D])
        d_down[...] = part.astype(bf16)
        d_post[...] = gain_row
    for step, copy in copies:
        pl.when(sends[step])(copy.wait_send)


def attn_backward(
    d_ffn, above, kept, weights, gains, tables, bias, planes, reach, ident, earlier=None
):
    tokens = above.shape[0]
    seqs, stretch, key_len = bias.shape
    shape = jax.ShapeDtypeStruct
    operands = [d_ffn, above, *kept, *weights, gains, *tables, bias] + list(earlier or [])
    outs = [
        shape((tokens, D), f32),
        shape((tokens, weights[0].shape[1]), bf16),
        shape((tokens, D), bf16),
        shape(gains.shape, f32),
    ]
    if earlier is not None:
        outs += [shape((tokens, D), bf16), shape((1, D), f32)]
    here = pl.BlockSpec(memory_space=pltpu.VMEM)
    vmem, dma = pltpu.VMEM, pltpu.SemaphoreType.DMA
    return pl.pallas_call(
        partial(attn_backward_kernel, planes, reach, earlier is not None),
        out_shape=outs,
        in_specs=[here] * len(operands),
        out_specs=[here] * len(outs),
        scratch_shapes=[
            vmem((seqs, key_len, 2 * HD), f32),
            vmem((seqs, reach * stretch, 2 * HD), bf16),
            vmem((seqs, reach, stretch, 2 * HD), bf16),
            vmem((tokens, HEADS * HD), bf16),
            dma((seqs, reach)),
            dma((seqs, reach)),
        ],
        compiler_params=pltpu.CompilerParams(
            collective_id=ident, has_side_effects=True, vmem_limit_bytes=56 * 2**20
        ),
    )(*operands)


GELU_SLOPE = math.sqrt(2.0 / math.pi)
GELU_CUBE = 0.044715
ACROSS = (((1,), (1,)), ((), ()))
ALONG = (((0,), (0,)), ((), ()))


class Plane:
    def __init__(self, own, bufs, sems):
        self.own = own
        self.rows, self.partial, self.other, self.lands, self.sums, self.arrived = bufs
        self.x_send, self.x_recv, self.f_send, self.f_recv = sems[:4]
        self.c_send, self.c_recv, self.p_send, self.p_recv, self.first = sems[4:]
        self.tp = lax.axis_index("tp")
        self.sibling = {"head": 1 - lax.axis_index("head")}

    def member(self, m):
        tp = self.tp
        upper = lax.rem(lax.div(tp, 2) + lax.div(m, 2), 2)
        lower = lax.rem(lax.rem(tp, 2) + lax.rem(m, 2), 2)
        return {"tp": upper * 2 + lower}

    def remote(self, src, dst, send, recv, device):
        return pltpu.make_async_remote_copy(
            src_ref=src,
            dst_ref=dst,
            send_sem=send,
            recv_sem=recv,
            device_id=device,
            device_id_type=MESH,
        )

    def push(self, m):
        return self.remote(
            self.own, self.rows.at[0, m], self.x_send.at[m], self.x_recv.at[m], self.member(m)
        )

    def keep(self):
        return pltpu.make_async_copy(self.own, self.rows.at[0, 0], self.first)

    def forward(self, m):
        return self.remote(
            self.rows.at[0, m],
            self.rows.at[1, m],
            self.f_send.at[m],
            self.f_recv.at[m],
            self.sibling,
        )

    def cross(self, m):
        return self.remote(
            self.other.at[m], self.lands.at[m], self.c_send.at[m], self.c_recv.at[m], self.sibling
        )

    def home(self, m):
        return self.remote(
            self.sums.at[m],
            self.arrived.at[m],
            self.p_send.at[m],
            self.p_recv.at[m],
            self.member(m),
        )

    def begin(self):
        self.keep().start()
        enter([self.sibling] + [self.member(jnp.int32(m)) for m in range(1, PLANE)])
        for m in range(1, PLANE):
            self.push(jnp.int32(m)).start()

    def work(self, compute):
        def settle(m):
            self.cross(m).wait_recv()

            def add(rows):
                value = self.partial[m, rows] + self.lands[m, rows].astype(f32)
                self.sums[m, rows] = value.astype(bf16)

            by_rows(self.partial.shape[1], add)
            self.home(m).start()

        def step(m, carry):
            @pl.when(m == 0)
            def _():
                self.keep().wait()

            @pl.when(m > 0)
            def _():
                self.push(m).wait_recv()

            self.forward(m).start()
            self.partial[m] = compute(0, m)
            self.forward(m).wait_recv()
            self.other[m] = compute(1, m).astype(bf16)
            self.cross(m).start()

            @pl.when(m >= 2)
            def _():
                settle(m - 1)

            return carry

        lax.fori_loop(0, PLANE, step, 0)
        settle(jnp.int32(PLANE - 1))

    def finish(self, result):
        self.cross(jnp.int32(0)).wait_recv()
        for m in range(1, PLANE):
            self.home(jnp.int32(m)).wait_recv()

        def add(rows):
            value = self.partial[0, rows] + self.lands[0, rows].astype(f32)
            for m in range(1, PLANE):
                value = value + self.arrived[m, rows].astype(f32)
            result[rows] = value

        by_rows(result.shape[0], add)
        for m in range(PLANE):
            m = jnp.int32(m)
            self.forward(m).wait_send()
            self.cross(m).wait_send()
        for m in range(1, PLANE):
            m = jnp.int32(m)
            self.push(m).wait_send()
            self.home(m).wait_send()


def chunks(extent, step=256):
    return [slice(at, min(at + step, extent)) for at in range(0, extent, step)]


def gate_up_copies(gu_ref, gate_up, sem):
    blocks = gu_ref.shape[0]
    rows = gate_up.shape[1] // blocks
    return [
        pltpu.make_async_copy(
            gu_ref.at[block, part],
            gate_up.at[part, pl.ds(block * rows, rows)],
            sem.at[2 * block + part],
        )
        for block in range(blocks)
        for part in range(2)
    ]


def ffn_forward_kernel(own, gu_ref, halves_ref, group, saved_down, result, *scratch):
    rows, gate_up, down = scratch[:3]
    plane = Plane(own, (rows,) + scratch[3:8], scratch[8:17])
    weight_sem, group_sem, halves, half_send, half_recv, half_own, save_sem = scratch[17:]
    core = lax.axis_index("head")
    share, width = halves.shape[1:]
    copies = gate_up_copies(gu_ref, gate_up, weight_sem)
    copies.append(
        pltpu.make_async_copy(
            halves_ref.at[0, pl.ds(pl.multiple_of(core * share, 16), share)],
            halves.at[core],
            half_own,
        )
    )
    for copy in copies:
        copy.start()
    plane.begin()
    half = plane.remote(
        halves_ref.at[0, pl.ds(pl.multiple_of((1 - core) * share, 16), share)],
        halves.at[core],
        half_send,
        half_recv,
        plane.sibling,
    )
    half.start()
    for copy in copies:
        copy.wait()
    pltpu.make_async_remote_copy(
        src_ref=halves_ref.at[0, pl.ds(pl.multiple_of((1 - core) * share, 16), share)],
        dst_ref=halves.at[1 - core],
        send_sem=half_send,
        recv_sem=half_recv,
        device_id=plane.sibling,
        device_id_type=MESH,
    ).wait_recv()

    def join(at):
        down[at] = jnp.concatenate([halves[h, at] for h in range(2)], axis=1)

    by_rows(share, join, 32)
    keep_down = pltpu.make_async_copy(down, saved_down, save_sem)
    keep_down.start()

    def compute(side, m):
        tokens, total = rows[side, m], None
        for columns in chunks(share):
            gate = matmul(tokens, gate_up[0, :, columns])
            up = matmul(tokens, gate_up[1, :, columns])
            bend = jnp.tanh(GELU_SLOPE * (gate + GELU_CUBE * (gate * gate * gate)))
            inner = (0.5 * gate * (1.0 + bend) * up).astype(bf16)
            part = matmul(inner, down[columns])
            total = part if total is None else total + part
        return total

    plane.work(compute)
    save = pltpu.make_async_copy(rows, group, group_sem)
    save.start()
    plane.finish(result)
    save.wait()
    keep_down.wait()
    half.wait_send()


def ffn_backward_kernel(
    own, group, gu_ref, down_ref, result, grad_gu, grad_down, *scratch
):
    rows, gate_up, down = scratch[:3]
    plane = Plane(own, (rows,) + scratch[3:8], scratch[8:17])
    weight_sem, group_sem, saved, d_gate, d_up, inner = scratch[17:23]
    down_sem, turned, down_halves, half_send, half_recv, half_own = scratch[23:29]
    core = lax.axis_index("head")
    copies = gate_up_copies(gu_ref, gate_up, weight_sem)
    copies.append(pltpu.make_async_copy(down_ref, down, down_sem))
    for copy in copies:
        copy.start()
    load = pltpu.make_async_copy(group, saved, group_sem)
    load.start()
    plane.begin()
    for copy in copies:
        copy.wait()
    load.wait()

    def recompute(index, carry):
        side, m = lax.div(index, PLANE), lax.rem(index, PLANE)
        tokens = saved[side, m]
        gate = matmul(tokens, gate_up[0])
        up = matmul(tokens, gate_up[1])
        square = gate * gate
        bend = jnp.tanh(GELU_SLOPE * (gate + GELU_CUBE * (square * gate)))
        half = 0.5 * (1.0 + bend)
        value = gate * half
        slope = half + (0.5 * GELU_SLOPE) * gate * (1.0 - bend * bend) * (
            1.0 + (3.0 * GELU_CUBE) * square
        )
        inner[side, m] = (value * up).astype(bf16)
        d_gate[side, m] = (slope * up).astype(bf16)
        d_up[side, m] = value.astype(bf16)
        return carry

    lax.fori_loop(0, 2 * PLANE, recompute, 0)

    def compute(side, m):
        d_inner = lax.dot_general(rows[side, m], down[...], ACROSS, preferred_element_type=f32)
        gate = (d_inner * d_gate[side, m].astype(f32)).astype(bf16)
        up = (d_inner * d_up[side, m].astype(f32)).astype(bf16)
        d_gate[side, m] = gate
        d_up[side, m] = up
        return lax.dot_general(
            gate, gate_up[0], ACROSS, preferred_element_type=f32
        ) + lax.dot_general(up, gate_up[1], ACROSS, preferred_element_type=f32)

    plane.work(compute)
    width = rows.shape[-1]
    step = width // 3

    by_planes = len(grad_gu.shape) == 4
    sides = scratch[29] if by_planes else grad_gu

    def tall(ref, columns=slice(None)):
        value = ref[:, :, :, columns]
        return value.reshape(-1, value.shape[-1])

    @pl.loop(0, 3)
    def _(index):
        at = pl.ds(pl.multiple_of(index * step, step), step)
        tokens = tall(saved, at)
        for part, other in enumerate((d_gate, d_up)):
            sides[part, at] = lax.dot_general(
                tokens, tall(other), ALONG, preferred_element_type=f32
            ).astype(bf16)
        turned[at] = lax.dot_general(
            tall(rows, at), tall(inner), ALONG, preferred_element_type=f32
        ).astype(bf16)

    stores = []
    if by_planes:
        for plane_at in range(grad_gu.shape[0]):
            for part in range(2):
                height = grad_gu.shape[2]
                copy = pltpu.make_async_copy(
                    sides.at[part, pl.ds(plane_at * height, height)],
                    grad_gu.at[plane_at, part],
                    scratch[30].at[2 * plane_at + part],
                )
                copy.start()
                stores.append(copy)
    half_width = down_halves.shape[2]
    for h in range(2):
        down_halves[h] = turned[h * half_width : (h + 1) * half_width].T
    half = plane.remote(
        down_halves.at[1 - core], grad_down.at[core], half_send, half_recv, plane.sibling
    )
    half.start()
    stay = pltpu.make_async_copy(down_halves.at[core], grad_down.at[core], half_own)
    stay.start()
    plane.finish(result)
    half.wait()
    stay.wait()
    for copy in stores:
        copy.wait()


def ffn(own, weights, ident, planes, group=None):
    gate_up, down = weights
    tokens, width = own.shape
    blocks, _, _, share = gate_up.shape
    vmem, dma = pltpu.VMEM, pltpu.SemaphoreType.DMA
    scratch = [
        vmem((2, PLANE, tokens, width), bf16),
        vmem((2, width, share), bf16),
        vmem((share, width), bf16),
        vmem((PLANE, tokens, width), f32),
    ]
    scratch += [vmem((PLANE, tokens, width), bf16)] * 4
    scratch += [dma((PLANE,))] * 8 + [dma, dma((2 * blocks,)), dma]
    here, there = pl.BlockSpec(memory_space=pltpu.VMEM), pl.BlockSpec(memory_space=pl.ANY)
    shape = jax.ShapeDtypeStruct
    summed = shape((tokens, width), f32)
    if group is None:
        kernel, operands = ffn_forward_kernel, (own, gate_up, down)
        in_specs, out_specs = [here, there, there], [there, there, here]
        out_shape = [
            shape((2, PLANE, tokens, width), bf16),
            shape((share, width), bf16),
            summed,
        ]
        scratch += [vmem((2, share, width // 2), bf16)] + [dma] * 4
    else:
        kernel, operands = ffn_backward_kernel, (own, group, gate_up, down)
        by_planes = width // planes % 16 == 0
        sides = (2, width, share)
        in_specs = [here, there, there, there]
        out_specs = [here, there if by_planes else here, there]
        out_shape = [
            summed,
            shape((planes, 2, width // planes, share) if by_planes else sides, bf16),
            shape((2, share, width // 2), bf16),
        ]
        scratch += [vmem((2, PLANE, tokens, width), bf16)]
        scratch += [vmem((2, PLANE, tokens, share), bf16)] * 3
        scratch += [dma, vmem((width, share), bf16), vmem((2, share, width // 2), bf16)]
        scratch += [dma] * 3
        if by_planes:
            scratch += [vmem(sides, bf16), dma((2 * planes,))]
    return pl.pallas_call(
        kernel,
        out_shape=out_shape,
        in_specs=in_specs,
        out_specs=out_specs,
        scratch_shapes=scratch,
        cost_estimate=LIGHT,
        compiler_params=pltpu.CompilerParams(
            collective_id=ident, has_side_effects=True, vmem_limit_bytes=60 * 2**20
        ),
    )(*operands)


def exact(left, right, dims=(((1,), (0,)), ((), ()))):
    return lax.dot_general(
        left, right, dims, precision=finest_precision, preferred_element_type=f32
    )


def update_kernel(sizes, counts, *refs):
    cores, planes, members = sizes
    rest = list(refs)
    take = lambda number: [rest.pop(0) for _ in range(number)]
    plain = [take(number) for number in counts]
    sides = take(cores)
    moments_in, weights_in, weights_out, moments_out = (take(4) for _ in range(4))
    moment, weight, gram, land, factor = (take(4) for _ in range(5))
    pieces, arrived = take(2)
    load_sem, store_sem, gram_send, gram_recv, factor_send, factor_recv = take(6)
    gu_send, gu_recv, gu_own = take(3)
    core, _, tp = (lax.axis_index(axis) for axis in EVERY)
    sibling = {"head": 1 - core}
    order = (0, 1, 3, 2)
    loads = {}
    for k in range(4):
        for part, source, target in ((0, moments_in, moment), (1, weights_in, weight)):
            copy = pltpu.make_async_copy(source[k], target[k], load_sem.at[part, k])
            copy.start()
            loads[part, k] = copy
    group = []
    for step in range(1, cores * members):
        far = lax.rem(core + step // members, cores), lax.rem(tp + step % members, members)
        group.append((dict(zip(GROUP, far)), linear(far, (cores, members))))
    enter([device for device, _ in group])
    rows = moment[2].shape[1]
    for part in range(cores):
        for j in range(members):
            for layer in range(cores):
                at = (part * members + j) * rows
                pieces[part * members + j, layer * rows : (layer + 1) * rows] = sides[layer][
                    at : at + rows
                ]
    if pieces.shape[1] > cores * rows:
        for piece in range(cores * members):
            pieces[piece, cores * rows :] = jnp.zeros(
                (pieces.shape[1] - cores * rows, pieces.shape[2]), bf16
            )
    me = linear((core, tp), (cores, members))
    moves, stores = [], []

    def send(src, dst, send_sem, recv_sem, device):
        copy = pltpu.make_async_remote_copy(
            src_ref=src,
            dst_ref=dst,
            send_sem=send_sem,
            recv_sem=recv_sem,
            device_id=device,
            device_id_type=MESH,
        )
        copy.start()
        return copy

    for step, (device, index) in enumerate(group):
        moves.append(
            send(pieces.at[index], arrived.at[me], gu_send.at[step], gu_recv.at[step], device)
        )
    own = pltpu.make_async_copy(pieces.at[me], arrived.at[me], gu_own)
    own.start()

    def store(part, k):
        source, target = (moment, moments_out) if part == 0 else (weight, weights_out)
        copy = pltpu.make_async_copy(source[k], target[k], store_sem.at[part, k])
        copy.start()
        stores.append(copy)

    def gram_of(k):
        def one(layer, carry):
            gram[k][layer] = exact(moment[k][layer], moment[k][layer], ACROSS)
            return carry

        lax.fori_loop(0, cores, one, 0)
        return send(
            gram[k].at[1 - core], land[k], gram_send.at[k], gram_recv.at[k], sibling
        )

    def unit(size):
        down = lax.broadcasted_iota(jnp.int32, (size, size), 0)
        return (down == lax.broadcasted_iota(jnp.int32, (size, size), 1)).astype(f32)

    def orthogonal(members_of):
        for k in members_of:
            total = gram[k][core] + land[k][...]
            one = unit(total.shape[0])
            trace = jnp.sum(jnp.sum(total * one, axis=1, keepdims=True), axis=0, keepdims=True)
            scale = 1.0 / (jnp.sqrt(trace) + 1e-07)
            land[k][...] = total * (scale * scale)
            factor[k][core] = one * scale

        def polynomial(present):
            square = exact(present, present)
            return newton_one * unit(present.shape[0]) + newton_two * present + (
                newton_three * square
            )

        def step(_, carry):
            for k in members_of:
                present = land[k][...]
                poly = polynomial(present)
                factor[k][core] = exact(poly, factor[k][core])
                land[k][...] = exact(exact(poly, present), poly)
            return carry

        lax.fori_loop(0, NS_ITERS - 1, step, 0)
        for k in members_of:
            factor[k][core] = exact(polynomial(land[k][...]), factor[k][core])
        return [
            send(factor[k].at[core], factor[k].at[core], factor_send.at[k], factor_recv.at[k], sibling)
            for k in members_of
        ]

    def apply(k):
        columns = weight[k].shape[2] * cores
        rate = muon_rate * muon_scale * math.sqrt(columns)

        def one(layer, carry):
            weight[k][layer] = weight[k][layer] * (1.0 - muon_rate * muon_shrink) - rate * exact(
                factor[k][layer], moment[k][layer]
            )
            return carry

        lax.fori_loop(0, cores, one, 0)
        store(1, k)

    def arrive(copies):
        for copy in copies:
            copy.wait_recv()

    sent = []
    for index, k in enumerate(order[:3]):
        loads[0, k].wait()
        height = moment[k].shape[1]
        for layer in range(cores):
            if len(plain[index]) == 1:
                gradient = plain[index][0][layer * height : (layer + 1) * height]
            else:
                gradient = plain[index][layer][...].astype(f32)
            moment[k][layer] = muon_decay * moment[k][layer] + gradient
        store(0, k)
        sent.append(gram_of(k))
    arrive(sent)
    crossed = orthogonal(order[:3])
    sent += crossed
    own.wait()
    for copy in moves:
        copy.wait_recv()
    loads[0, 2].wait()
    half = planes // cores
    block = arrived.shape[2] // half
    for layer in range(cores):
        cut = [
            arrived[
                c * members + j,
                layer * rows : (layer + 1) * rows,
                k * block : (k + 1) * block,
            ].astype(f32)
            for c in range(cores)
            for k in range(half)
            for j in range(members)
        ]
        moment[2][layer] = muon_decay * moment[2][layer] + jnp.concatenate(cut, axis=1)
    store(0, 2)
    last = gram_of(2)
    sent.append(last)
    arrive(crossed)
    for k in range(4):
        loads[1, k].wait()
    for k in order[:3]:
        apply(k)
    arrive([last])
    crossed = orthogonal(order[3:])
    sent += crossed
    arrive(crossed)
    apply(2)
    for copy in moves + sent:
        copy.wait_send()
    for copy in stores:
        copy.wait()


def update(gradients, sides, moments, weights, ident):
    sizes = tuple(lax.axis_size(axis) for axis in EVERY)
    cores, planes, members = sizes
    vmem, dma = pltpu.VMEM, pltpu.SemaphoreType.DMA
    layers, rows, columns = moments[2].shape
    piece = (
        cores * members,
        -(-layers * rows // 16) * 16,
        columns // (cores * members),
    )
    shapes = [m.shape for m in moments]
    square = [(s[1], s[1]) for s in shapes]
    scratch = [vmem(s, f32) for s in shapes] * 2
    scratch += [vmem((layers,) + s, f32) for s in square]
    scratch += [vmem(s, f32) for s in square]
    scratch += [vmem((layers,) + s, f32) for s in square]
    scratch += [vmem(piece, bf16)] * 2
    scratch += [dma((2, 4))] * 2 + [dma((4,))] * 4
    scratch += [dma((cores * members - 1,))] * 2 + [dma]
    here, there = pl.BlockSpec(memory_space=pltpu.VMEM), pl.BlockSpec(memory_space=pl.ANY)
    operands = sum(gradients, []) + sides
    return pl.pallas_call(
        partial(update_kernel, sizes, [len(g) for g in gradients]),
        out_shape=[jax.ShapeDtypeStruct(s, f32) for s in shapes] * 2,
        in_specs=[here] * len(operands) + [there] * 8,
        out_specs=[there] * 8,
        scratch_shapes=scratch,
        compiler_params=pltpu.CompilerParams(
            collective_id=ident, has_side_effects=True, vmem_limit_bytes=56 * 2**20
        ),
    )(*operands, *moments, *weights)


def padded(array, multiple=16):
    extra = -array.shape[-2] % multiple
    if extra == 0:
        return array
    return jnp.pad(array, [(0, 0)] * (array.ndim - 2) + [(0, extra), (0, 0)])


def rms_norm(values, norm_gain):
    return (
        values * lax.rsqrt(jnp.mean(values * values, axis=-1, keepdims=True) + norm_eps) * norm_gain
    )


def rope_tables(positions, head_dim):
    half_dim = head_dim // 2
    frequency = jnp.exp(
        jnp.arange(half_dim, dtype=jnp.float32) * (-2.0 * math.log(rope_base) / head_dim)
    )
    angles = positions.astype(jnp.float32)[:, None] * frequency[None, :]
    return (jnp.cos(angles), jnp.sin(angles))


def matmul(left, right):
    return jnp.dot(left, right, preferred_element_type=f32)


def body(
    inputs,
    cotangent,
    teacher,
    segments,
    valid_mask,
    w_qkv,
    w_out,
    w_gu,
    w_down,
    norm_gains,
    mom_qkv,
    mom_out,
    mom_gu,
    mom_down,
    gain_first,
    gain_second,
):
    cores = lax.axis_size("head")
    planes = lax.axis_size("zd")
    seq_devices = planes * PLANE
    core = lax.axis_index("head")
    seq_place = lax.axis_index("zd") * PLANE + lax.axis_index("tp")
    half_seqs, stretch_len = inputs.shape[:2]
    tokens = half_seqs * stretch_len
    all_seqs = half_seqs * cores
    seq_length = stretch_len * seq_devices
    reach = -(-WINDOW // stretch_len)
    key_len = (reach + 1) * stretch_len
    qkv_rows, qkv_cols = w_qkv.shape[1:]
    out_rows, out_cols = w_out.shape[1:]
    gu_rows = w_gu.shape[1]
    ff_block = w_down.shape[1]
    share = FF // (cores * PLANE)
    half_planes = planes // cores
    gain_cols = norm_gains.shape[-1]
    gain_len = gain_cols * seq_devices
    lanes = -(-gain_cols // 128) * 128

    packet = jnp.zeros((8, lanes), f32)
    packet = packet.at[:LAYERS, :gain_cols].set(norm_gains[:, 0].astype(bf16).astype(f32))
    packet = packet.at[LAYERS, 0].set(jnp.sum(valid_mask.astype(f32)))
    gu_pieces, packet = lax.optimization_barrier((exchanged_rows(w_gu, 1), packet))
    w_mixed, w_project, packets, *later = start(w_qkv, w_out, packet, 0)
    attn_weights = [w_mixed, w_project]
    gu_pieces = gu_pieces[:, : LAYERS * gu_rows].reshape(cores * PLANE, LAYERS, gu_rows, share)
    packets = packets.reshape(cores, seq_devices, 8, lanes)
    valid_count = jnp.sum(packets[:, :, LAYERS, 0])
    gain_rows = [
        packets[:, :, layer, :gain_cols].reshape(cores, gain_len) for layer in range(LAYERS)
    ]

    def gate_up_rows(layer):
        pieces = gu_pieces[:, layer].reshape(2, PLANE * gu_rows, share)
        pieces = lax.all_gather(pieces, "zd", axis=0)
        if PLANE * gu_rows % 16:
            pieces = pieces.transpose(1, 0, 2, 3).reshape(1, 2, D, share)
        return pieces

    def down_rows(layer):
        rows = w_down[layer : layer + 1].astype(bf16)
        return lax.all_gather(rows, "zd", axis=1, tiled=True)

    full = [(gate_up_rows(0), down_rows(0))] + [None] * (LAYERS - 1)

    own_places = seq_place * stretch_len + jnp.arange(stretch_len, dtype=jnp.int32)
    key_places = (seq_place - reach) * stretch_len + jnp.arange(key_len, dtype=jnp.int32)
    cosine_table, sine_table = rope_tables(own_places, HD)
    own_rows = lax.dynamic_slice_in_dim(segments, core * half_seqs, half_seqs, 0)
    own_segments = lax.dynamic_slice_in_dim(own_rows, seq_place * stretch_len, stretch_len, 1)
    padded_segments = jnp.pad(own_rows, ((0, 0), (reach * stretch_len, 0)), constant_values=-1)
    key_segments = lax.dynamic_slice_in_dim(padded_segments, seq_place * stretch_len, key_len, 1)
    spacing = own_places[:, None] - key_places[None, :]
    allowed = (spacing >= 0) & (spacing < WINDOW) & (key_places[None, :] >= 0)
    allowed = allowed[None] & (own_segments[:, :, None] == key_segments[:, None, :])

    tables = [jnp.tile(t, (half_seqs, 1)) for t in (cosine_table, sine_table)]
    bias = jnp.where(allowed, 0.0, -1e30).astype(f32)

    saved, previous = [], None
    base = inputs.reshape(tokens, D)
    for layer in range(LAYERS):
        weights = list(attn_weights)
        hidden, normed, mixed, queries, keyvals, attended, projected, half, normed_ffn = attn_forward(
            base, weights, gain_rows[layer], tables, bias, planes, reach, 3 + layer, previous
        )
        ffn_share = full[layer]
        if layer + 1 < LAYERS:
            gu_pieces, w_down, later, attended = lax.optimization_barrier(
                (gu_pieces, w_down, later, attended)
            )
            attn_weights = later_weights(later, w_qkv, w_out, layer + 1, 2 + 20 * layer)
            full[layer + 1] = (gate_up_rows(layer + 1), down_rows(layer + 1))
            normed_ffn, *attn_weights = lax.optimization_barrier((normed_ffn, *attn_weights))
        group_normed, whole_down, down_out = ffn(normed_ffn, ffn_share, 5 + layer, planes)
        full[layer] = (weights, (ffn_share[0], whole_down))
        saved.append(
            (
                [hidden, mixed, queries, keyvals, projected, half],
                [normed, attended],
                group_normed,
                down_out,
            )
        )
        base, previous = half, (down_out, gain_rows[layer])

    output, post_ffn_back = jax.vjp(rms_norm, down_out, gain_rows[-1][1, D : 2 * D])
    output = base + output
    target_gap = output - teacher.reshape(tokens, D).astype(f32)
    valid_weight = valid_mask.astype(f32).reshape(tokens, 1)
    square_sum = jnp.sum(valid_weight * target_gap * target_gap)
    loss_weight = float(all_seqs * seq_length * D // 4)
    grad_hidden = (
        cotangent.reshape(tokens, D).astype(f32)
        + 2.0 * loss_weight / (valid_count * D) * valid_weight * target_gap
    )
    d_down, d_post_ffn = post_ffn_back(grad_hidden)
    d_down, d_post_ffn = d_down.astype(bf16), d_post_ffn[None]

    tiled = ff_block % 16 == 0
    attn_acts = [None] * LAYERS
    down_grads = [None] * LAYERS
    gain_grads = [None] * LAYERS
    gu_sums = [None] * LAYERS
    for layer in reversed(range(LAYERS)):
        kept, (normed, attended), group_normed, _ = saved[layer]
        weights, ffn_share = full[layer]
        d_normed_ffn, grad_gu, grad_down = ffn(
            d_down, ffn_share, 9 + layer, planes, group_normed
        )
        if layer == 0 and tiled:
            first_down = grad_down.reshape(planes, ff_block, out_cols)
        else:
            down_grads[layer] = lax.psum_scatter(
                grad_down.reshape(planes * ff_block, out_cols),
                "zd",
                scatter_dimension=0,
                tiled=True,
            )
        if len(grad_gu.shape) == 3:
            grad_gu = grad_gu.reshape(2, planes, PLANE * gu_rows, share).transpose(1, 0, 2, 3)
        gu_sums[layer] = lax.psum_scatter(
            grad_gu.reshape(-1, share), "zd", scatter_dimension=0, tiled=True
        )
        earlier = (saved[layer - 1][3], gain_rows[layer - 1]) if layer > 0 else None
        grad_hidden, d_mixed, d_projected, gain_grads[layer], *d_rest = attn_backward(
            d_normed_ffn,
            grad_hidden,
            kept,
            weights,
            gain_rows[layer],
            tables,
            bias,
            planes,
            reach,
            17 + layer,
            earlier,
        )
        gain_grads[layer] = gain_grads[layer].at[1:, D : 2 * D].set(d_post_ffn)
        if layer > 0:
            d_down, d_post_ffn = d_rest
        attn_acts[layer] = [normed, d_mixed, attended, d_projected]
    attn_acts[0][1], gu_sums[1:], down_grads[1:] = lax.optimization_barrier(
        (attn_acts[0][1], gu_sums[1:], down_grads[1:])
    )

    packet = jnp.stack(gain_grads, axis=1).reshape(cores, LAYERS, planes, PLANE, gain_cols)
    packet = packet.transpose(0, 3, 2, 1, 4)
    packet = jnp.pad(packet, [(0, 0)] * 3 + [(0, 8 - LAYERS), (0, lanes - gain_cols)])
    packet = packet.at[:, :, :, LAYERS, 0].set(square_sum)
    packet = packet.reshape(cores, PLANE, planes * 8, lanes)
    down = first_down if tiled else None
    grad_qkv, grad_out, packet, *summed_down = collect(sum(attn_acts, []), packet, down, 19)
    if tiled:
        (down_grads[0],) = summed_down
    mse_loss = packet[LAYERS, 0] / (valid_count * D)
    gain_grad = packet[:LAYERS, None, :gain_cols]

    outcome = update(
        [[grad_qkv], [grad_out], down_grads],
        gu_sums,
        (mom_qkv, mom_out, mom_gu, mom_down),
        (w_qkv, w_out, w_gu, w_down),
        15,
    )
    new_weights, moments = outcome[:4], outcome[4:]
    gain_first_new = beta_one * gain_first + (1.0 - beta_one) * gain_grad
    gain_second_new = beta_two * gain_second + (1.0 - beta_two) * gain_grad * gain_grad
    gains_new = norm_gains - adam_rate * (gain_first_new / (1.0 - beta_one**STEP)) / (
        jnp.sqrt(gain_second_new / (1.0 - beta_two**STEP)) + adam_epsilon
    )
    return (
        mse_loss,
        output.reshape(inputs.shape),
        grad_hidden.reshape(inputs.shape),
        *new_weights,
        *moments,
        gains_new,
        gain_first_new,
        gain_second_new,
    )


def solution(mesh):
    cores, length = mesh.devices.shape
    split = Mesh(mesh.devices.reshape(cores, length // PLANE, PLANE), EVERY)
    stream = P("head", SEQ, None)
    matrix = P(None, SEQ, "head")
    gains = P(None, "head", SEQ)
    return jax.shard_map(
        body,
        mesh=split,
        in_specs=(stream, stream, stream, P(), P("head", SEQ))
        + (matrix,) * 4
        + (gains,)
        + (matrix,) * 4
        + (gains,) * 2,
        out_specs=(P(), stream, stream) + (matrix,) * 8 + (gains,) * 3,
        check_vma=False,
    )
```
